128 devices in a mesh: ctx: 16 (over z_hi, x, core), fsdp: 8 (over z_lo, y).
Axes of the slice: x: 4, y: 4, z: 4 (z_hi: 2, z_lo: 2; z = z_hi * 2 + z_lo), core: 2. Of those that a mesh axis runs over, the one named last changes fastest.
Arguments:
- layer_input: bfloat16 [8, 2048, 1536], P('fsdp', 'ctx'), may hold values from -6 to 6
- segments: int32 [8, 2048], P('fsdp', 'ctx'), may hold values from 0 to 3, as said below
- positions: int32 [8, 2048], P('fsdp', 'ctx'), may hold values from 0 to 4094, as said below
- attn_norm: bfloat16 [1536], P('fsdp'), may hold values from 0.099609375 to 1.8984375
- q_weight: bfloat16 [1536, 1536], P('fsdp'), may hold values from -0.15625 to 0.15625
- q_bias: bfloat16 [1536], P('fsdp'), may hold values from -3 to 3
- k_weight: bfloat16 [1536, 256], P('fsdp'), may hold values from -0.15625 to 0.15625
- k_bias: bfloat16 [256], P('fsdp'), may hold values from -3 to 3
- v_weight: bfloat16 [1536, 256], P('fsdp'), may hold values from -0.15625 to 0.15625
- v_bias: bfloat16 [256], P('fsdp'), may hold values from -3 to 3
- o_weight: bfloat16 [1536, 1536], P('fsdp'), may hold values from -1.25 to 1.25
- mlp_norm: bfloat16 [1536], P('fsdp'), may hold values from 0.099609375 to 1.8984375
- gate_weight: bfloat16 [1536, 8960], P('fsdp'), may hold values from -0.15625 to 0.15625
- up_weight: bfloat16 [1536, 8960], P('fsdp'), may hold values from -0.15625 to 0.15625
- down_weight: bfloat16 [8960, 1536], P('fsdp'), may hold values from -0.0625 to 0.0625
- out_cotangent: bfloat16 [8, 2048, 1536], P('fsdp', 'ctx'), may hold values from -6 to 6
Outputs:
- layer_output: bfloat16 [8, 2048, 1536], P('fsdp', 'ctx')
- input_grad: float32 [8, 2048, 1536], P('fsdp', 'ctx')
- attn_norm_grad: float32 [1536], P('fsdp')
- q_weight_grad: float32 [1536, 1536], P('fsdp')
- q_bias_grad: float32 [1536], P('fsdp')
- k_weight_grad: float32 [1536, 256], P('fsdp')
- k_bias_grad: float32 [256], P('fsdp')
- v_weight_grad: float32 [1536, 256], P('fsdp')
- v_bias_grad: float32 [256], P('fsdp')
- o_weight_grad: float32 [1536, 1536], P('fsdp')
- mlp_norm_grad: float32 [1536], P('fsdp')
- gate_weight_grad: float32 [1536, 8960], P('fsdp')
- up_weight_grad: float32 [1536, 8960], P('fsdp')
- down_weight_grad: float32 [8960, 1536], P('fsdp')
The draws below stay inside these ranges and needn't reach their ends.
Inputs may be any that keep to these rules, and one draw needn't show every extreme that they name: `segments`: in order of place, each sequence holds documents 1, 2 and 3, then at least one padding token (0) at its end; document 1 ends and document 2 begins within the first 64 places, document 2 ends within the last 64 places, padding takes at most 32 places. Within each document positions rise by one from place to place; document 1 starts at 0, documents 2 and 3 anywhere from 0 to 2047; a padding token's position is its place plus 2047.
All inputs are finite; a program needn't handle non-finite values.
Results may differ from the reference program's by a relative error of at most 0.025.
Values may be sent and summed in bfloat16 or wider, within the bound.
A program may use at most 320 MiB of HBM per device.

```python
import jax
import jax.numpy as jnp
from jax import lax

D = 1536
HEADS = 12
KV_HEADS = 2
HD = 128
FF = 8960
TOK_DEV = 128
SEQ = 2048
SEQS = 8
Q_WIDTH = 1536
KV_WIDTH = 256
N_CTX = 16


def document_layout(key):

    def single_row(row_key):
        pieces = jax.random.split(row_key, 4)
        start_long = jax.random.randint(pieces[0], (), 1, TOK_DEV // 2 + 1)
        end_long = jax.random.randint(pieces[1], (), SEQ - TOK_DEV // 2, SEQ - TOK_DEV // 4)
        padding = jax.random.randint(pieces[2], (), 1, TOK_DEV // 4 + 1)
        offsets = jax.random.randint(pieces[3], (3,), 0, 2048)
        location = jnp.arange(SEQ, dtype=jnp.int32)
        finish = SEQ - padding
        segment = jnp.where(location < start_long, 1, jnp.where(location < end_long, 2, jnp.where(location < finish, 3, 0))).astype(jnp.int32)
        position = jnp.where(segment == 1, location, jnp.where(segment == 2, offsets[1] + location - start_long, jnp.where(segment == 3, offsets[2] + location - end_long, location + 2047))).astype(jnp.int32)
        device_count = SEQ // TOK_DEV
        half_block = TOK_DEV // 2
        device = location // TOK_DEV
        within = location % TOK_DEV
        place = jnp.where(within < half_block, device * half_block + within, (2 * device_count - 1 - device) * half_block + within - half_block).astype(jnp.int32)
        return (segment[place], position[place])
    return jax.vmap(single_row)(jax.random.split(key, SEQS))


def draw_segments(key, part):
    shared = document_layout(key)
    return shared[0]


def draw_positions(key, part):
    shared = document_layout(key)
    return shared[1]


def level_of(rng, dims, cuts, least, largest):
    level, own = 1.0, jax.random.fold_in(rng, 6)
    for dim, shards_of in cuts:
        draws = jnp.exp(jax.random.uniform(jax.random.fold_in(own, dim), (shards_of,), jnp.float32, least / len(cuts), largest / len(cuts)))
        level = level * jnp.repeat(draws, dims[dim] // shards_of).reshape([-1 if axis == dim else 1 for axis in range(len(dims))])
    return level


def bell_draw(own_key, shape, scale, bound, cuts=(), kind=jnp.bfloat16):
    loudness = level_of(own_key, shape, cuts, -0.22, 0.18) if cuts else 1.0
    values = jax.random.normal(own_key, shape, jnp.float32) * scale * loudness
    return jnp.minimum(jnp.maximum(values, -bound), bound).astype(kind)


def setup_inputs(seed: int = 0) -> dict:
    seeds = jax.random.split(jax.random.key(seed), 17)
    return {
        "layer_input": bell_draw(seeds[0], (SEQS, SEQ, D), 1.0, 6.0, ((0, 8), (1, 16))),
        "segments": draw_segments(jax.random.fold_in(seeds[16], 71), 0),
        "positions": draw_positions(jax.random.fold_in(seeds[16], 71), 0),
        "attn_norm": jnp.clip(1.0 + 0.18 * jax.random.normal(seeds[3], (D,), jnp.float32), 0.099609375, 1.8984375).astype(jnp.bfloat16),
        "q_weight": bell_draw(seeds[4], (D, Q_WIDTH), D ** -0.5, 0.15625, ((0, 8),)),
        "q_bias": bell_draw(seeds[5], (Q_WIDTH,), 0.5, 3.0, ((0, 8),)),
        "k_weight": bell_draw(seeds[6], (D, KV_WIDTH), D ** -0.5, 0.15625, ((0, 8),)),
        "k_bias": bell_draw(seeds[7], (KV_WIDTH,), 0.5, 3.0, ((0, 8),)),
        "v_weight": bell_draw(seeds[8], (D, KV_WIDTH), D ** -0.5, 0.15625, ((0, 8),)),
        "v_bias": bell_draw(seeds[9], (KV_WIDTH,), 0.5, 3.0, ((0, 8),)),
        "o_weight": bell_draw(seeds[10], (Q_WIDTH, D), (Q_WIDTH // 64) ** -0.5, 1.25, ((0, 8),)),
        "mlp_norm": jnp.clip(1.0 + 0.18 * jax.random.normal(seeds[11], (D,), jnp.float32), 0.099609375, 1.8984375).astype(jnp.bfloat16),
        "gate_weight": bell_draw(seeds[12], (D, FF), D ** -0.5, 0.15625, ((0, 8),)),
        "up_weight": bell_draw(seeds[13], (D, FF), D ** -0.5, 0.15625, ((0, 8),)),
        "down_weight": bell_draw(seeds[14], (FF, D), FF ** -0.5, 0.0625, ((0, 8),)),
        "out_cotangent": bell_draw(seeds[15], (SEQS, SEQ, D), 1.0, 6.0, ((0, 8), (1, 16))),
    }


EPSILON = 1e-06
THETA = 1000000.0

@jax.custom_vjp
def low(v):
    return lax.optimization_barrier(v.astype(jnp.bfloat16)).astype(jnp.float32)

@jax.custom_vjp
def low_back(v):
    return v

def low_keep(v):
    return (low(v), None)

def low_pass(kept, grad):
    return (grad,)

def back_keep(v):
    return (v, None)

def back_low(kept, grad):
    return (low(grad),)
low.defvjp(low_keep, low_pass)
low_back.defvjp(back_keep, back_low)

def matmul(left, right):
    return jnp.dot(left, right, precision=lax.Precision.HIGHEST, preferred_element_type=jnp.float32)

def dealt_places(length):
    per_device = length // N_CTX
    half_block = per_device // 2
    stored = jnp.arange(length, dtype=jnp.int32)
    device = stored // per_device
    within = stored % per_device
    return jnp.where(within < half_block, device * half_block + within, (2 * N_CTX - 1 - device) * half_block + within - half_block).astype(jnp.int32)

def rope_tables(position, head_dim):
    freqs = THETA ** (-jnp.arange(0, head_dim, 2).astype(jnp.float32) / head_dim)
    angles = position.astype(jnp.float32)[:, None] * freqs[None, :]
    return (jnp.cos(angles), jnp.sin(angles))

def rotate(values, cosine, sine):
    middle = values.shape[-1] // 2
    front = values[..., :middle]
    behind = values[..., middle:]
    cos_head = cosine[:, None, :]
    sin_head = sine[:, None, :]
    return jnp.concatenate([front * cos_head - behind * sin_head, behind * cos_head + front * sin_head], axis=-1)

def block_forward(params, inputs, segment, position):
    gain_one, weight_q, bias_q, weight_k, bias_k, weight_v, bias_v, weight_o, gain_two, weight_gate, weight_up, weight_down = params
    length = inputs.shape[0]
    group_size = HEADS // KV_HEADS
    scale_one = lax.rsqrt(lax.optimization_barrier(jnp.mean(inputs * inputs, axis=-1, keepdims=True)) + EPSILON)
    normed_in = low(inputs * scale_one * gain_one)
    query = low_back(matmul(normed_in, weight_q) + bias_q)
    keyproj = low_back(matmul(normed_in, weight_k) + bias_k)
    valproj = low(low_back(matmul(normed_in, weight_v) + bias_v))
    cosine, sine = rope_tables(position, HD)
    query_rot = low(rotate(query.reshape(length, HEADS, HD), cosine, sine))
    key_rot = low(rotate(keyproj.reshape(length, KV_HEADS, HD), cosine, sine))
    query_group = query_rot.reshape(length, KV_HEADS, group_size, HD)
    raw_scores = low_back(jnp.einsum('qcgd,kcd->cgqk', query_group, key_rot, precision=lax.Precision.HIGHEST))
    scores = raw_scores * HD ** (-0.5)
    places = dealt_places(length)
    allowed = (places[None, :] <= places[:, None]) & (segment[None, :] == segment[:, None]) & (segment[:, None] > 0)
    masked = jnp.where(allowed, scores, -1e+30)
    highest = lax.optimization_barrier(jnp.max(masked, axis=-1, keepdims=True))
    exponent = jnp.where(allowed, jnp.exp(masked - highest), 0.0)
    totals = lax.optimization_barrier(jnp.sum(exponent, axis=-1, keepdims=True))
    totals = jnp.where(totals > 0.5, totals, 1.0)
    probability = low(exponent / totals)
    value_heads = valproj.reshape(length, KV_HEADS, HD)
    attended = jnp.einsum('cgqk,kcd->qcgd', probability, value_heads, precision=lax.Precision.HIGHEST)
    attended = low(low_back(attended.reshape(length, HEADS * HD)))
    middle_state = inputs + low_back(matmul(attended, weight_o))
    scale_two = lax.rsqrt(lax.optimization_barrier(jnp.mean(middle_state * middle_state, axis=-1, keepdims=True)) + EPSILON)
    normed_mid = low(middle_state * scale_two * gain_two)
    gate_pre = low_back(matmul(normed_mid, weight_gate))
    up_pre = low_back(matmul(normed_mid, weight_up))
    activation = low(jax.nn.silu(gate_pre) * up_pre)
    return middle_state + low_back(matmul(activation, weight_down))

def reference(layer_input, segments, positions, attn_norm, q_weight, q_bias, k_weight, k_bias, v_weight, v_bias, o_weight, mlp_norm, gate_weight, up_weight, down_weight, out_cotangent):
    params = tuple((weight.astype(jnp.float32) for weight in (attn_norm, q_weight, q_bias, k_weight, k_bias, v_weight, v_bias, o_weight, mlp_norm, gate_weight, up_weight, down_weight)))
    zero_grads = tuple((jnp.zeros(weight.shape, jnp.float32) for weight in params))

    def per_sequence(carry, item):
        rows, segment, position, cotangent = item
        inputs = rows.astype(jnp.float32)
        keep_mask = (segment > 0).astype(jnp.float32)[:, None]

        def forward_fn(weights, values):
            return block_forward(weights, values, segment, position)
        result, pullback = jax.vjp(forward_fn, params, inputs)
        param_grads, input_grads = pullback(cotangent.astype(jnp.float32) * keep_mask)
        summed = tuple((first + second for first, second in zip(carry, param_grads)))
        return (summed, (result.astype(jnp.bfloat16), input_grads))
    grads, (outputs, input_grads) = lax.scan(per_sequence, zero_grads, (layer_input, segments, positions, out_cotangent))
    return (outputs, input_grads, grads[0], grads[1], grads[2], grads[3], grads[4], grads[5], grads[6], grads[7], grads[8], grads[9], grads[10], grads[11])
```

```python
import functools

import jax
import jax.numpy as jnp
from jax import lax
from jax.experimental import pallas as pl
from jax.experimental.pallas import tpu as pltpu
from jax.sharding import PartitionSpec as P

HEADS = 12
KV_HEADS = 2
HD = 128
GROUP = HEADS // KV_HEADS
N_CTX = 16
N_FS = 8
EPSILON = 1e-06
THETA = 1000000.0
MESH = pl.DeviceIdType.MESH
BF = jnp.bfloat16
F32 = jnp.float32


def rope_tables(position, head_dim):
    freqs = THETA ** (-jnp.arange(0, head_dim, 2).astype(F32) / head_dim)
    angles = position.astype(F32)[:, None] * freqs[None, :]
    return (jnp.cos(angles), jnp.sin(angles))


def rotate(values, cosine, sine):
    middle = values.shape[-1] // 2
    front = values[..., :middle]
    behind = values[..., middle:]
    cos_head = cosine[:, None, :]
    sin_head = sine[:, None, :]
    return jnp.concatenate(
        [front * cos_head - behind * sin_head, behind * cos_head + front * sin_head], axis=-1
    )


def contract_rows(left, right):
    return lax.dot_general(
        left, right, (((0,), (0,)), ((), ())), preferred_element_type=F32
    )


def contract_cols(left, right):
    return lax.dot_general(
        left, right, (((1,), (1,)), ((), ())), preferred_element_type=F32
    )


def flip(value, mask):
    out = value
    bit = 1
    while bit <= mask:
        if mask & bit:
            out = out + bit * (1 - 2 * lax.rem(lax.div(value, bit), 2))
        bit *= 2
    return out


class Copies:
    def __init__(self, send, recv):
        self.send, self.recv, self.count, self.all = send, recv, 0, []

    def start(self, src, dst, device):
        copy = pltpu.make_async_remote_copy(
            src_ref=src,
            dst_ref=dst,
            send_sem=self.send.at[self.count],
            recv_sem=self.recv.at[self.count],
            device_id=device,
            device_id_type=MESH,
        )
        self.count += 1
        copy.start()
        self.all.append(copy)
        return copy


def greet(devices):
    barrier = pltpu.get_barrier_semaphore()
    for device in devices:
        pl.semaphore_signal(barrier, inc=1, device_id=device, device_id_type=MESH)
    pl.semaphore_wait(barrier, len(devices))


def exchange(kernel, name, cid, ins, outs, copies, locals_):
    return pl.pallas_call(
        kernel,
        name=name,
        out_shape=[jax.ShapeDtypeStruct(s, d) for s, d in outs],
        in_specs=[pl.BlockSpec(memory_space=pl.ANY)] * len(ins),
        out_specs=[pl.BlockSpec(memory_space=pl.ANY)] * len(outs),
        scratch_shapes=[
            pltpu.SemaphoreType.DMA((copies,)),
            pltpu.SemaphoreType.DMA((copies,)),
            pltpu.SemaphoreType.DMA((locals_,)),
        ],
        compiler_params=pltpu.CompilerParams(collective_id=cid, has_side_effects=True),
    )(*ins)


def first_kernel(w_ref, s_ref, g_ref, w_out, s_out, g_out, send, recv, local):
    c, f = lax.axis_index("ctx"), lax.axis_index("fsdp")
    core = lax.rem(c, 2)
    sibling = (flip(c, 1), f)
    peers = [(c, flip(f, i)) for i in range(1, N_FS)]
    greet(peers + [sibling])
    copies = Copies(send, recv)
    own = [
        pltpu.make_async_copy(w_ref, w_out.at[f], local.at[0]),
        pltpu.make_async_copy(s_ref, s_out.at[f], local.at[1]),
        pltpu.make_async_copy(g_ref.at[f], g_out.at[f], local.at[2]),
    ]
    for copy in own:
        copy.start()
    rest = [copies.start(s_ref, s_out.at[f], peer) for peer in peers]
    halves = [copies.start(w_ref.at[core], w_out.at[f, core], peer) for peer in peers]
    rest += [copies.start(g_ref.at[peer[1]], g_out.at[f], peer) for peer in peers]
    for half, peer in zip(halves, peers):
        half.wait_recv()
        place = w_out.at[peer[1], core]
        rest.append(copies.start(place, place, sibling))
    for half in halves:
        half.wait_send()
    for copy in rest + own:
        copy.wait()


def second_kernel(kv_ref, w_ref, kv_out, w_out, send, recv, local):
    c, f = lax.axis_index("ctx"), lax.axis_index("fsdp")
    core = lax.rem(c, 2)
    sibling = (flip(c, 1), f)
    ring = [(flip(c, 2 * i), f) for i in range(1, N_CTX // 2)]
    peers = [(c, flip(f, i)) for i in range(1, N_FS)]
    greet(ring + peers + [sibling])
    copies = Copies(send, recv)
    own = [
        pltpu.make_async_copy(kv_ref, kv_out.at[c], local.at[0]),
        pltpu.make_async_copy(w_ref, w_out.at[f], local.at[1]),
    ]
    for copy in own:
        copy.start()
    keys = [copies.start(kv_ref, kv_out.at[c], device) for device in ring]
    rest = [copies.start(kv_ref, kv_out.at[c], sibling)]
    halves = [copies.start(w_ref.at[core], w_out.at[f, core], peer) for peer in peers]
    for key, device in zip(keys, ring):
        key.wait_recv()
        place = kv_out.at[device[0]]
        rest.append(copies.start(place, place, sibling))
    for half, peer in zip(halves, peers):
        half.wait_recv()
        place = w_out.at[peer[1], core]
        rest.append(copies.start(place, place, sibling))
    for copy in keys + halves:
        copy.wait_send()
    for copy in rest + own:
        copy.wait()


def scatter_kernel(count, *refs):
    ins, outs = refs[:count], refs[count : 2 * count]
    send, recv, local = refs[2 * count :]
    c, f = lax.axis_index("ctx"), lax.axis_index("fsdp")
    ring = [(flip(c, 2 * i), f) for i in range(1, N_CTX // 2)]
    greet(ring)
    copies = Copies(send, recv)
    for i, device in enumerate(ring):
        for src, dst in zip(ins, outs):
            piece = lax.div(device[0], 2)
            if len(src.shape) == 4:
                copies.start(src.at[:, piece], dst.at[i], device)
            else:
                copies.start(src.at[piece], dst.at[i], device)
    for copy in copies.all:
        copy.wait()


def owner_kernel(count, *refs):
    ins, outs = refs[:count], refs[count : 2 * count]
    send, recv, local = refs[2 * count :]
    c, f = lax.axis_index("ctx"), lax.axis_index("fsdp")
    peers = [(c, flip(f, i)) for i in range(1, N_FS)]
    greet(peers)
    copies = Copies(send, recv)
    own = [
        pltpu.make_async_copy(src.at[f], dst.at[f], local.at[n])
        for n, (src, dst) in enumerate(zip(ins, outs))
    ]
    for copy in own:
        copy.start()
    for peer in peers:
        for src, dst in zip(ins, outs):
            copies.start(src.at[peer[1]], dst.at[f], peer)
    for copy in copies.all + own:
        copy.wait()


def gather_kernel(count, *refs):
    ins, outs = refs[:count], refs[count : 2 * count]
    send, recv, local = refs[2 * count :]
    c, f = lax.axis_index("ctx"), lax.axis_index("fsdp")
    sibling = (flip(c, 1), f)
    ring = [(flip(c, 2 * i), f) for i in range(1, N_CTX // 2)]
    greet(ring + [sibling])
    copies = Copies(send, recv)
    own = [
        pltpu.make_async_copy(src, dst.at[c], local.at[n])
        for n, (src, dst) in enumerate(zip(ins, outs))
    ]
    for copy in own:
        copy.start()
    near = [
        [copies.start(src, dst.at[c], device) for src, dst in zip(ins, outs)] for device in ring
    ]
    rest = [copies.start(src, dst.at[c], sibling) for src, dst in zip(ins, outs)]
    for group, device in zip(near, ring):
        for copy, dst in zip(group, outs):
            copy.wait_recv()
            place = dst.at[device[0]]
            rest.append(copies.start(place, place, sibling))
    for group in near:
        for copy in group:
            copy.wait_send()
    for copy in rest + own:
        copy.wait()


def gather_ctx(name, cid, arrays):
    count = len(arrays)
    return exchange(
        functools.partial(gather_kernel, count),
        name,
        cid,
        arrays,
        [((N_CTX,) + a.shape, a.dtype) for a in arrays],
        15 * count,
        count,
    )


def scatter_ctx(name, cid, arrays):
    count = len(arrays)
    outs = [
        ((7, a.shape[0]) + a.shape[2:] if a.ndim == 4 else (7,) + a.shape[1:], a.dtype)
        for a in arrays
    ]
    return exchange(
        functools.partial(scatter_kernel, count), name, cid, arrays, outs, 7 * count, 1
    )


def to_owner(name, cid, arrays):
    count = len(arrays)
    return exchange(
        functools.partial(owner_kernel, count),
        name,
        cid,
        arrays,
        [(a.shape, a.dtype) for a in arrays],
        7 * count,
        count,
    )


def swap_fs(value, mask):
    return lax.ppermute(value, "fsdp", [(s, s ^ mask) for s in range(N_FS)])


def swap_ctx(value, mask):
    return lax.ppermute(value, "ctx", [(s, s ^ mask) for s in range(N_CTX)])


CHUNK = 256


def attend_kernel(q_ref, k_ref, v_ref, row_ref, e_ref, o_ref, inv_ref, s_ref):
    tokens = k_ref.shape[1] - 16
    length = N_CTX * tokens
    half = tokens // 2
    scale = HD ** (-0.5)
    query = q_ref[0]
    row_place, row_seg = row_ref[0:1, :], row_ref[1:2, :]
    key_seg = k_ref[:, tokens : tokens + 16, :][:, 0, :].astype(F32).T
    within = lax.broadcasted_iota(jnp.int32, (tokens, tokens), 0)
    top = jnp.full((8, GROUP * tokens), -1e30, F32)
    for b in range(N_CTX):
        place = jnp.where(
            within < half, b * half + within, (2 * N_CTX - 1 - b) * half + within - half
        ).astype(F32)
        allowed = (place <= row_place) & (key_seg[:, b : b + 1] == row_seg) & (row_seg > 0.5)
        bias = jnp.where(allowed, 0.0, -1e30).astype(F32)
        scores = (
            lax.dot_general(
                k_ref[b, :tokens, :],
                query,
                (((1,), (1,)), ((), ())),
                preferred_element_type=F32,
            )
            * scale
            + jnp.concatenate([bias] * GROUP, axis=1)
        )
        s_ref[b * tokens : (b + 1) * tokens, :] = scores
        top = jnp.maximum(top, jnp.max(scores.reshape(tokens // 8, 8, -1), axis=0))
    highest = jnp.maximum(jnp.max(top, axis=0, keepdims=True), -1e29)
    total = jnp.zeros((8, GROUP * tokens), F32)
    mixed = jnp.zeros((HD, GROUP * tokens), F32)
    for j in range(length // CHUNK):
        part = jnp.exp(s_ref[j * CHUNK : (j + 1) * CHUNK, :] - highest)
        total = total + jnp.sum(part.reshape(CHUNK // 8, 8, -1), axis=0)
        low = part.astype(BF)
        e_ref[0, j * CHUNK : (j + 1) * CHUNK, :] = low
        values = v_ref[2 * j : 2 * j + 2, :tokens, :].reshape(CHUNK, HD)
        mixed = mixed + contract_rows(values, low)
    total = jnp.sum(total, axis=0, keepdims=True)
    inverse = 1.0 / jnp.where(total > 0.5, total, 1.0)
    o_ref[0] = mixed * inverse
    inv_ref[0] = jnp.broadcast_to(inverse, (8, GROUP * tokens))


def attend(query, keys_values, rows):
    tokens = rows.shape[1]
    wide = GROUP * tokens
    length = N_CTX * tokens
    return pl.pallas_call(
        attend_kernel,
        name="attend",
        grid=(KV_HEADS,),
        in_specs=[
            pl.BlockSpec((1, wide, HD), lambda h: (h, 0, 0)),
            pl.BlockSpec((N_CTX, tokens + 16, HD), lambda h: (0, 0, h)),
            pl.BlockSpec((N_CTX, tokens + 16, HD), lambda h: (0, 0, KV_HEADS + h)),
            pl.BlockSpec((2, tokens), lambda h: (0, 0)),
        ],
        out_specs=[
            pl.BlockSpec((1, length, wide), lambda h: (h, 0, 0)),
            pl.BlockSpec((1, HD, wide), lambda h: (h, 0, 0)),
            pl.BlockSpec((1, 8, wide), lambda h: (h, 0, 0)),
        ],
        out_shape=[
            jax.ShapeDtypeStruct((KV_HEADS, length, wide), BF),
            jax.ShapeDtypeStruct((KV_HEADS, HD, wide), F32),
            jax.ShapeDtypeStruct((KV_HEADS, 8, wide), F32),
        ],
        scratch_shapes=[pltpu.VMEM((length, wide), F32)],
        compiler_params=pltpu.CompilerParams(vmem_limit_bytes=48 * 2**20),
        cost_estimate=pl.CostEstimate(
            flops=4 * KV_HEADS * length * wide * HD,
            bytes_accessed=2 * KV_HEADS * length * wide + 4 * 2**20,
            transcendentals=KV_HEADS * length * wide,
        ),
    )(query, keys_values, keys_values, rows)


def attend_back_kernel(
    e_ref, q_ref, k_ref, v_ref, g_ref, o_ref, inv_ref, dq_ref, dk_ref, dv_ref
):
    tokens = k_ref.shape[1] - 16
    length = N_CTX * tokens
    scale = HD ** (-0.5)
    query, grad = q_ref[0], g_ref[0]
    inverse = inv_ref[0, 0:1, :]
    grad_turned = grad.astype(F32).T
    weighted = jnp.sum(grad_turned * o_ref[0], axis=0, keepdims=True)
    factor = inverse * scale
    shift = weighted * factor
    grad_scaled = (grad_turned * inverse).T.astype(BF)
    turned = jnp.zeros((HD, GROUP * tokens), F32)
    for j in range(length // CHUNK):
        part = e_ref[0, j * CHUNK : (j + 1) * CHUNK, :]
        keys = k_ref[2 * j : 2 * j + 2, :tokens, :].reshape(CHUNK, HD)
        values = v_ref[2 * j : 2 * j + 2, :tokens, :].reshape(CHUNK, HD)
        prob_grad = contract_cols(values, grad)
        score_grad = (part.astype(F32) * (prob_grad * factor - shift)).astype(BF)
        dk = jnp.dot(score_grad, query, preferred_element_type=F32)
        dv = jnp.dot(part, grad_scaled, preferred_element_type=F32)
        dk_ref[2 * j : 2 * j + 2] = dk.reshape(2, tokens, HD).astype(dk_ref.dtype)
        dv_ref[2 * j : 2 * j + 2] = dv.reshape(2, tokens, HD).astype(dv_ref.dtype)
        turned = turned + contract_rows(keys, score_grad)
    dq_ref[0] = turned


def attend_back(expo, query, keys_values, grad, mixed, inverse):
    wide = query.shape[1]
    tokens = wide // GROUP
    length = N_CTX * tokens
    return pl.pallas_call(
        attend_back_kernel,
        name="attend_back",
        grid=(KV_HEADS,),
        in_specs=[
            pl.BlockSpec((1, length, wide), lambda h: (h, 0, 0)),
            pl.BlockSpec((1, wide, HD), lambda h: (h, 0, 0)),
            pl.BlockSpec((N_CTX, tokens + 16, HD), lambda h: (0, 0, h)),
            pl.BlockSpec((N_CTX, tokens + 16, HD), lambda h: (0, 0, KV_HEADS + h)),
            pl.BlockSpec((1, wide, HD), lambda h: (h, 0, 0)),
            pl.BlockSpec((1, HD, wide), lambda h: (h, 0, 0)),
            pl.BlockSpec((1, 8, wide), lambda h: (h, 0, 0)),
        ],
        out_specs=[
            pl.BlockSpec((1, HD, wide), lambda h: (h, 0, 0)),
            pl.BlockSpec((N_CTX, tokens, HD), lambda h: (0, 0, h)),
            pl.BlockSpec((N_CTX, tokens, HD), lambda h: (0, 0, h)),
        ],
        out_shape=[
            jax.ShapeDtypeStruct((KV_HEADS, HD, wide), F32),
            jax.ShapeDtypeStruct((N_CTX, tokens, KV_HEADS * HD), BF),
            jax.ShapeDtypeStruct((N_CTX, tokens, KV_HEADS * HD), BF),
        ],
        compiler_params=pltpu.CompilerParams(vmem_limit_bytes=48 * 2**20),
        cost_estimate=pl.CostEstimate(
            flops=8 * KV_HEADS * length * wide * HD,
            bytes_accessed=2 * KV_HEADS * length * wide + 6 * 2**20,
            transcendentals=0,
        ),
    )(expo, query, keys_values, keys_values, grad, mixed, inverse)


def body(
    layer_input,
    segments,
    positions,
    attn_norm,
    q_weight,
    q_bias,
    k_weight,
    k_bias,
    v_weight,
    v_bias,
    o_weight,
    mlp_norm,
    gate_weight,
    up_weight,
    down_weight,
    out_cotangent,
):
    tokens, width = layer_input.shape[1:]
    rows = gate_weight.shape[0]
    units = gate_weight.shape[1] // N_FS
    q_width = HEADS * HD
    kv_width = KV_HEADS * HD
    half_block = tokens // 2
    ctx = lax.axis_index("ctx")
    core = lax.rem(ctx, 2)
    pair = lax.div(ctx, 2)
    x_part = lax.rem(ctx, N_FS)
    inputs = layer_input[0].astype(F32)
    segment = segments[0]
    position = positions[0]
    keep = (segment > 0).astype(F32)[:, None]
    cotangent = out_cotangent[0].astype(F32) * keep
    cot_low = cotangent.astype(BF)

    cot_all = jnp.concatenate([cot_low] + [swap_fs(cot_low, i) for i in range(1, N_FS)], axis=0)

    qkv = jnp.concatenate([q_weight, k_weight, v_weight], axis=1).reshape(2, rows // 2, -1)
    small = jnp.concatenate([attn_norm, mlp_norm, q_bias, k_bias, v_bias]).reshape(-1, 128)
    small = jnp.pad(small, ((0, 16 - small.shape[0]), (0, 0)))
    cut = rows // 4
    start = lax.rem(x_part, 4) * cut
    gate_cut = lax.dynamic_slice_in_dim(gate_weight, start, cut, 0)
    up_cut = lax.dynamic_slice_in_dim(up_weight, start, cut, 0)
    blocks = (
        jnp.where(x_part < 4, gate_cut, up_cut).reshape(cut, N_FS, units).transpose(1, 0, 2)
    )
    full_qkv, small_all, blocks_here = exchange(
        first_kernel,
        "gather_qkv",
        1,
        (qkv, small, blocks),
        [
            ((N_FS,) + qkv.shape, BF),
            ((N_FS,) + small.shape, BF),
            (blocks.shape, BF),
        ],
        28,
        3,
    )
    along = [blocks_here] + [swap_ctx(blocks_here, 2 * i) for i in range(1, 4)]
    along = jnp.stack(along)
    other = swap_ctx(along, 1)
    x_here = lax.div(x_part, 2)
    both = jnp.where(core == 0, jnp.stack([along, other]), jnp.stack([other, along]))
    order = jnp.bitwise_xor(jnp.arange(4), x_here)
    both = jnp.take(both, order, axis=1)
    both = both.transpose(1, 0, 2, 3, 4).reshape(2, 4, N_FS, cut, units)
    both = both.transpose(0, 2, 1, 3, 4).reshape(2, width, units)
    gate_cols, up_cols = both[0], both[1]

    flat = small_all[:, :5].reshape(N_FS, -1)
    marks = [0, rows, 2 * rows, 2 * rows + q_width // N_FS]
    marks += [marks[-1] + kv_width // N_FS, marks[-1] + 2 * kv_width // N_FS]
    gain_one, gain_two, bias_q, bias_k, bias_v = (
        flat[:, lo:hi].reshape(-1).astype(F32) for lo, hi in zip(marks[:-1], marks[1:])
    )
    bias_all = jnp.concatenate([bias_q, bias_k, bias_v])
    full_qkv = full_qkv.reshape(width, q_width + 2 * kv_width)

    scale_one = lax.rsqrt(jnp.mean(inputs * inputs, axis=-1, keepdims=True) + EPSILON)
    norm_first = inputs * scale_one
    normed_in = (norm_first * gain_one).astype(BF)
    projected = jnp.dot(normed_in, full_qkv, preferred_element_type=F32) + bias_all
    cosine, sine = rope_tables(position, HD)
    turned = rotate(
        projected[:, : q_width + kv_width].reshape(tokens, HEADS + KV_HEADS, HD), cosine, sine
    ).astype(BF)
    value_low = projected[:, q_width + kv_width :].astype(BF)
    query = (
        turned[:, :HEADS]
        .reshape(tokens, KV_HEADS, GROUP, HD)
        .transpose(1, 2, 0, 3)
        .reshape(KV_HEADS, GROUP * tokens, HD)
    )
    keys_values = jnp.concatenate([turned[:, HEADS:].reshape(tokens, kv_width), value_low], axis=1)
    segment_rows = jnp.broadcast_to(
        jnp.tile(segment.astype(BF)[None, :], (1, 2 * KV_HEADS)), (16, 2 * kv_width)
    )
    keys_values = jnp.concatenate([keys_values, segment_rows], axis=0)
    kv_all, full_o = exchange(
        second_kernel,
        "gather_kv_o",
        2,
        (keys_values, o_weight.reshape(2, rows // 2, width)),
        [((N_CTX,) + keys_values.shape, BF), ((N_FS, 2, rows // 2, width), BF)],
        29,
        2,
    )
    full_o = full_o.reshape(q_width, width)
    within = jnp.arange(tokens, dtype=jnp.int32)
    row_place = jnp.where(
        within < half_block,
        ctx * half_block + within,
        (2 * N_CTX - 1 - ctx) * half_block + within - half_block,
    )
    row_info = jnp.stack([row_place.astype(F32), segment.astype(F32)])
    expo, mixed, inverse = attend(query, kv_all, row_info)
    attended = (
        mixed.reshape(KV_HEADS, HD, GROUP, tokens).transpose(3, 0, 2, 1).reshape(tokens, q_width)
    ).astype(BF)
    middle = inputs + jnp.dot(attended, full_o, preferred_element_type=F32)
    scale_two = lax.rsqrt(jnp.mean(middle * middle, axis=-1, keepdims=True) + EPSILON)
    norm_second = middle * scale_two
    normed_mid = (norm_second * gain_two).astype(BF)

    nm_all = jnp.concatenate(
        [normed_mid] + [swap_fs(normed_mid, i) for i in range(1, N_FS)], axis=0
    )
    act_grad = contract_cols(cot_all, down_weight)
    gate_pre = jnp.dot(nm_all, gate_cols, preferred_element_type=F32)
    up_pre = jnp.dot(nm_all, up_cols, preferred_element_type=F32)
    sigma = jax.nn.sigmoid(gate_pre)
    swish = gate_pre * sigma
    activation = (swish * up_pre).astype(BF)
    gate_grad = (act_grad * up_pre * sigma * (1.0 + gate_pre * (1.0 - sigma))).astype(BF)
    up_grad = (act_grad * swish).astype(BF)
    part_sum = (contract_cols(gate_grad, gate_cols) + contract_cols(up_grad, up_cols)).astype(BF)
    part_sum = part_sum.reshape(N_FS, tokens, width)
    mid_norm_grad = part_sum[0].astype(F32)
    for i in range(1, N_FS):
        mid_norm_grad = mid_norm_grad + swap_fs(part_sum[i], i).astype(F32)
    out_part = jnp.dot(activation, down_weight, preferred_element_type=F32).astype(BF)
    out_part = out_part.reshape(N_FS, tokens, width)
    output_rows = middle + out_part[0].astype(F32)
    for i in range(1, N_FS):
        output_rows = output_rows + swap_fs(out_part[i], i).astype(F32)
    output_rows = output_rows.astype(BF)

    piece = rows // 8
    gate_part = contract_rows(nm_all, gate_grad).astype(BF)
    up_part = contract_rows(nm_all, up_grad).astype(BF)
    down_part = contract_rows(activation, cot_all).astype(BF).reshape(2, units // 2, width)
    keep_gu = jnp.where(core == 0, gate_part, up_part)
    send_gu = jnp.where(core == 0, up_part, gate_part)
    keep_down = jnp.where(core == 0, down_part[0], down_part[1])
    send_down = jnp.where(core == 0, down_part[1], down_part[0])
    sum_gu = (keep_gu.astype(F32) + swap_ctx(send_gu, 1).astype(F32)).astype(BF)
    sum_down = (keep_down.astype(F32) + swap_ctx(send_down, 1).astype(F32)).astype(BF)
    sum_gu = sum_gu.reshape(N_FS, 8, piece, units)
    sum_down = sum_down.reshape(8, units // 16, width)
    far_gu, far_down = scatter_ctx("scatter_mlp", 3, (sum_gu, sum_down))
    done_gu = (
        lax.dynamic_index_in_dim(sum_gu, pair, 1, False).astype(F32)
        + jnp.sum(far_gu.astype(F32), axis=0)
    ).astype(BF)
    done_down = (
        lax.dynamic_index_in_dim(sum_down, pair, 0, False).astype(F32)
        + jnp.sum(far_down.astype(F32), axis=0)
    ).astype(BF)

    gain_two_grad = jnp.sum(mid_norm_grad * norm_second, axis=0)
    scaled_two = mid_norm_grad * gain_two
    mid_grad = cotangent + scale_two * (
        scaled_two - norm_second * jnp.mean(scaled_two * norm_second, axis=-1, keepdims=True)
    )
    branch_low = mid_grad.astype(BF)
    attended_grad = contract_cols(branch_low, full_o).astype(BF)
    grad_rows = (
        attended_grad.reshape(tokens, KV_HEADS, GROUP, HD)
        .transpose(1, 2, 0, 3)
        .reshape(KV_HEADS, GROUP * tokens, HD)
    )
    turned_grad, key_part, value_part = attend_back(
        expo, query, kv_all, grad_rows, mixed, inverse
    )
    kv_part = jnp.concatenate([key_part, value_part], axis=2)
    kv_part = kv_part.reshape(N_CTX // 2, 2, tokens, 2 * kv_width)
    keep_kv = jnp.where(core == 0, kv_part[:, 0], kv_part[:, 1])
    send_kv = jnp.where(core == 0, kv_part[:, 1], kv_part[:, 0])
    sum_kv = (keep_kv.astype(F32) + swap_ctx(send_kv, 1).astype(F32)).astype(BF)
    (far_kv,) = scatter_ctx("scatter_kv", 4, (sum_kv,))
    own_kv = lax.dynamic_index_in_dim(sum_kv, pair, 0, False).astype(F32) + jnp.sum(
        far_kv.astype(F32), axis=0
    )
    query_rot_grad = (
        turned_grad.reshape(KV_HEADS, HD, GROUP, tokens)
        .transpose(3, 0, 2, 1)
        .reshape(tokens, HEADS, HD)
    )
    turned_back = rotate(
        jnp.concatenate(
            [query_rot_grad, own_kv[:, :kv_width].reshape(tokens, KV_HEADS, HD)], axis=1
        ),
        cosine,
        -sine,
    ).reshape(tokens, q_width + kv_width)
    proj_grad = jnp.concatenate([turned_back, own_kv[:, kv_width:]], axis=1).astype(BF)
    bias_grads = jnp.sum(proj_grad.astype(F32), axis=0)
    in_norm_grad = contract_cols(proj_grad, full_qkv)
    gain_one_grad = jnp.sum(in_norm_grad * norm_first, axis=0)
    scaled_one = in_norm_grad * gain_one
    input_rows = mid_grad + scale_one * (
        scaled_one - norm_first * jnp.mean(scaled_one * norm_first, axis=-1, keepdims=True)
    )

    q_part = contract_rows(normed_in, proj_grad).astype(BF)
    o_part = contract_rows(attended, branch_low).astype(BF)
    side = q_width // 2
    low_side = jnp.concatenate(
        [o_part[:, :side], q_part[:, :side], q_part[:, q_width : q_width + kv_width]], axis=1
    )
    high_side = jnp.concatenate(
        [o_part[:, side:], q_part[:, side:q_width], q_part[:, q_width + kv_width :]], axis=1
    )
    keep_at = jnp.where(core == 0, low_side, high_side)
    send_at = jnp.where(core == 0, high_side, low_side)
    sum_at = (keep_at.astype(F32) + swap_ctx(send_at, 1).astype(F32)).astype(BF)
    sum_at = sum_at.reshape(N_FS, 8, piece, -1)
    (far_at,) = scatter_ctx("scatter_attn", 5, (sum_at,))
    done_at = (
        lax.dynamic_index_in_dim(sum_at, pair, 1, False).astype(F32)
        + jnp.sum(far_at.astype(F32), axis=0)
    ).astype(BF)

    vectors = jnp.concatenate(
        [
            v.reshape(N_FS, -1)
            for v in (
                gain_one_grad,
                gain_two_grad,
                bias_grads[:q_width],
                bias_grads[q_width : q_width + kv_width],
                bias_grads[q_width + kv_width :],
            )
        ],
        axis=1,
    ).reshape(N_FS, 5, 128)
    vectors = jnp.pad(vectors, ((0, 0), (0, 3), (0, 0)))
    own_gu, own_at, own_vec = to_owner("to_owner", 6, (done_gu, done_at, vectors))
    own_at = jnp.sum(own_at.astype(F32), axis=0).astype(BF)
    own_vec = jnp.sum(own_vec, axis=0)
    all_gu, all_at, all_down, all_vec = gather_ctx(
        "gather_grads", 7, (own_gu, own_at, done_down, own_vec)
    )
    all_vec = jnp.sum(all_vec, axis=0)[:5].reshape(-1)
    sum_vec = [all_vec[lo:hi] for lo, hi in zip(marks[:-1], marks[1:])]
    all_gu = all_gu.reshape(8, 2, N_FS, piece, units).transpose(1, 0, 3, 2, 4)
    all_gu = all_gu.reshape(2, rows, N_FS * units)
    all_at = all_at.reshape(8, 2, piece, -1).transpose(1, 0, 2, 3).reshape(2, rows, -1)
    all_down = all_down.reshape(8, 2, units // 16, width).transpose(1, 0, 2, 3)
    o_grad = jnp.concatenate([all_at[0, :, :side], all_at[1, :, :side]], axis=1).astype(F32)
    q_grad = jnp.concatenate(
        [all_at[0, :, side:q_width], all_at[1, :, side:q_width]], axis=1
    ).astype(F32)
    return (
        output_rows[None],
        input_rows[None],
        sum_vec[0],
        q_grad,
        sum_vec[2],
        all_at[0, :, q_width:].astype(F32),
        sum_vec[3],
        all_at[1, :, q_width:].astype(F32),
        sum_vec[4],
        o_grad,
        sum_vec[1],
        all_gu[0].astype(F32),
        all_gu[1].astype(F32),
        all_down.reshape(units, width).astype(F32),
    )


def solution(mesh):
    placed = (
        P("fsdp", "ctx", None),
        P("fsdp", "ctx"),
        P("fsdp", "ctx"),
        P("fsdp"),
        P("fsdp", None),
        P("fsdp"),
        P("fsdp", None),
        P("fsdp"),
        P("fsdp", None),
        P("fsdp"),
        P("fsdp", None),
        P("fsdp"),
        P("fsdp", None),
        P("fsdp", None),
        P("fsdp", None),
        P("fsdp", "ctx", None),
    )
    return jax.shard_map(
        body,
        mesh=mesh,
        in_specs=placed,
        out_specs=(
            P("fsdp", "ctx", None),
            P("fsdp", "ctx", None),
            P("fsdp"),
            P("fsdp", None),
            P("fsdp"),
            P("fsdp", None),
            P("fsdp"),
            P("fsdp", None),
            P("fsdp"),
            P("fsdp", None),
            P("fsdp"),
            P("fsdp", None),
            P("fsdp", None),
            P("fsdp", None),
        ),
        check_vma=False,
    )
```

```python
import functools

import jax
import jax.numpy as jnp
from jax import lax
from jax.experimental import pallas as pl
from jax.experimental.pallas import tpu as pltpu
from jax.sharding import PartitionSpec as P

HEADS = 12
KV_HEADS = 2
HD = 128
GROUP = HEADS // KV_HEADS
N_CTX = 16
N_FS = 8
EPSILON = 1e-06
THETA = 1000000.0
MESH = pl.DeviceIdType.MESH
BF = jnp.bfloat16
F32 = jnp.float32


def rope_tables(position, head_dim):
    freqs = THETA ** (-jnp.arange(0, head_dim, 2).astype(F32) / head_dim)
    angles = position.astype(F32)[:, None] * freqs[None, :]
    return (jnp.cos(angles), jnp.sin(angles))


def rotate(values, cosine, sine):
    middle = values.shape[-1] // 2
    front = values[..., :middle]
    behind = values[..., middle:]
    cos_head = cosine[:, None, :]
    sin_head = sine[:, None, :]
    return jnp.concatenate(
        [front * cos_head - behind * sin_head, behind * cos_head + front * sin_head], axis=-1
    )


def contract_rows(left, right):
    return lax.dot_general(
        left, right, (((0,), (0,)), ((), ())), preferred_element_type=F32
    )


def contract_cols(left, right):
    return lax.dot_general(
        left, right, (((1,), (1,)), ((), ())), preferred_element_type=F32
    )


def flip(value, mask):
    out = value
    bit = 1
    while bit <= mask:
        if mask & bit:
            out = out + bit * (1 - 2 * lax.rem(lax.div(value, bit), 2))
        bit *= 2
    return out


class Copies:
    def __init__(self, send, recv):
        self.send, self.recv, self.count, self.all = send, recv, 0, []

    def start(self, src, dst, device):
        copy = pltpu.make_async_remote_copy(
            src_ref=src,
            dst_ref=dst,
            send_sem=self.send.at[self.count],
            recv_sem=self.recv.at[self.count],
            device_id=device,
            device_id_type=MESH,
        )
        self.count += 1
        copy.start()
        self.all.append(copy)
        return copy


def greet(devices):
    barrier = pltpu.get_barrier_semaphore()
    for device in devices:
        pl.semaphore_signal(barrier, inc=1, device_id=device, device_id_type=MESH)
    pl.semaphore_wait(barrier, len(devices))


def exchange(kernel, name, cid, ins, outs, copies, locals_):
    return pl.pallas_call(
        kernel,
        name=name,
        out_shape=[jax.ShapeDtypeStruct(s, d) for s, d in outs],
        in_specs=[pl.BlockSpec(memory_space=pl.ANY)] * len(ins),
        out_specs=[pl.BlockSpec(memory_space=pl.ANY)] * len(outs),
        scratch_shapes=[
            pltpu.SemaphoreType.DMA((copies,)),
            pltpu.SemaphoreType.DMA((copies,)),
            pltpu.SemaphoreType.DMA((locals_,)),
        ],
        compiler_params=pltpu.CompilerParams(collective_id=cid, has_side_effects=True),
    )(*ins)


def first_kernel(w_ref, s_ref, g_ref, w_out, s_out, g_out, send, recv, local):
    c, f = lax.axis_index("ctx"), lax.axis_index("fsdp")
    core = lax.rem(c, 2)
    sibling = (flip(c, 1), f)
    peers = [(c, flip(f, i)) for i in range(1, N_FS)]
    along = [(flip(c, 2 * i), f) for i in range(1, 4)]
    greet(peers + along + [sibling])
    copies = Copies(send, recv)

    def columns(device):
        part = lax.rem(device[0], N_FS)
        return g_out.at[lax.div(part, 4), :, lax.rem(part, 4)]

    def block(device, source):
        part = lax.rem(device[0], N_FS)
        return g_out.at[lax.div(part, 4), source, lax.rem(part, 4)]

    here = (c, f)
    own = [
        pltpu.make_async_copy(g_ref.at[f], block(here, f), local.at[2]),
        pltpu.make_async_copy(w_ref, w_out.at[f], local.at[0]),
        pltpu.make_async_copy(s_ref, s_out.at[f], local.at[1]),
    ]
    for copy in own:
        copy.start()
    rest = [copies.start(s_ref, s_out.at[f], peer) for peer in peers]
    blocks = [copies.start(g_ref.at[peer[1]], block(here, f), peer) for peer in peers]
    halves = [copies.start(w_ref.at[core], w_out.at[f, core], peer) for peer in peers]
    own[0].wait()
    for copy in blocks:
        copy.wait_recv()
    mine = columns(here)
    near = [copies.start(mine, mine, device) for device in along]
    rest.append(copies.start(mine, mine, sibling))
    for half, peer in zip(halves, peers):
        half.wait_recv()
        place = w_out.at[peer[1], core]
        rest.append(copies.start(place, place, sibling))
    for copy, device in zip(near, along):
        copy.wait_recv()
        place = columns(device)
        rest.append(copies.start(place, place, sibling))
    for copy in halves + blocks + near:
        copy.wait_send()
    for copy in rest + own[1:]:
        copy.wait()


def second_kernel(kv_ref, w_ref, t_ref, kv_out, w_out, t_out, send, recv, local):
    c, f = lax.axis_index("ctx"), lax.axis_index("fsdp")
    core = lax.rem(c, 2)
    sibling = (flip(c, 1), f)
    ring = [(flip(c, 2 * i), f) for i in range(1, N_CTX // 2)]
    peers = [(c, flip(f, i)) for i in range(1, N_FS)]
    greet(ring + peers + [sibling])
    copies = Copies(send, recv)
    own = [
        pltpu.make_async_copy(kv_ref, kv_out.at[c], local.at[0]),
        pltpu.make_async_copy(w_ref, w_out.at[f], local.at[1]),
        pltpu.make_async_copy(t_ref, t_out.at[0], local.at[2]),
    ]
    for copy in own:
        copy.start()
    keys = [copies.start(kv_ref, kv_out.at[c], device) for device in ring]
    rest = [copies.start(kv_ref, kv_out.at[c], sibling)]
    halves = [copies.start(w_ref.at[core], w_out.at[f, core], peer) for peer in peers]
    rest += [copies.start(t_ref, t_out.at[i + 1], peer) for i, peer in enumerate(peers)]
    for key, device in zip(keys, ring):
        key.wait_recv()
        place = kv_out.at[device[0]]
        rest.append(copies.start(place, place, sibling))
    for half, peer in zip(halves, peers):
        half.wait_recv()
        place = w_out.at[peer[1], core]
        rest.append(copies.start(place, place, sibling))
    for copy in keys + halves:
        copy.wait_send()
    for copy in rest + own:
        copy.wait()


def scatter_kernel(count, *refs):
    ins, outs = refs[:count], refs[count : 2 * count]
    send, recv, local = refs[2 * count :]
    c, f = lax.axis_index("ctx"), lax.axis_index("fsdp")
    ring = [(flip(c, 2 * i), f) for i in range(1, N_CTX // 2)]
    greet(ring)
    copies = Copies(send, recv)
    for i, device in enumerate(ring):
        for src, dst in zip(ins, outs):
            piece = lax.div(device[0], 2)
            if len(src.shape) == 4:
                copies.start(src.at[:, piece], dst.at[i], device)
            else:
                copies.start(src.at[piece], dst.at[i], device)
    for copy in copies.all:
        copy.wait()


def owner_kernel(count, *refs):
    ins, outs = refs[:count], refs[count : 2 * count]
    send, recv, local = refs[2 * count :]
    c, f = lax.axis_index("ctx"), lax.axis_index("fsdp")
    peers = [(c, flip(f, i)) for i in range(1, N_FS)]
    greet(peers)
    copies = Copies(send, recv)
    own = [
        pltpu.make_async_copy(src.at[f], dst.at[f], local.at[n])
        for n, (src, dst) in enumerate(zip(ins, outs))
    ]
    for copy in own:
        copy.start()
    for peer in peers:
        for src, dst in zip(ins, outs):
            copies.start(src.at[peer[1]], dst.at[f], peer)
    for copy in copies.all + own:
        copy.wait()


def gather_kernel(count, *refs):
    ins, outs = refs[:count], refs[count : 2 * count]
    send, recv, local = refs[2 * count :]
    c, f = lax.axis_index("ctx"), lax.axis_index("fsdp")
    sibling = (flip(c, 1), f)
    ring = [(flip(c, 2 * i), f) for i in range(1, N_CTX // 2)]
    greet(ring + [sibling])
    copies = Copies(send, recv)
    own = [
        pltpu.make_async_copy(src, dst.at[c], local.at[n])
        for n, (src, dst) in enumerate(zip(ins, outs))
    ]
    for copy in own:
        copy.start()
    near = [
        [copies.start(src, dst.at[c], device) for src, dst in zip(ins, outs)] for device in ring
    ]
    rest = [copies.start(src, dst.at[c], sibling) for src, dst in zip(ins, outs)]
    for group, device in zip(near, ring):
        for copy, dst in zip(group, outs):
            copy.wait_recv()
            place = dst.at[device[0]]
            rest.append(copies.start(place, place, sibling))
    for group in near:
        for copy in group:
            copy.wait_send()
    for copy in rest + own:
        copy.wait()


def gather_ctx(name, cid, arrays):
    count = len(arrays)
    return exchange(
        functools.partial(gather_kernel, count),
        name,
        cid,
        arrays,
        [((N_CTX,) + a.shape, a.dtype) for a in arrays],
        15 * count,
        count,
    )


def scatter_ctx(name, cid, arrays):
    count = len(arrays)
    outs = [
        ((7, a.shape[0]) + a.shape[2:] if a.ndim == 4 else (7,) + a.shape[1:], a.dtype)
        for a in arrays
    ]
    return exchange(
        functools.partial(scatter_kernel, count), name, cid, arrays, outs, 7 * count, 1
    )


def to_owner(name, cid, arrays):
    count = len(arrays)
    return exchange(
        functools.partial(owner_kernel, count),
        name,
        cid,
        arrays,
        [(a.shape, a.dtype) for a in arrays],
        7 * count,
        count,
    )


def swap_fs(value, mask):
    return lax.ppermute(value, "fsdp", [(s, s ^ mask) for s in range(N_FS)])


def swap_ctx(value, mask):
    return lax.ppermute(value, "ctx", [(s, s ^ mask) for s in range(N_CTX)])


CHUNK = 256


def attend_kernel(q_ref, k_ref, v_ref, row_ref, e_ref, o_ref, inv_ref, s_ref):
    tokens = k_ref.shape[1] - 16
    length = N_CTX * tokens
    half = tokens // 2
    scale = HD ** (-0.5)
    query = q_ref[0]
    row_place, row_seg = row_ref[0:1, :], row_ref[1:2, :]
    key_seg = k_ref[:, tokens : tokens + 16, :][:, 0, :].astype(F32).T
    within = lax.broadcasted_iota(jnp.int32, (tokens, tokens), 0)
    top = jnp.full((8, GROUP * tokens), -1e30, F32)
    for b in range(N_CTX):
        place = jnp.where(
            within < half, b * half + within, (2 * N_CTX - 1 - b) * half + within - half
        ).astype(F32)
        allowed = (place <= row_place) & (key_seg[:, b : b + 1] == row_seg) & (row_seg > 0.5)
        bias = jnp.where(allowed, 0.0, -1e30).astype(F32)
        scores = (
            lax.dot_general(
                k_ref[b, :tokens, :],
                query,
                (((1,), (1,)), ((), ())),
                preferred_element_type=F32,
            )
            * scale
            + jnp.concatenate([bias] * GROUP, axis=1)
        )
        s_ref[b * tokens : (b + 1) * tokens, :] = scores
        top = jnp.maximum(top, jnp.max(scores.reshape(tokens // 8, 8, -1), axis=0))
    highest = jnp.maximum(jnp.max(top, axis=0, keepdims=True), -1e29)
    total = jnp.zeros((8, GROUP * tokens), F32)
    mixed = jnp.zeros((HD, GROUP * tokens), F32)
    for j in range(length // CHUNK):
        part = jnp.exp(s_ref[j * CHUNK : (j + 1) * CHUNK, :] - highest)
        total = total + jnp.sum(part.reshape(CHUNK // 8, 8, -1), axis=0)
        low = part.astype(BF)
        e_ref[0, j * CHUNK : (j + 1) * CHUNK, :] = low
        values = v_ref[2 * j : 2 * j + 2, :tokens, :].reshape(CHUNK, HD)
        mixed = mixed + contract_rows(values, low)
    total = jnp.sum(total, axis=0, keepdims=True)
    inverse = 1.0 / jnp.where(total > 0.5, total, 1.0)
    o_ref[0] = mixed * inverse
    inv_ref[0] = jnp.broadcast_to(inverse, (8, GROUP * tokens))


def attend(query, keys_values, rows):
    tokens = rows.shape[1]
    wide = GROUP * tokens
    length = N_CTX * tokens
    return pl.pallas_call(
        attend_kernel,
        name="attend",
        grid=(KV_HEADS,),
        in_specs=[
            pl.BlockSpec((1, wide, HD), lambda h: (h, 0, 0)),
            pl.BlockSpec((N_CTX, tokens + 16, HD), lambda h: (0, 0, h)),
            pl.BlockSpec((N_CTX, tokens + 16, HD), lambda h: (0, 0, KV_HEADS + h)),
            pl.BlockSpec((2, tokens), lambda h: (0, 0)),
        ],
        out_specs=[
            pl.BlockSpec((1, length, wide), lambda h: (h, 0, 0)),
            pl.BlockSpec((1, HD, wide), lambda h: (h, 0, 0)),
            pl.BlockSpec((1, 8, wide), lambda h: (h, 0, 0)),
        ],
        out_shape=[
            jax.ShapeDtypeStruct((KV_HEADS, length, wide), BF),
            jax.ShapeDtypeStruct((KV_HEADS, HD, wide), F32),
            jax.ShapeDtypeStruct((KV_HEADS, 8, wide), F32),
        ],
        scratch_shapes=[pltpu.VMEM((length, wide), F32)],
        compiler_params=pltpu.CompilerParams(vmem_limit_bytes=48 * 2**20),
        cost_estimate=pl.CostEstimate(
            flops=4 * KV_HEADS * length * wide * HD,
            bytes_accessed=2 * KV_HEADS * length * wide + 4 * 2**20,
            transcendentals=KV_HEADS * length * wide,
        ),
    )(query, keys_values, keys_values, rows)


def attend_back_kernel(
    e_ref, q_ref, k_ref, v_ref, g_ref, o_ref, inv_ref, dq_ref, dk_ref, dv_ref
):
    tokens = k_ref.shape[1] - 16
    length = N_CTX * tokens
    scale = HD ** (-0.5)
    query, grad = q_ref[0], g_ref[0]
    inverse = inv_ref[0, 0:1, :]
    grad_turned = grad.astype(F32).T
    weighted = jnp.sum(grad_turned * o_ref[0], axis=0, keepdims=True)
    factor = inverse * scale
    shift = weighted * factor
    grad_scaled = (grad_turned * inverse).T.astype(BF)
    turned = jnp.zeros((HD, GROUP * tokens), F32)
    for j in range(length // CHUNK):
        part = e_ref[0, j * CHUNK : (j + 1) * CHUNK, :]
        keys = k_ref[2 * j : 2 * j + 2, :tokens, :].reshape(CHUNK, HD)
        values = v_ref[2 * j : 2 * j + 2, :tokens, :].reshape(CHUNK, HD)
        prob_grad = contract_cols(values, grad)
        score_grad = (part.astype(F32) * (prob_grad * factor - shift)).astype(BF)
        dk = jnp.dot(score_grad, query, preferred_element_type=F32)
        dv = jnp.dot(part, grad_scaled, preferred_element_type=F32)
        dk_ref[2 * j : 2 * j + 2] = dk.reshape(2, tokens, HD).astype(dk_ref.dtype)
        dv_ref[2 * j : 2 * j + 2] = dv.reshape(2, tokens, HD).astype(dv_ref.dtype)
        turned = turned + contract_rows(keys, score_grad)
    dq_ref[0] = turned


def attend_back(expo, query, keys_values, grad, mixed, inverse):
    wide = query.shape[1]
    tokens = wide // GROUP
    length = N_CTX * tokens
    return pl.pallas_call(
        attend_back_kernel,
        name="attend_back",
        grid=(KV_HEADS,),
        in_specs=[
            pl.BlockSpec((1, length, wide), lambda h: (h, 0, 0)),
            pl.BlockSpec((1, wide, HD), lambda h: (h, 0, 0)),
            pl.BlockSpec((N_CTX, tokens + 16, HD), lambda h: (0, 0, h)),
            pl.BlockSpec((N_CTX, tokens + 16, HD), lambda h: (0, 0, KV_HEADS + h)),
            pl.BlockSpec((1, wide, HD), lambda h: (h, 0, 0)),
            pl.BlockSpec((1, HD, wide), lambda h: (h, 0, 0)),
            pl.BlockSpec((1, 8, wide), lambda h: (h, 0, 0)),
        ],
        out_specs=[
            pl.BlockSpec((1, HD, wide), lambda h: (h, 0, 0)),
            pl.BlockSpec((N_CTX, tokens, HD), lambda h: (0, 0, h)),
            pl.BlockSpec((N_CTX, tokens, HD), lambda h: (0, 0, h)),
        ],
        out_shape=[
            jax.ShapeDtypeStruct((KV_HEADS, HD, wide), F32),
            jax.ShapeDtypeStruct((N_CTX, tokens, KV_HEADS * HD), BF),
            jax.ShapeDtypeStruct((N_CTX, tokens, KV_HEADS * HD), BF),
        ],
        compiler_params=pltpu.CompilerParams(vmem_limit_bytes=48 * 2**20),
        cost_estimate=pl.CostEstimate(
            flops=8 * KV_HEADS * length * wide * HD,
            bytes_accessed=2 * KV_HEADS * length * wide + 6 * 2**20,
            transcendentals=0,
        ),
    )(expo, query, keys_values, keys_values, grad, mixed, inverse)


def apart(value, mask):
    out = 0
    for bit in (1, 2, 4):
        out = out + bit * lax.rem(lax.div(value, bit) + lax.div(mask, bit), 2)
    return out


def mlp_kernel(
    nm_ref,
    cot_ref,
    gu_ref,
    down_ref,
    grad_ref,
    out_ref,
    sum_gu_ref,
    sum_dn_ref,
    nm,
    cot,
    gu,
    down,
    act,
    gate_low,
    up_low,
    part,
    part_in,
    outs,
    gu_in,
    dn_in,
    nm_send,
    nm_recv,
    part_send,
    part_recv,
    swap_send,
    swap_recv,
    local,
):
    c, f = lax.axis_index("ctx"), lax.axis_index("fsdp")
    core = lax.rem(c, 2)
    sibling = (flip(c, 1), f)
    tokens, width = nm_ref.shape
    units = down_ref.shape[0]
    rows = 2 * tokens
    greet([(c, flip(f, i)) for i in range(1, N_FS)] + [sibling])

    def normed_copy(i):
        return pltpu.make_async_remote_copy(
            src_ref=nm_ref,
            dst_ref=nm.at[i],
            send_sem=nm_send.at[i],
            recv_sem=nm_recv.at[i],
            device_id=(c, apart(f, i)),
            device_id_type=MESH,
        )

    def part_copy(i):
        return pltpu.make_async_remote_copy(
            src_ref=part.at[i],
            dst_ref=part_in.at[i],
            send_sem=part_send.at[i],
            recv_sem=part_recv.at[i],
            device_id=(c, apart(f, i)),
            device_id_type=MESH,
        )

    for i in range(1, N_FS):
        normed_copy(i).start()
    loads = [
        pltpu.make_async_copy(nm_ref, nm.at[0], local.at[0]),
        pltpu.make_async_copy(gu_ref, gu, local.at[1]),
        pltpu.make_async_copy(cot_ref, cot, local.at[2]),
        pltpu.make_async_copy(down_ref, down, local.at[3]),
    ]
    for load in loads:
        load.start()
    for load in loads:
        load.wait()

    def out_copy(s):
        return pltpu.make_async_copy(
            outs.at[lax.rem(s, 2)], out_ref.at[pl.ds(2 * s, 2)], local.at[4 + lax.rem(s, 2)]
        )

    def pair(s, carry):
        @pl.when(s > 0)
        def _():
            normed_copy(2 * s).wait_recv()

        normed_copy(2 * s + 1).wait_recv()
        at = pl.multiple_of(s * rows, rows)
        x = nm[pl.ds(2 * s, 2)].reshape(rows, width)
        gate = jnp.dot(x, gu[0], preferred_element_type=F32)
        up = jnp.dot(x, gu[1], preferred_element_type=F32)
        grad = contract_cols(cot[pl.ds(2 * s, 2)].reshape(rows, width), down[...])
        sigma = jax.nn.sigmoid(gate)
        swish = gate * sigma
        act[pl.ds(at, rows), :] = (swish * up).astype(BF)
        gate_low[pl.ds(at, rows), :] = (
            grad * up * sigma * (1.0 + gate * (1.0 - sigma))
        ).astype(BF)
        up_low[pl.ds(at, rows), :] = (grad * swish).astype(BF)
        summed = contract_cols(gate_low[pl.ds(at, rows), :], gu[0])
        summed = summed + contract_cols(up_low[pl.ds(at, rows), :], gu[1])
        part[pl.ds(2 * s, 2)] = summed.astype(BF).reshape(2, tokens, width)

        @pl.when(s > 0)
        def _():
            part_copy(2 * s).start()

        part_copy(2 * s + 1).start()

        @pl.when(s > 1)
        def _():
            out_copy(s - 2).wait()

        result = jnp.dot(act[pl.ds(at, rows), :], down[...], preferred_element_type=F32)
        outs[lax.rem(s, 2)] = result.astype(BF).reshape(2, tokens, width)
        out_copy(s).start()
        return carry

    lax.fori_loop(0, N_FS // 2, pair, 0)

    every = N_FS * tokens

    def gate_up(m, carry):
        at = pl.multiple_of(m * 256, 256)
        x = nm[:, :, pl.ds(at, 256)].reshape(every, 256)
        gu[0, pl.ds(at, 256), :] = contract_rows(x, gate_low[...]).astype(BF)
        gu[1, pl.ds(at, 256), :] = contract_rows(x, up_low[...]).astype(BF)
        return carry

    lax.fori_loop(0, width // 256, gate_up, 0)
    swap_gu = pltpu.make_async_remote_copy(
        src_ref=gu.at[1 - core],
        dst_ref=gu_in,
        send_sem=swap_send.at[0],
        recv_sem=swap_recv.at[0],
        device_id=sibling,
        device_id_type=MESH,
    )
    swap_gu.start()
    turned = cot[...].reshape(every, width)

    def down_rows(m, carry):
        at = pl.multiple_of(m * 256, 256)
        down[pl.ds(at, 256), :] = contract_rows(act[:, pl.ds(at, 256)], turned).astype(BF)
        return carry

    whole = units // 256
    lax.fori_loop(0, whole, down_rows, 0)
    if units % 256:
        down[whole * 256 :, :] = contract_rows(act[:, whole * 256 :], turned).astype(BF)
    half = units // 2
    swap_dn = pltpu.make_async_remote_copy(
        src_ref=down.at[pl.ds(pl.multiple_of((1 - core) * half, 16), half)],
        dst_ref=dn_in,
        send_sem=swap_send.at[1],
        recv_sem=swap_recv.at[1],
        device_id=sibling,
        device_id_type=MESH,
    )
    swap_dn.start()
    swap_gu.wait_recv()

    def add_gu(m, carry):
        at = pl.multiple_of(m * 256, 256)
        gu_in[pl.ds(at, 256), :] = (
            gu[core, pl.ds(at, 256), :].astype(F32) + gu_in[pl.ds(at, 256), :].astype(F32)
        ).astype(BF)
        return carry

    lax.fori_loop(0, width // 256, add_gu, 0)
    save_gu = pltpu.make_async_copy(gu_in, sum_gu_ref, local.at[6])
    save_gu.start()
    swap_dn.wait_recv()

    def add_dn(m, carry):
        at = pl.multiple_of(m * 112, 16)
        own = down[pl.ds(pl.multiple_of(core * half + m * 112, 16), 112), :]
        dn_in[pl.ds(at, 112), :] = (
            own.astype(F32) + dn_in[pl.ds(at, 112), :].astype(F32)
        ).astype(BF)
        return carry

    lax.fori_loop(0, half // 112, add_dn, 0)
    save_dn = pltpu.make_async_copy(dn_in, sum_dn_ref, local.at[7])
    save_dn.start()
    total = part[0].astype(F32)
    for i in range(1, N_FS):
        part_copy(i).wait_recv()
        total = total + part_in[i].astype(F32)
    grad_ref[...] = total
    for i in range(1, N_FS):
        normed_copy(i).wait_send()
        part_copy(i).wait_send()
    swap_gu.wait_send()
    swap_dn.wait_send()
    for copy in (out_copy(2), out_copy(3), save_gu, save_dn):
        copy.wait()


def feed_forward(cid, normed, cot_all, columns, down_weight):
    tokens, width = normed.shape
    units = down_weight.shape[0]
    every = N_FS * tokens
    return pl.pallas_call(
        mlp_kernel,
        name="feed_forward",
        out_shape=[
            jax.ShapeDtypeStruct((tokens, width), F32),
            jax.ShapeDtypeStruct((N_FS, tokens, width), BF),
            jax.ShapeDtypeStruct((width, units), BF),
            jax.ShapeDtypeStruct((units // 2, width), BF),
        ],
        in_specs=[pl.BlockSpec(memory_space=pl.ANY)] * 4,
        out_specs=[pl.BlockSpec(memory_space=pltpu.VMEM)]
        + [pl.BlockSpec(memory_space=pl.ANY)] * 3,
        scratch_shapes=[
            pltpu.VMEM((N_FS, tokens, width), BF),
            pltpu.VMEM((N_FS, tokens, width), BF),
            pltpu.VMEM((2, width, units), BF),
            pltpu.VMEM((units, width), BF),
            pltpu.VMEM((every, units), BF),
            pltpu.VMEM((every, units), BF),
            pltpu.VMEM((every, units), BF),
            pltpu.VMEM((N_FS, tokens, width), BF),
            pltpu.VMEM((N_FS, tokens, width), BF),
            pltpu.VMEM((2, 2, tokens, width), BF),
            pltpu.VMEM((width, units), BF),
            pltpu.VMEM((units // 2, width), BF),
            pltpu.SemaphoreType.DMA((N_FS,)),
            pltpu.SemaphoreType.DMA((N_FS,)),
            pltpu.SemaphoreType.DMA((N_FS,)),
            pltpu.SemaphoreType.DMA((N_FS,)),
            pltpu.SemaphoreType.DMA((2,)),
            pltpu.SemaphoreType.DMA((2,)),
            pltpu.SemaphoreType.DMA((8,)),
        ],
        compiler_params=pltpu.CompilerParams(
            collective_id=cid, has_side_effects=True, vmem_limit_bytes=60 * 2**20
        ),
    )(normed, cot_all, columns, down_weight)


def body(
    layer_input,
    segments,
    positions,
    attn_norm,
    q_weight,
    q_bias,
    k_weight,
    k_bias,
    v_weight,
    v_bias,
    o_weight,
    mlp_norm,
    gate_weight,
    up_weight,
    down_weight,
    out_cotangent,
):
    tokens, width = layer_input.shape[1:]
    rows = gate_weight.shape[0]
    units = gate_weight.shape[1] // N_FS
    q_width = HEADS * HD
    kv_width = KV_HEADS * HD
    half_block = tokens // 2
    ctx = lax.axis_index("ctx")
    core = lax.rem(ctx, 2)
    pair = lax.div(ctx, 2)
    x_part = lax.rem(ctx, N_FS)
    inputs = layer_input[0].astype(F32)
    segment = segments[0]
    position = positions[0]
    keep = (segment > 0).astype(F32)[:, None]
    cotangent = out_cotangent[0].astype(F32) * keep
    cot_low = cotangent.astype(BF)

    qkv = jnp.concatenate([q_weight, k_weight, v_weight], axis=1).reshape(2, rows // 2, -1)
    small = jnp.concatenate([attn_norm, mlp_norm, q_bias, k_bias, v_bias]).reshape(-1, 128)
    small = jnp.pad(small, ((0, 16 - small.shape[0]), (0, 0)))
    cut = rows // 4
    start = lax.rem(x_part, 4) * cut
    gate_cut = lax.dynamic_slice_in_dim(gate_weight, start, cut, 0)
    up_cut = lax.dynamic_slice_in_dim(up_weight, start, cut, 0)
    blocks = (
        jnp.where(x_part < 4, gate_cut, up_cut).reshape(cut, N_FS, units).transpose(1, 0, 2)
    )
    full_qkv, small_all, columns = exchange(
        first_kernel,
        "gather_qkv",
        1,
        (qkv, small, blocks),
        [
            ((N_FS,) + qkv.shape, BF),
            ((N_FS,) + small.shape, BF),
            ((2, N_FS, 4, cut, units), BF),
        ],
        35,
        3,
    )
    columns = columns.reshape(2, width, units)

    flat = small_all[:, :5].reshape(N_FS, -1)
    marks = [0, rows, 2 * rows, 2 * rows + q_width // N_FS]
    marks += [marks[-1] + kv_width // N_FS, marks[-1] + 2 * kv_width // N_FS]
    gain_one, gain_two, bias_q, bias_k, bias_v = (
        flat[:, lo:hi].reshape(-1).astype(F32) for lo, hi in zip(marks[:-1], marks[1:])
    )
    bias_all = jnp.concatenate([bias_q, bias_k, bias_v])
    full_qkv = full_qkv.reshape(width, q_width + 2 * kv_width)

    scale_one = lax.rsqrt(jnp.mean(inputs * inputs, axis=-1, keepdims=True) + EPSILON)
    norm_first = inputs * scale_one
    normed_in = (norm_first * gain_one).astype(BF)
    projected = jnp.dot(normed_in, full_qkv, preferred_element_type=F32) + bias_all
    cosine, sine = rope_tables(position, HD)
    turned = rotate(
        projected[:, : q_width + kv_width].reshape(tokens, HEADS + KV_HEADS, HD), cosine, sine
    ).astype(BF)
    value_low = projected[:, q_width + kv_width :].astype(BF)
    query = (
        turned[:, :HEADS]
        .reshape(tokens, KV_HEADS, GROUP, HD)
        .transpose(1, 2, 0, 3)
        .reshape(KV_HEADS, GROUP * tokens, HD)
    )
    keys_values = jnp.concatenate([turned[:, HEADS:].reshape(tokens, kv_width), value_low], axis=1)
    segment_rows = jnp.broadcast_to(
        jnp.tile(segment.astype(BF)[None, :], (1, 2 * KV_HEADS)), (16, 2 * kv_width)
    )
    keys_values = jnp.concatenate([keys_values, segment_rows], axis=0)
    kv_all, full_o, cot_all = exchange(
        second_kernel,
        "gather_kv_o",
        2,
        (keys_values, o_weight.reshape(2, rows // 2, width), cot_low),
        [
            ((N_CTX,) + keys_values.shape, BF),
            ((N_FS, 2, rows // 2, width), BF),
            ((N_FS, tokens, width), BF),
        ],
        36,
        3,
    )
    full_o = full_o.reshape(q_width, width)
    within = jnp.arange(tokens, dtype=jnp.int32)
    row_place = jnp.where(
        within < half_block,
        ctx * half_block + within,
        (2 * N_CTX - 1 - ctx) * half_block + within - half_block,
    )
    row_info = jnp.stack([row_place.astype(F32), segment.astype(F32)])
    expo, mixed, inverse = attend(query, kv_all, row_info)
    attended = (
        mixed.reshape(KV_HEADS, HD, GROUP, tokens).transpose(3, 0, 2, 1).reshape(tokens, q_width)
    ).astype(BF)
    middle = inputs + jnp.dot(attended, full_o, preferred_element_type=F32)
    scale_two = lax.rsqrt(jnp.mean(middle * middle, axis=-1, keepdims=True) + EPSILON)
    norm_second = middle * scale_two
    normed_mid = (norm_second * gain_two).astype(BF)

    piece = rows // 8
    mid_norm_grad, out_part, sum_gu, sum_down = feed_forward(
        8, normed_mid, cot_all, columns, down_weight
    )
    output_rows = middle + out_part[0].astype(F32)
    for i in range(1, N_FS):
        output_rows = output_rows + swap_fs(out_part[i], i).astype(F32)
    output_rows = output_rows.astype(BF)
    sum_gu = sum_gu.reshape(N_FS, 8, piece, units)
    sum_down = sum_down.reshape(8, units // 16, width)
    far_gu, far_down = scatter_ctx("scatter_mlp", 3, (sum_gu, sum_down))
    done_gu = (
        lax.dynamic_index_in_dim(sum_gu, pair, 1, False).astype(F32)
        + jnp.sum(far_gu.astype(F32), axis=0)
    ).astype(BF)
    done_down = (
        lax.dynamic_index_in_dim(sum_down, pair, 0, False).astype(F32)
        + jnp.sum(far_down.astype(F32), axis=0)
    ).astype(BF)

    gain_two_grad = jnp.sum(mid_norm_grad * norm_second, axis=0)
    scaled_two = mid_norm_grad * gain_two
    mid_grad = cotangent + scale_two * (
        scaled_two - norm_second * jnp.mean(scaled_two * norm_second, axis=-1, keepdims=True)
    )
    branch_low = mid_grad.astype(BF)
    attended_grad = contract_cols(branch_low, full_o).astype(BF)
    grad_rows = (
        attended_grad.reshape(tokens, KV_HEADS, GROUP, HD)
        .transpose(1, 2, 0, 3)
        .reshape(KV_HEADS, GROUP * tokens, HD)
    )
    turned_grad, key_part, value_part = attend_back(
        expo, query, kv_all, grad_rows, mixed, inverse
    )
    kv_part = jnp.concatenate([key_part, value_part], axis=2)
    kv_part = kv_part.reshape(N_CTX // 2, 2, tokens, 2 * kv_width)
    keep_kv = jnp.where(core == 0, kv_part[:, 0], kv_part[:, 1])
    send_kv = jnp.where(core == 0, kv_part[:, 1], kv_part[:, 0])
    sum_kv = (keep_kv.astype(F32) + swap_ctx(send_kv, 1).astype(F32)).astype(BF)
    (far_kv,) = scatter_ctx("scatter_kv", 4, (sum_kv,))
    own_kv = lax.dynamic_index_in_dim(sum_kv, pair, 0, False).astype(F32) + jnp.sum(
        far_kv.astype(F32), axis=0
    )
    query_rot_grad = (
        turned_grad.reshape(KV_HEADS, HD, GROUP, tokens)
        .transpose(3, 0, 2, 1)
        .reshape(tokens, HEADS, HD)
    )
    turned_back = rotate(
        jnp.concatenate(
            [query_rot_grad, own_kv[:, :kv_width].reshape(tokens, KV_HEADS, HD)], axis=1
        ),
        cosine,
        -sine,
    ).reshape(tokens, q_width + kv_width)
    proj_grad = jnp.concatenate([turned_back, own_kv[:, kv_width:]], axis=1).astype(BF)
    bias_grads = jnp.sum(proj_grad.astype(F32), axis=0)
    in_norm_grad = contract_cols(proj_grad, full_qkv)
    gain_one_grad = jnp.sum(in_norm_grad * norm_first, axis=0)
    scaled_one = in_norm_grad * gain_one
    input_rows = mid_grad + scale_one * (
        scaled_one - norm_first * jnp.mean(scaled_one * norm_first, axis=-1, keepdims=True)
    )

    q_part = contract_rows(normed_in, proj_grad).astype(BF)
    o_part = contract_rows(attended, branch_low).astype(BF)
    side = q_width // 2
    low_side = jnp.concatenate(
        [o_part[:, :side], q_part[:, :side], q_part[:, q_width : q_width + kv_width]], axis=1
    )
    high_side = jnp.concatenate(
        [o_part[:, side:], q_part[:, side:q_width], q_part[:, q_width + kv_width :]], axis=1
    )
    keep_at = jnp.where(core == 0, low_side, high_side)
    send_at = jnp.where(core == 0, high_side, low_side)
    sum_at = (keep_at.astype(F32) + swap_ctx(send_at, 1).astype(F32)).astype(BF)
    sum_at = sum_at.reshape(N_FS, 8, piece, -1)
    (far_at,) = scatter_ctx("scatter_attn", 5, (sum_at,))
    done_at = (
        lax.dynamic_index_in_dim(sum_at, pair, 1, False).astype(F32)
        + jnp.sum(far_at.astype(F32), axis=0)
    ).astype(BF)

    vectors = jnp.concatenate(
        [
            v.reshape(N_FS, -1)
            for v in (
                gain_one_grad,
                gain_two_grad,
                bias_grads[:q_width],
                bias_grads[q_width : q_width + kv_width],
                bias_grads[q_width + kv_width :],
            )
        ],
        axis=1,
    ).reshape(N_FS, 5, 128)
    vectors = jnp.pad(vectors, ((0, 0), (0, 3), (0, 0)))
    own_gu, own_at, own_vec = to_owner("to_owner", 6, (done_gu, done_at, vectors))
    own_at = jnp.sum(own_at.astype(F32), axis=0).astype(BF)
    own_vec = jnp.sum(own_vec, axis=0)
    all_gu, all_at, all_down, all_vec = gather_ctx(
        "gather_grads", 7, (own_gu, own_at, done_down, own_vec)
    )
    all_vec = jnp.sum(all_vec, axis=0)[:5].reshape(-1)
    sum_vec = [all_vec[lo:hi] for lo, hi in zip(marks[:-1], marks[1:])]
    all_gu = all_gu.reshape(8, 2, N_FS, piece, units).transpose(1, 0, 3, 2, 4)
    all_gu = all_gu.reshape(2, rows, N_FS * units)
    all_at = all_at.reshape(8, 2, piece, -1).transpose(1, 0, 2, 3).reshape(2, rows, -1)
    all_down = all_down.reshape(8, 2, units // 16, width).transpose(1, 0, 2, 3)
    o_grad = jnp.concatenate([all_at[0, :, :side], all_at[1, :, :side]], axis=1).astype(F32)
    q_grad = jnp.concatenate(
        [all_at[0, :, side:q_width], all_at[1, :, side:q_width]], axis=1
    ).astype(F32)
    return (
        output_rows[None],
        input_rows[None],
        sum_vec[0],
        q_grad,
        sum_vec[2],
        all_at[0, :, q_width:].astype(F32),
        sum_vec[3],
        all_at[1, :, q_width:].astype(F32),
        sum_vec[4],
        o_grad,
        sum_vec[1],
        all_gu[0].astype(F32),
        all_gu[1].astype(F32),
        all_down.reshape(units, width).astype(F32),
    )


def solution(mesh):
    placed = (
        P("fsdp", "ctx", None),
        P("fsdp", "ctx"),
        P("fsdp", "ctx"),
        P("fsdp"),
        P("fsdp", None),
        P("fsdp"),
        P("fsdp", None),
        P("fsdp"),
        P("fsdp", None),
        P("fsdp"),
        P("fsdp", None),
        P("fsdp"),
        P("fsdp", None),
        P("fsdp", None),
        P("fsdp", None),
        P("fsdp", "ctx", None),
    )
    return jax.shard_map(
        body,
        mesh=mesh,
        in_specs=placed,
        out_specs=(
            P("fsdp", "ctx", None),
            P("fsdp", "ctx", None),
            P("fsdp"),
            P("fsdp", None),
            P("fsdp"),
            P("fsdp", None),
            P("fsdp"),
            P("fsdp", None),
            P("fsdp"),
            P("fsdp", None),
            P("fsdp"),
            P("fsdp", None),
            P("fsdp", None),
            P("fsdp", None),
        ),
        check_vma=False,
    )
```

```python
import functools

import jax
import jax.numpy as jnp
from jax import lax
from jax.experimental import pallas as pl
from jax.experimental.pallas import tpu as pltpu
from jax.sharding import PartitionSpec as P

HEADS = 12
KV_HEADS = 2
HD = 128
GROUP = HEADS // KV_HEADS
N_CTX = 16
N_FS = 8
EPSILON = 1e-06
THETA = 1000000.0
MESH = pl.DeviceIdType.MESH
BF = jnp.bfloat16
F32 = jnp.float32


def rope_tables(position, head_dim):
    freqs = THETA ** (-jnp.arange(0, head_dim, 2).astype(F32) / head_dim)
    angles = position.astype(F32)[:, None] * freqs[None, :]
    return (jnp.cos(angles), jnp.sin(angles))


def rotate(values, cosine, sine):
    middle = values.shape[-1] // 2
    front = values[..., :middle]
    behind = values[..., middle:]
    cos_head = cosine[:, None, :]
    sin_head = sine[:, None, :]
    return jnp.concatenate(
        [front * cos_head - behind * sin_head, behind * cos_head + front * sin_head], axis=-1
    )


def contract_rows(left, right):
    return lax.dot_general(
        left, right, (((0,), (0,)), ((), ())), preferred_element_type=F32
    )


def contract_cols(left, right):
    return lax.dot_general(
        left, right, (((1,), (1,)), ((), ())), preferred_element_type=F32
    )


def flip(value, mask):
    out = value
    bit = 1
    while bit <= mask:
        if mask & bit:
            out = out + bit * (1 - 2 * lax.rem(lax.div(value, bit), 2))
        bit *= 2
    return out


class Copies:
    def __init__(self, send, recv):
        self.send, self.recv, self.count, self.all = send, recv, 0, []

    def start(self, src, dst, device):
        copy = pltpu.make_async_remote_copy(
            src_ref=src,
            dst_ref=dst,
            send_sem=self.send.at[self.count],
            recv_sem=self.recv.at[self.count],
            device_id=device,
            device_id_type=MESH,
        )
        self.count += 1
        copy.start()
        self.all.append(copy)
        return copy


def greet(devices):
    barrier = pltpu.get_barrier_semaphore()
    for device in devices:
        pl.semaphore_signal(barrier, inc=1, device_id=device, device_id_type=MESH)
    pl.semaphore_wait(barrier, len(devices))


def exchange(kernel, name, cid, ins, outs, copies, locals_):
    return pl.pallas_call(
        kernel,
        name=name,
        out_shape=[jax.ShapeDtypeStruct(s, d) for s, d in outs],
        in_specs=[pl.BlockSpec(memory_space=pl.ANY)] * len(ins),
        out_specs=[pl.BlockSpec(memory_space=pl.ANY)] * len(outs),
        scratch_shapes=[
            pltpu.SemaphoreType.DMA((copies,)),
            pltpu.SemaphoreType.DMA((copies,)),
            pltpu.SemaphoreType.DMA((locals_,)),
        ],
        compiler_params=pltpu.CompilerParams(collective_id=cid, has_side_effects=True),
    )(*ins)


def first_kernel(w_ref, s_ref, g_ref, w_out, s_out, g_out, send, recv, local):
    c, f = lax.axis_index("ctx"), lax.axis_index("fsdp")
    core = lax.rem(c, 2)
    sibling = (flip(c, 1), f)
    peers = [(c, flip(f, i)) for i in range(1, N_FS)]
    along = [(flip(c, 2 * i), f) for i in range(1, 4)]
    greet(peers + along + [sibling])
    copies = Copies(send, recv)

    def columns(device):
        part = lax.rem(device[0], N_FS)
        return g_out.at[lax.div(part, 4), :, lax.rem(part, 4)]

    def block(device, source):
        part = lax.rem(device[0], N_FS)
        return g_out.at[lax.div(part, 4), source, lax.rem(part, 4)]

    here = (c, f)
    own = [
        pltpu.make_async_copy(g_ref.at[f], block(here, f), local.at[2]),
        pltpu.make_async_copy(w_ref, w_out.at[f], local.at[0]),
        pltpu.make_async_copy(s_ref, s_out.at[f], local.at[1]),
    ]
    for copy in own:
        copy.start()
    rest = [copies.start(s_ref, s_out.at[f], peer) for peer in peers]
    blocks = [copies.start(g_ref.at[peer[1]], block(here, f), peer) for peer in peers]
    halves = [copies.start(w_ref.at[core], w_out.at[f, core], peer) for peer in peers]
    own[0].wait()
    for copy in blocks:
        copy.wait_recv()
    mine = columns(here)
    near = [copies.start(mine, mine, device) for device in along]
    rest.append(copies.start(mine, mine, sibling))
    for half, peer in zip(halves, peers):
        half.wait_recv()
        place = w_out.at[peer[1], core]
        rest.append(copies.start(place, place, sibling))
    for copy, device in zip(near, along):
        copy.wait_recv()
        place = columns(device)
        rest.append(copies.start(place, place, sibling))
    for copy in halves + blocks + near:
        copy.wait_send()
    for copy in rest + own[1:]:
        copy.wait()


def second_kernel(kv_ref, w_ref, t_ref, kv_out, w_out, t_out, send, recv, local):
    c, f = lax.axis_index("ctx"), lax.axis_index("fsdp")
    core = lax.rem(c, 2)
    sibling = (flip(c, 1), f)
    ring = [(flip(c, 2 * i), f) for i in range(1, N_CTX // 2)]
    peers = [(c, flip(f, i)) for i in range(1, N_FS)]
    greet(ring + peers + [sibling])
    copies = Copies(send, recv)
    own = [
        pltpu.make_async_copy(kv_ref, kv_out.at[c], local.at[0]),
        pltpu.make_async_copy(w_ref, w_out.at[f], local.at[1]),
        pltpu.make_async_copy(t_ref, t_out.at[0], local.at[2]),
    ]
    for copy in own:
        copy.start()
    keys = [copies.start(kv_ref, kv_out.at[c], device) for device in ring]
    rest = [copies.start(kv_ref, kv_out.at[c], sibling)]
    halves = [copies.start(w_ref.at[core], w_out.at[f, core], peer) for peer in peers]
    rest += [copies.start(t_ref, t_out.at[i + 1], peer) for i, peer in enumerate(peers)]
    for key, device in zip(keys, ring):
        key.wait_recv()
        place = kv_out.at[device[0]]
        rest.append(copies.start(place, place, sibling))
    for half, peer in zip(halves, peers):
        half.wait_recv()
        place = w_out.at[peer[1], core]
        rest.append(copies.start(place, place, sibling))
    for copy in keys + halves:
        copy.wait_send()
    for copy in rest + own:
        copy.wait()


CHUNK = 256


def attend_kernel(q_ref, k_ref, v_ref, row_ref, e_ref, o_ref, inv_ref, s_ref):
    tokens = k_ref.shape[1] - 16
    length = N_CTX * tokens
    half = tokens // 2
    scale = HD ** (-0.5)
    query = q_ref[0]
    row_place, row_seg = row_ref[0:1, :], row_ref[1:2, :]
    key_seg = k_ref[:, tokens : tokens + 16, :][:, 0, :].astype(F32).T
    within = lax.broadcasted_iota(jnp.int32, (tokens, tokens), 0)
    top = jnp.full((8, GROUP * tokens), -1e30, F32)
    for b in range(N_CTX):
        place = jnp.where(
            within < half, b * half + within, (2 * N_CTX - 1 - b) * half + within - half
        ).astype(F32)
        allowed = (place <= row_place) & (key_seg[:, b : b + 1] == row_seg) & (row_seg > 0.5)
        bias = jnp.where(allowed, 0.0, -1e30).astype(F32)
        scores = (
            lax.dot_general(
                k_ref[b, :tokens, :],
                query,
                (((1,), (1,)), ((), ())),
                preferred_element_type=F32,
            )
            * scale
            + jnp.concatenate([bias] * GROUP, axis=1)
        )
        s_ref[b * tokens : (b + 1) * tokens, :] = scores
        top = jnp.maximum(top, jnp.max(scores.reshape(tokens // 8, 8, -1), axis=0))
    highest = jnp.maximum(jnp.max(top, axis=0, keepdims=True), -1e29)
    total = jnp.zeros((8, GROUP * tokens), F32)
    mixed = jnp.zeros((HD, GROUP * tokens), F32)
    for j in range(length // CHUNK):
        part = jnp.exp(s_ref[j * CHUNK : (j + 1) * CHUNK, :] - highest)
        total = total + jnp.sum(part.reshape(CHUNK // 8, 8, -1), axis=0)
        low = part.astype(BF)
        e_ref[0, j * CHUNK : (j + 1) * CHUNK, :] = low
        values = v_ref[2 * j : 2 * j + 2, :tokens, :].reshape(CHUNK, HD)
        mixed = mixed + contract_rows(values, low)
    total = jnp.sum(total, axis=0, keepdims=True)
    inverse = 1.0 / jnp.where(total > 0.5, total, 1.0)
    o_ref[0] = mixed * inverse
    inv_ref[0] = jnp.broadcast_to(inverse, (8, GROUP * tokens))


def attend(query, keys_values, rows):
    tokens = rows.shape[1]
    wide = GROUP * tokens
    length = N_CTX * tokens
    return pl.pallas_call(
        attend_kernel,
        name="attend",
        grid=(KV_HEADS,),
        in_specs=[
            pl.BlockSpec((1, wide, HD), lambda h: (h, 0, 0)),
            pl.BlockSpec((N_CTX, tokens + 16, HD), lambda h: (0, 0, h)),
            pl.BlockSpec((N_CTX, tokens + 16, HD), lambda h: (0, 0, KV_HEADS + h)),
            pl.BlockSpec((2, tokens), lambda h: (0, 0)),
        ],
        out_specs=[
            pl.BlockSpec((1, length, wide), lambda h: (h, 0, 0)),
            pl.BlockSpec((1, HD, wide), lambda h: (h, 0, 0)),
            pl.BlockSpec((1, 8, wide), lambda h: (h, 0, 0)),
        ],
        out_shape=[
            jax.ShapeDtypeStruct((KV_HEADS, length, wide), BF),
            jax.ShapeDtypeStruct((KV_HEADS, HD, wide), F32),
            jax.ShapeDtypeStruct((KV_HEADS, 8, wide), F32),
        ],
        scratch_shapes=[pltpu.VMEM((length, wide), F32)],
        compiler_params=pltpu.CompilerParams(vmem_limit_bytes=48 * 2**20),
        cost_estimate=pl.CostEstimate(
            flops=4 * KV_HEADS * length * wide * HD,
            bytes_accessed=2 * KV_HEADS * length * wide + 4 * 2**20,
            transcendentals=KV_HEADS * length * wide,
        ),
    )(query, keys_values, keys_values, rows)


def apart(value, mask):
    out = 0
    for bit in (1, 2, 4):
        out = out + bit * lax.rem(lax.div(value, bit) + lax.div(mask, bit), 2)
    return out


def mlp_kernel(
    nm_ref,
    cot_ref,
    gu_ref,
    down_ref,
    grad_ref,
    out_ref,
    sum_gu_ref,
    sum_dn_ref,
    nm,
    cot,
    gu,
    down,
    act,
    gate_low,
    up_low,
    part,
    part_in,
    outs,
    gu_in,
    dn_in,
    nm_send,
    nm_recv,
    part_send,
    part_recv,
    swap_send,
    swap_recv,
    local,
):
    c, f = lax.axis_index("ctx"), lax.axis_index("fsdp")
    core = lax.rem(c, 2)
    sibling = (flip(c, 1), f)
    tokens, width = nm_ref.shape
    units = down_ref.shape[0]
    rows = 2 * tokens
    greet([(c, flip(f, i)) for i in range(1, N_FS)] + [sibling])

    def normed_copy(i):
        return pltpu.make_async_remote_copy(
            src_ref=nm_ref,
            dst_ref=nm.at[i],
            send_sem=nm_send.at[i],
            recv_sem=nm_recv.at[i],
            device_id=(c, apart(f, i)),
            device_id_type=MESH,
        )

    def part_copy(i):
        return pltpu.make_async_remote_copy(
            src_ref=part.at[i],
            dst_ref=part_in.at[i],
            send_sem=part_send.at[i],
            recv_sem=part_recv.at[i],
            device_id=(c, apart(f, i)),
            device_id_type=MESH,
        )

    for i in range(1, N_FS):
        normed_copy(i).start()
    loads = [
        pltpu.make_async_copy(nm_ref, nm.at[0], local.at[0]),
        pltpu.make_async_copy(gu_ref, gu, local.at[1]),
        pltpu.make_async_copy(cot_ref, cot, local.at[2]),
        pltpu.make_async_copy(down_ref, down, local.at[3]),
    ]
    for load in loads:
        load.start()
    for load in loads:
        load.wait()

    def out_copy(s):
        return pltpu.make_async_copy(
            outs.at[lax.rem(s, 2)], out_ref.at[pl.ds(2 * s, 2)], local.at[4 + lax.rem(s, 2)]
        )

    def pair(s, carry):
        @pl.when(s > 0)
        def _():
            normed_copy(2 * s).wait_recv()

        normed_copy(2 * s + 1).wait_recv()
        at = pl.multiple_of(s * rows, rows)
        x = nm[pl.ds(2 * s, 2)].reshape(rows, width)
        gate = jnp.dot(x, gu[0], preferred_element_type=F32)
        up = jnp.dot(x, gu[1], preferred_element_type=F32)
        grad = contract_cols(cot[pl.ds(2 * s, 2)].reshape(rows, width), down[...])
        sigma = jax.nn.sigmoid(gate)
        swish = gate * sigma
        act[pl.ds(at, rows), :] = (swish * up).astype(BF)
        gate_low[pl.ds(at, rows), :] = (
            grad * up * sigma * (1.0 + gate * (1.0 - sigma))
        ).astype(BF)
        up_low[pl.ds(at, rows), :] = (grad * swish).astype(BF)
        summed = contract_cols(gate_low[pl.ds(at, rows), :], gu[0])
        summed = summed + contract_cols(up_low[pl.ds(at, rows), :], gu[1])
        part[pl.ds(2 * s, 2)] = summed.astype(BF).reshape(2, tokens, width)

        @pl.when(s > 0)
        def _():
            part_copy(2 * s).start()

        part_copy(2 * s + 1).start()

        @pl.when(s > 1)
        def _():
            out_copy(s - 2).wait()

        result = jnp.dot(act[pl.ds(at, rows), :], down[...], preferred_element_type=F32)
        outs[lax.rem(s, 2)] = result.astype(BF).reshape(2, tokens, width)
        out_copy(s).start()
        return carry

    lax.fori_loop(0, N_FS // 2, pair, 0)

    every = N_FS * tokens

    def gate_up(m, carry):
        at = pl.multiple_of(m * 256, 256)
        x = nm[:, :, pl.ds(at, 256)].reshape(every, 256)
        gu[0, pl.ds(at, 256), :] = contract_rows(x, gate_low[...]).astype(BF)
        gu[1, pl.ds(at, 256), :] = contract_rows(x, up_low[...]).astype(BF)
        return carry

    lax.fori_loop(0, width // 256, gate_up, 0)
    swap_gu = pltpu.make_async_remote_copy(
        src_ref=gu.at[1 - core],
        dst_ref=gu_in,
        send_sem=swap_send.at[0],
        recv_sem=swap_recv.at[0],
        device_id=sibling,
        device_id_type=MESH,
    )
    swap_gu.start()
    turned = cot[...].reshape(every, width)

    def down_rows(m, carry):
        at = pl.multiple_of(m * 256, 256)
        down[pl.ds(at, 256), :] = contract_rows(act[:, pl.ds(at, 256)], turned).astype(BF)
        return carry

    whole = units // 256
    lax.fori_loop(0, whole, down_rows, 0)
    if units % 256:
        down[whole * 256 :, :] = contract_rows(act[:, whole * 256 :], turned).astype(BF)
    half = units // 2
    swap_dn = pltpu.make_async_remote_copy(
        src_ref=down.at[pl.ds(pl.multiple_of((1 - core) * half, 16), half)],
        dst_ref=dn_in,
        send_sem=swap_send.at[1],
        recv_sem=swap_recv.at[1],
        device_id=sibling,
        device_id_type=MESH,
    )
    swap_dn.start()
    swap_gu.wait_recv()

    def add_gu(m, carry):
        at = pl.multiple_of(m * 256, 256)
        gu_in[pl.ds(at, 256), :] = (
            gu[core, pl.ds(at, 256), :].astype(F32) + gu_in[pl.ds(at, 256), :].astype(F32)
        ).astype(BF)
        return carry

    lax.fori_loop(0, width // 256, add_gu, 0)
    save_gu = pltpu.make_async_copy(gu_in, sum_gu_ref, local.at[6])
    save_gu.start()
    swap_dn.wait_recv()

    def add_dn(m, carry):
        at = pl.multiple_of(m * 112, 16)
        own = down[pl.ds(pl.multiple_of(core * half + m * 112, 16), 112), :]
        dn_in[pl.ds(at, 112), :] = (
            own.astype(F32) + dn_in[pl.ds(at, 112), :].astype(F32)
        ).astype(BF)
        return carry

    lax.fori_loop(0, half // 112, add_dn, 0)
    save_dn = pltpu.make_async_copy(dn_in, sum_dn_ref, local.at[7])
    save_dn.start()
    total = part[0].astype(F32)
    for i in range(1, N_FS):
        part_copy(i).wait_recv()
        total = total + part_in[i].astype(F32)
    grad_ref[...] = total
    for i in range(1, N_FS):
        normed_copy(i).wait_send()
        part_copy(i).wait_send()
    swap_gu.wait_send()
    swap_dn.wait_send()
    for copy in (out_copy(2), out_copy(3), save_gu, save_dn):
        copy.wait()


def feed_forward(cid, normed, cot_all, columns, down_weight):
    tokens, width = normed.shape
    units = down_weight.shape[0]
    every = N_FS * tokens
    return pl.pallas_call(
        mlp_kernel,
        name="feed_forward",
        out_shape=[
            jax.ShapeDtypeStruct((tokens, width), F32),
            jax.ShapeDtypeStruct((N_FS, tokens, width), BF),
            jax.ShapeDtypeStruct((width, units), BF),
            jax.ShapeDtypeStruct((units // 2, width), BF),
        ],
        in_specs=[pl.BlockSpec(memory_space=pl.ANY)] * 4,
        out_specs=[pl.BlockSpec(memory_space=pltpu.VMEM)]
        + [pl.BlockSpec(memory_space=pl.ANY)] * 3,
        scratch_shapes=[
            pltpu.VMEM((N_FS, tokens, width), BF),
            pltpu.VMEM((N_FS, tokens, width), BF),
            pltpu.VMEM((2, width, units), BF),
            pltpu.VMEM((units, width), BF),
            pltpu.VMEM((every, units), BF),
            pltpu.VMEM((every, units), BF),
            pltpu.VMEM((every, units), BF),
            pltpu.VMEM((N_FS, tokens, width), BF),
            pltpu.VMEM((N_FS, tokens, width), BF),
            pltpu.VMEM((2, 2, tokens, width), BF),
            pltpu.VMEM((width, units), BF),
            pltpu.VMEM((units // 2, width), BF),
            pltpu.SemaphoreType.DMA((N_FS,)),
            pltpu.SemaphoreType.DMA((N_FS,)),
            pltpu.SemaphoreType.DMA((N_FS,)),
            pltpu.SemaphoreType.DMA((N_FS,)),
            pltpu.SemaphoreType.DMA((2,)),
            pltpu.SemaphoreType.DMA((2,)),
            pltpu.SemaphoreType.DMA((8,)),
        ],
        compiler_params=pltpu.CompilerParams(
            collective_id=cid, has_side_effects=True, vmem_limit_bytes=60 * 2**20
        ),
    )(normed, cot_all, columns, down_weight)


def turn_back(grad, cos_wide, sin_wide):
    half = grad.shape[1] // 2
    swapped = jnp.concatenate([grad[:, half:], grad[:, :half]], axis=1)
    return grad * cos_wide + swapped * sin_wide


def attention_back_kernel(
    sum_gu,
    sum_dn,
    expo_hbm,
    kv_hbm,
    o_hbm,
    mng_ref,
    middle_ref,
    cot_ref,
    gain_ref,
    query_ref,
    mixed_ref,
    inv_ref,
    attended_ref,
    normed_ref,
    cos_ref,
    sin_ref,
    done_gu,
    done_dn,
    own_kv,
    o_red,
    q_red,
    q_grad,
    mid_ref,
    gain_grad,
    expo,
    kv,
    full_o,
    branch,
    back,
    gu_mine,
    gu_z,
    gu_x,
    dn_mine,
    dn_x,
    dn_z,
    dkv,
    kv_in,
    kv_far,
    out_half,
    keep_half,
    o_in,
    q_in,
    o_far,
    q_far,
    send,
    recv,
    local,
):
    c, f = lax.axis_index("ctx"), lax.axis_index("fsdp")
    core, pair = lax.rem(c, 2), lax.div(c, 2)
    x_at, z_at = lax.rem(pair, 4), lax.div(pair, 4)
    sibling = (flip(c, 1), f)
    partner = (flip(c, 8), f)
    along = [(flip(c, 2 * i), f) for i in range(1, 4)]
    ring = [(flip(c, 2 * i), f) for i in range(1, N_CTX // 2)]
    peers = [(c, flip(f, i)) for i in range(1, N_FS)]
    greet(ring + peers + [sibling])
    copies = Copies(send, recv)
    tokens, width = mng_ref.shape
    strip = dn_mine.shape[1]
    window = dn_z.shape[0]
    shift = dn_mine.shape[0] - window
    side = width // 2
    scale = HD ** (-0.5)

    def x_of(device):
        return lax.rem(lax.div(device[0], 2), 4)

    def strip_of(ref, x):
        return ref.at[:, pl.ds(pl.multiple_of(x * strip, strip), strip)]

    def local_copy(src, dst, n):
        copy = pltpu.make_async_copy(src, dst, local.at[n])
        copy.start()
        return copy

    z_gu = copies.start(sum_gu.at[:, pl.ds(4 * (1 - z_at), 4)], gu_z, partner)
    x_dn = [
        copies.start(strip_of(sum_dn, x_of(device)), dn_x.at[i], device)
        for i, device in enumerate(along)
    ]
    loads_o = local_copy(o_hbm, full_o, 0)
    loads = [
        local_copy(kv_hbm, kv, 1),
        local_copy(expo_hbm, expo, 2),
    ]
    loads_own = [
        local_copy(sum_gu.at[:, pl.ds(4 * z_at, 4)], gu_mine, 3),
        local_copy(strip_of(sum_dn, x_at), dn_mine, 4),
    ]

    middle = middle_ref[...]
    scale_two = lax.rsqrt(jnp.mean(middle * middle, axis=-1, keepdims=True) + EPSILON)
    norm = middle * scale_two
    grad = mng_ref[...]
    gain_grad[...] = jnp.sum(grad * norm, axis=0, keepdims=True)
    scaled = grad * gain_ref[...]
    mid = cot_ref[...].astype(F32) + scale_two * (
        scaled - norm * jnp.mean(scaled * norm, axis=-1, keepdims=True)
    )
    mid_ref[...] = mid
    branch[...] = mid.astype(BF)
    loads_o.wait()
    back[...] = contract_cols(branch[...], full_o[...]).astype(BF)

    def columns_of(which):
        return pl.ds(pl.multiple_of(which * side, side), side)

    out_half[...] = contract_rows(attended_ref[...], branch[:, columns_of(1 - core)]).astype(BF)
    swap_o = copies.start(out_half, o_in, sibling)
    keep_half[...] = contract_rows(attended_ref[...], branch[:, columns_of(core)]).astype(BF)
    for load in loads:
        load.wait()

    length = N_CTX * tokens
    for h in range(KV_HEADS):
        query = query_ref[h]
        heads = back[:, h * GROUP * HD : (h + 1) * GROUP * HD]
        rows = jnp.concatenate([heads[:, i * HD : (i + 1) * HD] for i in range(GROUP)], axis=0)
        inverse = inv_ref[h, 0:1, :]
        turned = rows.astype(F32).T
        weighted = jnp.sum(turned * mixed_ref[h], axis=0, keepdims=True)
        factor = inverse * scale
        offset = weighted * factor
        rows_scaled = (turned * inverse).T.astype(BF)
        dq = jnp.zeros((HD, GROUP * tokens), F32)
        for j in range(length // CHUNK):
            part = expo[h, j * CHUNK : (j + 1) * CHUNK, :]
            keys = kv[2 * j : 2 * j + 2, :tokens, h * HD : (h + 1) * HD].reshape(CHUNK, HD)
            values = kv[
                2 * j : 2 * j + 2, :tokens, (KV_HEADS + h) * HD : (KV_HEADS + h + 1) * HD
            ].reshape(CHUNK, HD)
            prob_grad = contract_cols(values, rows)
            score_grad = (part.astype(F32) * (prob_grad * factor - offset)).astype(BF)
            dk = jnp.dot(score_grad, query, preferred_element_type=F32).astype(BF)
            dv = jnp.dot(part, rows_scaled, preferred_element_type=F32).astype(BF)
            for side_core in range(2):
                cut = slice(side_core * tokens, (side_core + 1) * tokens)
                dkv[side_core, j, :, h * HD : (h + 1) * HD] = dk[cut]
                dkv[side_core, j, :, (KV_HEADS + h) * HD : (KV_HEADS + h + 1) * HD] = dv[cut]
            dq = dq + contract_rows(keys, score_grad)
        for i in range(GROUP):
            at = (h * GROUP + i) * HD
            q_grad[:, at : at + HD] = turn_back(
                dq[:, i * tokens : (i + 1) * tokens].T, cos_ref[...], sin_ref[...]
            ).astype(BF)
    swap_kv = copies.start(dkv.at[1 - core], kv_in, sibling)

    def add_half(ref):
        def step(m, carry):
            at = pl.multiple_of(m * 192, 192)
            ref[pl.ds(at, 192), :] = (
                ref[pl.ds(at, 192), :].astype(F32) + keep_half[pl.ds(at, 192), :].astype(F32)
            ).astype(BF)
            return carry

        lax.fori_loop(0, width // 192, step, 0)

    def owner_rows(ref, owner):
        return ref.at[pl.ds(pl.multiple_of(owner * 192, 192), 192)]

    swap_o.wait_recv()
    add_half(o_in)
    o_sends = [
        copies.start(owner_rows(o_in, peer[1]), o_far.at[i], peer) for i, peer in enumerate(peers)
    ]

    swap_kv.wait_recv()
    kv_in[...] = (dkv[core].astype(F32) + kv_in[...].astype(F32)).astype(BF)
    kv_sends = [
        copies.start(kv_in.at[lax.div(device[0], 2)], kv_far.at[i], device)
        for i, device in enumerate(ring)
    ]

    swap_o.wait_send()
    out_half[...] = contract_rows(normed_ref[...], q_grad[:, columns_of(1 - core)]).astype(BF)
    swap_q = copies.start(out_half, q_in, sibling)
    keep_half[...] = contract_rows(normed_ref[...], q_grad[:, columns_of(core)]).astype(BF)
    for load in loads_own:
        load.wait()
    for copy in x_dn:
        copy.wait_recv()
    dn_mine[...] = (
        dn_mine[...].astype(F32)
        + dn_x[0].astype(F32)
        + dn_x[1].astype(F32)
        + dn_x[2].astype(F32)
    ).astype(BF)

    def window_of(z):
        return pl.ds(pl.multiple_of(z * shift, 16), window)

    z_dn = copies.start(dn_mine.at[window_of(1 - z_at)], dn_z, partner)
    swap_q.wait_recv()
    add_half(q_in)
    q_sends = [
        copies.start(owner_rows(q_in, peer[1]), q_far.at[i], peer) for i, peer in enumerate(peers)
    ]
    z_gu.wait_recv()

    def add_gu(g, carry):
        gu_z[g] = (gu_z[g].astype(F32) + gu_mine[g].astype(F32)).astype(BF)
        return carry

    lax.fori_loop(0, N_FS, add_gu, 0)
    x_gu = [
        copies.start(gu_z.at[:, x_of(device)], gu_x.at[i], device)
        for i, device in enumerate(along)
    ]
    for copy in kv_sends:
        copy.wait_recv()
    total = kv_in[pair].astype(F32)
    for i in range(N_CTX // 2 - 1):
        total = total + kv_far[i].astype(F32)
    own_kv[...] = total
    for ref, sends, far, out in ((o_in, o_sends, o_far, o_red), (q_in, q_sends, q_far, q_red)):
        for copy in sends:
            copy.wait_recv()
        total = ref[pl.ds(pl.multiple_of(f * 192, 192), 192), :].astype(F32)
        for i in range(N_FS - 1):
            total = total + far[i].astype(F32)
        out[...] = total.astype(BF)
    z_dn.wait_recv()
    done_dn[...] = (dn_mine[window_of(z_at), :].astype(F32) + dn_z[...].astype(F32)).astype(BF)
    for copy in x_gu:
        copy.wait_recv()

    def sum_gu_x(g, carry):
        done_gu[g] = (
            gu_z[g, x_at].astype(F32)
            + gu_x[0, g].astype(F32)
            + gu_x[1, g].astype(F32)
            + gu_x[2, g].astype(F32)
        ).astype(BF)
        return carry

    lax.fori_loop(0, N_FS, sum_gu_x, 0)
    for copy in [z_gu, z_dn, swap_kv, swap_q] + x_dn + x_gu + kv_sends + o_sends + q_sends:
        copy.wait_send()


def attention_back(cid, arrays, vmem_arrays):
    sum_gu, sum_dn, expo, kv_all, full_o = arrays
    tokens, width = vmem_arrays[0].shape
    piece, units = sum_gu.shape[2:]
    half = sum_dn.shape[0]
    strip = width // 4
    window = half // 2 + 8
    side = width // 2
    kv_width = KV_HEADS * HD
    rows = width // N_FS
    anywhere = pl.BlockSpec(memory_space=pl.ANY)
    vmem = pl.BlockSpec(memory_space=pltpu.VMEM)
    outs = [
        jax.ShapeDtypeStruct((N_FS, piece, units), BF),
        jax.ShapeDtypeStruct((window, strip), BF),
        jax.ShapeDtypeStruct((tokens, 2 * kv_width), F32),
        jax.ShapeDtypeStruct((rows, side), BF),
        jax.ShapeDtypeStruct((rows, side), BF),
        jax.ShapeDtypeStruct((tokens, width), BF),
        jax.ShapeDtypeStruct((tokens, width), F32),
        jax.ShapeDtypeStruct((1, width), F32),
    ]
    return pl.pallas_call(
        attention_back_kernel,
        name="attention_back",
        out_shape=outs,
        in_specs=[anywhere] * len(arrays) + [vmem] * len(vmem_arrays),
        out_specs=[vmem] * len(outs),
        scratch_shapes=[
            pltpu.VMEM(expo.shape, BF),
            pltpu.VMEM(kv_all.shape, BF),
            pltpu.VMEM(full_o.shape, BF),
            pltpu.VMEM((tokens, width), BF),
            pltpu.VMEM((tokens, width), BF),
            pltpu.VMEM((N_FS, 4, piece, units), BF),
            pltpu.VMEM((N_FS, 4, piece, units), BF),
            pltpu.VMEM((3, N_FS, piece, units), BF),
            pltpu.VMEM((half, strip), BF),
            pltpu.VMEM((3, half, strip), BF),
            pltpu.VMEM((window, strip), BF),
            pltpu.VMEM((2, N_CTX // 2, tokens, 2 * kv_width), BF),
            pltpu.VMEM((N_CTX // 2, tokens, 2 * kv_width), BF),
            pltpu.VMEM((N_CTX // 2 - 1, tokens, 2 * kv_width), BF),
            pltpu.VMEM((width, side), BF),
            pltpu.VMEM((width, side), BF),
            pltpu.VMEM((width, side), BF),
            pltpu.VMEM((width, side), BF),
            pltpu.VMEM((N_FS - 1, rows, side), BF),
            pltpu.VMEM((N_FS - 1, rows, side), BF),
            pltpu.SemaphoreType.DMA((32,)),
            pltpu.SemaphoreType.DMA((32,)),
            pltpu.SemaphoreType.DMA((5,)),
        ],
        compiler_params=pltpu.CompilerParams(
            collective_id=cid, has_side_effects=True, vmem_limit_bytes=62 * 2**20
        ),
    )(*arrays, *vmem_arrays)


def last_kernel(
    done_gu,
    done_dn,
    parts,
    qkv_hbm,
    own_kv,
    q_grad,
    o_red,
    q_red,
    normed_ref,
    input_ref,
    gain_ref,
    mid_ref,
    middle_ref,
    gain_two_grad,
    cos_ref,
    sin_ref,
    all_gu,
    all_dn,
    all_at,
    vec_sum,
    out_rows,
    in_rows,
    full_qkv,
    proj,
    own_gu,
    kv_out,
    kv_keep,
    kv_in,
    kv_far,
    at_all,
    at_far,
    at_own,
    vec,
    vec_fs,
    vec_mid,
    vec_ctx,
    out_in,
    send,
    recv,
    local,
):
    c, f = lax.axis_index("ctx"), lax.axis_index("fsdp")
    core, pair = lax.rem(c, 2), lax.div(c, 2)
    x_at, z_at = lax.rem(pair, 4), lax.div(pair, 4)
    sibling = (flip(c, 1), f)
    partner = (flip(c, 8), f)
    along = [(flip(c, 2 * i), f) for i in range(1, 4)]
    ring = [(flip(c, 2 * i), f) for i in range(1, N_CTX // 2)]
    peers = [(c, flip(f, i)) for i in range(1, N_FS)]
    greet(ring + peers + [sibling])
    copies = Copies(send, recv)
    tokens, width = normed_ref.shape
    kv_width = KV_HEADS * HD
    strip = done_dn.shape[1]
    at_rows, at_cols = at_own.shape
    rest, own = [], []

    def local_copy(src, dst, n):
        copy = pltpu.make_async_copy(src, dst, local.at[n])
        copy.start()
        own.append(copy)
        return copy

    def x_of(device):
        return lax.rem(lax.div(device[0], 2), 4)

    def z_of(device):
        return lax.div(device[0], 8)

    def gu_place(device):
        return all_gu.at[lax.rem(device[0], 2), lax.div(device[0], 2)]

    def dn_place(device):
        columns = pl.ds(pl.multiple_of(x_of(device) * strip, strip), strip)
        return all_dn.at[lax.rem(device[0], 2), z_of(device), :, columns]

    def at_piece(ref, device):
        return ref.at[
            pl.ds(pl.multiple_of(x_of(device) * at_rows, at_rows), at_rows),
            pl.ds(pl.multiple_of(z_of(device) * at_cols, at_cols), at_cols),
        ]

    def at_place(device):
        return at_piece(all_at.at[lax.rem(device[0], 2)], device)

    here = (c, f)
    far = (partner[0], f)
    gu_own = local_copy(done_gu.at[f], own_gu.at[f], 0)
    gu_sends = [copies.start(done_gu.at[peer[1]], own_gu.at[f], peer) for peer in peers]
    local_copy(done_dn, dn_place(here), 1)
    dn_z = copies.start(done_dn, dn_place(here), partner)
    dn_x = [copies.start(done_dn, dn_place(here), device) for device in along]
    rest.append(copies.start(done_dn, dn_place(here), sibling))
    load_qkv = local_copy(qkv_hbm, full_qkv, 2)

    for h in range(KV_HEADS):
        at = width + h * HD
        proj[:, at : at + HD] = turn_back(
            own_kv[:, h * HD : (h + 1) * HD], cos_ref[...], sin_ref[...]
        ).astype(BF)
    proj[:, width + kv_width :] = own_kv[:, kv_width:].astype(BF)
    proj[:, :width] = q_grad[...]

    def side_of(which):
        return pl.ds(pl.multiple_of(width + which * kv_width, kv_width), kv_width)

    kv_out[...] = contract_rows(normed_ref[...], proj[:, side_of(1 - core)]).astype(BF)
    swap_kv = copies.start(kv_out, kv_in, sibling)
    kv_keep[...] = contract_rows(normed_ref[...], proj[:, side_of(core)]).astype(BF)

    gu_own.wait()
    for copy in gu_sends:
        copy.wait_recv()
    gu_x = [copies.start(own_gu, gu_place(here), device) for device in along]
    gu_z = [copies.start(own_gu, gu_place(here), partner)]
    rest.append(copies.start(own_gu, gu_place(here), sibling))
    local_copy(own_gu, gu_place(here), 3)

    swap_kv.wait_recv()
    kv_in[...] = (kv_in[...].astype(F32) + kv_keep[...].astype(F32)).astype(BF)

    def owner_rows(owner):
        return pl.ds(pl.multiple_of(owner * 192, 192), 192)

    kv_sends = [
        copies.start(kv_in.at[owner_rows(peer[1])], kv_far.at[i], peer)
        for i, peer in enumerate(peers)
    ]
    out_sends = [
        copies.start(parts.at[i + 1], out_in.at[i], peer) for i, peer in enumerate(peers)
    ]
    out_own = local_copy(parts.at[0], out_in.at[N_FS - 1], 4)

    load_qkv.wait()
    in_norm_grad = contract_cols(proj[...], full_qkv[...])
    inputs = input_ref[...].astype(F32)
    scale_one = lax.rsqrt(jnp.mean(inputs * inputs, axis=-1, keepdims=True) + EPSILON)
    norm = inputs * scale_one
    gain_one_grad = jnp.sum(in_norm_grad * norm, axis=0, keepdims=True)
    scaled = in_norm_grad * gain_ref[...]
    in_rows[...] = mid_ref[...] + scale_one * (
        scaled - norm * jnp.mean(scaled * norm, axis=-1, keepdims=True)
    )
    bias_grad = jnp.sum(proj[...].astype(F32), axis=0, keepdims=True)
    row = 0
    for vector in (gain_one_grad, gain_two_grad[...], bias_grad):
        for n in range(vector.shape[1] // 128):
            vec[row : row + 1, :] = vector[:, n * 128 : (n + 1) * 128]
            row += 1
    vec_sends = [copies.start(vec, vec_fs.at[i], peer) for i, peer in enumerate(peers)]

    dn_z.wait_recv()
    dn_x2 = [copies.start(dn_place(far), dn_place(far), device) for device in along]
    rest.append(copies.start(dn_place(far), dn_place(far), sibling))

    for copy in kv_sends:
        copy.wait_recv()
    total = kv_in[owner_rows(f), :].astype(F32)
    for i in range(N_FS - 1):
        total = total + kv_far[i].astype(F32)
    side = width // 2
    at_all[:, :side] = o_red[...]
    at_all[:, side : 2 * side] = q_red[...]
    at_all[:, 2 * side :] = total.astype(BF)
    at_sends = [
        copies.start(at_piece(at_all, device), at_far.at[i], device)
        for i, device in enumerate(ring)
    ]
    for copy in vec_sends:
        copy.wait_recv()
    total = vec[...]
    for i in range(N_FS - 1):
        total = total + vec_fs[i]
    vec_mid[...] = total
    vec_near = [copies.start(vec_mid, vec_ctx.at[c], device) for device in ring]
    rest.append(copies.start(vec_mid, vec_ctx.at[c], sibling))
    vec_ctx[pl.ds(c, 1)] = total[None]

    for copy, device in zip(gu_x, along):
        copy.wait_recv()
        gu_z.append(copies.start(gu_place(device), gu_place(device), partner))
        rest.append(copies.start(gu_place(device), gu_place(device), sibling))

    for copy in at_sends:
        copy.wait_recv()
    total = at_all[
        pl.ds(pl.multiple_of(x_at * at_rows, at_rows), at_rows),
        pl.ds(pl.multiple_of(z_at * at_cols, at_cols), at_cols),
    ].astype(F32)
    for i in range(N_CTX // 2 - 1):
        total = total + at_far[i].astype(F32)
    at_own[...] = total.astype(BF)
    at_near = [copies.start(at_own, at_place(here), device) for device in ring]
    rest.append(copies.start(at_own, at_place(here), sibling))
    local_copy(at_own, at_place(here), 5)

    for copy, device in zip(vec_near, ring):
        copy.wait_recv()
        place = vec_ctx.at[device[0]]
        rest.append(copies.start(place, place, sibling))
    for one, two, device in zip(dn_x, dn_x2, along):
        one.wait_recv()
        rest.append(copies.start(dn_place(device), dn_place(device), sibling))
        two.wait_recv()
        other = (flip(device[0], 8), f)
        rest.append(copies.start(dn_place(other), dn_place(other), sibling))
    for copy in out_sends:
        copy.wait_recv()
    out_own.wait()
    total = middle_ref[...]
    for i in range(N_FS):
        total = total + out_in[i].astype(F32)
    out_rows[...] = total.astype(BF)
    for copy, device in zip(at_near, ring):
        copy.wait_recv()
        rest.append(copies.start(at_place(device), at_place(device), sibling))
    for copy, device in zip(gu_z, [here] + along):
        copy.wait_recv()
        other = (flip(device[0], 8), f)
        rest.append(copies.start(gu_place(other), gu_place(other), sibling))
    for copy in (
        gu_sends + [dn_z] + dn_x + dn_x2 + gu_x + gu_z + [swap_kv] + kv_sends + out_sends
        + vec_sends + vec_near + at_sends + at_near
    ):
        copy.wait_send()
    for copy in rest:
        copy.wait()
    total = vec_ctx[0]
    for i in range(1, N_CTX):
        total = total + vec_ctx[i]
    vec_sum[...] = total
    for copy in own:
        if copy is not gu_own and copy is not load_qkv and copy is not out_own:
            copy.wait()


def last_exchange(cid, arrays, vmem_arrays):
    done_gu, done_dn, parts, full_qkv = arrays
    tokens, width = parts.shape[1:]
    piece, units = done_gu.shape[1:]
    window, strip = done_dn.shape
    rows = width // N_FS
    kv_width = KV_HEADS * HD
    at_width = width + kv_width
    anywhere = pl.BlockSpec(memory_space=pl.ANY)
    vmem = pl.BlockSpec(memory_space=pltpu.VMEM)
    outs = [
        jax.ShapeDtypeStruct((2, N_CTX // 2, N_FS, piece, units), BF),
        jax.ShapeDtypeStruct((2, 2, window, width), BF),
        jax.ShapeDtypeStruct((2, rows, at_width), BF),
        jax.ShapeDtypeStruct((40, 128), F32),
        jax.ShapeDtypeStruct((tokens, width), BF),
        jax.ShapeDtypeStruct((tokens, width), F32),
    ]
    return pl.pallas_call(
        last_kernel,
        name="last_exchange",
        out_shape=outs,
        in_specs=[anywhere] * len(arrays) + [vmem] * len(vmem_arrays),
        out_specs=[anywhere] * 3 + [vmem] * 3,
        scratch_shapes=[
            pltpu.VMEM(full_qkv.shape, BF),
            pltpu.VMEM((tokens, width + 2 * kv_width), BF),
            pltpu.VMEM((N_FS, piece, units), BF),
            pltpu.VMEM((width, kv_width), BF),
            pltpu.VMEM((width, kv_width), BF),
            pltpu.VMEM((width, kv_width), BF),
            pltpu.VMEM((N_FS - 1, rows, kv_width), BF),
            pltpu.VMEM((rows, at_width), BF),
            pltpu.VMEM((N_CTX // 2 - 1, rows // 4, at_width // 2), BF),
            pltpu.VMEM((rows // 4, at_width // 2), BF),
            pltpu.VMEM((40, 128), F32),
            pltpu.VMEM((N_FS - 1, 40, 128), F32),
            pltpu.VMEM((40, 128), F32),
            pltpu.VMEM((N_CTX, 40, 128), F32),
            pltpu.VMEM((N_FS, tokens, width), BF),
            pltpu.SemaphoreType.DMA((100,)),
            pltpu.SemaphoreType.DMA((100,)),
            pltpu.SemaphoreType.DMA((6,)),
        ],
        compiler_params=pltpu.CompilerParams(
            collective_id=cid, has_side_effects=True, vmem_limit_bytes=48 * 2**20
        ),
    )(*arrays, *vmem_arrays)


def wide_kernel(gu_ref, gate_ref, up_ref):
    for which, out in enumerate((gate_ref, up_ref)):
        out[...] = jnp.concatenate(
            [gu_ref[which, 0, source].astype(F32) for source in range(N_FS)], axis=1
        )


def wide_results(all_gu):
    piece, units = all_gu.shape[3:]
    parts = all_gu.shape[1]
    shape = jax.ShapeDtypeStruct((parts * piece, N_FS * units), F32)
    return pl.pallas_call(
        wide_kernel,
        name="wide_results",
        grid=(parts,),
        in_specs=[pl.BlockSpec((2, 1, N_FS, piece, units), lambda p: (0, p, 0, 0, 0))],
        out_specs=[pl.BlockSpec((piece, N_FS * units), lambda p: (p, 0))] * 2,
        out_shape=[shape, shape],
        compiler_params=pltpu.CompilerParams(vmem_limit_bytes=32 * 2**20),
    )(all_gu)


def rest_kernel(dn_ref, at_ref, down_ref, o_ref, q_ref, k_ref, v_ref):
    z = lax.rem(pl.program_id(0), 2)
    rows = down_ref.shape[0]
    block = dn_ref[0, 0].astype(F32)
    down_ref[...] = jnp.where(z == 0, block[:rows], block[8 : 8 + rows])
    side = o_ref.shape[1] // 2
    for n in range(2):
        part = at_ref[n].astype(F32)
        o_ref[:, n * side : (n + 1) * side] = part[:, :side]
        q_ref[:, n * side : (n + 1) * side] = part[:, side : 2 * side]
        (k_ref, v_ref)[n][...] = part[:, 2 * side :]


def rest_results(all_dn, all_at):
    window, width = all_dn.shape[2:]
    rows = window - 8
    own, at_width = all_at.shape[1:]
    kv_width = KV_HEADS * HD
    return pl.pallas_call(
        rest_kernel,
        name="rest_results",
        grid=(4,),
        in_specs=[
            pl.BlockSpec((1, 1, window, width), lambda n: (n // 2, n % 2, 0, 0)),
            pl.BlockSpec((2, own // 4, at_width), lambda n: (0, n, 0)),
        ],
        out_specs=[
            pl.BlockSpec((rows, width), lambda n: (n, 0)),
            pl.BlockSpec((own // 4, width), lambda n: (n, 0)),
            pl.BlockSpec((own // 4, width), lambda n: (n, 0)),
            pl.BlockSpec((own // 4, kv_width), lambda n: (n, 0)),
            pl.BlockSpec((own // 4, kv_width), lambda n: (n, 0)),
        ],
        out_shape=[
            jax.ShapeDtypeStruct((4 * rows, width), F32),
            jax.ShapeDtypeStruct((own, width), F32),
            jax.ShapeDtypeStruct((own, width), F32),
            jax.ShapeDtypeStruct((own, kv_width), F32),
            jax.ShapeDtypeStruct((own, kv_width), F32),
        ],
        compiler_params=pltpu.CompilerParams(vmem_limit_bytes=32 * 2**20),
    )(all_dn, all_at)


def body(
    layer_input,
    segments,
    positions,
    attn_norm,
    q_weight,
    q_bias,
    k_weight,
    k_bias,
    v_weight,
    v_bias,
    o_weight,
    mlp_norm,
    gate_weight,
    up_weight,
    down_weight,
    out_cotangent,
):
    tokens, width = layer_input.shape[1:]
    rows = gate_weight.shape[0]
    units = gate_weight.shape[1] // N_FS
    q_width = HEADS * HD
    kv_width = KV_HEADS * HD
    half_block = tokens // 2
    ctx = lax.axis_index("ctx")
    core = lax.rem(ctx, 2)
    pair = lax.div(ctx, 2)
    x_part = lax.rem(ctx, N_FS)
    inputs = layer_input[0].astype(F32)
    segment = segments[0]
    position = positions[0]
    keep = (segment > 0).astype(F32)[:, None]
    cotangent = out_cotangent[0].astype(F32) * keep
    cot_low = cotangent.astype(BF)

    qkv = jnp.concatenate([q_weight, k_weight, v_weight], axis=1).reshape(2, rows // 2, -1)
    small = jnp.concatenate([attn_norm, mlp_norm, q_bias, k_bias, v_bias]).reshape(-1, 128)
    small = jnp.pad(small, ((0, 16 - small.shape[0]), (0, 0)))
    cut = rows // 4
    start = lax.rem(x_part, 4) * cut
    gate_cut = lax.dynamic_slice_in_dim(gate_weight, start, cut, 0)
    up_cut = lax.dynamic_slice_in_dim(up_weight, start, cut, 0)
    blocks = (
        jnp.where(x_part < 4, gate_cut, up_cut).reshape(cut, N_FS, units).transpose(1, 0, 2)
    )
    full_qkv, small_all, columns = exchange(
        first_kernel,
        "gather_qkv",
        1,
        (qkv, small, blocks),
        [
            ((N_FS,) + qkv.shape, BF),
            ((N_FS,) + small.shape, BF),
            ((2, N_FS, 4, cut, units), BF),
        ],
        35,
        3,
    )
    columns = columns.reshape(2, width, units)

    flat = small_all[:, :5].reshape(N_FS, -1)
    marks = [0, rows, 2 * rows, 2 * rows + q_width // N_FS]
    marks += [marks[-1] + kv_width // N_FS, marks[-1] + 2 * kv_width // N_FS]
    gain_one, gain_two, bias_q, bias_k, bias_v = (
        flat[:, lo:hi].reshape(-1).astype(F32) for lo, hi in zip(marks[:-1], marks[1:])
    )
    bias_all = jnp.concatenate([bias_q, bias_k, bias_v])
    full_qkv = full_qkv.reshape(width, q_width + 2 * kv_width)

    scale_one = lax.rsqrt(jnp.mean(inputs * inputs, axis=-1, keepdims=True) + EPSILON)
    norm_first = inputs * scale_one
    normed_in = (norm_first * gain_one).astype(BF)
    projected = jnp.dot(normed_in, full_qkv, preferred_element_type=F32) + bias_all
    cosine, sine = rope_tables(position, HD)
    turned = rotate(
        projected[:, : q_width + kv_width].reshape(tokens, HEADS + KV_HEADS, HD), cosine, sine
    ).astype(BF)
    value_low = projected[:, q_width + kv_width :].astype(BF)
    query = (
        turned[:, :HEADS]
        .reshape(tokens, KV_HEADS, GROUP, HD)
        .transpose(1, 2, 0, 3)
        .reshape(KV_HEADS, GROUP * tokens, HD)
    )
    keys_values = jnp.concatenate([turned[:, HEADS:].reshape(tokens, kv_width), value_low], axis=1)
    segment_rows = jnp.broadcast_to(
        jnp.tile(segment.astype(BF)[None, :], (1, 2 * KV_HEADS)), (16, 2 * kv_width)
    )
    keys_values = jnp.concatenate([keys_values, segment_rows], axis=0)
    kv_all, full_o, cot_all = exchange(
        second_kernel,
        "gather_kv_o",
        2,
        (keys_values, o_weight.reshape(2, rows // 2, width), cot_low),
        [
            ((N_CTX,) + keys_values.shape, BF),
            ((N_FS, 2, rows // 2, width), BF),
            ((N_FS, tokens, width), BF),
        ],
        36,
        3,
    )
    full_o = full_o.reshape(q_width, width)
    within = jnp.arange(tokens, dtype=jnp.int32)
    row_place = jnp.where(
        within < half_block,
        ctx * half_block + within,
        (2 * N_CTX - 1 - ctx) * half_block + within - half_block,
    )
    row_info = jnp.stack([row_place.astype(F32), segment.astype(F32)])
    expo, mixed, inverse = attend(query, kv_all, row_info)
    attended = (
        mixed.reshape(KV_HEADS, HD, GROUP, tokens).transpose(3, 0, 2, 1).reshape(tokens, q_width)
    ).astype(BF)
    middle = inputs + jnp.dot(attended, full_o, preferred_element_type=F32)
    scale_two = lax.rsqrt(jnp.mean(middle * middle, axis=-1, keepdims=True) + EPSILON)
    norm_second = middle * scale_two
    normed_mid = (norm_second * gain_two).astype(BF)

    piece = rows // 8
    mid_norm_grad, out_part, sum_gu, sum_down = feed_forward(
        8, normed_mid, cot_all, columns, down_weight
    )
    cos_wide = jnp.concatenate([cosine, cosine], axis=1)
    sin_wide = jnp.concatenate([sine, -sine], axis=1)
    done_gu, done_dn, own_kv, o_red, q_red, q_grad, mid_grad, gain_two_grad = attention_back(
        3,
        (sum_gu.reshape(N_FS, 8, piece, units), sum_down, expo, kv_all, full_o),
        (
            mid_norm_grad,
            middle,
            cot_low,
            gain_two[None],
            query,
            mixed,
            inverse,
            attended,
            normed_in,
            cos_wide,
            sin_wide,
        ),
    )
    all_gu, all_dn, all_at, all_vec, output_rows, input_rows = last_exchange(
        4,
        (done_gu, done_dn, out_part, full_qkv),
        (
            own_kv,
            q_grad,
            o_red,
            q_red,
            normed_in,
            layer_input[0],
            gain_one[None],
            mid_grad,
            middle,
            gain_two_grad,
            cos_wide,
            sin_wide,
        ),
    )
    gate_grad, up_grad = wide_results(all_gu)
    down_grad, o_grad, q_weight_grad, k_grad, v_grad = rest_results(all_dn, all_at)
    flat_vec = all_vec.reshape(-1)
    mine = lax.axis_index("fsdp")
    vectors = []
    start = 0
    for whole in (width, width, q_width, kv_width, kv_width):
        part = whole // N_FS
        vectors.append(lax.dynamic_slice_in_dim(flat_vec, start + mine * part, part, 0))
        start += whole
    return (
        output_rows[None],
        input_rows[None],
        vectors[0],
        q_weight_grad,
        vectors[2],
        k_grad,
        vectors[3],
        v_grad,
        vectors[4],
        o_grad,
        vectors[1],
        gate_grad,
        up_grad,
        down_grad,
    )


def solution(mesh):
    placed = (
        P("fsdp", "ctx", None),
        P("fsdp", "ctx"),
        P("fsdp", "ctx"),
        P("fsdp"),
        P("fsdp", None),
        P("fsdp"),
        P("fsdp", None),
        P("fsdp"),
        P("fsdp", None),
        P("fsdp"),
        P("fsdp", None),
        P("fsdp"),
        P("fsdp", None),
        P("fsdp", None),
        P("fsdp", None),
        P("fsdp", "ctx", None),
    )
    return jax.shard_map(
        body,
        mesh=mesh,
        in_specs=placed,
        out_specs=(
            P("fsdp", "ctx", None),
            P("fsdp", "ctx", None),
            P("fsdp"),
            P("fsdp", None),
            P("fsdp"),
            P("fsdp", None),
            P("fsdp"),
            P("fsdp", None),
            P("fsdp"),
            P("fsdp", None),
            P("fsdp"),
            P("fsdp", None),
            P("fsdp", None),
            P("fsdp", None),
        ),
        check_vma=False,
    )
```

```python
import functools

import jax
import jax.numpy as jnp
from jax import lax
from jax.experimental import pallas as pl
from jax.experimental.pallas import tpu as pltpu
from jax.sharding import PartitionSpec as P

HEADS = 12
KV_HEADS = 2
HD = 128
GROUP = HEADS // KV_HEADS
N_CTX = 16
N_FS = 8
EPSILON = 1e-06
THETA = 1000000.0
MESH = pl.DeviceIdType.MESH
BF = jnp.bfloat16
F32 = jnp.float32


def rope_tables(position, head_dim):
    freqs = THETA ** (-jnp.arange(0, head_dim, 2).astype(F32) / head_dim)
    angles = position.astype(F32)[:, None] * freqs[None, :]
    return (jnp.cos(angles), jnp.sin(angles))


def contract_rows(left, right):
    return lax.dot_general(
        left, right, (((0,), (0,)), ((), ())), preferred_element_type=F32
    )


def contract_cols(left, right):
    return lax.dot_general(
        left, right, (((1,), (1,)), ((), ())), preferred_element_type=F32
    )


def flip(value, mask):
    out = value
    bit = 1
    while bit <= mask:
        if mask & bit:
            out = out + bit * (1 - 2 * lax.rem(lax.div(value, bit), 2))
        bit *= 2
    return out


class Copies:
    def __init__(self, send, recv):
        self.send, self.recv, self.count, self.all = send, recv, 0, []

    def start(self, src, dst, device):
        copy = pltpu.make_async_remote_copy(
            src_ref=src,
            dst_ref=dst,
            send_sem=self.send.at[self.count],
            recv_sem=self.recv.at[self.count],
            device_id=device,
            device_id_type=MESH,
        )
        self.count += 1
        copy.start()
        self.all.append(copy)
        return copy


def greet(devices):
    barrier = pltpu.get_barrier_semaphore()
    for device in devices:
        pl.semaphore_signal(barrier, inc=1, device_id=device, device_id_type=MESH)
    pl.semaphore_wait(barrier, len(devices))


def cross_peers(c, f):
    away = c + lax.rem(c, 2) * (flip(c, 8) - c)
    return [(c if i < 4 else away, flip(f, i)) for i in range(1, N_FS)]


class SharedRows:
    def __init__(self, copies, ref, c, f, columns=None):
        core = lax.rem(c, 2)
        self.copies, self.f = copies, f
        self.sibling = (flip(c, 1), f)
        self.over = (c + core * (flip(c, 8) - c), flip(f, 4))
        self.one, self.three = (c, flip(f, 1)), (c, flip(f, 3))
        rows = ref.shape[1] // 2

        def place(owner, part=None):
            if part is None:
                span = pl.ds(pl.multiple_of(core * rows, 16), rows)
            else:
                span = pl.ds(pl.multiple_of(core * rows + part * (rows // 2), 16), rows // 2)
            if columns is None:
                return ref.at[owner, span]
            return ref.at[owner, span, columns]

        self.place = place
        mine = place(f)
        self.from_one = copies.start(mine, mine, self.one)
        self.from_three = copies.start(mine, mine, self.three)
        self.z_copies = [copies.start(mine, mine, self.over)]
        self.sent = [self.from_one, self.from_three]
        self.rest = []

    def send(self, here, device):
        return self.copies.start(here, here, device)

    def pass_y(self):
        one, three = flip(self.f, 1), flip(self.f, 3)
        self.from_one.wait_recv()
        self.far = [self.send(self.place(one, 0), self.three)]
        self.z_copies.append(self.send(self.place(one), self.over))
        self.from_three.wait_recv()
        self.far.append(self.send(self.place(three, 1), self.one))
        self.z_copies.append(self.send(self.place(three), self.over))
        self.rest.append(self.send(self.place(one), self.sibling))
        self.rest.append(self.send(self.place(three), self.sibling))
        for copy in self.far:
            copy.wait_recv()
        two = self.place(flip(self.f, 2))
        self.z_copies.append(self.send(two, self.over))
        self.rest.append(self.send(two, self.sibling))

    def pass_z(self):
        for copy, mask in zip(self.z_copies, (4, 5, 7, 6)):
            copy.wait_recv()
            self.rest.append(self.send(self.place(flip(self.f, mask)), self.sibling))

    def wait(self):
        for copy in self.rest:
            copy.wait_recv()

    def finish(self):
        for copy in self.sent + self.far + self.z_copies + self.rest:
            copy.wait_send()


CHUNK = 256


def turn_back(grad, cos_wide, sin_wide):
    half = grad.shape[1] // 2
    swapped = jnp.concatenate([grad[:, half:], grad[:, :half]], axis=1)
    return grad * cos_wide + swapped * sin_wide


def front_kernel(
    q_hbm,
    k_hbm,
    v_hbm,
    o_hbm,
    gate_hbm,
    up_hbm,
    cot_ref,
    small_ref,
    input_ref,
    row_ref,
    cos_ref,
    sin_ref,
    w_out,
    o_out,
    kv_out,
    g_out,
    t_out,
    e_out,
    gains_ref,
    normed_ref,
    query_ref,
    mixed_ref,
    inv_ref,
    attended_ref,
    middle_ref,
    normed_mid_ref,
    weights,
    full_o,
    small_all,
    strip,
    stage,
    kv_own,
    kv,
    s_ref,
    expo,
    send,
    recv,
    local,
):
    c, f = lax.axis_index("ctx"), lax.axis_index("fsdp")
    core = lax.rem(c, 2)
    sibling = (flip(c, 1), f)
    here = (c, f)
    peers = [(c, flip(f, i)) for i in range(1, N_FS)]
    ring = [(flip(c, 2 * i), f) for i in range(1, N_CTX // 2)]
    along = ring[:3]
    near, turn = peers[:3], peers[3]
    greet(peers + ring + [sibling, (flip(c, 8), flip(f, 4))])
    copies = Copies(send, recv)
    tokens, width = input_ref.shape
    rows = q_hbm.shape[0]
    kv_width = KV_HEADS * HD
    cut, units = stage.shape[1:]
    x_part = lax.rem(c, N_FS)

    def local_copy(src, dst, n):
        copy = pltpu.make_async_copy(src, dst, local.at[n])
        copy.start()
        return copy

    mine = weights.at[f]
    q_columns, kv_columns = pl.ds(0, width), pl.ds(width, 2 * kv_width)
    load_k = local_copy(k_hbm, mine.at[:, pl.ds(width, kv_width)], 1)
    load_v = local_copy(v_hbm, mine.at[:, pl.ds(width + kv_width, kv_width)], 2)
    block_rows = pl.ds(pl.multiple_of(lax.rem(x_part, 4) * cut, cut), cut)
    load_gate = local_copy(gate_hbm.at[block_rows], strip.at[0], 3)
    load_up = local_copy(up_hbm.at[block_rows], strip.at[1], 4)
    load_q = local_copy(q_hbm, mine.at[:, q_columns], 0)
    load_o = local_copy(o_hbm, full_o.at[f], 5)
    load_t = local_copy(cot_ref, t_out.at[0], 6)
    small_own = local_copy(small_ref, small_all.at[f], 7)
    small_sends = [copies.start(small_ref, small_all.at[f], peer) for peer in peers]
    load_k.wait()
    load_v.wait()
    share_kv = SharedRows(copies, weights, c, f, kv_columns)

    def columns(device, part=None):
        where = lax.rem(device[0], N_FS)
        if part is None:
            return g_out.at[lax.div(where, 4), :, lax.rem(where, 4)]
        half = N_FS // 2
        return g_out.at[lax.div(where, 4), pl.ds(part * half, half), lax.rem(where, 4)]

    def block(device, source):
        where = lax.rem(device[0], N_FS)
        return g_out.at[lax.div(where, 4), source, lax.rem(where, 4)]

    load_gate.wait()
    load_up.wait()
    which = lax.div(x_part, 4)
    for owner in range(N_FS):
        stage[owner] = strip[which, :, owner * units : (owner + 1) * units]
    block_own = local_copy(stage.at[f], block(here, f), 8)
    blocks = [copies.start(stage.at[peer[1]], block(here, f), peer) for peer in peers]
    load_q.wait()
    share_q = SharedRows(copies, weights, c, f, q_columns)

    inputs = input_ref[...].astype(F32)
    norm = inputs * lax.rsqrt(jnp.mean(inputs * inputs, axis=-1, keepdims=True) + EPSILON)
    small_own.wait()
    for copy in small_sends:
        copy.wait_recv()

    def vector(n, part):
        pieces = [small_all[owner, n : n + 1, :part] for owner in range(N_FS)]
        return jnp.concatenate(pieces, axis=1)

    gain_one, gain_two, bias_q = vector(0, rows), vector(1, rows), vector(2, rows)
    bias_k, bias_v = vector(3, kv_width // N_FS), vector(4, kv_width // N_FS)
    gains_ref[0:1, :] = gain_one
    gains_ref[1:2, :] = gain_two
    normed_ref[...] = (norm * gain_one).astype(BF)

    share_kv.pass_y()
    share_kv.pass_z()
    share_kv.wait()
    cos_wide, sin_wide = cos_ref[...], -sin_ref[...]
    full = weights[:, :, width:].reshape(width, 2 * kv_width)
    projected = jnp.dot(normed_ref[...], full, preferred_element_type=F32)
    projected = projected + jnp.concatenate([bias_k, bias_v], axis=1)
    for h in range(KV_HEADS):
        cols = slice(h * HD, (h + 1) * HD)
        kv_own[:tokens, cols] = turn_back(projected[:, cols], cos_wide, sin_wide).astype(BF)
    kv_own[:tokens, kv_width:] = projected[:, kv_width:].astype(BF)
    marks = jnp.concatenate([row_ref[1:2, :]] * (2 * KV_HEADS), axis=1)
    kv_own[tokens:, :] = jnp.broadcast_to(marks, (16, 2 * kv_width)).astype(BF)
    keep_kv = local_copy(kv_own, kv.at[c], 9)
    keys = [copies.start(kv_own, kv.at[c], device) for device in ring]
    kv_rest = [copies.start(kv_own, kv.at[c], sibling)]

    block_own.wait()
    for copy in blocks:
        copy.wait_recv()
    x_one, x_two, x_three = along
    from_one = copies.start(columns(here), columns(here), x_one)
    from_three = copies.start(columns(here), columns(here), x_three)
    g_rest = [copies.start(columns(here), columns(here), sibling)]

    share_q.pass_y()
    load_o.wait()
    share_o = SharedRows(copies, full_o, c, f)
    half = tokens // 2
    upper, lower = pl.ds(0, half), pl.ds(half, half)
    low_z = copies.start(cot_ref.at[lower], t_out.at[4, lower], turn)
    up_y = [
        copies.start(cot_ref.at[upper], t_out.at[i + 1, upper], device)
        for i, device in enumerate(near)
    ]
    up_z = [copies.start(cot_ref.at[upper], t_out.at[4, upper], turn)]
    low_y = [
        copies.start(cot_ref.at[lower], t_out.at[i + 1, lower], device)
        for i, device in enumerate(near)
    ]
    for key, device in zip(keys, ring):
        key.wait_recv()
        place = kv.at[device[0]]
        kv_rest.append(copies.start(place, place, sibling))
    share_q.pass_z()
    share_q.wait()

    full = weights[:, :, :width].reshape(width, width)
    projected = jnp.dot(normed_ref[...], full, preferred_element_type=F32) + bias_q
    for n in range(HEADS):
        at = (n % GROUP) * tokens
        query_ref[n // GROUP, at : at + tokens, :] = turn_back(
            projected[:, n * HD : (n + 1) * HD], cos_wide, sin_wide
        ).astype(BF)
    save_w = local_copy(weights, w_out, 0)

    from_one.wait_recv()
    far = [copies.start(columns(x_one, 0), columns(x_one, 0), x_three)]
    from_three.wait_recv()
    far.append(copies.start(columns(x_three, 1), columns(x_three, 1), x_one))
    for device in (x_one, x_three):
        g_rest.append(copies.start(columns(device), columns(device), sibling))
    share_o.pass_y()
    keep_kv.wait()
    for copy in kv_rest:
        copy.wait_recv()
    save_kv = local_copy(kv, kv_out, 1)

    length = N_CTX * tokens
    scale = HD ** (-0.5)
    row_place, row_seg = row_ref[0:1, :], row_ref[1:2, :]
    key_seg = kv[:, tokens : tokens + 16, :HD][:, 0, :].astype(F32).T
    within = lax.broadcasted_iota(jnp.int32, (tokens, tokens), 0)
    saves = []
    for h in range(KV_HEADS):
        query = query_ref[h]
        top = jnp.full((8, GROUP * tokens), -1e30, F32)
        for b in range(N_CTX):
            place = jnp.where(
                within < half, b * half + within, (2 * N_CTX - 1 - b) * half + within - half
            ).astype(F32)
            allowed = (place <= row_place) & (key_seg[:, b : b + 1] == row_seg) & (row_seg > 0.5)
            bias = jnp.where(allowed, 0.0, -1e30).astype(F32)
            scores = contract_cols(kv[b, :tokens, h * HD : (h + 1) * HD], query) * scale
            scores = scores + jnp.concatenate([bias] * GROUP, axis=1)
            s_ref[b * tokens : (b + 1) * tokens, :] = scores
            top = jnp.maximum(top, jnp.max(scores.reshape(tokens // 8, 8, -1), axis=0))
        highest = jnp.maximum(jnp.max(top, axis=0, keepdims=True), -1e29)
        total = jnp.zeros((8, GROUP * tokens), F32)
        mixed = jnp.zeros((HD, GROUP * tokens), F32)
        for j in range(length // CHUNK):
            part = jnp.exp(s_ref[j * CHUNK : (j + 1) * CHUNK, :] - highest)
            total = total + jnp.sum(part.reshape(CHUNK // 8, 8, -1), axis=0)
            low = part.astype(BF)
            expo[h, j * CHUNK : (j + 1) * CHUNK, :] = low
            at = (KV_HEADS + h) * HD
            values = kv[2 * j : 2 * j + 2, :tokens, at : at + HD].reshape(CHUNK, HD)
            mixed = mixed + contract_rows(values, low)
        total = jnp.sum(total, axis=0, keepdims=True)
        inverse = 1.0 / jnp.where(total > 0.5, total, 1.0)
        mixed = mixed * inverse
        mixed_ref[h] = mixed
        inv_ref[h] = jnp.broadcast_to(inverse, (8, GROUP * tokens))
        for i in range(GROUP):
            at = (h * GROUP + i) * HD
            attended_ref[:, at : at + HD] = mixed[:, i * tokens : (i + 1) * tokens].T.astype(BF)
        saves.append(local_copy(expo.at[h], e_out.at[h], 2 + h))
        if h == 0:
            low_z.wait_recv()
            for i, device in enumerate(near):
                low_y.append(copies.start(t_out.at[4, lower], t_out.at[5 + i, lower], device))
            for i, copy in enumerate(up_y):
                copy.wait_recv()
                up_z.append(copies.start(t_out.at[i + 1, upper], t_out.at[5 + i, upper], turn))
            for copy in far:
                copy.wait_recv()
            g_rest.append(copies.start(columns(x_two), columns(x_two), sibling))
            share_o.pass_z()

    share_o.wait()
    product = jnp.dot(
        attended_ref[...], full_o[...].reshape(width, width), preferred_element_type=F32
    )
    middle = input_ref[...].astype(F32) + product
    middle_ref[...] = middle
    scale_two = lax.rsqrt(jnp.mean(middle * middle, axis=-1, keepdims=True) + EPSILON)
    normed_mid_ref[...] = (middle * scale_two * gains_ref[1:2, :]).astype(BF)
    save_o = local_copy(full_o, o_out, 4)
    for copy in low_y + up_z + g_rest:
        copy.wait_recv()
    for share in (share_kv, share_q, share_o):
        share.finish()
    for copy in (
        small_sends + blocks + [from_one, from_three] + far + g_rest + low_y + up_z + up_y
        + [low_z] + keys + kv_rest
    ):
        copy.wait_send()
    for copy in saves + [save_w, save_kv, save_o, load_t]:
        copy.wait()


def front(cid, arrays, vmem_arrays):
    tokens, width = vmem_arrays[1].shape
    rows, all_units = arrays[4].shape
    units = all_units // N_FS
    cut = rows // 4
    kv_width = KV_HEADS * HD
    wide = GROUP * tokens
    length = N_CTX * tokens
    anywhere = pl.BlockSpec(memory_space=pl.ANY)
    vmem = pl.BlockSpec(memory_space=pltpu.VMEM)
    weights = (N_FS, rows, width + 2 * kv_width)
    full_o = (N_FS, rows, width)
    kv = (N_CTX, tokens + 16, 2 * kv_width)
    expo = (KV_HEADS, length, wide)
    return pl.pallas_call(
        front_kernel,
        name="front",
        out_shape=[
            jax.ShapeDtypeStruct(weights, BF),
            jax.ShapeDtypeStruct(full_o, BF),
            jax.ShapeDtypeStruct(kv, BF),
            jax.ShapeDtypeStruct((2, N_FS, 4, cut, units), BF),
            jax.ShapeDtypeStruct((N_FS, tokens, width), BF),
            jax.ShapeDtypeStruct(expo, BF),
            jax.ShapeDtypeStruct((2, width), F32),
            jax.ShapeDtypeStruct((tokens, width), BF),
            jax.ShapeDtypeStruct((KV_HEADS, wide, HD), BF),
            jax.ShapeDtypeStruct((KV_HEADS, HD, wide), F32),
            jax.ShapeDtypeStruct((KV_HEADS, 8, wide), F32),
            jax.ShapeDtypeStruct((tokens, width), BF),
            jax.ShapeDtypeStruct((tokens, width), F32),
            jax.ShapeDtypeStruct((tokens, width), BF),
        ],
        in_specs=[anywhere] * len(arrays) + [vmem] * len(vmem_arrays),
        out_specs=[anywhere] * 6 + [vmem] * 8,
        scratch_shapes=[
            pltpu.VMEM(weights, BF),
            pltpu.VMEM(full_o, BF),
            pltpu.VMEM((N_FS,) + vmem_arrays[0].shape, F32),
            pltpu.VMEM((2, cut, all_units), BF),
            pltpu.VMEM((N_FS, cut, units), BF),
            pltpu.VMEM(kv[1:], BF),
            pltpu.VMEM(kv, BF),
            pltpu.VMEM((length, wide), F32),
            pltpu.VMEM(expo, BF),
            pltpu.SemaphoreType.DMA((104,)),
            pltpu.SemaphoreType.DMA((104,)),
            pltpu.SemaphoreType.DMA((10,)),
        ],
        compiler_params=pltpu.CompilerParams(
            collective_id=cid, has_side_effects=True, vmem_limit_bytes=60 * 2**20
        ),
    )(*arrays, *vmem_arrays)


def apart(value, mask):
    out = 0
    for bit in (1, 2, 4):
        out = out + bit * lax.rem(lax.div(value, bit) + lax.div(mask, bit), 2)
    return out


def mlp_kernel(
    nm_ref,
    cot_ref,
    gu_ref,
    down_ref,
    grad_ref,
    out_ref,
    sum_gu_ref,
    sum_dn_ref,
    nm,
    cot,
    gu,
    down,
    act,
    gate_low,
    up_low,
    part,
    part_in,
    outs,
    gu_in,
    dn_in,
    nm_send,
    nm_recv,
    part_send,
    part_recv,
    swap_send,
    swap_recv,
    local,
):
    c, f = lax.axis_index("ctx"), lax.axis_index("fsdp")
    core = lax.rem(c, 2)
    sibling = (flip(c, 1), f)
    tokens, width = nm_ref.shape
    units = down_ref.shape[0]
    rows = 2 * tokens
    greet([(c, flip(f, i)) for i in range(1, N_FS)] + [sibling])

    def normed_copy(i):
        return pltpu.make_async_remote_copy(
            src_ref=nm_ref,
            dst_ref=nm.at[i],
            send_sem=nm_send.at[i],
            recv_sem=nm_recv.at[i],
            device_id=(c, apart(f, i)),
            device_id_type=MESH,
        )

    def part_copy(i):
        return pltpu.make_async_remote_copy(
            src_ref=part.at[i],
            dst_ref=part_in.at[i],
            send_sem=part_send.at[i],
            recv_sem=part_recv.at[i],
            device_id=(c, apart(f, i)),
            device_id_type=MESH,
        )

    for i in range(1, N_FS):
        normed_copy(i).start()
    loads = [
        pltpu.make_async_copy(nm_ref, nm.at[0], local.at[0]),
        pltpu.make_async_copy(gu_ref, gu, local.at[1]),
        pltpu.make_async_copy(cot_ref, cot, local.at[2]),
        pltpu.make_async_copy(down_ref, down, local.at[3]),
    ]
    for load in loads:
        load.start()
    for load in loads:
        load.wait()

    def out_copy(s):
        return pltpu.make_async_copy(
            outs.at[lax.rem(s, 2)], out_ref.at[pl.ds(2 * s, 2)], local.at[4 + lax.rem(s, 2)]
        )

    def pair(s, carry):
        @pl.when(s > 0)
        def _():
            normed_copy(2 * s).wait_recv()

        normed_copy(2 * s + 1).wait_recv()
        at = pl.multiple_of(s * rows, rows)
        x = nm[pl.ds(2 * s, 2)].reshape(rows, width)
        gate = jnp.dot(x, gu[0], preferred_element_type=F32)
        up = jnp.dot(x, gu[1], preferred_element_type=F32)
        grad = contract_cols(cot[pl.ds(2 * s, 2)].reshape(rows, width), down[...])
        sigma = jax.nn.sigmoid(gate)
        swish = gate * sigma
        act[pl.ds(at, rows), :] = (swish * up).astype(BF)
        gate_low[pl.ds(at, rows), :] = (
            grad * up * sigma * (1.0 + gate * (1.0 - sigma))
        ).astype(BF)
        up_low[pl.ds(at, rows), :] = (grad * swish).astype(BF)
        summed = contract_cols(gate_low[pl.ds(at, rows), :], gu[0])
        summed = summed + contract_cols(up_low[pl.ds(at, rows), :], gu[1])
        part[pl.ds(2 * s, 2)] = summed.astype(BF).reshape(2, tokens, width)

        @pl.when(s > 0)
        def _():
            part_copy(2 * s).start()

        part_copy(2 * s + 1).start()

        @pl.when(s > 1)
        def _():
            out_copy(s - 2).wait()

        result = jnp.dot(act[pl.ds(at, rows), :], down[...], preferred_element_type=F32)
        outs[lax.rem(s, 2)] = result.astype(BF).reshape(2, tokens, width)
        out_copy(s).start()
        return carry

    lax.fori_loop(0, N_FS // 2, pair, 0)

    every = N_FS * tokens

    def gate_up(m, carry):
        at = pl.multiple_of(m * 256, 256)
        x = nm[:, :, pl.ds(at, 256)].reshape(every, 256)
        gu[0, pl.ds(at, 256), :] = contract_rows(x, gate_low[...]).astype(BF)
        gu[1, pl.ds(at, 256), :] = contract_rows(x, up_low[...]).astype(BF)
        return carry

    lax.fori_loop(0, width // 256, gate_up, 0)
    swap_gu = pltpu.make_async_remote_copy(
        src_ref=gu.at[1 - core],
        dst_ref=gu_in,
        send_sem=swap_send.at[0],
        recv_sem=swap_recv.at[0],
        device_id=sibling,
        device_id_type=MESH,
    )
    swap_gu.start()
    turned = cot[...].reshape(every, width)

    def down_rows(m, carry):
        at = pl.multiple_of(m * 256, 256)
        down[pl.ds(at, 256), :] = contract_rows(act[:, pl.ds(at, 256)], turned).astype(BF)
        return carry

    whole = units // 256
    lax.fori_loop(0, whole, down_rows, 0)
    if units % 256:
        down[whole * 256 :, :] = contract_rows(act[:, whole * 256 :], turned).astype(BF)
    half = units // 2
    swap_dn = pltpu.make_async_remote_copy(
        src_ref=down.at[pl.ds(pl.multiple_of((1 - core) * half, 16), half)],
        dst_ref=dn_in,
        send_sem=swap_send.at[1],
        recv_sem=swap_recv.at[1],
        device_id=sibling,
        device_id_type=MESH,
    )
    swap_dn.start()
    swap_gu.wait_recv()

    def add_gu(m, carry):
        at = pl.multiple_of(m * 256, 256)
        gu_in[pl.ds(at, 256), :] = (
            gu[core, pl.ds(at, 256), :].astype(F32) + gu_in[pl.ds(at, 256), :].astype(F32)
        ).astype(BF)
        return carry

    lax.fori_loop(0, width // 256, add_gu, 0)
    save_gu = pltpu.make_async_copy(gu_in, sum_gu_ref, local.at[6])
    save_gu.start()
    swap_dn.wait_recv()

    def add_dn(m, carry):
        at = pl.multiple_of(m * 112, 16)
        own = down[pl.ds(pl.multiple_of(core * half + m * 112, 16), 112), :]
        dn_in[pl.ds(at, 112), :] = (
            own.astype(F32) + dn_in[pl.ds(at, 112), :].astype(F32)
        ).astype(BF)
        return carry

    lax.fori_loop(0, half // 112, add_dn, 0)
    save_dn = pltpu.make_async_copy(dn_in, sum_dn_ref, local.at[7])
    save_dn.start()
    total = part[0].astype(F32)
    for i in range(1, N_FS):
        part_copy(i).wait_recv()
        total = total + part_in[i].astype(F32)
    grad_ref[...] = total
    for i in range(1, N_FS):
        normed_copy(i).wait_send()
        part_copy(i).wait_send()
    swap_gu.wait_send()
    swap_dn.wait_send()
    for copy in (out_copy(2), out_copy(3), save_gu, save_dn):
        copy.wait()


def feed_forward(cid, normed, cot_all, columns, down_weight):
    tokens, width = normed.shape
    units = down_weight.shape[0]
    every = N_FS * tokens
    return pl.pallas_call(
        mlp_kernel,
        name="feed_forward",
        out_shape=[
            jax.ShapeDtypeStruct((tokens, width), F32),
            jax.ShapeDtypeStruct((N_FS, tokens, width), BF),
            jax.ShapeDtypeStruct((width, units), BF),
            jax.ShapeDtypeStruct((units // 2, width), BF),
        ],
        in_specs=[pl.BlockSpec(memory_space=pl.ANY)] * 4,
        out_specs=[pl.BlockSpec(memory_space=pltpu.VMEM)]
        + [pl.BlockSpec(memory_space=pl.ANY)] * 3,
        scratch_shapes=[
            pltpu.VMEM((N_FS, tokens, width), BF),
            pltpu.VMEM((N_FS, tokens, width), BF),
            pltpu.VMEM((2, width, units), BF),
            pltpu.VMEM((units, width), BF),
            pltpu.VMEM((every, units), BF),
            pltpu.VMEM((every, units), BF),
            pltpu.VMEM((every, units), BF),
            pltpu.VMEM((N_FS, tokens, width), BF),
            pltpu.VMEM((N_FS, tokens, width), BF),
            pltpu.VMEM((2, 2, tokens, width), BF),
            pltpu.VMEM((width, units), BF),
            pltpu.VMEM((units // 2, width), BF),
            pltpu.SemaphoreType.DMA((N_FS,)),
            pltpu.SemaphoreType.DMA((N_FS,)),
            pltpu.SemaphoreType.DMA((N_FS,)),
            pltpu.SemaphoreType.DMA((N_FS,)),
            pltpu.SemaphoreType.DMA((2,)),
            pltpu.SemaphoreType.DMA((2,)),
            pltpu.SemaphoreType.DMA((8,)),
        ],
        compiler_params=pltpu.CompilerParams(
            collective_id=cid, has_side_effects=True, vmem_limit_bytes=60 * 2**20
        ),
    )(normed, cot_all, columns, down_weight)


def attention_back_kernel(
    sum_gu,
    sum_dn,
    expo_hbm,
    kv_hbm,
    o_hbm,
    mng_ref,
    middle_ref,
    cot_ref,
    gain_ref,
    query_ref,
    mixed_ref,
    inv_ref,
    attended_ref,
    normed_ref,
    cos_ref,
    sin_ref,
    done_gu,
    done_dn,
    own_kv,
    o_red,
    q_red,
    q_grad,
    mid_ref,
    gain_grad,
    expo,
    kv,
    full_o,
    branch,
    back,
    gu_mine,
    gu_z,
    gu_x,
    dn_mine,
    dn_x,
    dn_z,
    dkv,
    kv_in,
    kv_far,
    out_half,
    keep_half,
    o_in,
    q_in,
    o_far,
    q_far,
    send,
    recv,
    local,
):
    c, f = lax.axis_index("ctx"), lax.axis_index("fsdp")
    core, pair = lax.rem(c, 2), lax.div(c, 2)
    x_at, z_at = lax.rem(pair, 4), lax.div(pair, 4)
    sibling = (flip(c, 1), f)
    partner = (flip(c, 8), f)
    along = [(flip(c, 2 * i), f) for i in range(1, 4)]
    ring = [(flip(c, 2 * i), f) for i in range(1, N_CTX // 2)]
    peers = cross_peers(c, f)
    greet(ring + peers + [sibling])
    copies = Copies(send, recv)
    tokens, width = mng_ref.shape
    strip = dn_mine.shape[1]
    window = dn_z.shape[0]
    shift = dn_mine.shape[0] - window
    side = width // 2
    scale = HD ** (-0.5)

    def x_of(device):
        return lax.rem(lax.div(device[0], 2), 4)

    def strip_of(ref, x):
        return ref.at[:, pl.ds(pl.multiple_of(x * strip, strip), strip)]

    def local_copy(src, dst, n):
        copy = pltpu.make_async_copy(src, dst, local.at[n])
        copy.start()
        return copy

    x_gu = [
        copies.start(sum_gu.at[:, :, x_of(device)], gu_x.at[i], device)
        for i, device in enumerate(along)
    ]
    x_dn = [
        copies.start(strip_of(sum_dn, x_of(device)), dn_x.at[i], device)
        for i, device in enumerate(along)
    ]
    loads_o = local_copy(o_hbm, full_o, 0)
    loads = [
        local_copy(kv_hbm, kv, 1),
        local_copy(expo_hbm, expo, 2),
    ]
    loads_own = [
        local_copy(sum_gu.at[:, :, x_at], gu_mine, 3),
        local_copy(strip_of(sum_dn, x_at), dn_mine, 4),
    ]

    middle = middle_ref[...]
    scale_two = lax.rsqrt(jnp.mean(middle * middle, axis=-1, keepdims=True) + EPSILON)
    norm = middle * scale_two
    grad = mng_ref[...]
    gain_grad[...] = jnp.sum(grad * norm, axis=0, keepdims=True)
    scaled = grad * gain_ref[...]
    mid = cot_ref[...].astype(F32) + scale_two * (
        scaled - norm * jnp.mean(scaled * norm, axis=-1, keepdims=True)
    )
    mid_ref[...] = mid
    branch[...] = mid.astype(BF)
    loads_o.wait()
    back[...] = contract_cols(branch[...], full_o[...]).astype(BF)

    def columns_of(which):
        return pl.ds(pl.multiple_of(which * side, side), side)

    out_half[...] = contract_rows(attended_ref[...], branch[:, columns_of(1 - core)]).astype(BF)
    swap_o = copies.start(out_half, o_in, sibling)
    keep_half[...] = contract_rows(attended_ref[...], branch[:, columns_of(core)]).astype(BF)
    for load in loads:
        load.wait()

    length = N_CTX * tokens
    for h in range(KV_HEADS):
        query = query_ref[h]
        heads = back[:, h * GROUP * HD : (h + 1) * GROUP * HD]
        rows = jnp.concatenate([heads[:, i * HD : (i + 1) * HD] for i in range(GROUP)], axis=0)
        inverse = inv_ref[h, 0:1, :]
        turned = rows.astype(F32).T
        weighted = jnp.sum(turned * mixed_ref[h], axis=0, keepdims=True)
        factor = inverse * scale
        offset = weighted * factor
        rows_scaled = (turned * inverse).T.astype(BF)
        dq = jnp.zeros((HD, GROUP * tokens), F32)
        for j in range(length // CHUNK):
            part = expo[h, j * CHUNK : (j + 1) * CHUNK, :]
            keys = kv[2 * j : 2 * j + 2, :tokens, h * HD : (h + 1) * HD].reshape(CHUNK, HD)
            values = kv[
                2 * j : 2 * j + 2, :tokens, (KV_HEADS + h) * HD : (KV_HEADS + h + 1) * HD
            ].reshape(CHUNK, HD)
            prob_grad = contract_cols(values, rows)
            score_grad = (part.astype(F32) * (prob_grad * factor - offset)).astype(BF)
            dk = jnp.dot(score_grad, query, preferred_element_type=F32).astype(BF)
            dv = jnp.dot(part, rows_scaled, preferred_element_type=F32).astype(BF)
            for side_core in range(2):
                cut = slice(side_core * tokens, (side_core + 1) * tokens)
                dkv[side_core, j, :, h * HD : (h + 1) * HD] = dk[cut]
                dkv[side_core, j, :, (KV_HEADS + h) * HD : (KV_HEADS + h + 1) * HD] = dv[cut]
            dq = dq + contract_rows(keys, score_grad)
        for i in range(GROUP):
            at = (h * GROUP + i) * HD
            q_grad[:, at : at + HD] = turn_back(
                dq[:, i * tokens : (i + 1) * tokens].T, cos_ref[...], sin_ref[...]
            ).astype(BF)
    swap_kv = copies.start(dkv.at[1 - core], kv_in, sibling)

    def add_half(ref):
        def step(m, carry):
            at = pl.multiple_of(m * 192, 192)
            ref[pl.ds(at, 192), :] = (
                ref[pl.ds(at, 192), :].astype(F32) + keep_half[pl.ds(at, 192), :].astype(F32)
            ).astype(BF)
            return carry

        lax.fori_loop(0, width // 192, step, 0)

    def owner_rows(ref, owner):
        return ref.at[pl.ds(pl.multiple_of(owner * 192, 192), 192)]

    swap_o.wait_recv()
    add_half(o_in)
    o_sends = [
        copies.start(owner_rows(o_in, peer[1]), o_far.at[i], peer) for i, peer in enumerate(peers)
    ]

    swap_kv.wait_recv()
    kv_in[...] = (dkv[core].astype(F32) + kv_in[...].astype(F32)).astype(BF)
    kv_sends = [
        copies.start(kv_in.at[lax.div(device[0], 2)], kv_far.at[i], device)
        for i, device in enumerate(ring)
    ]

    swap_o.wait_send()
    out_half[...] = contract_rows(normed_ref[...], q_grad[:, columns_of(1 - core)]).astype(BF)
    swap_q = copies.start(out_half, q_in, sibling)
    keep_half[...] = contract_rows(normed_ref[...], q_grad[:, columns_of(core)]).astype(BF)
    for load in loads_own:
        load.wait()
    for copy in x_dn:
        copy.wait_recv()
    dn_mine[...] = (
        dn_mine[...].astype(F32)
        + dn_x[0].astype(F32)
        + dn_x[1].astype(F32)
        + dn_x[2].astype(F32)
    ).astype(BF)

    def window_of(z):
        return pl.ds(pl.multiple_of(z * shift, 16), window)

    z_dn = copies.start(dn_mine.at[window_of(1 - z_at)], dn_z, partner)
    swap_q.wait_recv()
    add_half(q_in)
    q_sends = [
        copies.start(owner_rows(q_in, peer[1]), q_far.at[i], peer) for i, peer in enumerate(peers)
    ]
    for copy in x_gu:
        copy.wait_recv()

    def sum_gu_x(g, carry):
        gu_mine[g] = (
            gu_mine[g].astype(F32)
            + gu_x[0, g].astype(F32)
            + gu_x[1, g].astype(F32)
            + gu_x[2, g].astype(F32)
        ).astype(BF)
        return carry

    lax.fori_loop(0, N_FS, sum_gu_x, 0)
    z_gu = copies.start(gu_mine.at[:, 1 - z_at], gu_z, partner)
    for copy in kv_sends:
        copy.wait_recv()
    total = kv_in[pair].astype(F32)
    for i in range(N_CTX // 2 - 1):
        total = total + kv_far[i].astype(F32)
    own_kv[...] = total
    for ref, sends, far, out in ((o_in, o_sends, o_far, o_red), (q_in, q_sends, q_far, q_red)):
        for copy in sends:
            copy.wait_recv()
        total = ref[pl.ds(pl.multiple_of(f * 192, 192), 192), :].astype(F32)
        for i in range(N_FS - 1):
            total = total + far[i].astype(F32)
        out[...] = total.astype(BF)
    z_dn.wait_recv()
    done_dn[...] = (dn_mine[window_of(z_at), :].astype(F32) + dn_z[...].astype(F32)).astype(BF)
    z_gu.wait_recv()

    def add_gu(g, carry):
        done_gu[g] = (gu_mine[g, z_at].astype(F32) + gu_z[g].astype(F32)).astype(BF)
        return carry

    lax.fori_loop(0, N_FS, add_gu, 0)
    for copy in [z_gu, z_dn, swap_kv, swap_q] + x_dn + x_gu + kv_sends + o_sends + q_sends:
        copy.wait_send()


def attention_back(cid, arrays, vmem_arrays):
    sum_gu, sum_dn, expo, kv_all, full_o = arrays
    tokens, width = vmem_arrays[0].shape
    piece, units = sum_gu.shape[3:]
    half = sum_dn.shape[0]
    strip = width // 4
    window = half // 2 + 8
    side = width // 2
    kv_width = KV_HEADS * HD
    rows = width // N_FS
    anywhere = pl.BlockSpec(memory_space=pl.ANY)
    vmem = pl.BlockSpec(memory_space=pltpu.VMEM)
    outs = [
        jax.ShapeDtypeStruct((N_FS, piece, units), BF),
        jax.ShapeDtypeStruct((window, strip), BF),
        jax.ShapeDtypeStruct((tokens, 2 * kv_width), F32),
        jax.ShapeDtypeStruct((rows, side), BF),
        jax.ShapeDtypeStruct((rows, side), BF),
        jax.ShapeDtypeStruct((tokens, width), BF),
        jax.ShapeDtypeStruct((tokens, width), F32),
        jax.ShapeDtypeStruct((1, width), F32),
    ]
    return pl.pallas_call(
        attention_back_kernel,
        name="attention_back",
        out_shape=outs,
        in_specs=[anywhere] * len(arrays) + [vmem] * len(vmem_arrays),
        out_specs=[vmem] * len(outs),
        scratch_shapes=[
            pltpu.VMEM(expo.shape, BF),
            pltpu.VMEM(kv_all.shape, BF),
            pltpu.VMEM(full_o.shape, BF),
            pltpu.VMEM((tokens, width), BF),
            pltpu.VMEM((tokens, width), BF),
            pltpu.VMEM((N_FS, 2, piece, units), BF),
            pltpu.VMEM((N_FS, piece, units), BF),
            pltpu.VMEM((3, N_FS, 2, piece, units), BF),
            pltpu.VMEM((half, strip), BF),
            pltpu.VMEM((3, half, strip), BF),
            pltpu.VMEM((window, strip), BF),
            pltpu.VMEM((2, N_CTX // 2, tokens, 2 * kv_width), BF),
            pltpu.VMEM((N_CTX // 2, tokens, 2 * kv_width), BF),
            pltpu.VMEM((N_CTX // 2 - 1, tokens, 2 * kv_width), BF),
            pltpu.VMEM((width, side), BF),
            pltpu.VMEM((width, side), BF),
            pltpu.VMEM((width, side), BF),
            pltpu.VMEM((width, side), BF),
            pltpu.VMEM((N_FS - 1, rows, side), BF),
            pltpu.VMEM((N_FS - 1, rows, side), BF),
            pltpu.SemaphoreType.DMA((32,)),
            pltpu.SemaphoreType.DMA((32,)),
            pltpu.SemaphoreType.DMA((5,)),
        ],
        compiler_params=pltpu.CompilerParams(
            collective_id=cid, has_side_effects=True, vmem_limit_bytes=62 * 2**20
        ),
    )(*arrays, *vmem_arrays)


def last_kernel(
    done_gu,
    done_dn,
    parts,
    qkv_hbm,
    own_kv,
    q_grad,
    o_red,
    q_red,
    normed_ref,
    input_ref,
    gain_ref,
    mid_ref,
    middle_ref,
    gain_two_grad,
    cos_ref,
    sin_ref,
    all_gu,
    all_dn,
    all_at,
    vec_sum,
    out_rows,
    in_rows,
    full_qkv,
    proj,
    own_gu,
    kv_out,
    kv_keep,
    kv_in,
    kv_far,
    at_all,
    at_far,
    at_own,
    vec,
    vec_fs,
    vec_mid,
    vec_ctx,
    out_in,
    send,
    recv,
    local,
):
    c, f = lax.axis_index("ctx"), lax.axis_index("fsdp")
    core, pair = lax.rem(c, 2), lax.div(c, 2)
    x_at, z_at = lax.rem(pair, 4), lax.div(pair, 4)
    sibling = (flip(c, 1), f)
    partner = (flip(c, 8), f)
    along = [(flip(c, 2 * i), f) for i in range(1, 4)]
    ring = [(flip(c, 2 * i), f) for i in range(1, N_CTX // 2)]
    peers = [(c, flip(f, i)) for i in range(1, N_FS)]
    cross = cross_peers(c, f)
    greet(ring + peers + [(flip(c, 8), flip(f, i)) for i in range(4, N_FS)] + [sibling])
    copies = Copies(send, recv)
    tokens, width = normed_ref.shape
    kv_width = KV_HEADS * HD
    strip = done_dn.shape[1]
    at_rows, at_cols = at_own.shape
    rest, own = [], []

    def local_copy(src, dst, n):
        copy = pltpu.make_async_copy(src, dst, local.at[n])
        copy.start()
        own.append(copy)
        return copy

    def x_of(device):
        return lax.rem(lax.div(device[0], 2), 4)

    def z_of(device):
        return lax.div(device[0], 8)

    def gu_place(device):
        return all_gu.at[lax.rem(device[0], 2), lax.div(device[0], 2)]

    def dn_place(device):
        columns = pl.ds(pl.multiple_of(x_of(device) * strip, strip), strip)
        return all_dn.at[lax.rem(device[0], 2), z_of(device), :, columns]

    def at_piece(ref, device):
        return ref.at[
            pl.ds(pl.multiple_of(x_of(device) * at_rows, at_rows), at_rows),
            pl.ds(pl.multiple_of(z_of(device) * at_cols, at_cols), at_cols),
        ]

    def at_place(device):
        return at_piece(all_at.at[lax.rem(device[0], 2)], device)

    here = (c, f)
    far = (partner[0], f)
    gu_own = local_copy(done_gu.at[f], own_gu.at[f], 0)
    gu_sends = [copies.start(done_gu.at[peer[1]], own_gu.at[f], peer) for peer in peers]
    local_copy(done_dn, dn_place(here), 1)
    dn_z = copies.start(done_dn, dn_place(here), partner)
    dn_x = [copies.start(done_dn, dn_place(here), device) for device in along]
    rest.append(copies.start(done_dn, dn_place(here), sibling))
    load_qkv = local_copy(qkv_hbm, full_qkv, 2)

    for h in range(KV_HEADS):
        at = width + h * HD
        proj[:, at : at + HD] = turn_back(
            own_kv[:, h * HD : (h + 1) * HD], cos_ref[...], sin_ref[...]
        ).astype(BF)
    proj[:, width + kv_width :] = own_kv[:, kv_width:].astype(BF)
    proj[:, :width] = q_grad[...]

    def side_of(which):
        return pl.ds(pl.multiple_of(width + which * kv_width, kv_width), kv_width)

    kv_out[...] = contract_rows(normed_ref[...], proj[:, side_of(1 - core)]).astype(BF)
    swap_kv = copies.start(kv_out, kv_in, sibling)
    kv_keep[...] = contract_rows(normed_ref[...], proj[:, side_of(core)]).astype(BF)

    gu_own.wait()
    for copy in gu_sends:
        copy.wait_recv()
    gu_z = copies.start(own_gu, gu_place(here), partner)
    gu_x = [copies.start(own_gu, gu_place(here), device) for device in along]
    rest.append(copies.start(own_gu, gu_place(here), sibling))
    local_copy(own_gu, gu_place(here), 3)

    swap_kv.wait_recv()
    kv_in[...] = (kv_in[...].astype(F32) + kv_keep[...].astype(F32)).astype(BF)

    def owner_rows(owner):
        return pl.ds(pl.multiple_of(owner * 192, 192), 192)

    kv_sends = [
        copies.start(kv_in.at[owner_rows(peer[1])], kv_far.at[i], peer)
        for i, peer in enumerate(cross)
    ]
    out_sends = [
        copies.start(parts.at[i + 1], out_in.at[i], peer) for i, peer in enumerate(peers)
    ]
    out_own = local_copy(parts.at[0], out_in.at[N_FS - 1], 4)

    load_qkv.wait()
    in_norm_grad = contract_cols(proj[...], full_qkv[...])
    inputs = input_ref[...].astype(F32)
    scale_one = lax.rsqrt(jnp.mean(inputs * inputs, axis=-1, keepdims=True) + EPSILON)
    norm = inputs * scale_one
    gain_one_grad = jnp.sum(in_norm_grad * norm, axis=0, keepdims=True)
    scaled = in_norm_grad * gain_ref[...]
    in_rows[...] = mid_ref[...] + scale_one * (
        scaled - norm * jnp.mean(scaled * norm, axis=-1, keepdims=True)
    )
    bias_grad = jnp.sum(proj[...].astype(F32), axis=0, keepdims=True)
    row = 0
    for vector in (gain_one_grad, gain_two_grad[...], bias_grad):
        for n in range(vector.shape[1] // 128):
            vec[row : row + 1, :] = vector[:, n * 128 : (n + 1) * 128]
            row += 1
    vec_sends = [copies.start(vec, vec_fs.at[i], peer) for i, peer in enumerate(peers)]

    dn_z.wait_recv()
    dn_x2 = [copies.start(dn_place(far), dn_place(far), device) for device in along]
    rest.append(copies.start(dn_place(far), dn_place(far), sibling))

    for copy in kv_sends:
        copy.wait_recv()
    total = kv_in[owner_rows(f), :].astype(F32)
    for i in range(N_FS - 1):
        total = total + kv_far[i].astype(F32)
    side = width // 2
    at_all[:, :side] = o_red[...]
    at_all[:, side : 2 * side] = q_red[...]
    at_all[:, 2 * side :] = total.astype(BF)
    at_sends = [
        copies.start(at_piece(at_all, device), at_far.at[i], device)
        for i, device in enumerate(ring)
    ]
    for copy in vec_sends:
        copy.wait_recv()
    total = vec[...]
    for i in range(N_FS - 1):
        total = total + vec_fs[i]
    vec_mid[...] = total
    vec_near = [copies.start(vec_mid, vec_ctx.at[c], device) for device in ring]
    rest.append(copies.start(vec_mid, vec_ctx.at[c], sibling))
    vec_ctx[pl.ds(c, 1)] = total[None]

    gu_z.wait_recv()
    gu_x2 = [copies.start(gu_place(far), gu_place(far), device) for device in along]
    rest.append(copies.start(gu_place(far), gu_place(far), sibling))

    for copy in at_sends:
        copy.wait_recv()
    total = at_all[
        pl.ds(pl.multiple_of(x_at * at_rows, at_rows), at_rows),
        pl.ds(pl.multiple_of(z_at * at_cols, at_cols), at_cols),
    ].astype(F32)
    for i in range(N_CTX // 2 - 1):
        total = total + at_far[i].astype(F32)
    at_own[...] = total.astype(BF)
    at_near = [copies.start(at_own, at_place(here), device) for device in ring]
    rest.append(copies.start(at_own, at_place(here), sibling))
    local_copy(at_own, at_place(here), 5)

    for copy, device in zip(vec_near, ring):
        copy.wait_recv()
        place = vec_ctx.at[device[0]]
        rest.append(copies.start(place, place, sibling))
    for one, two, device in zip(dn_x, dn_x2, along):
        one.wait_recv()
        rest.append(copies.start(dn_place(device), dn_place(device), sibling))
        two.wait_recv()
        other = (flip(device[0], 8), f)
        rest.append(copies.start(dn_place(other), dn_place(other), sibling))
    for copy in out_sends:
        copy.wait_recv()
    out_own.wait()
    total = middle_ref[...]
    for i in range(N_FS):
        total = total + out_in[i].astype(F32)
    out_rows[...] = total.astype(BF)
    for copy, device in zip(at_near, ring):
        copy.wait_recv()
        rest.append(copies.start(at_place(device), at_place(device), sibling))
    for one, two, device in zip(gu_x, gu_x2, along):
        one.wait_recv()
        rest.append(copies.start(gu_place(device), gu_place(device), sibling))
        two.wait_recv()
        other = (flip(device[0], 8), f)
        rest.append(copies.start(gu_place(other), gu_place(other), sibling))
    for copy in (
        gu_sends + [dn_z] + dn_x + dn_x2 + gu_x + [gu_z] + gu_x2 + [swap_kv] + kv_sends + out_sends
        + vec_sends + vec_near + at_sends + at_near
    ):
        copy.wait_send()
    for copy in rest:
        copy.wait()
    total = vec_ctx[0]
    for i in range(1, N_CTX):
        total = total + vec_ctx[i]
    vec_sum[...] = total
    for copy in own:
        if copy is not gu_own and copy is not load_qkv and copy is not out_own:
            copy.wait()


def last_exchange(cid, arrays, vmem_arrays):
    done_gu, done_dn, parts, full_qkv = arrays
    tokens, width = parts.shape[1:]
    piece, units = done_gu.shape[1:]
    window, strip = done_dn.shape
    rows = width // N_FS
    kv_width = KV_HEADS * HD
    at_width = width + kv_width
    anywhere = pl.BlockSpec(memory_space=pl.ANY)
    vmem = pl.BlockSpec(memory_space=pltpu.VMEM)
    outs = [
        jax.ShapeDtypeStruct((2, N_CTX // 2, N_FS, piece, units), BF),
        jax.ShapeDtypeStruct((2, 2, window, width), BF),
        jax.ShapeDtypeStruct((2, rows, at_width), BF),
        jax.ShapeDtypeStruct((40, 128), F32),
        jax.ShapeDtypeStruct((tokens, width), BF),
        jax.ShapeDtypeStruct((tokens, width), F32),
    ]
    return pl.pallas_call(
        last_kernel,
        name="last_exchange",
        out_shape=outs,
        in_specs=[anywhere] * len(arrays) + [vmem] * len(vmem_arrays),
        out_specs=[anywhere] * 3 + [vmem] * 3,
        scratch_shapes=[
            pltpu.VMEM(full_qkv.shape, BF),
            pltpu.VMEM((tokens, width + 2 * kv_width), BF),
            pltpu.VMEM((N_FS, piece, units), BF),
            pltpu.VMEM((width, kv_width), BF),
            pltpu.VMEM((width, kv_width), BF),
            pltpu.VMEM((width, kv_width), BF),
            pltpu.VMEM((N_FS - 1, rows, kv_width), BF),
            pltpu.VMEM((rows, at_width), BF),
            pltpu.VMEM((N_CTX // 2 - 1, rows // 4, at_width // 2), BF),
            pltpu.VMEM((rows // 4, at_width // 2), BF),
            pltpu.VMEM((40, 128), F32),
            pltpu.VMEM((N_FS - 1, 40, 128), F32),
            pltpu.VMEM((40, 128), F32),
            pltpu.VMEM((N_CTX, 40, 128), F32),
            pltpu.VMEM((N_FS, tokens, width), BF),
            pltpu.SemaphoreType.DMA((100,)),
            pltpu.SemaphoreType.DMA((100,)),
            pltpu.SemaphoreType.DMA((6,)),
        ],
        compiler_params=pltpu.CompilerParams(
            collective_id=cid, has_side_effects=True, vmem_limit_bytes=48 * 2**20
        ),
    )(*arrays, *vmem_arrays)


def wide_kernel(gu_ref, gate_ref, up_ref):
    for which, out in enumerate((gate_ref, up_ref)):
        out[...] = jnp.concatenate(
            [gu_ref[which, 0, source].astype(F32) for source in range(N_FS)], axis=1
        )


def wide_results(all_gu):
    piece, units = all_gu.shape[3:]
    parts = all_gu.shape[1]
    shape = jax.ShapeDtypeStruct((parts * piece, N_FS * units), F32)
    return pl.pallas_call(
        wide_kernel,
        name="wide_results",
        grid=(parts,),
        in_specs=[pl.BlockSpec((2, 1, N_FS, piece, units), lambda p: (0, p, 0, 0, 0))],
        out_specs=[pl.BlockSpec((piece, N_FS * units), lambda p: (p, 0))] * 2,
        out_shape=[shape, shape],
        compiler_params=pltpu.CompilerParams(vmem_limit_bytes=32 * 2**20),
    )(all_gu)


def rest_kernel(dn_ref, at_ref, down_ref, o_ref, q_ref, k_ref, v_ref):
    z = lax.rem(pl.program_id(0), 2)
    rows = down_ref.shape[0]
    block = dn_ref[0, 0].astype(F32)
    down_ref[...] = jnp.where(z == 0, block[:rows], block[8 : 8 + rows])
    side = o_ref.shape[1] // 2
    for n in range(2):
        part = at_ref[n].astype(F32)
        o_ref[:, n * side : (n + 1) * side] = part[:, :side]
        q_ref[:, n * side : (n + 1) * side] = part[:, side : 2 * side]
        (k_ref, v_ref)[n][...] = part[:, 2 * side :]


def rest_results(all_dn, all_at):
    window, width = all_dn.shape[2:]
    rows = window - 8
    own, at_width = all_at.shape[1:]
    kv_width = KV_HEADS * HD
    return pl.pallas_call(
        rest_kernel,
        name="rest_results",
        grid=(4,),
        in_specs=[
            pl.BlockSpec((1, 1, window, width), lambda n: (n // 2, n % 2, 0, 0)),
            pl.BlockSpec((2, own // 4, at_width), lambda n: (0, n, 0)),
        ],
        out_specs=[
            pl.BlockSpec((rows, width), lambda n: (n, 0)),
            pl.BlockSpec((own // 4, width), lambda n: (n, 0)),
            pl.BlockSpec((own // 4, width), lambda n: (n, 0)),
            pl.BlockSpec((own // 4, kv_width), lambda n: (n, 0)),
            pl.BlockSpec((own // 4, kv_width), lambda n: (n, 0)),
        ],
        out_shape=[
            jax.ShapeDtypeStruct((4 * rows, width), F32),
            jax.ShapeDtypeStruct((own, width), F32),
            jax.ShapeDtypeStruct((own, width), F32),
            jax.ShapeDtypeStruct((own, kv_width), F32),
            jax.ShapeDtypeStruct((own, kv_width), F32),
        ],
        compiler_params=pltpu.CompilerParams(vmem_limit_bytes=32 * 2**20),
    )(all_dn, all_at)


def body(
    layer_input,
    segments,
    positions,
    attn_norm,
    q_weight,
    q_bias,
    k_weight,
    k_bias,
    v_weight,
    v_bias,
    o_weight,
    mlp_norm,
    gate_weight,
    up_weight,
    down_weight,
    out_cotangent,
):
    tokens, width = layer_input.shape[1:]
    rows = gate_weight.shape[0]
    units = gate_weight.shape[1] // N_FS
    q_width = HEADS * HD
    kv_width = KV_HEADS * HD
    half_block = tokens // 2
    ctx = lax.axis_index("ctx")
    segment = segments[0]
    cot_low = jnp.where((segment > 0)[:, None], out_cotangent[0], 0)
    small = jnp.stack(
        [
            jnp.pad(v.astype(F32), (0, 256 - v.shape[0]))
            for v in (attn_norm, mlp_norm, q_bias, k_bias, v_bias)
        ]
        + [jnp.zeros((256,), F32)] * 3
    )
    cosine, sine = rope_tables(positions[0], HD)
    cos_wide = jnp.concatenate([cosine, cosine], axis=1)
    sin_wide = jnp.concatenate([sine, -sine], axis=1)
    within = jnp.arange(tokens, dtype=jnp.int32)
    row_place = jnp.where(
        within < half_block,
        ctx * half_block + within,
        (2 * N_CTX - 1 - ctx) * half_block + within - half_block,
    )
    row_info = jnp.stack([row_place.astype(F32), segment.astype(F32)])
    (
        full_qkv,
        full_o,
        kv_all,
        columns,
        cot_all,
        expo,
        gains,
        normed_in,
        query,
        mixed,
        inverse,
        attended,
        middle,
        normed_mid,
    ) = front(
        1,
        (q_weight, k_weight, v_weight, o_weight, gate_weight, up_weight, cot_low),
        (small, layer_input[0], row_info, cos_wide, sin_wide),
    )
    full_qkv = full_qkv.reshape(width, q_width + 2 * kv_width)
    full_o = full_o.reshape(q_width, width)
    columns = columns.reshape(2, width, units)
    gain_one, gain_two = gains[0:1], gains[1:2]

    piece = rows // 8
    mid_norm_grad, out_part, sum_gu, sum_down = feed_forward(
        8, normed_mid, cot_all, columns, down_weight
    )
    done_gu, done_dn, own_kv, o_red, q_red, q_grad, mid_grad, gain_two_grad = attention_back(
        3,
        (sum_gu.reshape(N_FS, 2, 4, piece, units), sum_down, expo, kv_all, full_o),
        (
            mid_norm_grad,
            middle,
            cot_low,
            gain_two,
            query,
            mixed,
            inverse,
            attended,
            normed_in,
            cos_wide,
            sin_wide,
        ),
    )
    all_gu, all_dn, all_at, all_vec, output_rows, input_rows = last_exchange(
        4,
        (done_gu, done_dn, out_part, full_qkv),
        (
            own_kv,
            q_grad,
            o_red,
            q_red,
            normed_in,
            layer_input[0],
            gain_one,
            mid_grad,
            middle,
            gain_two_grad,
            cos_wide,
            sin_wide,
        ),
    )
    gate_grad, up_grad = wide_results(all_gu)
    down_grad, o_grad, q_weight_grad, k_grad, v_grad = rest_results(all_dn, all_at)
    flat_vec = all_vec.reshape(-1)
    mine = lax.axis_index("fsdp")
    vectors = []
    start = 0
    for whole in (width, width, q_width, kv_width, kv_width):
        part = whole // N_FS
        vectors.append(lax.dynamic_slice_in_dim(flat_vec, start + mine * part, part, 0))
        start += whole
    return (
        output_rows[None],
        input_rows[None],
        vectors[0],
        q_weight_grad,
        vectors[2],
        k_grad,
        vectors[3],
        v_grad,
        vectors[4],
        o_grad,
        vectors[1],
        gate_grad,
        up_grad,
        down_grad,
    )


def solution(mesh):
    placed = (
        P("fsdp", "ctx", None),
        P("fsdp", "ctx"),
        P("fsdp", "ctx"),
        P("fsdp"),
        P("fsdp", None),
        P("fsdp"),
        P("fsdp", None),
        P("fsdp"),
        P("fsdp", None),
        P("fsdp"),
        P("fsdp", None),
        P("fsdp"),
        P("fsdp", None),
        P("fsdp", None),
        P("fsdp", None),
        P("fsdp", "ctx", None),
    )
    return jax.shard_map(
        body,
        mesh=mesh,
        in_specs=placed,
        out_specs=(
            P("fsdp", "ctx", None),
            P("fsdp", "ctx", None),
            P("fsdp"),
            P("fsdp", None),
            P("fsdp"),
            P("fsdp", None),
            P("fsdp"),
            P("fsdp", None),
            P("fsdp"),
            P("fsdp", None),
            P("fsdp"),
            P("fsdp", None),
            P("fsdp", None),
            P("fsdp", None),
        ),
        check_vma=False,
    )
```

```python
import functools

import jax
import jax.numpy as jnp
from jax import lax
from jax.experimental import pallas as pl
from jax.experimental.pallas import tpu as pltpu
from jax.sharding import PartitionSpec as P

HEADS = 12
KV_HEADS = 2
HD = 128
GROUP = HEADS // KV_HEADS
N_CTX = 16
N_FS = 8
EPSILON = 1e-06
THETA = 1000000.0
MESH = pl.DeviceIdType.MESH
BF = jnp.bfloat16
F32 = jnp.float32


def rope_tables(position, head_dim):
    freqs = THETA ** (-jnp.arange(0, head_dim, 2).astype(F32) / head_dim)
    angles = position.astype(F32)[:, None] * freqs[None, :]
    return (jnp.cos(angles), jnp.sin(angles))


def contract_rows(left, right):
    return lax.dot_general(
        left, right, (((0,), (0,)), ((), ())), preferred_element_type=F32
    )


def contract_cols(left, right):
    return lax.dot_general(
        left, right, (((1,), (1,)), ((), ())), preferred_element_type=F32
    )


def flip(value, mask):
    out = value
    bit = 1
    while bit <= mask:
        if mask & bit:
            out = out + bit * (1 - 2 * lax.rem(lax.div(value, bit), 2))
        bit *= 2
    return out


class Copies:
    def __init__(self, send, recv):
        self.send, self.recv, self.count = send, recv, 0

    def start(self, src, dst, device):
        copy = self.make(src, dst, device)
        copy.start()
        return copy

    def make(self, src, dst, device):
        copy = pltpu.make_async_remote_copy(
            src_ref=src,
            dst_ref=dst,
            send_sem=self.send.at[self.count],
            recv_sem=self.recv.at[self.count],
            device_id=device,
            device_id_type=MESH,
        )
        self.count += 1
        return copy


def greet(devices):
    barrier = pltpu.get_barrier_semaphore()
    for device in devices:
        pl.semaphore_signal(barrier, inc=1, device_id=device, device_id_type=MESH)
    pl.semaphore_wait(barrier, len(devices))


def cross_peers(c, f):
    away = c + lax.rem(c, 2) * (flip(c, 8) - c)
    return [(c if i < 4 else away, flip(f, i)) for i in range(1, N_FS)]


class SharedRows:
    def __init__(self, copies, ref, c, f, columns=None):
        core = lax.rem(c, 2)
        self.copies, self.f = copies, f
        self.sibling = (flip(c, 1), f)
        self.over = (c + core * (flip(c, 8) - c), flip(f, 4))
        self.one, self.three = (c, flip(f, 1)), (c, flip(f, 3))
        rows = ref.shape[1] // 2

        def place(owner, part=None):
            if part is None:
                span = pl.ds(pl.multiple_of(core * rows, 16), rows)
            else:
                span = pl.ds(pl.multiple_of(core * rows + part * (rows // 2), 16), rows // 2)
            if columns is None:
                return ref.at[owner, span]
            return ref.at[owner, span, columns]

        self.place = place
        mine = place(f)
        self.from_one = copies.start(mine, mine, self.one)
        self.from_three = copies.start(mine, mine, self.three)
        self.z_copies = [copies.start(mine, mine, self.over)]
        self.sent = [self.from_one, self.from_three]
        self.rest = []

    def send(self, here, device):
        return self.copies.start(here, here, device)

    def pass_y(self):
        one, three = flip(self.f, 1), flip(self.f, 3)
        self.from_one.wait_recv()
        self.far = [self.send(self.place(one, 0), self.three)]
        self.z_copies.append(self.send(self.place(one), self.over))
        self.from_three.wait_recv()
        self.far.append(self.send(self.place(three, 1), self.one))
        self.z_copies.append(self.send(self.place(three), self.over))
        self.rest.append(self.send(self.place(one), self.sibling))
        self.rest.append(self.send(self.place(three), self.sibling))
        for copy in self.far:
            copy.wait_recv()
        two = self.place(flip(self.f, 2))
        self.z_copies.append(self.send(two, self.over))
        self.rest.append(self.send(two, self.sibling))

    def pass_z(self):
        for copy, mask in zip(self.z_copies, (4, 5, 7, 6)):
            copy.wait_recv()
            self.rest.append(self.send(self.place(flip(self.f, mask)), self.sibling))

    def wait(self):
        for copy in self.rest:
            copy.wait_recv()

    def finish(self):
        for copy in self.sent + self.far + self.z_copies + self.rest:
            copy.wait_send()


CHUNK = 256


def turn_back(grad, cos_wide, sin_wide):
    half = grad.shape[1] // 2
    swapped = jnp.concatenate([grad[:, half:], grad[:, :half]], axis=1)
    return grad * cos_wide + swapped * sin_wide


def front_kernel(
    q_hbm,
    k_hbm,
    v_hbm,
    o_hbm,
    gate_hbm,
    up_hbm,
    cot_ref,
    small_ref,
    input_ref,
    row_ref,
    cos_ref,
    sin_ref,
    w_out,
    o_out,
    kv_out,
    g_out,
    t_out,
    e_out,
    gains_ref,
    normed_ref,
    query_ref,
    mixed_ref,
    inv_ref,
    attended_ref,
    middle_ref,
    normed_mid_ref,
    weights,
    full_o,
    small_all,
    strip,
    stage,
    kv_own,
    kv,
    s_ref,
    expo,
    send,
    recv,
    local,
):
    c, f = lax.axis_index("ctx"), lax.axis_index("fsdp")
    core = lax.rem(c, 2)
    sibling = (flip(c, 1), f)
    here = (c, f)
    peers = [(c, flip(f, i)) for i in range(1, N_FS)]
    ring = [(flip(c, 2 * i), f) for i in range(1, N_CTX // 2)]
    along = ring[:3]
    near, turn = peers[:3], peers[3]
    greet(peers + ring + [sibling, (flip(c, 8), flip(f, 4))])
    copies = Copies(send, recv)
    tokens, width = input_ref.shape
    rows = q_hbm.shape[0]
    kv_width = KV_HEADS * HD
    cut, units = stage.shape[1:]
    x_part = lax.rem(c, N_FS)

    def local_copy(src, dst, n):
        copy = pltpu.make_async_copy(src, dst, local.at[n])
        copy.start()
        return copy

    mine = weights.at[f]
    q_columns, kv_columns = pl.ds(0, width), pl.ds(width, 2 * kv_width)
    load_k = local_copy(k_hbm, mine.at[:, pl.ds(width, kv_width)], 1)
    load_v = local_copy(v_hbm, mine.at[:, pl.ds(width + kv_width, kv_width)], 2)
    block_rows = pl.ds(pl.multiple_of(lax.rem(x_part, 4) * cut, cut), cut)
    load_gate = local_copy(gate_hbm.at[block_rows], strip.at[0], 3)
    load_up = local_copy(up_hbm.at[block_rows], strip.at[1], 4)
    load_q = local_copy(q_hbm, mine.at[:, q_columns], 0)
    load_o = local_copy(o_hbm, full_o.at[f], 5)
    load_t = local_copy(cot_ref, t_out.at[0], 6)
    small_own = local_copy(small_ref, small_all.at[f], 7)
    small_sends = [copies.start(small_ref, small_all.at[f], peer) for peer in peers]
    load_k.wait()
    load_v.wait()
    share_kv = SharedRows(copies, weights, c, f, kv_columns)

    def columns(device, part=None):
        where = lax.rem(device[0], N_FS)
        if part is None:
            return g_out.at[lax.div(where, 4), :, lax.rem(where, 4)]
        half = N_FS // 2
        return g_out.at[lax.div(where, 4), pl.ds(part * half, half), lax.rem(where, 4)]

    def block(device, source):
        where = lax.rem(device[0], N_FS)
        return g_out.at[lax.div(where, 4), source, lax.rem(where, 4)]

    load_gate.wait()
    load_up.wait()
    which = lax.div(x_part, 4)
    for owner in range(N_FS):
        stage[owner] = strip[which, :, owner * units : (owner + 1) * units]
    block_own = local_copy(stage.at[f], block(here, f), 8)
    blocks = [copies.start(stage.at[peer[1]], block(here, f), peer) for peer in peers]
    load_q.wait()
    share_q = SharedRows(copies, weights, c, f, q_columns)

    inputs = input_ref[...].astype(F32)
    norm = inputs * lax.rsqrt(jnp.mean(inputs * inputs, axis=-1, keepdims=True) + EPSILON)
    small_own.wait()
    for copy in small_sends:
        copy.wait_recv()

    def vector(n, part):
        pieces = [small_all[owner, n : n + 1, :part] for owner in range(N_FS)]
        return jnp.concatenate(pieces, axis=1)

    gain_one, gain_two, bias_q = vector(0, rows), vector(1, rows), vector(2, rows)
    bias_k, bias_v = vector(3, kv_width // N_FS), vector(4, kv_width // N_FS)
    gains_ref[0:1, :] = gain_one
    gains_ref[1:2, :] = gain_two
    normed_ref[...] = (norm * gain_one).astype(BF)

    share_kv.pass_y()
    share_kv.pass_z()
    share_kv.wait()
    cos_wide, sin_wide = cos_ref[...], -sin_ref[...]
    full = weights[:, :, width:].reshape(width, 2 * kv_width)
    projected = jnp.dot(normed_ref[...], full, preferred_element_type=F32)
    projected = projected + jnp.concatenate([bias_k, bias_v], axis=1)
    for h in range(KV_HEADS):
        cols = slice(h * HD, (h + 1) * HD)
        kv_own[:tokens, cols] = turn_back(projected[:, cols], cos_wide, sin_wide).astype(BF)
    kv_own[:tokens, kv_width:] = projected[:, kv_width:].astype(BF)
    marks = jnp.concatenate([row_ref[1:2, :]] * (2 * KV_HEADS), axis=1)
    kv_own[tokens:, :] = jnp.broadcast_to(marks, (16, 2 * kv_width)).astype(BF)
    keep_kv = local_copy(kv_own, kv.at[c], 9)
    keys = [copies.start(kv_own, kv.at[c], device) for device in ring]
    kv_rest = [copies.start(kv_own, kv.at[c], sibling)]

    block_own.wait()
    for copy in blocks:
        copy.wait_recv()
    x_one, x_two, x_three = along
    from_one = copies.start(columns(here), columns(here), x_one)
    from_three = copies.start(columns(here), columns(here), x_three)
    g_rest = [copies.start(columns(here), columns(here), sibling)]

    share_q.pass_y()
    load_o.wait()
    share_o = SharedRows(copies, full_o, c, f)
    half = tokens // 2
    upper, lower = pl.ds(0, half), pl.ds(half, half)
    low_z = copies.start(cot_ref.at[lower], t_out.at[4, lower], turn)
    up_y = [
        copies.start(cot_ref.at[upper], t_out.at[i + 1, upper], device)
        for i, device in enumerate(near)
    ]
    up_z = [copies.start(cot_ref.at[upper], t_out.at[4, upper], turn)]
    low_y = [
        copies.start(cot_ref.at[lower], t_out.at[i + 1, lower], device)
        for i, device in enumerate(near)
    ]
    for key, device in zip(keys, ring):
        key.wait_recv()
        place = kv.at[device[0]]
        kv_rest.append(copies.start(place, place, sibling))
    share_q.pass_z()
    share_q.wait()

    full = weights[:, :, :width].reshape(width, width)
    projected = jnp.dot(normed_ref[...], full, preferred_element_type=F32) + bias_q
    for n in range(HEADS):
        at = (n % GROUP) * tokens
        query_ref[n // GROUP, at : at + tokens, :] = turn_back(
            projected[:, n * HD : (n + 1) * HD], cos_wide, sin_wide
        ).astype(BF)
    save_w = local_copy(weights, w_out, 0)

    from_one.wait_recv()
    far = [copies.start(columns(x_one, 0), columns(x_one, 0), x_three)]
    from_three.wait_recv()
    far.append(copies.start(columns(x_three, 1), columns(x_three, 1), x_one))
    for device in (x_one, x_three):
        g_rest.append(copies.start(columns(device), columns(device), sibling))
    share_o.pass_y()
    keep_kv.wait()
    for copy in kv_rest:
        copy.wait_recv()
    save_kv = local_copy(kv, kv_out, 1)

    length = N_CTX * tokens
    scale = HD ** (-0.5)
    row_place, row_seg = row_ref[0:1, :], row_ref[1:2, :]
    key_seg = kv[:, tokens : tokens + 16, :HD][:, 0, :].astype(F32).T
    within = lax.broadcasted_iota(jnp.int32, (tokens, tokens), 0)
    saves = []
    for h in range(KV_HEADS):
        query = query_ref[h]
        top = jnp.full((8, GROUP * tokens), -1e30, F32)
        for b in range(N_CTX):
            place = jnp.where(
                within < half, b * half + within, (2 * N_CTX - 1 - b) * half + within - half
            ).astype(F32)
            allowed = (place <= row_place) & (key_seg[:, b : b + 1] == row_seg) & (row_seg > 0.5)
            bias = jnp.where(allowed, 0.0, -1e30).astype(F32)
            scores = contract_cols(kv[b, :tokens, h * HD : (h + 1) * HD], query) * scale
            scores = scores + jnp.concatenate([bias] * GROUP, axis=1)
            s_ref[b * tokens : (b + 1) * tokens, :] = scores
            top = jnp.maximum(top, jnp.max(scores.reshape(tokens // 8, 8, -1), axis=0))
        highest = jnp.maximum(jnp.max(top, axis=0, keepdims=True), -1e29)
        total = jnp.zeros((8, GROUP * tokens), F32)
        mixed = jnp.zeros((HD, GROUP * tokens), F32)
        for j in range(length // CHUNK):
            part = jnp.exp(s_ref[j * CHUNK : (j + 1) * CHUNK, :] - highest)
            total = total + jnp.sum(part.reshape(CHUNK // 8, 8, -1), axis=0)
            low = part.astype(BF)
            expo[h, j * CHUNK : (j + 1) * CHUNK, :] = low
            at = (KV_HEADS + h) * HD
            values = kv[2 * j : 2 * j + 2, :tokens, at : at + HD].reshape(CHUNK, HD)
            mixed = mixed + contract_rows(values, low)
        total = jnp.sum(total, axis=0, keepdims=True)
        inverse = 1.0 / jnp.where(total > 0.5, total, 1.0)
        mixed = mixed * inverse
        mixed_ref[h] = mixed
        inv_ref[h] = jnp.broadcast_to(inverse, (8, GROUP * tokens))
        for i in range(GROUP):
            at = (h * GROUP + i) * HD
            attended_ref[:, at : at + HD] = mixed[:, i * tokens : (i + 1) * tokens].T.astype(BF)
        saves.append(local_copy(expo.at[h], e_out.at[h], 2 + h))
        if h == 0:
            low_z.wait_recv()
            for i, device in enumerate(near):
                low_y.append(copies.start(t_out.at[4, lower], t_out.at[5 + i, lower], device))
            for i, copy in enumerate(up_y):
                copy.wait_recv()
                up_z.append(copies.start(t_out.at[i + 1, upper], t_out.at[5 + i, upper], turn))
            for copy in far:
                copy.wait_recv()
            g_rest.append(copies.start(columns(x_two), columns(x_two), sibling))
            share_o.pass_z()

    share_o.wait()
    product = jnp.dot(
        attended_ref[...], full_o[...].reshape(width, width), preferred_element_type=F32
    )
    middle = input_ref[...].astype(F32) + product
    middle_ref[...] = middle
    scale_two = lax.rsqrt(jnp.mean(middle * middle, axis=-1, keepdims=True) + EPSILON)
    normed_mid_ref[...] = (middle * scale_two * gains_ref[1:2, :]).astype(BF)
    save_o = local_copy(full_o, o_out, 4)
    for copy in low_y + up_z + g_rest:
        copy.wait_recv()
    for share in (share_kv, share_q, share_o):
        share.finish()
    for copy in (
        small_sends + blocks + [from_one, from_three] + far + g_rest + low_y + up_z + up_y
        + [low_z] + keys + kv_rest
    ):
        copy.wait_send()
    for copy in saves + [save_w, save_kv, save_o, load_t]:
        copy.wait()


def front(cid, arrays, vmem_arrays):
    tokens, width = vmem_arrays[1].shape
    rows, all_units = arrays[4].shape
    units = all_units // N_FS
    cut = rows // 4
    kv_width = KV_HEADS * HD
    wide = GROUP * tokens
    length = N_CTX * tokens
    anywhere = pl.BlockSpec(memory_space=pl.ANY)
    vmem = pl.BlockSpec(memory_space=pltpu.VMEM)
    weights = (N_FS, rows, width + 2 * kv_width)
    full_o = (N_FS, rows, width)
    kv = (N_CTX, tokens + 16, 2 * kv_width)
    expo = (KV_HEADS, length, wide)
    return pl.pallas_call(
        front_kernel,
        name="front",
        out_shape=[
            jax.ShapeDtypeStruct(weights, BF),
            jax.ShapeDtypeStruct(full_o, BF),
            jax.ShapeDtypeStruct(kv, BF),
            jax.ShapeDtypeStruct((2, N_FS, 4, cut, units), BF),
            jax.ShapeDtypeStruct((N_FS, tokens, width), BF),
            jax.ShapeDtypeStruct(expo, BF),
            jax.ShapeDtypeStruct((2, width), F32),
            jax.ShapeDtypeStruct((tokens, width), BF),
            jax.ShapeDtypeStruct((KV_HEADS, wide, HD), BF),
            jax.ShapeDtypeStruct((KV_HEADS, HD, wide), F32),
            jax.ShapeDtypeStruct((KV_HEADS, 8, wide), F32),
            jax.ShapeDtypeStruct((tokens, width), BF),
            jax.ShapeDtypeStruct((tokens, width), F32),
            jax.ShapeDtypeStruct((tokens, width), BF),
        ],
        in_specs=[anywhere] * len(arrays) + [vmem] * len(vmem_arrays),
        out_specs=[anywhere] * 6 + [vmem] * 8,
        scratch_shapes=[
            pltpu.VMEM(weights, BF),
            pltpu.VMEM(full_o, BF),
            pltpu.VMEM((N_FS,) + vmem_arrays[0].shape, F32),
            pltpu.VMEM((2, cut, all_units), BF),
            pltpu.VMEM((N_FS, cut, units), BF),
            pltpu.VMEM(kv[1:], BF),
            pltpu.VMEM(kv, BF),
            pltpu.VMEM((length, wide), F32),
            pltpu.VMEM(expo, BF),
            pltpu.SemaphoreType.DMA((104,)),
            pltpu.SemaphoreType.DMA((104,)),
            pltpu.SemaphoreType.DMA((10,)),
        ],
        compiler_params=pltpu.CompilerParams(
            collective_id=cid, has_side_effects=True, vmem_limit_bytes=60 * 2**20
        ),
    )(*arrays, *vmem_arrays)


def back_kernel(
    nm_ref,
    cot_ref,
    gu_ref,
    down_ref,
    expo_hbm,
    kv_hbm,
    o_hbm,
    middle_hbm,
    query_hbm,
    mixed_hbm,
    attended_hbm,
    normed_hbm,
    gain_ref,
    inv_ref,
    cos_ref,
    sin_ref,
    out_ref,
    out_in,
    gu_x,
    dn_x,
    o_far,
    q_far,
    kv_far,
    done_gu,
    done_dn,
    own_kv,
    o_red,
    q_red,
    q_grad,
    mid_ref,
    gain_grad,
    nm,
    part_in,
    gu_in,
    dn_in,
    gu_z,
    dn_mine,
    dn_z,
    kv_in,
    o_in,
    q_in,
    part_send,
    part_recv,
    send,
    recv,
    local,
):
    c, f = lax.axis_index("ctx"), lax.axis_index("fsdp")
    core, pair_at = lax.rem(c, 2), lax.div(c, 2)
    x_at, z_at = lax.rem(pair_at, 4), lax.div(pair_at, 4)
    sibling = (flip(c, 1), f)
    partner = (flip(c, 8), f)
    ring = [(flip(c, 2 * i), f) for i in range(1, N_CTX // 2)]
    along = ring[:3]
    peers = [(c, flip(f, i)) for i in range(1, N_FS)]
    cross = cross_peers(c, f)
    greet(ring + peers + [(flip(c, 8), flip(f, i)) for i in range(4, N_FS)] + [sibling])
    copies = Copies(send, recv)
    tokens, width = nm_ref.shape
    units = down_ref.shape[0]
    rows = 2 * tokens
    every = N_FS * tokens
    strip = dn_mine.shape[1]
    window = dn_z.shape[0]
    half = units // 2
    side = width // 2
    length = N_CTX * tokens
    scale = HD ** (-0.5)
    near, turn = peers[:3], peers[3]

    def local_copy(src, dst, n):
        copy = pltpu.make_async_copy(src, dst, local.at[n])
        copy.start()
        return copy

    upper, lower = pl.ds(0, tokens // 2), pl.ds(tokens // 2, tokens // 2)
    up_y = [copies.start(nm_ref.at[upper], nm.at[i + 1, upper], near[i]) for i in range(3)]
    low_z = copies.start(nm_ref.at[lower], nm.at[4, lower], turn)
    low_y = [copies.start(nm_ref.at[lower], nm.at[i + 1, lower], near[i]) for i in range(3)]
    up_z = [copies.start(nm_ref.at[upper], nm.at[4, upper], turn)]

    def part_copy(part, i):
        return pltpu.make_async_remote_copy(
            src_ref=part.at[i],
            dst_ref=part_in.at[i],
            send_sem=part_send.at[i],
            recv_sem=part_recv.at[i],
            device_id=(c, flip(f, i)),
            device_id_type=MESH,
        )

    def x_of(device):
        return lax.rem(lax.div(device[0], 2), 4)

    def strip_of(ref, x):
        return ref.at[:, pl.ds(pl.multiple_of(x * strip, strip), strip)]

    def owner_rows(ref, owner):
        return ref.at[pl.ds(pl.multiple_of(owner * 192, 192), 192)]

    low_y += [
        copies.make(nm.at[4, lower], nm.at[4 + i, lower], near[i - 1]) for i in range(1, 4)
    ]
    up_z += [copies.make(nm.at[i, upper], nm.at[4 + i, upper], turn) for i in range(1, 4)]
    x_gu = [
        copies.make(gu_in.at[:, x_of(device)], gu_x.at[i], device)
        for i, device in enumerate(along)
    ]
    x_dn = [
        copies.make(strip_of(dn_in, x_of(device)), dn_x.at[i], device)
        for i, device in enumerate(along)
    ]
    o_sends = [
        copies.make(owner_rows(o_in, peer[1]), o_far.at[i], peer) for i, peer in enumerate(cross)
    ]
    q_sends = [
        copies.make(owner_rows(q_in, peer[1]), q_far.at[i], peer) for i, peer in enumerate(cross)
    ]
    kv_sends = [
        copies.make(kv_in.at[lax.div(device[0], 2)], kv_far.at[i], device)
        for i, device in enumerate(ring)
    ]

    def begin(group):
        for copy in group:
            copy.start()

    def feed_forward(cot, gu, down, act, gate_low, up_low, part, outs):
        loads = [
            local_copy(nm_ref, nm.at[0], 0),
            local_copy(gu_ref, gu, 1),
            local_copy(cot_ref, cot, 2),
            local_copy(down_ref, down, 3),
        ]
        for load in loads:
            load.wait()

        def weight(which):
            return gu[which].reshape(width, units)

        saves = []

        def pair(s):
            at = s * rows
            span = slice(at, at + rows)
            x = nm[2 * s : 2 * s + 2].reshape(rows, width)
            gate = jnp.dot(x, weight(0), preferred_element_type=F32)
            up = jnp.dot(x, weight(1), preferred_element_type=F32)
            grad = contract_cols(cot[2 * s : 2 * s + 2].reshape(rows, width), down[...])
            sigma = jax.nn.sigmoid(gate)
            swish = gate * sigma
            act[span, :] = (swish * up).astype(BF)
            gate_low[span, :] = (grad * up * sigma * (1.0 + gate * (1.0 - sigma))).astype(BF)
            up_low[span, :] = (grad * swish).astype(BF)
            summed = contract_cols(gate_low[span, :], weight(0))
            summed = summed + contract_cols(up_low[span, :], weight(1))
            part[2 * s : 2 * s + 2] = summed.astype(BF).reshape(2, tokens, width)
            for i in (2 * s, 2 * s + 1):
                if i:
                    part_copy(part, i).start()
            if s > 1:
                saves[s - 2].wait()
            result = jnp.dot(act[span, :], down[...], preferred_element_type=F32)
            outs[s % 2] = result.astype(BF).reshape(2, tokens, width)
            saves.append(local_copy(outs.at[s % 2], out_ref.at[pl.ds(2 * s, 2)], 4 + s % 2))

        def arrived(i):
            up_y[i - 1].wait_recv()
            up_z[i].start()
            low_y[i - 1].wait_recv()

        arrived(1)
        pair(0)
        low_z.wait_recv()
        begin(low_y[3:])
        arrived(2)
        arrived(3)
        pair(1)
        up_z[0].wait_recv()
        up_z[1].wait_recv()
        low_y[3].wait_recv()
        pair(2)
        for i in (2, 3):
            up_z[i].wait_recv()
            low_y[2 + i].wait_recv()
        pair(3)

        def gate_up(m, carry):
            at = pl.multiple_of(m * 384, 384)
            x = nm[:, :, pl.ds(at, 384)].reshape(every, 384)
            for which, low in enumerate((gate_low, up_low)):
                grad = contract_rows(x, low[...]).astype(BF)
                gu[which, pl.ds(2 * m, 2)] = grad.reshape((2,) + gu.shape[2:])
            return carry

        lax.fori_loop(0, width // 384, gate_up, 0)
        swap_gu = copies.start(gu.at[1 - core], gu_in, sibling)
        turned = cot[...].reshape(every, width)

        def down_rows(m, carry):
            at = pl.multiple_of(m * 256, 256)
            down[pl.ds(at, 256), :] = contract_rows(act[:, pl.ds(at, 256)], turned).astype(BF)
            return carry

        whole = units // 256
        lax.fori_loop(0, whole, down_rows, 0)
        if units % 256:
            down[whole * 256 :, :] = contract_rows(act[:, whole * 256 :], turned).astype(BF)
        swap_dn = copies.start(
            down.at[pl.ds(pl.multiple_of((1 - core) * half, 16), half)], dn_in, sibling
        )
        swap_gu.wait_recv()

        def add_gu(g, carry):
            gu_in[g] = (gu[core, g].astype(F32) + gu_in[g].astype(F32)).astype(BF)
            return carry

        lax.fori_loop(0, N_FS, add_gu, 0)
        begin(x_gu)
        swap_dn.wait_recv()

        def add_dn(m, carry):
            at = pl.multiple_of(m * 112, 16)
            own = down[pl.ds(pl.multiple_of(core * half + m * 112, 16), 112), :]
            dn_in[pl.ds(at, 112), :] = (
                own.astype(F32) + dn_in[pl.ds(at, 112), :].astype(F32)
            ).astype(BF)
            return carry

        lax.fori_loop(0, half // 112, add_dn, 0)
        begin(x_dn)
        total = part[0].astype(F32)
        for i in range(1, N_FS):
            part_copy(part, i).wait_recv()
            total = total + part_in[i].astype(F32)
        mid_ref[...] = total
        for i in range(1, N_FS):
            part_copy(part, i).wait_send()
        for copy in [swap_gu, swap_dn]:
            copy.wait_send()
        for copy in saves[2:]:
            copy.wait()

    pl.run_scoped(
        feed_forward,
        pltpu.VMEM(cot_ref.shape, BF),
        pltpu.VMEM(gu_ref.shape, BF),
        pltpu.VMEM(down_ref.shape, BF),
        pltpu.VMEM((every, units), BF),
        pltpu.VMEM((every, units), BF),
        pltpu.VMEM((every, units), BF),
        pltpu.VMEM((N_FS, tokens, width), BF),
        pltpu.VMEM((2, 2, tokens, width), BF),
    )
    out_sends = [
        copies.start(out_ref.at[i + 1], out_in.at[i], peer) for i, peer in enumerate(peers)
    ]

    def columns_of(which):
        return pl.ds(pl.multiple_of(which * side, side), side)

    def half_product(left, right, which, out):
        def step(m, carry):
            at = pl.multiple_of(m * 256, 256)
            out[pl.ds(at, 256), :] = contract_rows(
                left[:, pl.ds(at, 256)], right[:, columns_of(which)]
            ).astype(BF)
            return carry

        lax.fori_loop(0, width // 256, step, 0)

    def add_product(left, right, out):
        def step(m, carry):
            at = pl.multiple_of(m * 256, 256)
            product = contract_rows(left[:, pl.ds(at, 256)], right[:, columns_of(core)])
            out[pl.ds(at, 256), :] = (product + out[pl.ds(at, 256), :].astype(F32)).astype(BF)
            return carry

        lax.fori_loop(0, width // 256, step, 0)

    def attention(branch, back, attended, normed, out_half, dkv):
        load_at = local_copy(attended_hbm, attended, 0)
        load_nm = local_copy(normed_hbm, normed, 1)

        def second_norm(full_o, middle_ref):
            load_mid = local_copy(middle_hbm, middle_ref, 2)
            load_o = local_copy(o_hbm, full_o, 3)
            load_mid.wait()
            middle = middle_ref[...]
            scale_two = lax.rsqrt(jnp.mean(middle * middle, axis=-1, keepdims=True) + EPSILON)
            norm = middle * scale_two
            grad = mid_ref[...]
            gain_grad[...] = jnp.sum(grad * norm, axis=0, keepdims=True)
            scaled = grad * gain_ref[...]
            cot_copy = local_copy(cot_ref.at[0], back, 6)
            cot_copy.wait()
            mid = back[...].astype(F32) + scale_two * (
                scaled - norm * jnp.mean(scaled * norm, axis=-1, keepdims=True)
            )
            mid_ref[...] = mid
            branch[...] = mid.astype(BF)
            load_o.wait()
            back[...] = contract_cols(branch[...], full_o[...]).astype(BF)

        pl.run_scoped(second_norm, pltpu.VMEM(o_hbm.shape, BF), pltpu.VMEM((tokens, width), F32))
        load_at.wait()
        load_nm.wait()
        half_product(attended, branch, 1 - core, out_half)
        swap_o = copies.start(out_half, o_in, sibling)

        def heads(expo, kv, query_ref, mixed_ref):
            loads = [
                local_copy(kv_hbm, kv, 2),
                local_copy(query_hbm, query_ref, 3),
                local_copy(mixed_hbm, mixed_ref, 4),
                local_copy(expo_hbm, expo, 5),
            ]
            for load in loads:
                load.wait()
            for h in range(KV_HEADS):
                query = query_ref[h]
                head = back[:, h * GROUP * HD : (h + 1) * GROUP * HD]
                grads = jnp.concatenate(
                    [head[:, i * HD : (i + 1) * HD] for i in range(GROUP)], axis=0
                )
                inverse = inv_ref[h, 0:1, :]
                turned = grads.astype(F32).T
                weighted = jnp.sum(turned * mixed_ref[h], axis=0, keepdims=True)
                factor = inverse * scale
                offset = weighted * factor
                grads_scaled = (turned * inverse).T.astype(BF)
                dq = jnp.zeros((HD, GROUP * tokens), F32)
                for j in range(length // CHUNK):
                    part = expo[h, j * CHUNK : (j + 1) * CHUNK, :]
                    cols = slice(h * HD, (h + 1) * HD)
                    keys = kv[2 * j : 2 * j + 2, :tokens, cols].reshape(CHUNK, HD)
                    v_cols = slice((KV_HEADS + h) * HD, (KV_HEADS + h + 1) * HD)
                    values = kv[2 * j : 2 * j + 2, :tokens, v_cols].reshape(CHUNK, HD)
                    prob_grad = contract_cols(values, grads)
                    score_grad = (part.astype(F32) * (prob_grad * factor - offset)).astype(BF)
                    dk = jnp.dot(score_grad, query, preferred_element_type=F32).astype(BF)
                    dv = jnp.dot(part, grads_scaled, preferred_element_type=F32).astype(BF)
                    for side_core in range(2):
                        cut = slice(side_core * tokens, (side_core + 1) * tokens)
                        dkv[side_core, j, :, cols] = dk[cut]
                        dkv[side_core, j, :, v_cols] = dv[cut]
                    dq = dq + contract_rows(keys, score_grad)
                for i in range(GROUP):
                    at = (h * GROUP + i) * HD
                    q_grad[:, at : at + HD] = turn_back(
                        dq[:, i * tokens : (i + 1) * tokens].T, cos_ref[...], sin_ref[...]
                    ).astype(BF)

        pl.run_scoped(
            heads,
            pltpu.VMEM(expo_hbm.shape, BF),
            pltpu.VMEM(kv_hbm.shape, BF),
            pltpu.VMEM(query_hbm.shape, BF),
            pltpu.VMEM(mixed_hbm.shape, F32),
        )
        swap_kv = copies.start(dkv.at[1 - core], kv_in, sibling)

        swap_o.wait_recv()
        add_product(attended, branch, o_in)
        begin(o_sends)

        swap_kv.wait_recv()
        kv_in[...] = (dkv[core].astype(F32) + kv_in[...].astype(F32)).astype(BF)
        begin(kv_sends)

        swap_o.wait_send()
        half_product(normed, q_grad, 1 - core, out_half)
        swap_q = copies.start(out_half, q_in, sibling)
        swap_q.wait_recv()
        add_product(normed, q_grad, q_in)
        begin(q_sends)
        swap_kv.wait_send()
        swap_q.wait_send()

    pl.run_scoped(
        attention,
        pltpu.VMEM((tokens, width), BF),
        pltpu.VMEM((tokens, width), BF),
        pltpu.VMEM((tokens, width), BF),
        pltpu.VMEM((tokens, width), BF),
        pltpu.VMEM((width, side), BF),
        pltpu.VMEM((2, N_CTX // 2, tokens, kv_in.shape[2]), BF),
    )

    def sums(gu_buf, dn_buf, far_buf, kv_buf):
        for copy in x_gu:
            copy.wait_recv()
        local_copy(gu_x, gu_buf, 0).wait()

        def sum_gu_x(g, carry):
            total = gu_in[g, x_at].astype(F32)
            for i in range(3):
                total = total + gu_buf[i, g].astype(F32)
            gu_buf[0, g] = total.astype(BF)
            return carry

        lax.fori_loop(0, N_FS, sum_gu_x, 0)
        count = N_FS // 2
        z_gu = copies.start(
            gu_buf.at[0, pl.ds(pl.multiple_of((1 - z_at) * count, count), count)], gu_z, partner
        )
        for copy in x_dn:
            copy.wait_recv()
        local_copy(dn_x, dn_buf, 1).wait()
        total = dn_in[:, pl.ds(pl.multiple_of(x_at * strip, strip), strip)].astype(F32)
        for i in range(3):
            total = total + dn_buf[i].astype(F32)
        dn_mine[...] = total.astype(BF)

        def window_of(z):
            return pl.ds(pl.multiple_of(z * (half - window), 16), window)

        z_dn = copies.start(dn_mine.at[window_of(1 - z_at)], dn_z, partner)
        for copy in kv_sends:
            copy.wait_recv()
        local_copy(kv_far, kv_buf, 2).wait()
        total = kv_in[pair_at].astype(F32)
        for i in range(N_CTX // 2 - 1):
            total = total + kv_buf[i].astype(F32)
        own_kv[...] = total
        for ref, sends, far, out in ((o_in, o_sends, o_far, o_red), (q_in, q_sends, q_far, q_red)):
            for copy in sends:
                copy.wait_recv()
            local_copy(far, far_buf, 3).wait()
            total = ref[pl.ds(pl.multiple_of(f * 192, 192), 192), :].astype(F32)
            for i in range(N_FS - 1):
                total = total + far_buf[i].astype(F32)
            out[...] = total.astype(BF)
        z_dn.wait_recv()
        done_dn[...] = (dn_mine[window_of(z_at), :].astype(F32) + dn_z[...].astype(F32)).astype(BF)
        z_gu.wait_recv()

        def add_gu_z(j, carry):
            mine = gu_buf[0, z_at * count + j].astype(F32)
            done_gu[j] = (mine + gu_z[j].astype(F32)).astype(BF)
            return carry

        lax.fori_loop(0, count, add_gu_z, 0)
        z_gu.wait_send()
        z_dn.wait_send()

    pl.run_scoped(
        sums,
        pltpu.VMEM(gu_x.shape, BF),
        pltpu.VMEM(dn_x.shape, BF),
        pltpu.VMEM(o_far.shape, BF),
        pltpu.VMEM(kv_far.shape, BF),
    )
    for copy in out_sends:
        copy.wait_recv()
    for copy in (
        up_y + [low_z] + low_y + up_z + x_gu + x_dn + out_sends + o_sends + q_sends + kv_sends
    ):
        copy.wait_send()


def backward(cid, arrays, vmem_arrays):
    normed, cot_all, columns, down_weight, expo, kv_all, full_o = arrays[:7]
    tokens, width = normed.shape
    units = down_weight.shape[0]
    piece = columns.shape[3]
    half = units // 2
    strip = width // 4
    window = half // 2 + 8
    side = width // 2
    kv_width = KV_HEADS * HD
    rows = width // N_FS
    anywhere = pl.BlockSpec(memory_space=pl.ANY)
    vmem = pl.BlockSpec(memory_space=pltpu.VMEM)
    in_place = [
        ((N_FS, tokens, width), BF),
        ((N_FS - 1, tokens, width), BF),
        ((3, N_FS, piece, units), BF),
        ((3, half, strip), BF),
        ((N_FS - 1, rows, side), BF),
        ((N_FS - 1, rows, side), BF),
        ((N_CTX // 2 - 1, tokens, 2 * kv_width), BF),
    ]
    in_vmem = [
        ((N_FS // 2, piece, units), BF),
        ((window, strip), BF),
        ((tokens, 2 * kv_width), F32),
        ((rows, side), BF),
        ((rows, side), BF),
        ((tokens, width), BF),
        ((tokens, width), F32),
        ((1, width), F32),
    ]
    results = pl.pallas_call(
        back_kernel,
        name="back",
        out_shape=[jax.ShapeDtypeStruct(*o) for o in in_place + in_vmem],
        in_specs=[anywhere] * len(arrays) + [vmem] * len(vmem_arrays),
        out_specs=[anywhere] * len(in_place) + [vmem] * len(in_vmem),
        scratch_shapes=[
            pltpu.VMEM((N_FS, tokens, width), BF),
            pltpu.VMEM((N_FS, tokens, width), BF),
            pltpu.VMEM((N_FS, 4, piece, units), BF),
            pltpu.VMEM((half, width), BF),
            pltpu.VMEM((N_FS // 2, piece, units), BF),
            pltpu.VMEM((half, strip), BF),
            pltpu.VMEM((window, strip), BF),
            pltpu.VMEM((N_CTX // 2, tokens, 2 * kv_width), BF),
            pltpu.VMEM((width, side), BF),
            pltpu.VMEM((width, side), BF),
            pltpu.SemaphoreType.DMA((N_FS,)),
            pltpu.SemaphoreType.DMA((N_FS,)),
            pltpu.SemaphoreType.DMA((60,)),
            pltpu.SemaphoreType.DMA((60,)),
            pltpu.SemaphoreType.DMA((8,)),
        ],
        compiler_params=pltpu.CompilerParams(
            collective_id=cid, has_side_effects=True, vmem_limit_bytes=62 * 2**20
        ),
    )(*arrays, *vmem_arrays)
    return results[:2] + results[7:]


def last_kernel(
    done_gu,
    done_dn,
    parts,
    parts_far,
    qkv_hbm,
    own_kv,
    q_grad,
    o_red,
    q_red,
    normed_ref,
    input_ref,
    gain_ref,
    mid_ref,
    middle_ref,
    gain_two_grad,
    cos_ref,
    sin_ref,
    all_gu,
    all_dn,
    all_at,
    vec_sum,
    out_rows,
    in_rows,
    full_qkv,
    proj,
    own_gu,
    kv_out,
    kv_keep,
    kv_in,
    kv_far,
    at_all,
    at_far,
    at_own,
    vec,
    vec_fs,
    vec_mid,
    vec_ctx,
    out_in,
    own_send,
    own_recv,
    send,
    recv,
    local,
):
    c, f = lax.axis_index("ctx"), lax.axis_index("fsdp")
    core, pair = lax.rem(c, 2), lax.div(c, 2)
    x_at, z_at = lax.rem(pair, 4), lax.div(pair, 4)
    sibling = (flip(c, 1), f)
    partner = (flip(c, 8), f)
    along = [(flip(c, 2 * i), f) for i in range(1, 4)]
    ring = [(flip(c, 2 * i), f) for i in range(1, N_CTX // 2)]
    peers = [(c, flip(f, i)) for i in range(1, N_FS)]
    cross = cross_peers(c, f)
    greet(ring + peers + [(flip(c, 8), flip(f, i)) for i in range(4, N_FS)] + [sibling])
    copies = Copies(send, recv)
    tokens, width = normed_ref.shape
    kv_width = KV_HEADS * HD
    strip = done_dn.shape[1]
    at_rows, at_cols = at_own.shape
    rest, own = [], []

    def local_copy(src, dst, n):
        copy = pltpu.make_async_copy(src, dst, local.at[n])
        copy.start()
        own.append(copy)
        return copy

    def x_of(device):
        return lax.rem(lax.div(device[0], 2), 4)

    def z_of(device):
        return lax.div(device[0], 8)

    def gu_place(device, part=None):
        count = N_FS // 2 if part is None else N_FS // 4
        start = N_FS // 2 * z_of(device) + (0 if part is None else part * count)
        return all_gu.at[lax.rem(device[0], 2), x_of(device), pl.ds(start, count)]

    def dn_place(device, part=None):
        columns = pl.ds(pl.multiple_of(x_of(device) * strip, strip), strip)
        count = done_dn.shape[0] // (1 if part is None else 2)
        span = pl.ds(0 if part is None else part * count, count)
        return all_dn.at[lax.rem(device[0], 2), z_of(device), span, columns]

    def at_piece(ref, device):
        return ref.at[
            pl.ds(pl.multiple_of(x_of(device) * at_rows, at_rows), at_rows),
            pl.ds(pl.multiple_of(z_of(device) * at_cols, at_cols), at_cols),
        ]

    def at_place(device):
        return at_piece(all_at.at[lax.rem(device[0], 2)], device)

    here = (c, f)
    far = (partner[0], f)
    plane, spot = lax.div(f, 4), lax.rem(f, 4)
    owners = [
        (8 * plane + lax.rem(c, 8), 4 * z_at + lax.rem(flip(f, i), 4)) for i in range(4)
    ]

    def gu_copy(i):
        return pltpu.make_async_remote_copy(
            src_ref=done_gu.at[lax.rem(flip(f, i), 4)],
            dst_ref=own_gu.at[spot],
            send_sem=own_send.at[i],
            recv_sem=own_recv.at[i],
            device_id=owners[i],
            device_id_type=MESH,
        )

    gu_own = pltpu.make_async_copy(done_gu.at[spot], own_gu.at[spot], local.at[0])

    @pl.when(plane == z_at)
    def _():
        gu_own.start()

    @pl.when(plane != z_at)
    def _():
        gu_copy(0).start()

    for i in range(1, 4):
        gu_copy(i).start()
    x_one, x_two, x_three = along
    local_copy(done_dn, dn_place(here), 1)
    dn_z = copies.start(done_dn, dn_place(here), partner)
    dn_x = [copies.start(done_dn, dn_place(here), device) for device in (x_one, x_three)]
    rest.append(copies.start(done_dn, dn_place(here), sibling))
    load_qkv = local_copy(qkv_hbm, full_qkv, 2)

    for h in range(KV_HEADS):
        at = width + h * HD
        proj[:, at : at + HD] = turn_back(
            own_kv[:, h * HD : (h + 1) * HD], cos_ref[...], sin_ref[...]
        ).astype(BF)
    proj[:, width + kv_width :] = own_kv[:, kv_width:].astype(BF)
    proj[:, :width] = q_grad[...]

    def side_of(which):
        return pl.ds(pl.multiple_of(width + which * kv_width, kv_width), kv_width)

    kv_out[...] = contract_rows(normed_ref[...], proj[:, side_of(1 - core)]).astype(BF)
    swap_kv = copies.start(kv_out, kv_in, sibling)
    kv_keep[...] = contract_rows(normed_ref[...], proj[:, side_of(core)]).astype(BF)

    @pl.when(plane == z_at)
    def _():
        gu_own.wait()

    @pl.when(plane != z_at)
    def _():
        gu_copy(0).wait()

    for i in range(1, 4):
        gu_copy(i).wait()
    gu_z = copies.start(own_gu, gu_place(here), partner)
    gu_x = [copies.start(own_gu, gu_place(here), device) for device in (x_one, x_three)]
    rest.append(copies.start(own_gu, gu_place(here), sibling))
    local_copy(own_gu, gu_place(here), 3)

    swap_kv.wait_recv()
    kv_in[...] = (kv_in[...].astype(F32) + kv_keep[...].astype(F32)).astype(BF)

    def owner_rows(owner):
        return pl.ds(pl.multiple_of(owner * 192, 192), 192)

    kv_sends = [
        copies.start(kv_in.at[owner_rows(peer[1])], kv_far.at[i], peer)
        for i, peer in enumerate(cross)
    ]
    out_own = local_copy(parts.at[0], out_in.at[N_FS - 1], 4)
    out_far = local_copy(parts_far, out_in.at[pl.ds(0, N_FS - 1)], 6)

    load_qkv.wait()
    in_norm_grad = contract_cols(proj[...], full_qkv[...])
    inputs = input_ref[...].astype(F32)
    scale_one = lax.rsqrt(jnp.mean(inputs * inputs, axis=-1, keepdims=True) + EPSILON)
    norm = inputs * scale_one
    gain_one_grad = jnp.sum(in_norm_grad * norm, axis=0, keepdims=True)
    scaled = in_norm_grad * gain_ref[...]
    in_rows[...] = mid_ref[...] + scale_one * (
        scaled - norm * jnp.mean(scaled * norm, axis=-1, keepdims=True)
    )
    bias_grad = jnp.sum(proj[...].astype(F32), axis=0, keepdims=True)
    row = 0
    for vector in (gain_one_grad, gain_two_grad[...], bias_grad):
        for n in range(vector.shape[1] // 128):
            vec[row : row + 1, :] = vector[:, n * 128 : (n + 1) * 128]
            row += 1
    vec_sends = [copies.start(vec, vec_fs.at[i], peer) for i, peer in enumerate(peers)]

    dn_z.wait_recv()
    dn_x2 = [copies.start(dn_place(far), dn_place(far), device) for device in (x_one, x_three)]
    rest.append(copies.start(dn_place(far), dn_place(far), sibling))
    gu_z.wait_recv()
    gu_x2 = [copies.start(gu_place(far), gu_place(far), device) for device in (x_one, x_three)]
    rest.append(copies.start(gu_place(far), gu_place(far), sibling))

    def around(place, one, three, z):
        forwards = []
        for copy, device, part, other in ((one, x_one, 0, x_three), (three, x_three, 1, x_one)):
            at = (flip(device[0], 8), f) if z else device
            copy.wait_recv()
            forwards.append(copies.start(place(at, part), place(at, part), other))
            rest.append(copies.start(place(at), place(at), sibling))
        return forwards

    def opposite(place, forwards, z):
        at = (flip(x_two[0], 8), f) if z else x_two
        for copy in forwards:
            copy.wait_recv()
        rest.append(copies.start(place(at), place(at), sibling))

    for copy in kv_sends:
        copy.wait_recv()
    total = kv_in[owner_rows(f), :].astype(F32)
    for i in range(N_FS - 1):
        total = total + kv_far[i].astype(F32)
    side = width // 2
    at_all[:, :side] = o_red[...]
    at_all[:, side : 2 * side] = q_red[...]
    at_all[:, 2 * side :] = total.astype(BF)
    at_sends = [
        copies.start(at_piece(at_all, device), at_far.at[i], device)
        for i, device in enumerate(ring)
    ]
    for copy in vec_sends:
        copy.wait_recv()
    total = vec[...]
    for i in range(N_FS - 1):
        total = total + vec_fs[i]
    vec_mid[...] = total
    vec_near = [copies.start(vec_mid, vec_ctx.at[c], device) for device in ring]
    rest.append(copies.start(vec_mid, vec_ctx.at[c], sibling))
    vec_ctx[pl.ds(c, 1)] = total[None]

    dn_f = around(dn_place, *dn_x, False)
    gu_f = around(gu_place, *gu_x, False)
    for copy in at_sends:
        copy.wait_recv()
    total = at_all[
        pl.ds(pl.multiple_of(x_at * at_rows, at_rows), at_rows),
        pl.ds(pl.multiple_of(z_at * at_cols, at_cols), at_cols),
    ].astype(F32)
    for i in range(N_CTX // 2 - 1):
        total = total + at_far[i].astype(F32)
    at_own[...] = total.astype(BF)
    at_near = [copies.start(at_own, at_place(here), device) for device in ring]
    rest.append(copies.start(at_own, at_place(here), sibling))
    local_copy(at_own, at_place(here), 5)

    for copy, device in zip(vec_near, ring):
        copy.wait_recv()
        place = vec_ctx.at[device[0]]
        rest.append(copies.start(place, place, sibling))
    dn_f2 = around(dn_place, *dn_x2, True)
    gu_f2 = around(gu_place, *gu_x2, True)
    opposite(dn_place, dn_f, False)
    opposite(gu_place, gu_f, False)
    out_far.wait()
    out_own.wait()
    total = middle_ref[...]
    for i in range(N_FS):
        total = total + out_in[i].astype(F32)
    out_rows[...] = total.astype(BF)
    for copy, device in zip(at_near, ring):
        copy.wait_recv()
        rest.append(copies.start(at_place(device), at_place(device), sibling))
    opposite(dn_place, dn_f2, True)
    opposite(gu_place, gu_f2, True)
    for copy in (
        [dn_z] + dn_x + dn_x2 + dn_f + dn_f2 + [gu_z] + gu_x + gu_x2 + gu_f + gu_f2
        + [swap_kv] + kv_sends + vec_sends + vec_near + at_sends + at_near
    ):
        copy.wait_send()
    for copy in rest:
        copy.wait()
    total = vec_ctx[0]
    for i in range(1, N_CTX):
        total = total + vec_ctx[i]
    vec_sum[...] = total
    for copy in own:
        if not any(copy is done for done in (load_qkv, out_own, out_far)):
            copy.wait()


def last_exchange(cid, arrays, vmem_arrays):
    done_gu, done_dn, parts, parts_far, full_qkv = arrays
    tokens, width = parts.shape[1:]
    piece, units = done_gu.shape[1:]
    window, strip = done_dn.shape
    rows = width // N_FS
    kv_width = KV_HEADS * HD
    at_width = width + kv_width
    anywhere = pl.BlockSpec(memory_space=pl.ANY)
    vmem = pl.BlockSpec(memory_space=pltpu.VMEM)
    outs = [
        jax.ShapeDtypeStruct((2, 4, N_FS, piece, units), BF),
        jax.ShapeDtypeStruct((2, 2, window, width), BF),
        jax.ShapeDtypeStruct((2, rows, at_width), BF),
        jax.ShapeDtypeStruct((40, 128), F32),
        jax.ShapeDtypeStruct((tokens, width), BF),
        jax.ShapeDtypeStruct((tokens, width), F32),
    ]
    return pl.pallas_call(
        last_kernel,
        name="last_exchange",
        out_shape=outs,
        in_specs=[anywhere] * len(arrays) + [vmem] * len(vmem_arrays),
        out_specs=[anywhere] * 3 + [vmem] * 3,
        scratch_shapes=[
            pltpu.VMEM(full_qkv.shape, BF),
            pltpu.VMEM((tokens, width + 2 * kv_width), BF),
            pltpu.VMEM((N_FS // 2, piece, units), BF),
            pltpu.VMEM((width, kv_width), BF),
            pltpu.VMEM((width, kv_width), BF),
            pltpu.VMEM((width, kv_width), BF),
            pltpu.VMEM((N_FS - 1, rows, kv_width), BF),
            pltpu.VMEM((rows, at_width), BF),
            pltpu.VMEM((N_CTX // 2 - 1, rows // 4, at_width // 2), BF),
            pltpu.VMEM((rows // 4, at_width // 2), BF),
            pltpu.VMEM((40, 128), F32),
            pltpu.VMEM((N_FS - 1, 40, 128), F32),
            pltpu.VMEM((40, 128), F32),
            pltpu.VMEM((N_CTX, 40, 128), F32),
            pltpu.VMEM((N_FS, tokens, width), BF),
            pltpu.SemaphoreType.DMA((4,)),
            pltpu.SemaphoreType.DMA((4,)),
            pltpu.SemaphoreType.DMA((100,)),
            pltpu.SemaphoreType.DMA((100,)),
            pltpu.SemaphoreType.DMA((7,)),
        ],
        compiler_params=pltpu.CompilerParams(
            collective_id=cid, has_side_effects=True, vmem_limit_bytes=48 * 2**20
        ),
    )(*arrays, *vmem_arrays)


def wide_kernel(gu_ref, gate_ref, up_ref):
    for which, out in enumerate((gate_ref, up_ref)):
        out[...] = jnp.concatenate(
            [gu_ref[which, 0, source].astype(F32) for source in range(N_FS)], axis=1
        )


def wide_results(all_gu):
    piece, units = all_gu.shape[3:]
    parts = all_gu.shape[1]
    shape = jax.ShapeDtypeStruct((parts * piece, N_FS * units), F32)
    return pl.pallas_call(
        wide_kernel,
        name="wide_results",
        grid=(parts,),
        in_specs=[pl.BlockSpec((2, 1, N_FS, piece, units), lambda p: (0, p, 0, 0, 0))],
        out_specs=[pl.BlockSpec((piece, N_FS * units), lambda p: (p, 0))] * 2,
        out_shape=[shape, shape],
        compiler_params=pltpu.CompilerParams(vmem_limit_bytes=32 * 2**20),
    )(all_gu)


def rest_kernel(dn_ref, at_ref, down_ref, o_ref, q_ref, k_ref, v_ref):
    z = lax.rem(pl.program_id(0), 2)
    rows = down_ref.shape[0]
    block = dn_ref[0, 0].astype(F32)
    down_ref[...] = jnp.where(z == 0, block[:rows], block[8 : 8 + rows])
    side = o_ref.shape[1] // 2
    for n in range(2):
        part = at_ref[n].astype(F32)
        o_ref[:, n * side : (n + 1) * side] = part[:, :side]
        q_ref[:, n * side : (n + 1) * side] = part[:, side : 2 * side]
        (k_ref, v_ref)[n][...] = part[:, 2 * side :]


def rest_results(all_dn, all_at):
    window, width = all_dn.shape[2:]
    rows = window - 8
    own, at_width = all_at.shape[1:]
    kv_width = KV_HEADS * HD
    return pl.pallas_call(
        rest_kernel,
        name="rest_results",
        grid=(4,),
        in_specs=[
            pl.BlockSpec((1, 1, window, width), lambda n: (n // 2, n % 2, 0, 0)),
            pl.BlockSpec((2, own // 4, at_width), lambda n: (0, n, 0)),
        ],
        out_specs=[
            pl.BlockSpec((rows, width), lambda n: (n, 0)),
            pl.BlockSpec((own // 4, width), lambda n: (n, 0)),
            pl.BlockSpec((own // 4, width), lambda n: (n, 0)),
            pl.BlockSpec((own // 4, kv_width), lambda n: (n, 0)),
            pl.BlockSpec((own // 4, kv_width), lambda n: (n, 0)),
        ],
        out_shape=[
            jax.ShapeDtypeStruct((4 * rows, width), F32),
            jax.ShapeDtypeStruct((own, width), F32),
            jax.ShapeDtypeStruct((own, width), F32),
            jax.ShapeDtypeStruct((own, kv_width), F32),
            jax.ShapeDtypeStruct((own, kv_width), F32),
        ],
        compiler_params=pltpu.CompilerParams(vmem_limit_bytes=32 * 2**20),
    )(all_dn, all_at)


def body(
    layer_input,
    segments,
    positions,
    attn_norm,
    q_weight,
    q_bias,
    k_weight,
    k_bias,
    v_weight,
    v_bias,
    o_weight,
    mlp_norm,
    gate_weight,
    up_weight,
    down_weight,
    out_cotangent,
):
    tokens, width = layer_input.shape[1:]
    rows = gate_weight.shape[0]
    units = gate_weight.shape[1] // N_FS
    q_width = HEADS * HD
    kv_width = KV_HEADS * HD
    half_block = tokens // 2
    ctx = lax.axis_index("ctx")
    segment = segments[0]
    cot_low = jnp.where((segment > 0)[:, None], out_cotangent[0], 0)
    small = jnp.stack(
        [
            jnp.pad(v.astype(F32), (0, 256 - v.shape[0]))
            for v in (attn_norm, mlp_norm, q_bias, k_bias, v_bias)
        ]
        + [jnp.zeros((256,), F32)] * 3
    )
    cosine, sine = rope_tables(positions[0], HD)
    cos_wide = jnp.concatenate([cosine, cosine], axis=1)
    sin_wide = jnp.concatenate([sine, -sine], axis=1)
    within = jnp.arange(tokens, dtype=jnp.int32)
    row_place = jnp.where(
        within < half_block,
        ctx * half_block + within,
        (2 * N_CTX - 1 - ctx) * half_block + within - half_block,
    )
    row_info = jnp.stack([row_place.astype(F32), segment.astype(F32)])
    (
        full_qkv,
        full_o,
        kv_all,
        columns,
        cot_all,
        expo,
        gains,
        normed_in,
        query,
        mixed,
        inverse,
        attended,
        middle,
        normed_mid,
    ) = front(
        1,
        (q_weight, k_weight, v_weight, o_weight, gate_weight, up_weight, cot_low),
        (small, layer_input[0], row_info, cos_wide, sin_wide),
    )
    full_qkv = full_qkv.reshape(width, q_width + 2 * kv_width)
    full_o = full_o.reshape(q_width, width)
    gain_one, gain_two = gains[0:1], gains[1:2]

    (
        out_part,
        out_far,
        done_gu,
        done_dn,
        own_kv,
        o_red,
        q_red,
        q_grad,
        mid_grad,
        gain_two_grad,
    ) = backward(
        3,
        (
            normed_mid,
            cot_all,
            columns,
            down_weight,
            expo,
            kv_all,
            full_o,
            middle,
            query,
            mixed,
            attended,
            normed_in,
        ),
        (gain_two, inverse, cos_wide, sin_wide),
    )
    all_gu, all_dn, all_at, all_vec, output_rows, input_rows = last_exchange(
        4,
        (done_gu, done_dn, out_part, out_far, full_qkv),
        (
            own_kv,
            q_grad,
            o_red,
            q_red,
            normed_in,
            layer_input[0],
            gain_one,
            mid_grad,
            middle,
            gain_two_grad,
            cos_wide,
            sin_wide,
        ),
    )
    gate_grad, up_grad = wide_results(all_gu)
    down_grad, o_grad, q_weight_grad, k_grad, v_grad = rest_results(all_dn, all_at)
    flat_vec = all_vec.reshape(-1)
    mine = lax.axis_index("fsdp")
    vectors = []
    start = 0
    for whole in (width, width, q_width, kv_width, kv_width):
        part = whole // N_FS
        vectors.append(lax.dynamic_slice_in_dim(flat_vec, start + mine * part, part, 0))
        start += whole
    return (
        output_rows[None],
        input_rows[None],
        vectors[0],
        q_weight_grad,
        vectors[2],
        k_grad,
        vectors[3],
        v_grad,
        vectors[4],
        o_grad,
        vectors[1],
        gate_grad,
        up_grad,
        down_grad,
    )


def solution(mesh):
    placed = (
        P("fsdp", "ctx", None),
        P("fsdp", "ctx"),
        P("fsdp", "ctx"),
        P("fsdp"),
        P("fsdp", None),
        P("fsdp"),
        P("fsdp", None),
        P("fsdp"),
        P("fsdp", None),
        P("fsdp"),
        P("fsdp", None),
        P("fsdp"),
        P("fsdp", None),
        P("fsdp", None),
        P("fsdp", None),
        P("fsdp", "ctx", None),
    )
    return jax.shard_map(
        body,
        mesh=mesh,
        in_specs=placed,
        out_specs=(
            P("fsdp", "ctx", None),
            P("fsdp", "ctx", None),
            P("fsdp"),
            P("fsdp", None),
            P("fsdp"),
            P("fsdp", None),
            P("fsdp"),
            P("fsdp", None),
            P("fsdp"),
            P("fsdp", None),
            P("fsdp"),
            P("fsdp", None),
            P("fsdp", None),
            P("fsdp", None),
        ),
        check_vma=False,
    )
```

```python
import functools

import jax
import jax.numpy as jnp
from jax import lax
from jax.experimental import pallas as pl
from jax.experimental.pallas import tpu as pltpu
from jax.sharding import PartitionSpec as P

HEADS = 12
KV_HEADS = 2
HD = 128
GROUP = HEADS // KV_HEADS
N_CTX = 16
N_FS = 8
EPSILON = 1e-06
THETA = 1000000.0
MESH = pl.DeviceIdType.MESH
BF = jnp.bfloat16
F32 = jnp.float32


def rope_tables(position, head_dim):
    freqs = THETA ** (-jnp.arange(0, head_dim, 2).astype(F32) / head_dim)
    angles = position.astype(F32)[:, None] * freqs[None, :]
    return (jnp.cos(angles), jnp.sin(angles))


def contract_rows(left, right):
    return lax.dot_general(
        left, right, (((0,), (0,)), ((), ())), preferred_element_type=F32
    )


def contract_cols(left, right):
    return lax.dot_general(
        left, right, (((1,), (1,)), ((), ())), preferred_element_type=F32
    )


def flip(value, mask):
    out = value
    bit = 1
    while bit <= mask:
        if mask & bit:
            out = out + bit * (1 - 2 * lax.rem(lax.div(value, bit), 2))
        bit *= 2
    return out


class Copies:
    def __init__(self, send, recv):
        self.send, self.recv, self.count = send, recv, 0

    def start(self, src, dst, device):
        copy = self.make(src, dst, device)
        copy.start()
        return copy

    def make(self, src, dst, device):
        copy = pltpu.make_async_remote_copy(
            src_ref=src,
            dst_ref=dst,
            send_sem=self.send.at[self.count],
            recv_sem=self.recv.at[self.count],
            device_id=device,
            device_id_type=MESH,
        )
        self.count += 1
        return copy


def greet(devices):
    barrier = pltpu.get_barrier_semaphore()
    for device in devices:
        pl.semaphore_signal(barrier, inc=1, device_id=device, device_id_type=MESH)
    pl.semaphore_wait(barrier, len(devices))


class SharedRows:
    def __init__(self, copies, ref, c, f, columns=None):
        core = lax.rem(c, 2)
        self.copies, self.f = copies, f
        self.sibling = (flip(c, 1), f)
        self.over = (c + core * (flip(c, 8) - c), flip(f, 4))
        self.one, self.three = (c, flip(f, 1)), (c, flip(f, 3))
        rows = ref.shape[1] // 2

        def place(owner, part=None):
            if part is None:
                span = pl.ds(pl.multiple_of(core * rows, 16), rows)
            else:
                span = pl.ds(pl.multiple_of(core * rows + part * (rows // 2), 16), rows // 2)
            if columns is None:
                return ref.at[owner, span]
            return ref.at[owner, span, columns]

        self.place = place
        mine = place(f)
        self.from_one = copies.start(mine, mine, self.one)
        self.from_three = copies.start(mine, mine, self.three)
        self.z_copies = [copies.start(mine, mine, self.over)]
        self.sent = [self.from_one, self.from_three]
        self.rest = []

    def send(self, here, device):
        return self.copies.start(here, here, device)

    def pass_y(self):
        one, three = flip(self.f, 1), flip(self.f, 3)
        self.from_one.wait_recv()
        self.far = [self.send(self.place(one, 0), self.three)]
        self.z_copies.append(self.send(self.place(one), self.over))
        self.from_three.wait_recv()
        self.far.append(self.send(self.place(three, 1), self.one))
        self.z_copies.append(self.send(self.place(three), self.over))
        self.rest.append(self.send(self.place(one), self.sibling))
        self.rest.append(self.send(self.place(three), self.sibling))
        for copy in self.far:
            copy.wait_recv()
        two = self.place(flip(self.f, 2))
        self.z_copies.append(self.send(two, self.over))
        self.rest.append(self.send(two, self.sibling))

    def pass_z(self):
        for copy, mask in zip(self.z_copies, (4, 5, 7, 6)):
            copy.wait_recv()
            self.rest.append(self.send(self.place(flip(self.f, mask)), self.sibling))

    def wait(self):
        for copy in self.rest:
            copy.wait_recv()

    def finish(self):
        for copy in self.sent + self.far + self.z_copies + self.rest:
            copy.wait_send()


CHUNK = 256


def turn_back(grad, cos_wide, sin_wide):
    half = grad.shape[1] // 2
    swapped = jnp.concatenate([grad[:, half:], grad[:, :half]], axis=1)
    return grad * cos_wide + swapped * sin_wide


def front_kernel(
    q_hbm,
    k_hbm,
    v_hbm,
    o_hbm,
    gate_hbm,
    up_hbm,
    small_ref,
    input_ref,
    out_cot_ref,
    row_ref,
    cos_ref,
    sin_ref,
    w_out,
    o_out,
    kv_out,
    g_out,
    t_out,
    e_out,
    gains_ref,
    normed_ref,
    query_ref,
    mixed_ref,
    inv_ref,
    attended_ref,
    middle_ref,
    normed_mid_ref,
    weights,
    full_o,
    small_all,
    strip,
    stage,
    cot_ref,
    kv_own,
    kv,
    s_ref,
    expo,
    send,
    recv,
    local,
):
    c, f = lax.axis_index("ctx"), lax.axis_index("fsdp")
    core = lax.rem(c, 2)
    sibling = (flip(c, 1), f)
    here = (c, f)
    peers = [(c, flip(f, i)) for i in range(1, N_FS)]
    ring = [(flip(c, 2 * i), f) for i in range(1, N_CTX // 2)]
    along = ring[:3]
    near, turn = peers[:3], peers[3]
    greet(peers + ring + [sibling, (flip(c, 8), flip(f, 4))])
    copies = Copies(send, recv)
    tokens, width = input_ref.shape
    rows = q_hbm.shape[0]
    kv_width = KV_HEADS * HD
    cut, units = stage.shape[1:]
    x_part = lax.rem(c, N_FS)

    def local_copy(src, dst, n):
        copy = pltpu.make_async_copy(src, dst, local.at[n])
        copy.start()
        return copy

    mine = weights.at[f]
    q_columns, kv_columns = pl.ds(0, width), pl.ds(width, 2 * kv_width)
    load_k = local_copy(k_hbm, mine.at[:, pl.ds(width, kv_width)], 1)
    load_v = local_copy(v_hbm, mine.at[:, pl.ds(width + kv_width, kv_width)], 2)
    block_rows = pl.ds(pl.multiple_of(lax.rem(x_part, 4) * cut, cut), cut)
    load_gate = local_copy(gate_hbm.at[block_rows], strip.at[0], 3)
    load_up = local_copy(up_hbm.at[block_rows], strip.at[1], 4)
    load_q = local_copy(q_hbm, mine.at[:, q_columns], 0)
    load_o = local_copy(o_hbm, full_o.at[f], 5)
    small_own = local_copy(small_ref, small_all.at[f], 7)
    small_sends = [copies.start(small_ref, small_all.at[f], peer) for peer in peers]
    load_k.wait()
    load_v.wait()
    share_kv = SharedRows(copies, weights, c, f, kv_columns)

    def columns(device, part=None):
        where = lax.rem(device[0], N_FS)
        if part is None:
            return g_out.at[lax.div(where, 4), :, lax.rem(where, 4)]
        half = N_FS // 2
        return g_out.at[lax.div(where, 4), pl.ds(part * half, half), lax.rem(where, 4)]

    def block(device, source):
        where = lax.rem(device[0], N_FS)
        return g_out.at[lax.div(where, 4), source, lax.rem(where, 4)]

    load_q.wait()
    share_q = SharedRows(copies, weights, c, f, q_columns)
    inputs = input_ref[...].astype(F32)
    norm = inputs * lax.rsqrt(jnp.mean(inputs * inputs, axis=-1, keepdims=True) + EPSILON)
    small_own.wait()
    for copy in small_sends:
        copy.wait_recv()

    marks = [0, rows, 2 * rows, 3 * rows, 3 * rows + kv_width // N_FS, small_ref.shape[1]]
    gain_one, gain_two, bias_q, bias_k, bias_v = (
        jnp.concatenate([small_all[owner, :, lo:hi] for owner in range(N_FS)], axis=1)
        for lo, hi in zip(marks[:-1], marks[1:])
    )
    gains_ref[0:1, :] = gain_one
    gains_ref[1:2, :] = gain_two
    normed_ref[...] = (norm * gain_one).astype(BF)
    keep = jnp.where(row_ref[1:2, :] > 0.5, 1.0, 0.0)
    keep = jnp.broadcast_to(keep, (8, tokens)).T[:, 0:1]
    cot_ref[...] = (out_cot_ref[...].astype(F32) * keep).astype(BF)
    load_t = local_copy(cot_ref, t_out.at[0], 6)

    load_gate.wait()
    load_up.wait()
    which = lax.div(x_part, 4)
    for owner in range(N_FS):
        stage[owner] = strip[which, :, owner * units : (owner + 1) * units]
    share_kv.pass_y()
    block_own = local_copy(stage.at[f], block(here, f), 8)
    blocks = [copies.start(stage.at[peer[1]], block(here, f), peer) for peer in peers]
    share_kv.pass_z()
    share_kv.wait()
    cos_wide = jnp.concatenate([cos_ref[...], cos_ref[...]], axis=1)
    sin_wide = jnp.concatenate([-sin_ref[...], sin_ref[...]], axis=1)
    full = weights[:, :, width:].reshape(width, 2 * kv_width)
    projected = jnp.dot(normed_ref[...], full, preferred_element_type=F32)
    projected = projected + jnp.concatenate([bias_k, bias_v], axis=1)
    for h in range(KV_HEADS):
        cols = slice(h * HD, (h + 1) * HD)
        kv_own[:tokens, cols] = turn_back(projected[:, cols], cos_wide, sin_wide).astype(BF)
    kv_own[:tokens, kv_width:] = projected[:, kv_width:].astype(BF)
    marks = jnp.concatenate([row_ref[1:2, :]] * (2 * KV_HEADS), axis=1)
    kv_own[tokens:, :] = jnp.broadcast_to(marks, (16, 2 * kv_width)).astype(BF)
    keep_kv = local_copy(kv_own, kv.at[c], 9)
    keys = [copies.start(kv_own, kv.at[c], device) for device in ring]
    kv_rest = [copies.start(kv_own, kv.at[c], sibling)]

    block_own.wait()
    for copy in blocks:
        copy.wait_recv()
    x_one, x_two, x_three = along
    from_one = copies.start(columns(here), columns(here), x_one)
    from_three = copies.start(columns(here), columns(here), x_three)
    g_rest = [copies.start(columns(here), columns(here), sibling)]

    share_q.pass_y()
    load_o.wait()
    share_o = SharedRows(copies, full_o, c, f)
    half = tokens // 2
    upper, lower = pl.ds(0, half), pl.ds(half, half)
    low_z = copies.start(cot_ref.at[lower], t_out.at[4, lower], turn)
    up_y = [
        copies.start(cot_ref.at[upper], t_out.at[i + 1, upper], device)
        for i, device in enumerate(near)
    ]
    up_z = [copies.start(cot_ref.at[upper], t_out.at[4, upper], turn)]
    low_y = [
        copies.start(cot_ref.at[lower], t_out.at[i + 1, lower], device)
        for i, device in enumerate(near)
    ]
    for key, device in zip(keys, ring):
        key.wait_recv()
        place = kv.at[device[0]]
        kv_rest.append(copies.start(place, place, sibling))
    share_q.pass_z()
    share_q.wait()

    full = weights[:, :, :width].reshape(width, width)
    projected = jnp.dot(normed_ref[...], full, preferred_element_type=F32) + bias_q
    for n in range(HEADS):
        at = (n % GROUP) * tokens
        query_ref[n // GROUP, at : at + tokens, :] = turn_back(
            projected[:, n * HD : (n + 1) * HD], cos_wide, sin_wide
        ).astype(BF)
    save_w = local_copy(weights, w_out, 0)

    from_one.wait_recv()
    far = [copies.start(columns(x_one, 0), columns(x_one, 0), x_three)]
    from_three.wait_recv()
    far.append(copies.start(columns(x_three, 1), columns(x_three, 1), x_one))
    for device in (x_one, x_three):
        g_rest.append(copies.start(columns(device), columns(device), sibling))
    share_o.pass_y()
    keep_kv.wait()
    for copy in kv_rest:
        copy.wait_recv()
    save_kv = local_copy(kv, kv_out, 1)

    length = N_CTX * tokens
    scale = HD ** (-0.5)
    row_place, row_seg = row_ref[0:1, :], row_ref[1:2, :]
    key_seg = kv[:, tokens : tokens + 16, :HD][:, 0, :].astype(F32).T
    within = lax.broadcasted_iota(jnp.int32, (tokens, tokens), 0)
    saves = []
    for h in range(KV_HEADS):
        query = query_ref[h]
        top = jnp.full((8, GROUP * tokens), -1e30, F32)
        for b in range(N_CTX):
            place = jnp.where(
                within < half, b * half + within, (2 * N_CTX - 1 - b) * half + within - half
            ).astype(F32)
            allowed = (place <= row_place) & (key_seg[:, b : b + 1] == row_seg) & (row_seg > 0.5)
            bias = jnp.where(allowed, 0.0, -1e30).astype(F32)
            scores = contract_cols(kv[b, :tokens, h * HD : (h + 1) * HD], query) * scale
            scores = scores + jnp.concatenate([bias] * GROUP, axis=1)
            s_ref[b * tokens : (b + 1) * tokens, :] = scores
            top = jnp.maximum(top, jnp.max(scores.reshape(tokens // 8, 8, -1), axis=0))
        highest = jnp.maximum(jnp.max(top, axis=0, keepdims=True), -1e29)
        total = jnp.zeros((8, GROUP * tokens), F32)
        mixed = jnp.zeros((HD, GROUP * tokens), F32)
        for j in range(length // CHUNK):
            part = jnp.exp(s_ref[j * CHUNK : (j + 1) * CHUNK, :] - highest)
            total = total + jnp.sum(part.reshape(CHUNK // 8, 8, -1), axis=0)
            low = part.astype(BF)
            expo[h, j * CHUNK : (j + 1) * CHUNK, :] = low
            at = (KV_HEADS + h) * HD
            values = kv[2 * j : 2 * j + 2, :tokens, at : at + HD].reshape(CHUNK, HD)
            mixed = mixed + contract_rows(values, low)
        total = jnp.sum(total, axis=0, keepdims=True)
        inverse = 1.0 / jnp.where(total > 0.5, total, 1.0)
        mixed = mixed * inverse
        mixed_ref[h] = mixed
        inv_ref[h] = jnp.broadcast_to(inverse, (8, GROUP * tokens))
        for i in range(GROUP):
            at = (h * GROUP + i) * HD
            attended_ref[:, at : at + HD] = mixed[:, i * tokens : (i + 1) * tokens].T.astype(BF)
        saves.append(local_copy(expo.at[h], e_out.at[h], 2 + h))
        if h == 0:
            low_z.wait_recv()
            for i, device in enumerate(near):
                low_y.append(copies.start(t_out.at[4, lower], t_out.at[5 + i, lower], device))
            for i, copy in enumerate(up_y):
                copy.wait_recv()
                up_z.append(copies.start(t_out.at[i + 1, upper], t_out.at[5 + i, upper], turn))
            for copy in far:
                copy.wait_recv()
            g_rest.append(copies.start(columns(x_two), columns(x_two), sibling))
            share_o.pass_z()

    share_o.wait()
    product = jnp.dot(
        attended_ref[...], full_o[...].reshape(width, width), preferred_element_type=F32
    )
    middle = input_ref[...].astype(F32) + product
    middle_ref[...] = middle
    scale_two = lax.rsqrt(jnp.mean(middle * middle, axis=-1, keepdims=True) + EPSILON)
    normed_mid_ref[...] = (middle * scale_two * gains_ref[1:2, :]).astype(BF)
    save_o = local_copy(full_o, o_out, 4)
    for copy in low_y + up_z + g_rest:
        copy.wait_recv()
    for share in (share_kv, share_q, share_o):
        share.finish()
    for copy in (
        small_sends + blocks + [from_one, from_three] + far + g_rest + low_y + up_z + up_y
        + [low_z] + keys + kv_rest
    ):
        copy.wait_send()
    for copy in saves + [save_w, save_kv, save_o, load_t]:
        copy.wait()


def front(cid, arrays, vmem_arrays):
    tokens, width = vmem_arrays[1].shape
    rows, all_units = arrays[4].shape
    units = all_units // N_FS
    cut = rows // 4
    kv_width = KV_HEADS * HD
    wide = GROUP * tokens
    length = N_CTX * tokens
    anywhere = pl.BlockSpec(memory_space=pl.ANY)
    vmem = pl.BlockSpec(memory_space=pltpu.VMEM)
    weights = (N_FS, rows, width + 2 * kv_width)
    full_o = (N_FS, rows, width)
    kv = (N_CTX, tokens + 16, 2 * kv_width)
    expo = (KV_HEADS, length, wide)
    return pl.pallas_call(
        front_kernel,
        name="front",
        out_shape=[
            jax.ShapeDtypeStruct(weights, BF),
            jax.ShapeDtypeStruct(full_o, BF),
            jax.ShapeDtypeStruct(kv, BF),
            jax.ShapeDtypeStruct((2, N_FS, 4, cut, units), BF),
            jax.ShapeDtypeStruct((N_FS, tokens, width), BF),
            jax.ShapeDtypeStruct(expo, BF),
            jax.ShapeDtypeStruct((2, width), F32),
            jax.ShapeDtypeStruct((tokens, width), BF),
            jax.ShapeDtypeStruct((KV_HEADS, wide, HD), BF),
            jax.ShapeDtypeStruct((KV_HEADS, HD, wide), F32),
            jax.ShapeDtypeStruct((KV_HEADS, 8, wide), F32),
            jax.ShapeDtypeStruct((tokens, width), BF),
            jax.ShapeDtypeStruct((tokens, width), F32),
            jax.ShapeDtypeStruct((tokens, width), BF),
        ],
        in_specs=[anywhere] * len(arrays) + [vmem] * len(vmem_arrays),
        out_specs=[anywhere] * 6 + [vmem] * 8,
        scratch_shapes=[
            pltpu.VMEM(weights, BF),
            pltpu.VMEM(full_o, BF),
            pltpu.VMEM((N_FS,) + vmem_arrays[0].shape, F32),
            pltpu.VMEM((2, cut, all_units), BF),
            pltpu.VMEM((N_FS, cut, units), BF),
            pltpu.VMEM((tokens, width), BF),
            pltpu.VMEM(kv[1:], BF),
            pltpu.VMEM(kv, BF),
            pltpu.VMEM((length, wide), F32),
            pltpu.VMEM(expo, BF),
            pltpu.SemaphoreType.DMA((104,)),
            pltpu.SemaphoreType.DMA((104,)),
            pltpu.SemaphoreType.DMA((10,)),
        ],
        compiler_params=pltpu.CompilerParams(
            collective_id=cid, has_side_effects=True, vmem_limit_bytes=60 * 2**20
        ),
    )(*arrays, *vmem_arrays)


def back_kernel(
    nm_ref,
    cot_ref,
    gu_ref,
    down_ref,
    expo_hbm,
    kv_hbm,
    o_hbm,
    middle_hbm,
    query_hbm,
    mixed_hbm,
    attended_hbm,
    normed_hbm,
    qkv_hbm,
    gains_ref,
    inv_ref,
    cos_ref,
    sin_ref,
    input_ref,
    all_gu,
    all_dn,
    all_at,
    out_ref,
    out_in,
    gu_x,
    dn_x,
    o_far,
    q_far,
    kv_far,
    vec_sum,
    out_rows,
    in_rows,
    nm,
    part_in,
    gu_in,
    dn_in,
    gu_z,
    dn_mine,
    dn_z,
    kv_in,
    o_in,
    q_in,
    o_over,
    q_over,
    kv_over,
    q_grad,
    mid_ref,
    gain_grad,
    done_gu,
    done_dn,
    own_gu,
    kv_part,
    kv_parts,
    at_far,
    at_own,
    vec,
    vec_fs,
    vec_mid,
    vec_ctx,
    own_send,
    own_recv,
    part_send,
    part_recv,
    send,
    recv,
    local,
):
    c, f = lax.axis_index("ctx"), lax.axis_index("fsdp")
    core, pair_at = lax.rem(c, 2), lax.div(c, 2)
    x_at, z_at = lax.rem(pair_at, 4), lax.div(pair_at, 4)
    sibling = (flip(c, 1), f)
    partner = (flip(c, 8), f)
    ring = [(flip(c, 2 * i), f) for i in range(1, N_CTX // 2)]
    along = ring[:3]
    peers = [(c, flip(f, i)) for i in range(1, N_FS)]
    greet(ring + peers + [(flip(c, 8), flip(f, i)) for i in range(4, N_FS)] + [sibling])
    copies = Copies(send, recv)
    tokens, width = nm_ref.shape
    units = down_ref.shape[0]
    rows = 2 * tokens
    every = N_FS * tokens
    strip = dn_mine.shape[1]
    window = dn_z.shape[0]
    half = units // 2
    side = width // 2
    length = N_CTX * tokens
    scale = HD ** (-0.5)
    near, turn = peers[:3], peers[3]
    cos_wide = jnp.concatenate([cos_ref[...], cos_ref[...]], axis=1)
    sin_wide = jnp.concatenate([sin_ref[...], -sin_ref[...]], axis=1)

    def local_copy(src, dst, n):
        copy = pltpu.make_async_copy(src, dst, local.at[n])
        copy.start()
        return copy

    upper, lower = pl.ds(0, tokens // 2), pl.ds(tokens // 2, tokens // 2)
    up_y = [copies.start(nm_ref.at[upper], nm.at[i + 1, upper], near[i]) for i in range(3)]
    low_z = copies.start(nm_ref.at[lower], nm.at[4, lower], turn)
    low_y = [copies.start(nm_ref.at[lower], nm.at[i + 1, lower], near[i]) for i in range(3)]
    up_z = [copies.start(nm_ref.at[upper], nm.at[4, upper], turn)]

    def part_copy(part, i):
        return pltpu.make_async_remote_copy(
            src_ref=part.at[i],
            dst_ref=part_in.at[i],
            send_sem=part_send.at[i],
            recv_sem=part_recv.at[i],
            device_id=(c, flip(f, i)),
            device_id_type=MESH,
        )

    def x_of(device):
        return lax.rem(lax.div(device[0], 2), 4)

    def strip_of(ref, x):
        return ref.at[:, pl.ds(pl.multiple_of(x * strip, strip), strip)]

    def owner_rows(ref, owner):
        return ref.at[pl.ds(pl.multiple_of(owner * 192, 192), 192)]

    low_y += [
        copies.make(nm.at[4, lower], nm.at[4 + i, lower], near[i - 1]) for i in range(1, 4)
    ]
    up_z += [copies.make(nm.at[i, upper], nm.at[4 + i, upper], turn) for i in range(1, 4)]
    x_gu = [
        copies.make(gu_in.at[:, x_of(device)], gu_x.at[i], device)
        for i, device in enumerate(along)
    ]
    x_dn = [
        copies.make(strip_of(dn_in, x_of(device)), dn_x.at[i], device)
        for i, device in enumerate(along)
    ]
    plane = lax.div(f, 4)
    over = (c + core * (flip(c, 8) - c), flip(f, 4))
    block = 4 * 192

    def plane_rows(which):
        return pl.ds(pl.multiple_of(which * block, block), block)

    o_z = copies.make(o_in.at[plane_rows(1 - plane)], o_over, over)
    q_z = copies.make(q_in.at[plane_rows(1 - plane)], q_over, over)
    o_sends = [
        copies.make(owner_rows(o_in, peer[1]), o_far.at[i], peer) for i, peer in enumerate(near)
    ]
    q_sends = [
        copies.make(owner_rows(q_in, peer[1]), q_far.at[i], peer) for i, peer in enumerate(near)
    ]

    def add_over(ref, came):
        def step(m, carry):
            at = pl.multiple_of(m * 192, 192)
            rows = pl.ds(pl.multiple_of(plane * block + m * 192, 192), 192)
            ref[rows, :] = (ref[rows, :].astype(F32) + came[pl.ds(at, 192), :].astype(F32)).astype(BF)
            return carry

        lax.fori_loop(0, 4, step, 0)
    out_sends = [
        copies.make(out_ref.at[i + 1], out_in.at[i], peer) for i, peer in enumerate(peers)
    ]
    kv_sends = [
        copies.make(kv_in.at[lax.div(device[0], 2)], kv_far.at[i], device)
        for i, device in enumerate(ring)
    ]

    def begin(group):
        for copy in group:
            copy.start()

    def feed_forward(cot, gu, down, act, low, part, outs):
        loads = [
            local_copy(nm_ref, nm.at[0], 0),
            local_copy(gu_ref, gu, 1),
            local_copy(cot_ref, cot, 2),
            local_copy(down_ref, down, 3),
        ]
        for load in loads:
            load.wait()

        def weight(which):
            return gu[which].reshape(width, units)

        saves = []

        def pair(s):
            at = s * rows
            span = slice(at, at + rows)
            x = nm[2 * s : 2 * s + 2].reshape(rows, width)
            gate = jnp.dot(x, weight(0), preferred_element_type=F32)
            up = jnp.dot(x, weight(1), preferred_element_type=F32)
            grad = contract_cols(cot[2 * s : 2 * s + 2].reshape(rows, width), down[...])
            sigma = jax.nn.sigmoid(gate)
            swish = gate * sigma
            act[span, :] = (swish * up).astype(BF)
            low[0, span, :] = (grad * up * sigma * (1.0 + gate * (1.0 - sigma))).astype(BF)
            low[1, span, :] = (grad * swish).astype(BF)
            summed = contract_cols(low[0, span, :], weight(0))
            summed = summed + contract_cols(low[1, span, :], weight(1))
            part[2 * s : 2 * s + 2] = summed.astype(BF).reshape(2, tokens, width)
            for i in (2 * s, 2 * s + 1):
                if i:
                    part_copy(part, i).start()
            if s > 1:
                saves[s - 2].wait()
            result = jnp.dot(act[span, :], down[...], preferred_element_type=F32)
            outs[s % 2] = result.astype(BF).reshape(2, tokens, width)
            saves.append(local_copy(outs.at[s % 2], out_ref.at[pl.ds(2 * s, 2)], 4 + s % 2))

        def arrived(i):
            up_y[i - 1].wait_recv()
            up_z[i].start()
            low_y[i - 1].wait_recv()

        arrived(1)
        pair(0)
        low_z.wait_recv()
        begin(low_y[3:])
        arrived(2)
        arrived(3)
        pair(1)
        up_z[0].wait_recv()
        up_z[1].wait_recv()
        low_y[3].wait_recv()
        pair(2)
        for i in (2, 3):
            up_z[i].wait_recv()
            low_y[2 + i].wait_recv()
        pair(3)

        def gate_up(which):
            def step(m, carry):
                at = pl.multiple_of(m * 384, 384)
                x = nm[:, :, pl.ds(at, 384)].reshape(every, 384)
                grad = contract_rows(x, low[which]).astype(BF)
                gu[which, pl.ds(2 * m, 2)] = grad.reshape((2,) + gu.shape[2:])
                return carry

            lax.fori_loop(0, width // 384, step, 0)

        gate_up(1 - core)
        swap_gu = copies.start(gu.at[1 - core], gu_in, sibling)
        gate_up(core)
        swap_gu.wait_recv()

        def add_gu(g, carry):
            gu_in[g] = (gu[core, g].astype(F32) + gu_in[g].astype(F32)).astype(BF)
            return carry

        lax.fori_loop(0, N_FS, add_gu, 0)
        begin(x_gu)
        turned = cot[...].reshape(every, width)

        def down_rows(m, carry):
            at = pl.multiple_of(m * 256, 256)
            down[pl.ds(at, 256), :] = contract_rows(act[:, pl.ds(at, 256)], turned).astype(BF)
            return carry

        whole = units // 256
        lax.fori_loop(0, whole, down_rows, 0)
        if units % 256:
            down[whole * 256 :, :] = contract_rows(act[:, whole * 256 :], turned).astype(BF)
        swap_dn = copies.start(
            down.at[pl.ds(pl.multiple_of((1 - core) * half, 16), half)], dn_in, sibling
        )
        swap_dn.wait_recv()

        def add_dn(m, carry):
            at = pl.multiple_of(m * 112, 16)
            own = down[pl.ds(pl.multiple_of(core * half + m * 112, 16), 112), :]
            dn_in[pl.ds(at, 112), :] = (
                own.astype(F32) + dn_in[pl.ds(at, 112), :].astype(F32)
            ).astype(BF)
            return carry

        lax.fori_loop(0, half // 112, add_dn, 0)
        total = part[0].astype(F32)
        for i in range(1, N_FS):
            part_copy(part, i).wait_recv()
            total = total + part_in[i].astype(F32)
        mid_ref[...] = total
        for i in range(1, N_FS):
            part_copy(part, i).wait_send()
        for copy in [swap_gu, swap_dn]:
            copy.wait_send()
        for copy in saves[2:]:
            copy.wait()

    pl.run_scoped(
        feed_forward,
        pltpu.VMEM(cot_ref.shape, BF),
        pltpu.VMEM(gu_ref.shape, BF),
        pltpu.VMEM(down_ref.shape, BF),
        pltpu.VMEM((every, units), BF),
        pltpu.VMEM((2, every, units), BF),
        pltpu.VMEM((N_FS, tokens, width), BF),
        pltpu.VMEM((2, 2, tokens, width), BF),
    )
    begin(out_sends[:5])

    def columns_of(which):
        return pl.ds(pl.multiple_of(which * side, side), side)

    def half_product(left, right, which, out):
        def step(m, carry):
            at = pl.multiple_of(m * 256, 256)
            out[pl.ds(at, 256), :] = contract_rows(
                left[:, pl.ds(at, 256)], right[:, columns_of(which)]
            ).astype(BF)
            return carry

        lax.fori_loop(0, width // 256, step, 0)

    def add_product(left, right, out):
        def step(m, carry):
            at = pl.multiple_of(m * 256, 256)
            product = contract_rows(left[:, pl.ds(at, 256)], right[:, columns_of(core)])
            out[pl.ds(at, 256), :] = (product + out[pl.ds(at, 256), :].astype(F32)).astype(BF)
            return carry

        lax.fori_loop(0, width // 256, step, 0)

    def attention(branch, back, attended, normed, out_half, dkv):
        load_at = local_copy(attended_hbm, attended, 0)
        load_nm = local_copy(normed_hbm, normed, 1)

        def second_norm(full_o, middle_ref):
            load_mid = local_copy(middle_hbm, middle_ref, 2)
            load_o = local_copy(o_hbm, full_o, 3)
            load_mid.wait()
            middle = middle_ref[...]
            scale_two = lax.rsqrt(jnp.mean(middle * middle, axis=-1, keepdims=True) + EPSILON)
            norm = middle * scale_two
            grad = mid_ref[...]
            gain_grad[...] = jnp.sum(grad * norm, axis=0, keepdims=True)
            scaled = grad * gains_ref[1:2, :]
            cot_copy = local_copy(cot_ref.at[0], back, 6)
            cot_copy.wait()
            mid = back[...].astype(F32) + scale_two * (
                scaled - norm * jnp.mean(scaled * norm, axis=-1, keepdims=True)
            )
            mid_ref[...] = mid
            branch[...] = mid.astype(BF)
            load_o.wait()
            back[...] = contract_cols(branch[...], full_o[...]).astype(BF)

        pl.run_scoped(second_norm, pltpu.VMEM(o_hbm.shape, BF), pltpu.VMEM((tokens, width), F32))
        load_at.wait()
        load_nm.wait()
        half_product(attended, branch, 1 - core, out_half)
        swap_o = copies.start(out_half, o_in, sibling)

        def heads(expo, kv, query_ref, mixed_ref):
            loads = [
                local_copy(kv_hbm, kv, 2),
                local_copy(query_hbm, query_ref, 3),
                local_copy(mixed_hbm, mixed_ref, 4),
                local_copy(expo_hbm, expo, 5),
            ]
            for load in loads:
                load.wait()
            for h in range(KV_HEADS):
                if h == 1:
                    swap_o.wait_recv()
                    add_product(attended, branch, o_in)
                    o_z.start()
                query = query_ref[h]
                head = back[:, h * GROUP * HD : (h + 1) * GROUP * HD]
                grads = jnp.concatenate(
                    [head[:, i * HD : (i + 1) * HD] for i in range(GROUP)], axis=0
                )
                inverse = inv_ref[h, 0:1, :]
                turned = grads.astype(F32).T
                weighted = jnp.sum(turned * mixed_ref[h], axis=0, keepdims=True)
                factor = inverse * scale
                offset = weighted * factor
                grads_scaled = (turned * inverse).T.astype(BF)
                dq = jnp.zeros((HD, GROUP * tokens), F32)
                for j in range(length // CHUNK):
                    part = expo[h, j * CHUNK : (j + 1) * CHUNK, :]
                    cols = slice(h * HD, (h + 1) * HD)
                    keys = kv[2 * j : 2 * j + 2, :tokens, cols].reshape(CHUNK, HD)
                    v_cols = slice((KV_HEADS + h) * HD, (KV_HEADS + h + 1) * HD)
                    values = kv[2 * j : 2 * j + 2, :tokens, v_cols].reshape(CHUNK, HD)
                    prob_grad = contract_cols(values, grads)
                    score_grad = (part.astype(F32) * (prob_grad * factor - offset)).astype(BF)
                    dk = jnp.dot(score_grad, query, preferred_element_type=F32).astype(BF)
                    dv = jnp.dot(part, grads_scaled, preferred_element_type=F32).astype(BF)
                    for side_core in range(2):
                        cut = slice(side_core * tokens, (side_core + 1) * tokens)
                        dkv[side_core, j, :, cols] = dk[cut]
                        dkv[side_core, j, :, v_cols] = dv[cut]
                    dq = dq + contract_rows(keys, score_grad)
                for i in range(GROUP):
                    at = (h * GROUP + i) * HD
                    q_grad[:, at : at + HD] = turn_back(
                        dq[:, i * tokens : (i + 1) * tokens].T, cos_wide, sin_wide
                    ).astype(BF)

        pl.run_scoped(
            heads,
            pltpu.VMEM(expo_hbm.shape, BF),
            pltpu.VMEM(kv_hbm.shape, BF),
            pltpu.VMEM(query_hbm.shape, BF),
            pltpu.VMEM(mixed_hbm.shape, F32),
        )
        swap_kv = copies.start(dkv.at[1 - core], kv_in, sibling)

        swap_o.wait_send()
        half_product(normed, q_grad, 1 - core, out_half)
        swap_q = copies.start(out_half, q_in, sibling)
        swap_kv.wait_recv()
        kv_in[...] = (dkv[core].astype(F32) + kv_in[...].astype(F32)).astype(BF)
        begin(kv_sends)
        begin(x_dn)
        o_z.wait_recv()
        add_over(o_in, o_over)
        begin(o_sends)
        swap_q.wait_recv()
        add_product(normed, q_grad, q_in)
        swap_kv.wait_send()
        swap_q.wait_send()

    pl.run_scoped(
        attention,
        pltpu.VMEM((tokens, width), BF),
        pltpu.VMEM((tokens, width), BF),
        pltpu.VMEM((tokens, width), BF),
        pltpu.VMEM((tokens, width), BF),
        pltpu.VMEM((width, side), BF),
        pltpu.VMEM((2, N_CTX // 2, tokens, kv_in.shape[2]), BF),
    )

    here, far = (c, f), (partner[0], f)
    x_one, x_two, x_three = along
    kv_width = KV_HEADS * HD
    at_rows, at_cols = at_own.shape
    count = N_FS // 2

    def z_of(device):
        return lax.div(device[0], 8)

    def gu_place(device, part=None):
        size = count if part is None else count // 2
        start = count * z_of(device) + (0 if part is None else part * size)
        return all_gu.at[lax.rem(device[0], 2), x_of(device), pl.ds(start, size)]

    def dn_place(device, part=None):
        columns = pl.ds(pl.multiple_of(x_of(device) * strip, strip), strip)
        size = window // (1 if part is None else 2)
        span = pl.ds(0 if part is None else part * size, size)
        return all_dn.at[lax.rem(device[0], 2), z_of(device), span, columns]

    def at_span(device):
        return (
            pl.ds(pl.multiple_of(x_of(device) * at_rows, at_rows), at_rows),
            pl.ds(pl.multiple_of(z_of(device) * at_cols, at_cols), at_cols),
        )

    def at_place(device):
        return all_at.at[(lax.rem(device[0], 2),) + at_span(device)]

    def tail(gu_buf, dn_buf, far_buf, kv_buf, full_qkv, proj, kv_out, kv_keep, at_all, out_buf):
        rest, own = [], []
        load_qkv = local_copy(qkv_hbm, full_qkv, 0)
        load_nm = local_copy(normed_hbm, out_buf.at[N_FS - 1], 1)

        for copy in x_gu:
            copy.wait_recv()
        local_copy(gu_x, gu_buf, 2).wait()

        def sum_gu_x(g, carry):
            total = gu_in[g, x_at].astype(F32)
            for i in range(3):
                total = total + gu_buf[i, g].astype(F32)
            gu_buf[0, g] = total.astype(BF)
            return carry

        lax.fori_loop(0, N_FS, sum_gu_x, 0)
        z_gu = copies.start(
            gu_buf.at[0, pl.ds(pl.multiple_of((1 - z_at) * count, count), count)], gu_z, partner
        )

        q_z.start()

        load_qkv.wait()
        in_norm_grad = contract_cols(q_grad[...], full_qkv[:, :width])

        for copy in kv_sends:
            copy.wait_recv()
        local_copy(kv_far, kv_buf, 3).wait()
        total = kv_in[pair_at].astype(F32)
        for i in range(N_CTX // 2 - 1):
            total = total + kv_buf[i].astype(F32)
        for h in range(KV_HEADS):
            at = width + h * HD
            proj[:, at : at + HD] = turn_back(
                total[:, h * HD : (h + 1) * HD], cos_wide, sin_wide
            ).astype(BF)
        proj[:, width + kv_width :] = total[:, kv_width:].astype(BF)
        proj[:, :width] = q_grad[...]

        def side_of(which):
            return pl.ds(pl.multiple_of(width + which * kv_width, kv_width), kv_width)

        load_nm.wait()
        normed = out_buf[N_FS - 1]
        kv_out[...] = contract_rows(normed, proj[:, side_of(1 - core)]).astype(BF)
        swap_part = copies.start(kv_out, kv_part, sibling)
        kv_keep[...] = contract_rows(normed, proj[:, side_of(core)]).astype(BF)

        z_gu.wait_recv()

        def add_gu_z(j, carry):
            mine = gu_buf[0, z_at * count + j].astype(F32)
            done_gu[j] = (mine + gu_z[j].astype(F32)).astype(BF)
            return carry

        lax.fori_loop(0, count, add_gu_z, 0)
        spot = lax.rem(f, 4)
        owners = [
            (8 * plane + lax.rem(c, 8), 4 * z_at + lax.rem(flip(f, i), 4)) for i in range(4)
        ]

        def gu_copy(i):
            return pltpu.make_async_remote_copy(
                src_ref=done_gu.at[lax.rem(flip(f, i), 4)],
                dst_ref=own_gu.at[spot],
                send_sem=own_send.at[i],
                recv_sem=own_recv.at[i],
                device_id=owners[i],
                device_id_type=MESH,
            )

        gu_own = pltpu.make_async_copy(done_gu.at[spot], own_gu.at[spot], local.at[4])

        @pl.when(plane == z_at)
        def _():
            gu_own.start()

        @pl.when(plane != z_at)
        def _():
            gu_copy(0).start()

        for i in range(1, 4):
            gu_copy(i).start()
        swap_part.wait_recv()
        kv_part[...] = (kv_part[...].astype(F32) + kv_keep[...].astype(F32)).astype(BF)

        def rows_of(owner):
            return pl.ds(pl.multiple_of(owner * 192, 192), 192)

        part_z = copies.start(kv_part.at[plane_rows(1 - plane)], kv_over, over)
        q_z.wait_recv()
        add_over(q_in, q_over)
        begin(q_sends)

        @pl.when(plane == z_at)
        def _():
            gu_own.wait()

        @pl.when(plane != z_at)
        def _():
            gu_copy(0).wait()

        for i in range(1, 4):
            gu_copy(i).wait()
        gather_z = [copies.start(own_gu, gu_place(here), partner)]
        gu_xs = [copies.start(own_gu, gu_place(here), device) for device in (x_one, x_three)]
        rest.append(copies.start(own_gu, gu_place(here), sibling))
        own.append(local_copy(own_gu, gu_place(here), 6))

        forwards = []

        def around(place, one, three, z):
            sent = []
            for copy, device, part, other in ((one, x_one, 0, x_three), (three, x_three, 1, x_one)):
                at = (flip(device[0], 8), f) if z else device
                copy.wait_recv()
                sent.append(copies.start(place(at, part), place(at, part), other))
                rest.append(copies.start(place(at), place(at), sibling))
            forwards.extend(sent)
            return sent

        def opposite(place, sent, z):
            at = (flip(x_two[0], 8), f) if z else x_two
            for copy in sent:
                copy.wait_recv()
            rest.append(copies.start(place(at), place(at), sibling))

        part_z.wait_recv()
        add_over(kv_part, kv_over)
        part_sends = [
            copies.start(kv_part.at[rows_of(peer[1])], kv_parts.at[i], peer)
            for i, peer in enumerate(near)
        ]

        in_norm_grad = in_norm_grad + contract_cols(proj[:, width:], full_qkv[:, width:])
        inputs = input_ref[...].astype(F32)
        scale_one = lax.rsqrt(jnp.mean(inputs * inputs, axis=-1, keepdims=True) + EPSILON)
        norm = inputs * scale_one
        gain_one_grad = jnp.sum(in_norm_grad * norm, axis=0, keepdims=True)
        scaled = in_norm_grad * gains_ref[0:1, :]
        in_rows[...] = mid_ref[...] + scale_one * (
            scaled - norm * jnp.mean(scaled * norm, axis=-1, keepdims=True)
        )
        bias_grad = jnp.sum(proj[...].astype(F32), axis=0, keepdims=True)
        row = 0
        for vector in (gain_one_grad, gain_grad[...], bias_grad):
            for n in range(vector.shape[1] // 128):
                vec[row : row + 1, :] = vector[:, n * 128 : (n + 1) * 128]
                row += 1
        vec_sends = [copies.start(vec, vec_fs.at[i], peer) for i, peer in enumerate(peers)]


        for copy in x_dn:
            copy.wait_recv()
        local_copy(dn_x, dn_buf, 5).wait()
        total = dn_in[:, pl.ds(pl.multiple_of(x_at * strip, strip), strip)].astype(F32)
        for i in range(3):
            total = total + dn_buf[i].astype(F32)
        dn_mine[...] = total.astype(BF)

        def window_of(z):
            return pl.ds(pl.multiple_of(z * (half - window), 16), window)

        z_dn = copies.start(dn_mine.at[window_of(1 - z_at)], dn_z, partner)

        gather_z[0].wait_recv()
        gu_xs2 = [copies.start(gu_place(far), gu_place(far), device) for device in (x_one, x_three)]
        rest.append(copies.start(gu_place(far), gu_place(far), sibling))
        load_mid = local_copy(middle_hbm, mid_ref, 10)
        gu_f = around(gu_place, *gu_xs, False)
        z_dn.wait_recv()
        done_dn[...] = (dn_mine[window_of(z_at), :].astype(F32) + dn_z[...].astype(F32)).astype(BF)
        own.append(local_copy(done_dn, dn_place(here), 7))
        gather_z.append(copies.start(done_dn, dn_place(here), partner))
        dn_xs = [copies.start(done_dn, dn_place(here), device) for device in (x_one, x_three)]
        rest.append(copies.start(done_dn, dn_place(here), sibling))

        owned = pl.ds(pl.multiple_of(f * 192, 192), 192)
        for n, (ref, sends, arrived) in enumerate(((o_in, o_sends, o_far), (q_in, q_sends, q_far))):
            for copy in sends:
                copy.wait_recv()
            local_copy(arrived, far_buf, 8 + n).wait()
            total = ref[owned, :].astype(F32)
            for i in range(3):
                total = total + far_buf[i].astype(F32)
            at_all[:, n * side : (n + 1) * side] = total.astype(BF)
        for copy in part_sends:
            copy.wait_recv()
        total = kv_part[owned, :].astype(F32)
        for i in range(3):
            total = total + kv_parts[i].astype(F32)
        at_all[:, 2 * side :] = total.astype(BF)
        at_sends = [
            copies.start(at_all.at[at_span(device)], at_far.at[i], device)
            for i, device in enumerate(ring)
        ]
        gather_z[1].wait_recv()
        dn_xs2 = [copies.start(dn_place(far), dn_place(far), device) for device in (x_one, x_three)]
        rest.append(copies.start(dn_place(far), dn_place(far), sibling))
        gu_f2 = around(gu_place, *gu_xs2, True)
        for copy in vec_sends:
            copy.wait_recv()
        total = vec[...]
        for i in range(N_FS - 1):
            total = total + vec_fs[i]
        vec_mid[...] = total
        vec_near = [copies.start(vec_mid, vec_ctx.at[c], device) for device in ring]
        rest.append(copies.start(vec_mid, vec_ctx.at[c], sibling))
        vec_ctx[pl.ds(c, 1)] = total[None]
        for copy in at_sends:
            copy.wait_recv()
        total = at_all[at_span(here)].astype(F32)
        for i in range(N_CTX // 2 - 1):
            total = total + at_far[i].astype(F32)
        at_own[...] = total.astype(BF)
        at_near = [copies.start(at_own, at_place(here), device) for device in ring]
        rest.append(copies.start(at_own, at_place(here), sibling))
        begin(out_sends[5:])
        own.append(local_copy(at_own, at_place(here), 11))
        dn_f = around(dn_place, *dn_xs, False)
        for copy, device in zip(vec_near, ring):
            copy.wait_recv()
            place = vec_ctx.at[device[0]]
            rest.append(copies.start(place, place, sibling))
        dn_f2 = around(dn_place, *dn_xs2, True)
        opposite(gu_place, gu_f, False)
        opposite(dn_place, dn_f, False)
        for copy in out_sends:
            copy.wait_recv()
        local_copy(out_ref.at[0], out_buf.at[N_FS - 1], 1).wait()
        local_copy(out_in, out_buf.at[pl.ds(0, N_FS - 1)], 3).wait()
        load_mid.wait()
        total = mid_ref[...]
        for i in range(N_FS):
            total = total + out_buf[i].astype(F32)
        out_rows[...] = total.astype(BF)
        opposite(gu_place, gu_f2, True)
        opposite(dn_place, dn_f2, True)
        for copy, device in zip(at_near, ring):
            copy.wait_recv()
            rest.append(copies.start(at_place(device), at_place(device), sibling))
        for copy in (
            [z_gu, z_dn, swap_part, part_z] + part_sends + gather_z + gu_xs + dn_xs + gu_xs2 + dn_xs2
            + forwards + at_sends + at_near + vec_sends + vec_near
        ):
            copy.wait_send()
        for copy in rest:
            copy.wait()
        total = vec_ctx[0]
        for i in range(1, N_CTX):
            total = total + vec_ctx[i]
        vec_sum[...] = total
        for copy in own:
            copy.wait()

    pl.run_scoped(
        tail,
        pltpu.VMEM(gu_x.shape, BF),
        pltpu.VMEM(dn_x.shape, BF),
        pltpu.VMEM(o_far.shape, BF),
        pltpu.VMEM(kv_far.shape, BF),
        pltpu.VMEM(qkv_hbm.shape, BF),
        pltpu.VMEM((tokens, qkv_hbm.shape[1]), BF),
        pltpu.VMEM(kv_part.shape, BF),
        pltpu.VMEM(kv_part.shape, BF),
        pltpu.VMEM((width // N_FS, width + kv_width), BF),
        pltpu.VMEM((N_FS, tokens, width), BF),
    )
    for copy in (
        up_y + [low_z] + low_y + up_z + x_gu + x_dn + o_sends + q_sends + kv_sends + out_sends
        + [o_z, q_z]
    ):
        copy.wait_send()


def backward(cid, arrays, vmem_arrays):
    normed, cot_all, columns, down_weight, expo, kv_all, full_o = arrays[:7]
    tokens, width = normed.shape
    units = down_weight.shape[0]
    piece = columns.shape[3]
    half = units // 2
    strip = width // 4
    window = half // 2 + 8
    side = width // 2
    kv_width = KV_HEADS * HD
    rows = width // N_FS
    anywhere = pl.BlockSpec(memory_space=pl.ANY)
    vmem = pl.BlockSpec(memory_space=pltpu.VMEM)
    at_width = width + kv_width
    in_place = [
        ((2, 4, N_FS, piece, units), BF),
        ((2, 2, window, width), BF),
        ((2, rows, at_width), BF),
        ((N_FS, tokens, width), BF),
        ((N_FS - 1, tokens, width), BF),
        ((3, N_FS, piece, units), BF),
        ((3, half, strip), BF),
        ((3, rows, side), BF),
        ((3, rows, side), BF),
        ((N_CTX // 2 - 1, tokens, 2 * kv_width), BF),
    ]
    in_vmem = [((40, 128), F32), ((tokens, width), BF), ((tokens, width), F32)]
    results = pl.pallas_call(
        back_kernel,
        name="back",
        out_shape=[jax.ShapeDtypeStruct(*o) for o in in_place + in_vmem],
        in_specs=[anywhere] * len(arrays) + [vmem] * len(vmem_arrays),
        out_specs=[anywhere] * len(in_place) + [vmem] * len(in_vmem),
        scratch_shapes=[
            pltpu.VMEM((N_FS, tokens, width), BF),
            pltpu.VMEM((N_FS, tokens, width), BF),
            pltpu.VMEM((N_FS, 4, piece, units), BF),
            pltpu.VMEM((half, width), BF),
            pltpu.VMEM((N_FS // 2, piece, units), BF),
            pltpu.VMEM((half, strip), BF),
            pltpu.VMEM((window, strip), BF),
            pltpu.VMEM((N_CTX // 2, tokens, 2 * kv_width), BF),
            pltpu.VMEM((width, side), BF),
            pltpu.VMEM((width, side), BF),
            pltpu.VMEM((width // 2, side), BF),
            pltpu.VMEM((width // 2, side), BF),
            pltpu.VMEM((width // 2, kv_width), BF),
            pltpu.VMEM((tokens, width), BF),
            pltpu.VMEM((tokens, width), F32),
            pltpu.VMEM((1, width), F32),
            pltpu.VMEM((N_FS // 2, piece, units), BF),
            pltpu.VMEM((window, strip), BF),
            pltpu.VMEM((N_FS // 2, piece, units), BF),
            pltpu.VMEM((width, kv_width), BF),
            pltpu.VMEM((3, rows, kv_width), BF),
            pltpu.VMEM((N_CTX // 2 - 1, rows // 4, at_width // 2), BF),
            pltpu.VMEM((rows // 4, at_width // 2), BF),
            pltpu.VMEM((40, 128), F32),
            pltpu.VMEM((N_FS - 1, 40, 128), F32),
            pltpu.VMEM((40, 128), F32),
            pltpu.VMEM((N_CTX, 40, 128), F32),
            pltpu.SemaphoreType.DMA((4,)),
            pltpu.SemaphoreType.DMA((4,)),
            pltpu.SemaphoreType.DMA((N_FS,)),
            pltpu.SemaphoreType.DMA((N_FS,)),
            pltpu.SemaphoreType.DMA((150,)),
            pltpu.SemaphoreType.DMA((150,)),
            pltpu.SemaphoreType.DMA((12,)),
        ],
        compiler_params=pltpu.CompilerParams(
            collective_id=cid, has_side_effects=True, vmem_limit_bytes=62 * 2**20
        ),
    )(*arrays, *vmem_arrays)
    return results[:3] + results[len(in_place) :]


def wide_kernel(gu_ref, gate_ref, up_ref):
    for which, out in enumerate((gate_ref, up_ref)):
        out[...] = jnp.concatenate(
            [gu_ref[which, 0, source].astype(F32) for source in range(N_FS)], axis=1
        )


def wide_results(all_gu):
    piece, units = all_gu.shape[3:]
    parts = all_gu.shape[1]
    shape = jax.ShapeDtypeStruct((parts * piece, N_FS * units), F32)
    return pl.pallas_call(
        wide_kernel,
        name="wide_results",
        grid=(parts,),
        in_specs=[pl.BlockSpec((2, 1, N_FS, piece, units), lambda p: (0, p, 0, 0, 0))],
        out_specs=[pl.BlockSpec((piece, N_FS * units), lambda p: (p, 0))] * 2,
        out_shape=[shape, shape],
        compiler_params=pltpu.CompilerParams(vmem_limit_bytes=60 * 2**20),
    )(all_gu)


def rest_kernel(dn_ref, at_ref, down_ref, o_ref, q_ref, k_ref, v_ref):
    z = lax.rem(pl.program_id(0), 2)
    rows = down_ref.shape[0]
    block = dn_ref[0, 0].astype(F32)
    down_ref[...] = jnp.where(z == 0, block[:rows], block[8 : 8 + rows])
    side = o_ref.shape[1] // 2
    for n in range(2):
        part = at_ref[n].astype(F32)
        o_ref[:, n * side : (n + 1) * side] = part[:, :side]
        q_ref[:, n * side : (n + 1) * side] = part[:, side : 2 * side]
        (k_ref, v_ref)[n][...] = part[:, 2 * side :]


def rest_results(all_dn, all_at):
    window, width = all_dn.shape[2:]
    rows = window - 8
    own, at_width = all_at.shape[1:]
    kv_width = KV_HEADS * HD
    return pl.pallas_call(
        rest_kernel,
        name="rest_results",
        grid=(4,),
        in_specs=[
            pl.BlockSpec((1, 1, window, width), lambda n: (n // 2, n % 2, 0, 0)),
            pl.BlockSpec((2, own // 4, at_width), lambda n: (0, n, 0)),
        ],
        out_specs=[
            pl.BlockSpec((rows, width), lambda n: (n, 0)),
            pl.BlockSpec((own // 4, width), lambda n: (n, 0)),
            pl.BlockSpec((own // 4, width), lambda n: (n, 0)),
            pl.BlockSpec((own // 4, kv_width), lambda n: (n, 0)),
            pl.BlockSpec((own // 4, kv_width), lambda n: (n, 0)),
        ],
        out_shape=[
            jax.ShapeDtypeStruct((4 * rows, width), F32),
            jax.ShapeDtypeStruct((own, width), F32),
            jax.ShapeDtypeStruct((own, width), F32),
            jax.ShapeDtypeStruct((own, kv_width), F32),
            jax.ShapeDtypeStruct((own, kv_width), F32),
        ],
        compiler_params=pltpu.CompilerParams(vmem_limit_bytes=60 * 2**20),
    )(all_dn, all_at)


def body(
    layer_input,
    segments,
    positions,
    attn_norm,
    q_weight,
    q_bias,
    k_weight,
    k_bias,
    v_weight,
    v_bias,
    o_weight,
    mlp_norm,
    gate_weight,
    up_weight,
    down_weight,
    out_cotangent,
):
    tokens, width = layer_input.shape[1:]
    rows = gate_weight.shape[0]
    units = gate_weight.shape[1] // N_FS
    q_width = HEADS * HD
    kv_width = KV_HEADS * HD
    half_block = tokens // 2
    ctx = lax.axis_index("ctx")
    segment = segments[0]
    small = jnp.concatenate([attn_norm, mlp_norm, q_bias, k_bias, v_bias]).astype(F32)[None]
    cosine, sine = rope_tables(positions[0], HD)
    within = jnp.arange(tokens, dtype=jnp.int32)
    row_place = jnp.where(
        within < half_block,
        ctx * half_block + within,
        (2 * N_CTX - 1 - ctx) * half_block + within - half_block,
    )
    row_info = jnp.stack([row_place.astype(F32), segment.astype(F32)])
    (
        full_qkv,
        full_o,
        kv_all,
        columns,
        cot_all,
        expo,
        gains,
        normed_in,
        query,
        mixed,
        inverse,
        attended,
        middle,
        normed_mid,
    ) = front(
        1,
        (q_weight, k_weight, v_weight, o_weight, gate_weight, up_weight),
        (small, layer_input[0], out_cotangent[0], row_info, cosine, sine),
    )
    full_qkv = full_qkv.reshape(width, q_width + 2 * kv_width)
    full_o = full_o.reshape(q_width, width)
    all_gu, all_dn, all_at, all_vec, output_rows, input_rows = backward(
        3,
        (
            normed_mid,
            cot_all,
            columns,
            down_weight,
            expo,
            kv_all,
            full_o,
            middle,
            query,
            mixed,
            attended,
            normed_in,
            full_qkv,
        ),
        (gains, inverse, cosine, sine, layer_input[0]),
    )
    gate_grad, up_grad = wide_results(all_gu)
    down_grad, o_grad, q_weight_grad, k_grad, v_grad = rest_results(all_dn, all_at)
    flat_vec = all_vec.reshape(-1)
    mine = lax.axis_index("fsdp")
    vectors = []
    start = 0
    for whole in (width, width, q_width, kv_width, kv_width):
        part = whole // N_FS
        vectors.append(lax.dynamic_slice_in_dim(flat_vec, start + mine * part, part, 0))
        start += whole
    return (
        output_rows[None],
        input_rows[None],
        vectors[0],
        q_weight_grad,
        vectors[2],
        k_grad,
        vectors[3],
        v_grad,
        vectors[4],
        o_grad,
        vectors[1],
        gate_grad,
        up_grad,
        down_grad,
    )


def solution(mesh):
    placed = (
        P("fsdp", "ctx", None),
        P("fsdp", "ctx"),
        P("fsdp", "ctx"),
        P("fsdp"),
        P("fsdp", None),
        P("fsdp"),
        P("fsdp", None),
        P("fsdp"),
        P("fsdp", None),
        P("fsdp"),
        P("fsdp", None),
        P("fsdp"),
        P("fsdp", None),
        P("fsdp", None),
        P("fsdp", None),
        P("fsdp", "ctx", None),
    )
    return jax.shard_map(
        body,
        mesh=mesh,
        in_specs=placed,
        out_specs=(
            P("fsdp", "ctx", None),
            P("fsdp", "ctx", None),
            P("fsdp"),
            P("fsdp", None),
            P("fsdp"),
            P("fsdp", None),
            P("fsdp"),
            P("fsdp", None),
            P("fsdp"),
            P("fsdp", None),
            P("fsdp"),
            P("fsdp", None),
            P("fsdp", None),
            P("fsdp", None),
        ),
        check_vma=False,
    )
```

```python
import functools

import jax
import jax.numpy as jnp
from jax import lax
from jax.experimental import pallas as pl
from jax.experimental.pallas import tpu as pltpu
from jax.sharding import PartitionSpec as P

HEADS = 12
KV_HEADS = 2
HD = 128
GROUP = HEADS // KV_HEADS
N_CTX = 16
N_FS = 8
EPSILON = 1e-06
THETA = 1000000.0
MESH = pl.DeviceIdType.MESH
BF = jnp.bfloat16
F32 = jnp.float32


def rope_tables(position, head_dim):
    freqs = THETA ** (-jnp.arange(0, head_dim, 2).astype(F32) / head_dim)
    angles = position.astype(F32)[:, None] * freqs[None, :]
    return (jnp.cos(angles), jnp.sin(angles))


def contract_rows(left, right):
    return lax.dot_general(
        left, right, (((0,), (0,)), ((), ())), preferred_element_type=F32
    )


def contract_cols(left, right):
    return lax.dot_general(
        left, right, (((1,), (1,)), ((), ())), preferred_element_type=F32
    )


def flip(value, mask):
    out = value
    bit = 1
    while bit <= mask:
        if mask & bit:
            out = out + bit * (1 - 2 * lax.rem(lax.div(value, bit), 2))
        bit *= 2
    return out


class Copies:
    def __init__(self, send, recv):
        self.send, self.recv, self.count = send, recv, 0

    def start(self, src, dst, device):
        copy = self.make(src, dst, device)
        copy.start()
        return copy

    def make(self, src, dst, device):
        copy = pltpu.make_async_remote_copy(
            src_ref=src,
            dst_ref=dst,
            send_sem=self.send.at[self.count],
            recv_sem=self.recv.at[self.count],
            device_id=device,
            device_id_type=MESH,
        )
        self.count += 1
        return copy


def greet(devices):
    barrier = pltpu.get_barrier_semaphore()
    for device in devices:
        pl.semaphore_signal(barrier, inc=1, device_id=device, device_id_type=MESH)
    pl.semaphore_wait(barrier, len(devices))


class SharedRows:
    def __init__(self, copies, ref, c, f, columns=None, direct=False):
        core = lax.rem(c, 2)
        self.copies, self.f = copies, f
        self.sibling = (flip(c, 1), f)
        self.over = (c + core * (flip(c, 8) - c), flip(f, 4))
        self.one, self.three = (c, flip(f, 1)), (c, flip(f, 3))
        rows = ref.shape[1] // 2

        def place(owner, part=None):
            if part is None:
                span = pl.ds(pl.multiple_of(core * rows, 16), rows)
            else:
                span = pl.ds(pl.multiple_of(core * rows + part * (rows // 2), 16), rows // 2)
            if columns is None:
                return ref.at[owner, span]
            return ref.at[owner, span, columns]

        self.place = place
        mine = place(f)
        self.from_one = copies.start(mine, mine, self.one)
        self.from_three = copies.start(mine, mine, self.three)
        self.z_copies = [copies.start(mine, mine, self.over)]
        self.sent = [self.from_one, self.from_three]
        self.far = [copies.start(mine, mine, (c, flip(f, 2)))] if direct else None
        self.rest = []

    def send(self, here, device):
        return self.copies.start(here, here, device)

    def pass_y(self):
        one, three = flip(self.f, 1), flip(self.f, 3)
        self.from_one.wait_recv()
        direct = self.far is not None
        if not direct:
            self.far = [self.send(self.place(one, 0), self.three)]
        self.z_copies.append(self.send(self.place(one), self.over))
        self.from_three.wait_recv()
        if not direct:
            self.far.append(self.send(self.place(three, 1), self.one))
        self.z_copies.append(self.send(self.place(three), self.over))
        self.rest.append(self.send(self.place(one), self.sibling))
        self.rest.append(self.send(self.place(three), self.sibling))
        for copy in self.far:
            copy.wait_recv()
        two = self.place(flip(self.f, 2))
        self.z_copies.append(self.send(two, self.over))
        self.rest.append(self.send(two, self.sibling))

    def pass_z(self):
        for copy, mask in zip(self.z_copies, (4, 5, 7, 6)):
            copy.wait_recv()
            self.rest.append(self.send(self.place(flip(self.f, mask)), self.sibling))

    def wait(self):
        for copy in self.rest:
            copy.wait_recv()

    def finish(self):
        for copy in self.sent + self.far + self.z_copies + self.rest:
            copy.wait_send()


CHUNK = 256


def turn_back(grad, cos_wide, sin_wide):
    half = grad.shape[1] // 2
    swapped = jnp.concatenate([grad[:, half:], grad[:, :half]], axis=1)
    return grad * cos_wide + swapped * sin_wide


def front_kernel(
    q_hbm,
    k_hbm,
    v_hbm,
    o_hbm,
    gate_hbm,
    up_hbm,
    small_ref,
    input_ref,
    out_cot_ref,
    row_ref,
    cos_ref,
    sin_ref,
    w_out,
    o_out,
    kv_out,
    g_out,
    t_out,
    e_out,
    gains_ref,
    normed_ref,
    query_ref,
    mixed_ref,
    inv_ref,
    attended_ref,
    middle_ref,
    normed_mid_ref,
    weights,
    full_o,
    small_all,
    strip,
    stage,
    cot_ref,
    kv_own,
    kv,
    s_ref,
    expo,
    send,
    recv,
    local,
):
    c, f = lax.axis_index("ctx"), lax.axis_index("fsdp")
    core = lax.rem(c, 2)
    sibling = (flip(c, 1), f)
    here = (c, f)
    peers = [(c, flip(f, i)) for i in range(1, N_FS)]
    ring = [(flip(c, 2 * i), f) for i in range(1, N_CTX // 2)]
    along = ring[:3]
    near, turn = peers[:3], peers[3]
    greet(peers + ring + [sibling, (flip(c, 8), flip(f, 4))])
    copies = Copies(send, recv)
    tokens, width = input_ref.shape
    rows = q_hbm.shape[0]
    kv_width = KV_HEADS * HD
    cut, units = stage.shape[1:]
    x_part = lax.rem(c, N_FS)

    def local_copy(src, dst, n):
        copy = pltpu.make_async_copy(src, dst, local.at[n])
        copy.start()
        return copy

    mine = weights.at[f]
    q_columns, kv_columns = pl.ds(0, width), pl.ds(width, 2 * kv_width)
    load_k = local_copy(k_hbm, mine.at[:, pl.ds(width, kv_width)], 1)
    load_v = local_copy(v_hbm, mine.at[:, pl.ds(width + kv_width, kv_width)], 2)
    block_rows = pl.ds(pl.multiple_of(lax.rem(x_part, 4) * cut, cut), cut)
    load_gate = local_copy(gate_hbm.at[block_rows], strip.at[0], 3)
    load_up = local_copy(up_hbm.at[block_rows], strip.at[1], 4)
    load_q = local_copy(q_hbm, mine.at[:, q_columns], 0)
    load_o = local_copy(o_hbm, full_o.at[f], 5)
    small_own = local_copy(small_ref, small_all.at[f], 7)
    small_sends = [copies.start(small_ref, small_all.at[f], peer) for peer in peers]
    load_k.wait()
    load_v.wait()
    share_kv = SharedRows(copies, weights, c, f, kv_columns, True)

    def columns(device, part=None):
        where = lax.rem(device[0], N_FS)
        if part is None:
            return g_out.at[lax.div(where, 4), :, lax.rem(where, 4)]
        half = N_FS // 2
        return g_out.at[lax.div(where, 4), pl.ds(part * half, half), lax.rem(where, 4)]

    def block(device, source):
        where = lax.rem(device[0], N_FS)
        return g_out.at[lax.div(where, 4), source, lax.rem(where, 4)]

    load_gate.wait()
    load_up.wait()
    which = lax.div(x_part, 4)
    for owner in range(N_FS):
        stage[owner] = strip[which, :, owner * units : (owner + 1) * units]
    block_own = local_copy(stage.at[f], block(here, f), 8)
    blocks = [copies.start(stage.at[peer[1]], block(here, f), peer) for peer in peers]
    load_q.wait()
    share_q = SharedRows(copies, weights, c, f, q_columns)
    inputs = input_ref[...].astype(F32)
    norm = inputs * lax.rsqrt(jnp.mean(inputs * inputs, axis=-1, keepdims=True) + EPSILON)
    small_own.wait()
    for copy in small_sends:
        copy.wait_recv()

    marks = [0, rows, 2 * rows, 3 * rows, 3 * rows + kv_width // N_FS, small_ref.shape[1]]
    gain_one, gain_two, bias_q, bias_k, bias_v = (
        jnp.concatenate([small_all[owner, :, lo:hi] for owner in range(N_FS)], axis=1)
        for lo, hi in zip(marks[:-1], marks[1:])
    )
    gains_ref[0:1, :] = gain_one
    gains_ref[1:2, :] = gain_two
    normed_ref[...] = (norm * gain_one).astype(BF)
    keep = jnp.where(row_ref[1:2, :] > 0.5, 1.0, 0.0)
    keep = jnp.broadcast_to(keep, (8, tokens)).T[:, 0:1]
    cot_ref[...] = (out_cot_ref[...].astype(F32) * keep).astype(BF)
    load_t = local_copy(cot_ref, t_out.at[0], 6)

    share_kv.pass_y()
    share_kv.pass_z()
    block_own.wait()
    for copy in blocks:
        copy.wait_recv()
    x_one, x_two, x_three = along
    from_one = [copies.start(columns(here, 0), columns(here, 0), x_one)]
    from_three = [copies.start(columns(here, 1), columns(here, 1), x_three)]
    share_kv.wait()
    cos_wide = jnp.concatenate([cos_ref[...], cos_ref[...]], axis=1)
    sin_wide = jnp.concatenate([-sin_ref[...], sin_ref[...]], axis=1)
    full = weights[:, :, width:].reshape(width, 2 * kv_width)
    projected = jnp.dot(normed_ref[...], full, preferred_element_type=F32)
    projected = projected + jnp.concatenate([bias_k, bias_v], axis=1)
    for h in range(KV_HEADS):
        cols = slice(h * HD, (h + 1) * HD)
        kv_own[:tokens, cols] = turn_back(projected[:, cols], cos_wide, sin_wide).astype(BF)
    kv_own[:tokens, kv_width:] = projected[:, kv_width:].astype(BF)
    marks = jnp.concatenate([row_ref[1:2, :]] * (2 * KV_HEADS), axis=1)
    kv_own[tokens:, :] = jnp.broadcast_to(marks, (16, 2 * kv_width)).astype(BF)
    keep_kv = local_copy(kv_own, kv.at[c], 9)
    keys = [copies.start(kv_own, kv.at[c], device) for device in ring]
    kv_rest = [copies.start(kv_own, kv.at[c], sibling)]

    from_one.append(copies.start(columns(here, 1), columns(here, 1), x_one))
    from_three.append(copies.start(columns(here, 0), columns(here, 0), x_three))
    g_rest = [copies.start(columns(here), columns(here), sibling)]

    share_q.pass_y()
    load_o.wait()
    share_o = SharedRows(copies, full_o, c, f)
    half = tokens // 2
    upper, lower = pl.ds(0, half), pl.ds(half, half)
    low_z = copies.start(cot_ref.at[lower], t_out.at[4, lower], turn)
    up_y = [
        copies.start(cot_ref.at[upper], t_out.at[i + 1, upper], device)
        for i, device in enumerate(near)
    ]
    up_z = [copies.start(cot_ref.at[upper], t_out.at[4, upper], turn)]
    low_y = [
        copies.start(cot_ref.at[lower], t_out.at[i + 1, lower], device)
        for i, device in enumerate(near)
    ]
    for key, device in zip(keys, ring):
        key.wait_recv()
        place = kv.at[device[0]]
        kv_rest.append(copies.start(place, place, sibling))
    share_q.pass_z()
    share_q.wait()

    full = weights[:, :, :width].reshape(width, width)
    projected = jnp.dot(normed_ref[...], full, preferred_element_type=F32) + bias_q
    for n in range(HEADS):
        at = (n % GROUP) * tokens
        query_ref[n // GROUP, at : at + tokens, :] = turn_back(
            projected[:, n * HD : (n + 1) * HD], cos_wide, sin_wide
        ).astype(BF)
    save_w = local_copy(weights, w_out, 0)

    from_one[0].wait_recv()
    far = [copies.start(columns(x_one, 0), columns(x_one, 0), x_three)]
    from_three[0].wait_recv()
    far.append(copies.start(columns(x_three, 1), columns(x_three, 1), x_one))
    share_o.pass_y()
    keep_kv.wait()
    for copy in kv_rest:
        copy.wait_recv()
    save_kv = local_copy(kv, kv_out, 1)

    length = N_CTX * tokens
    scale = HD ** (-0.5)
    row_place, row_seg = row_ref[0:1, :], row_ref[1:2, :]
    key_seg = kv[:, tokens : tokens + 16, :HD][:, 0, :].astype(F32).T
    within = lax.broadcasted_iota(jnp.int32, (tokens, tokens), 0)
    saves = []
    for h in range(KV_HEADS):
        query = query_ref[h]
        top = jnp.full((8, GROUP * tokens), -1e30, F32)
        for b in range(N_CTX):
            place = jnp.where(
                within < half, b * half + within, (2 * N_CTX - 1 - b) * half + within - half
            ).astype(F32)
            allowed = (place <= row_place) & (key_seg[:, b : b + 1] == row_seg) & (row_seg > 0.5)
            bias = jnp.where(allowed, 0.0, -1e30).astype(F32)
            scores = contract_cols(kv[b, :tokens, h * HD : (h + 1) * HD], query) * scale
            scores = scores + jnp.concatenate([bias] * GROUP, axis=1)
            s_ref[b * tokens : (b + 1) * tokens, :] = scores
            top = jnp.maximum(top, jnp.max(scores.reshape(tokens // 8, 8, -1), axis=0))
        highest = jnp.maximum(jnp.max(top, axis=0, keepdims=True), -1e29)
        total = jnp.zeros((8, GROUP * tokens), F32)
        mixed = jnp.zeros((HD, GROUP * tokens), F32)
        for j in range(length // CHUNK):
            part = jnp.exp(s_ref[j * CHUNK : (j + 1) * CHUNK, :] - highest)
            total = total + jnp.sum(part.reshape(CHUNK // 8, 8, -1), axis=0)
            low = part.astype(BF)
            expo[h, j * CHUNK : (j + 1) * CHUNK, :] = low
            at = (KV_HEADS + h) * HD
            values = kv[2 * j : 2 * j + 2, :tokens, at : at + HD].reshape(CHUNK, HD)
            mixed = mixed + contract_rows(values, low)
        total = jnp.sum(total, axis=0, keepdims=True)
        inverse = 1.0 / jnp.where(total > 0.5, total, 1.0)
        mixed = mixed * inverse
        mixed_ref[h] = mixed
        inv_ref[h] = jnp.broadcast_to(inverse, (8, GROUP * tokens))
        for i in range(GROUP):
            at = (h * GROUP + i) * HD
            attended_ref[:, at : at + HD] = mixed[:, i * tokens : (i + 1) * tokens].T.astype(BF)
        saves.append(local_copy(expo.at[h], e_out.at[h], 2 + h))
        if h == 0:
            low_z.wait_recv()
            for i, device in enumerate(near):
                low_y.append(copies.start(t_out.at[4, lower], t_out.at[5 + i, lower], device))
            for i, copy in enumerate(up_y):
                copy.wait_recv()
                up_z.append(copies.start(t_out.at[i + 1, upper], t_out.at[5 + i, upper], turn))
            share_o.pass_z()
            for copy, device in ((from_one[1], x_one), (from_three[1], x_three)):
                copy.wait_recv()
                g_rest.append(copies.start(columns(device), columns(device), sibling))

    for copy in far:
        copy.wait_recv()
    g_rest.append(copies.start(columns(x_two), columns(x_two), sibling))

    share_o.wait()
    product = jnp.dot(
        attended_ref[...], full_o[...].reshape(width, width), preferred_element_type=F32
    )
    middle = input_ref[...].astype(F32) + product
    middle_ref[...] = middle
    scale_two = lax.rsqrt(jnp.mean(middle * middle, axis=-1, keepdims=True) + EPSILON)
    normed_mid_ref[...] = (middle * scale_two * gains_ref[1:2, :]).astype(BF)
    save_o = local_copy(full_o, o_out, 4)
    for copy in low_y + up_z + g_rest:
        copy.wait_recv()
    for share in (share_kv, share_q, share_o):
        share.finish()
    for copy in (
        small_sends + blocks + from_one + from_three + far + g_rest + low_y + up_z + up_y
        + [low_z] + keys + kv_rest
    ):
        copy.wait_send()
    for copy in saves + [save_w, save_kv, save_o, load_t]:
        copy.wait()


def front(cid, arrays, vmem_arrays):
    tokens, width = vmem_arrays[1].shape
    rows, all_units = arrays[4].shape
    units = all_units // N_FS
    cut = rows // 4
    kv_width = KV_HEADS * HD
    wide = GROUP * tokens
    length = N_CTX * tokens
    anywhere = pl.BlockSpec(memory_space=pl.ANY)
    vmem = pl.BlockSpec(memory_space=pltpu.VMEM)
    weights = (N_FS, rows, width + 2 * kv_width)
    full_o = (N_FS, rows, width)
    kv = (N_CTX, tokens + 16, 2 * kv_width)
    expo = (KV_HEADS, length, wide)
    return pl.pallas_call(
        front_kernel,
        name="front",
        out_shape=[
            jax.ShapeDtypeStruct(weights, BF),
            jax.ShapeDtypeStruct(full_o, BF),
            jax.ShapeDtypeStruct(kv, BF),
            jax.ShapeDtypeStruct((2, N_FS, 4, cut, units), BF),
            jax.ShapeDtypeStruct((N_FS, tokens, width), BF),
            jax.ShapeDtypeStruct(expo, BF),
            jax.ShapeDtypeStruct((2, width), F32),
            jax.ShapeDtypeStruct((tokens, width), BF),
            jax.ShapeDtypeStruct((KV_HEADS, wide, HD), BF),
            jax.ShapeDtypeStruct((KV_HEADS, HD, wide), F32),
            jax.ShapeDtypeStruct((KV_HEADS, 8, wide), F32),
            jax.ShapeDtypeStruct((tokens, width), BF),
            jax.ShapeDtypeStruct((tokens, width), F32),
            jax.ShapeDtypeStruct((tokens, width), BF),
        ],
        in_specs=[anywhere] * len(arrays) + [vmem] * len(vmem_arrays),
        out_specs=[anywhere] * 6 + [vmem] * 8,
        scratch_shapes=[
            pltpu.VMEM(weights, BF),
            pltpu.VMEM(full_o, BF),
            pltpu.VMEM((N_FS,) + vmem_arrays[0].shape, F32),
            pltpu.VMEM((2, cut, all_units), BF),
            pltpu.VMEM((N_FS, cut, units), BF),
            pltpu.VMEM((tokens, width), BF),
            pltpu.VMEM(kv[1:], BF),
            pltpu.VMEM(kv, BF),
            pltpu.VMEM((length, wide), F32),
            pltpu.VMEM(expo, BF),
            pltpu.SemaphoreType.DMA((104,)),
            pltpu.SemaphoreType.DMA((104,)),
            pltpu.SemaphoreType.DMA((10,)),
        ],
        compiler_params=pltpu.CompilerParams(
            collective_id=cid, has_side_effects=True, vmem_limit_bytes=60 * 2**20
        ),
    )(*arrays, *vmem_arrays)


def back_kernel(
    nm_ref,
    cot_ref,
    gu_ref,
    down_ref,
    expo_hbm,
    kv_hbm,
    o_hbm,
    middle_hbm,
    query_hbm,
    mixed_hbm,
    attended_hbm,
    normed_hbm,
    qkv_hbm,
    gains_ref,
    inv_ref,
    cos_ref,
    sin_ref,
    input_ref,
    all_gu,
    all_dn,
    all_at,
    out_ref,
    out_in,
    gu_x,
    dn_x,
    o_far,
    q_far,
    kv_far,
    vec_sum,
    out_rows,
    in_rows,
    nm,
    part_in,
    gu_in,
    dn_in,
    gu_z,
    dn_z,
    kv_in,
    o_in,
    q_in,
    o_over,
    q_over,
    kv_over,
    q_grad,
    mid_ref,
    gain_grad,
    done_gu,
    done_dn,
    own_gu,
    kv_part,
    kv_parts,
    at_far,
    at_own,
    vec,
    vec_fs,
    vec_mid,
    vec_ctx,
    own_send,
    own_recv,
    part_send,
    part_recv,
    send,
    recv,
    local,
):
    c, f = lax.axis_index("ctx"), lax.axis_index("fsdp")
    core, pair_at = lax.rem(c, 2), lax.div(c, 2)
    x_at, z_at = lax.rem(pair_at, 4), lax.div(pair_at, 4)
    sibling = (flip(c, 1), f)
    partner = (flip(c, 8), f)
    ring = [(flip(c, 2 * i), f) for i in range(1, N_CTX // 2)]
    along = ring[:3]
    peers = [(c, flip(f, i)) for i in range(1, N_FS)]
    greet(ring + peers + [(flip(c, 8), flip(f, i)) for i in range(4, N_FS)] + [sibling])
    copies = Copies(send, recv)
    tokens, width = nm_ref.shape
    units = down_ref.shape[0]
    rows = 2 * tokens
    every = N_FS * tokens
    window, strip = done_dn.shape
    half = units // 2
    side = width // 2
    length = N_CTX * tokens
    scale = HD ** (-0.5)
    near, turn = peers[:3], peers[3]
    cos_wide = jnp.concatenate([cos_ref[...], cos_ref[...]], axis=1)
    sin_wide = jnp.concatenate([sin_ref[...], -sin_ref[...]], axis=1)

    def local_copy(src, dst, n):
        copy = pltpu.make_async_copy(src, dst, local.at[n])
        copy.start()
        return copy

    upper, lower = pl.ds(0, tokens // 2), pl.ds(tokens // 2, tokens // 2)
    up_y = [copies.start(nm_ref.at[upper], nm.at[i + 1, upper], near[i]) for i in range(3)]
    low_z = copies.start(nm_ref.at[lower], nm.at[4, lower], turn)
    low_y = [copies.start(nm_ref.at[lower], nm.at[i + 1, lower], near[i]) for i in range(3)]
    up_z = [copies.start(nm_ref.at[upper], nm.at[4, upper], turn)]

    def part_copy(part, i):
        return pltpu.make_async_remote_copy(
            src_ref=part.at[i],
            dst_ref=part_in.at[i],
            send_sem=part_send.at[i],
            recv_sem=part_recv.at[i],
            device_id=(c, flip(f, i)),
            device_id_type=MESH,
        )

    def x_of(device):
        return lax.rem(lax.div(device[0], 2), 4)

    def strip_of(ref, x):
        return ref.at[:, pl.ds(pl.multiple_of(x * strip, strip), strip)]

    def owner_rows(ref, owner):
        return ref.at[pl.ds(pl.multiple_of(owner * 192, 192), 192)]

    low_y += [
        copies.make(nm.at[4, lower], nm.at[4 + i, lower], near[i - 1]) for i in range(1, 4)
    ]
    up_z += [copies.make(nm.at[i, upper], nm.at[4 + i, upper], turn) for i in range(1, 4)]
    count = N_FS // 2

    def owners_of(z):
        return pl.ds(pl.multiple_of(z * count, count), count)

    def window_of(z):
        return pl.ds(pl.multiple_of(z * (half - window), 16), window)

    x_first, x_second = (
        [
            copies.make(gu_in.at[owners_of(z), x_of(device)], gu_x.at[i, owners_of(z)], device)
            for i, device in enumerate(along)
        ]
        for z in (1 - z_at, z_at)
    )
    z_gu = copies.make(gu_in.at[owners_of(1 - z_at), x_at], gu_z, partner)
    z_dn = copies.make(dn_in.at[window_of(1 - z_at)], dn_z, partner)
    x_dn = [
        copies.make(strip_of(dn_z, x_of(device)), dn_x.at[i], device)
        for i, device in enumerate(along)
    ]

    def sum_gu_x(z, gu_buf, n):
        local_copy(gu_x.at[:, owners_of(z)], gu_buf, n).wait()

        def step(j, carry):
            total = gu_in[z * count + j, x_at].astype(F32)
            for i in range(3):
                total = total + gu_buf[i, j].astype(F32)
            gu_in[z * count + j, x_at] = total.astype(BF)
            return carry

        lax.fori_loop(0, count, step, 0)

    plane = lax.div(f, 4)
    over = (c + core * (flip(c, 8) - c), flip(f, 4))
    block = 4 * 192

    def plane_rows(which):
        return pl.ds(pl.multiple_of(which * block, block), block)

    o_z = copies.make(o_in.at[plane_rows(1 - plane)], o_over, over)
    q_z = copies.make(q_in.at[plane_rows(1 - plane)], q_over, over)
    o_sends = [
        copies.make(owner_rows(o_in, peer[1]), o_far.at[i], peer) for i, peer in enumerate(near)
    ]
    q_sends = [
        copies.make(owner_rows(q_in, peer[1]), q_far.at[i], peer) for i, peer in enumerate(near)
    ]

    def add_over(ref, came):
        def step(m, carry):
            at = pl.multiple_of(m * 192, 192)
            rows = pl.ds(pl.multiple_of(plane * block + m * 192, 192), 192)
            ref[rows, :] = (ref[rows, :].astype(F32) + came[pl.ds(at, 192), :].astype(F32)).astype(BF)
            return carry

        lax.fori_loop(0, 4, step, 0)
    out_sends = [copies.make(out_ref.at[i + 1], out_in.at[i], near[i]) for i in range(3)]
    out_sends += [copies.make(out_ref.at[i + 5], out_in.at[i + 3], near[i]) for i in range(3)]
    kv_sends = [
        copies.make(kv_in.at[lax.div(device[0], 2)], kv_far.at[i], device)
        for i, device in enumerate(ring)
    ]

    def begin(group):
        for copy in group:
            copy.start()

    def feed_forward(cot, gu, down, act, low, part, outs):
        loads = [
            local_copy(nm_ref, nm.at[0], 0),
            local_copy(gu_ref, gu, 1),
            local_copy(cot_ref, cot, 2),
            local_copy(down_ref, down, 3),
        ]
        for load in loads:
            load.wait()

        def weight(which):
            return gu[which].reshape(width, units)

        saves = []

        def pair(s):
            at = s * rows
            span = slice(at, at + rows)
            x = nm[2 * s : 2 * s + 2].reshape(rows, width)
            gate = jnp.dot(x, weight(0), preferred_element_type=F32)
            up = jnp.dot(x, weight(1), preferred_element_type=F32)
            grad = contract_cols(cot[2 * s : 2 * s + 2].reshape(rows, width), down[...])
            sigma = jax.nn.sigmoid(gate)
            swish = gate * sigma
            act[span, :] = (swish * up).astype(BF)
            low[0, span, :] = (grad * up * sigma * (1.0 + gate * (1.0 - sigma))).astype(BF)
            low[1, span, :] = (grad * swish).astype(BF)
            summed = contract_cols(low[0, span, :], weight(0))
            summed = summed + contract_cols(low[1, span, :], weight(1))
            part[2 * s : 2 * s + 2] = summed.astype(BF).reshape(2, tokens, width)
            for i in (2 * s, 2 * s + 1):
                if i:
                    part_copy(part, i).start()
            if s > 1:
                saves[s - 2].wait()
            result = jnp.dot(act[span, :], down[...], preferred_element_type=F32)
            outs[s % 2] = result.astype(BF).reshape(2, tokens, width)
            saves.append(local_copy(outs.at[s % 2], out_ref.at[pl.ds(2 * s, 2)], 4 + s % 2))

        def arrived(i):
            up_y[i - 1].wait_recv()
            up_z[i].start()
            low_y[i - 1].wait_recv()

        arrived(1)
        pair(0)
        low_z.wait_recv()
        begin(low_y[3:])
        arrived(2)
        arrived(3)
        pair(1)
        up_z[0].wait_recv()
        up_z[1].wait_recv()
        low_y[3].wait_recv()
        pair(2)
        for i in (2, 3):
            up_z[i].wait_recv()
            low_y[2 + i].wait_recv()
        pair(3)

        def gate_up(which):
            def step(m, carry):
                at = pl.multiple_of(m * 384, 384)
                x = nm[:, :, pl.ds(at, 384)].reshape(every, 384)
                grad = contract_rows(x, low[which]).astype(BF)
                gu[which, pl.ds(2 * m, 2)] = grad.reshape((2,) + gu.shape[2:])
                return carry

            lax.fori_loop(0, width // 384, step, 0)

        gate_up(1 - core)
        swap_gu = copies.start(gu.at[1 - core], gu_in, sibling)
        gate_up(core)
        swap_gu.wait_recv()

        def add_gu(g, carry):
            gu_in[g] = (gu[core, g].astype(F32) + gu_in[g].astype(F32)).astype(BF)
            return carry

        lax.fori_loop(0, N_FS, add_gu, 0)
        begin(x_first)
        begin(x_second)
        turned = cot[...].reshape(every, width)

        def down_rows(m, carry):
            at = pl.multiple_of(m * 256, 256)
            down[pl.ds(at, 256), :] = contract_rows(act[:, pl.ds(at, 256)], turned).astype(BF)
            return carry

        whole = units // 256
        lax.fori_loop(0, whole, down_rows, 0)
        if units % 256:
            down[whole * 256 :, :] = contract_rows(act[:, whole * 256 :], turned).astype(BF)
        swap_dn = copies.start(
            down.at[pl.ds(pl.multiple_of((1 - core) * half, 16), half)], dn_in, sibling
        )
        swap_dn.wait_recv()

        def add_dn(m, carry):
            at = pl.multiple_of(m * 112, 16)
            own = down[pl.ds(pl.multiple_of(core * half + m * 112, 16), 112), :]
            dn_in[pl.ds(at, 112), :] = (
                own.astype(F32) + dn_in[pl.ds(at, 112), :].astype(F32)
            ).astype(BF)
            return carry

        lax.fori_loop(0, half // 112, add_dn, 0)
        z_dn.start()
        total = part[0].astype(F32)
        for i in range(1, N_FS):
            part_copy(part, i).wait_recv()
            total = total + part_in[i].astype(F32)
        mid_ref[...] = total
        for i in range(1, N_FS):
            part_copy(part, i).wait_send()
        for copy in [swap_gu, swap_dn]:
            copy.wait_send()
        for copy in saves[2:]:
            copy.wait()

    pl.run_scoped(
        feed_forward,
        pltpu.VMEM(cot_ref.shape, BF),
        pltpu.VMEM(gu_ref.shape, BF),
        pltpu.VMEM(down_ref.shape, BF),
        pltpu.VMEM((every, units), BF),
        pltpu.VMEM((2, every, units), BF),
        pltpu.VMEM((N_FS, tokens, width), BF),
        pltpu.VMEM((2, 2, tokens, width), BF),
    )
    begin(out_sends)

    def columns_of(which):
        return pl.ds(pl.multiple_of(which * side, side), side)

    def half_product(left, right, which, out):
        def step(m, carry):
            at = pl.multiple_of(m * 256, 256)
            out[pl.ds(at, 256), :] = contract_rows(
                left[:, pl.ds(at, 256)], right[:, columns_of(which)]
            ).astype(BF)
            return carry

        lax.fori_loop(0, width // 256, step, 0)

    def add_product(left, right, out):
        def step(m, carry):
            at = pl.multiple_of(m * 256, 256)
            product = contract_rows(left[:, pl.ds(at, 256)], right[:, columns_of(core)])
            out[pl.ds(at, 256), :] = (product + out[pl.ds(at, 256), :].astype(F32)).astype(BF)
            return carry

        lax.fori_loop(0, width // 256, step, 0)

    def attention(branch, back, attended, normed, out_half, dkv):
        load_at = local_copy(attended_hbm, attended, 0)
        load_nm = local_copy(normed_hbm, normed, 1)

        def second_norm(full_o, middle_ref):
            load_mid = local_copy(middle_hbm, middle_ref, 2)
            load_o = local_copy(o_hbm, full_o, 3)
            load_mid.wait()
            middle = middle_ref[...]
            scale_two = lax.rsqrt(jnp.mean(middle * middle, axis=-1, keepdims=True) + EPSILON)
            norm = middle * scale_two
            grad = mid_ref[...]
            gain_grad[...] = jnp.sum(grad * norm, axis=0, keepdims=True)
            scaled = grad * gains_ref[1:2, :]
            cot_copy = local_copy(cot_ref.at[0], back, 6)
            cot_copy.wait()
            mid = back[...].astype(F32) + scale_two * (
                scaled - norm * jnp.mean(scaled * norm, axis=-1, keepdims=True)
            )
            mid_ref[...] = mid
            branch[...] = mid.astype(BF)
            load_o.wait()
            back[...] = contract_cols(branch[...], full_o[...]).astype(BF)

        pl.run_scoped(second_norm, pltpu.VMEM(o_hbm.shape, BF), pltpu.VMEM((tokens, width), F32))
        load_at.wait()
        load_nm.wait()
        half_product(attended, branch, 1 - core, out_half)
        swap_o = copies.start(out_half, o_in, sibling)

        def heads(expo, kv, query_ref, mixed_ref, gu_buf):
            loads = [
                local_copy(kv_hbm, kv, 2),
                local_copy(query_hbm, query_ref, 3),
                local_copy(mixed_hbm, mixed_ref, 4),
                local_copy(expo_hbm, expo, 5),
            ]
            for load in loads:
                load.wait()
            for h in range(KV_HEADS):
                if h == 1:
                    swap_o.wait_recv()
                    add_product(attended, branch, o_in)
                    o_z.start()
                    for copy in x_first:
                        copy.wait_recv()
                    sum_gu_x(1 - z_at, gu_buf, 6)
                    z_gu.start()
                query = query_ref[h]
                head = back[:, h * GROUP * HD : (h + 1) * GROUP * HD]
                grads = jnp.concatenate(
                    [head[:, i * HD : (i + 1) * HD] for i in range(GROUP)], axis=0
                )
                inverse = inv_ref[h, 0:1, :]
                turned = grads.astype(F32).T
                weighted = jnp.sum(turned * mixed_ref[h], axis=0, keepdims=True)
                factor = inverse * scale
                offset = weighted * factor
                grads_scaled = (turned * inverse).T.astype(BF)
                dq = jnp.zeros((HD, GROUP * tokens), F32)
                for j in range(length // CHUNK):
                    part = expo[h, j * CHUNK : (j + 1) * CHUNK, :]
                    cols = slice(h * HD, (h + 1) * HD)
                    keys = kv[2 * j : 2 * j + 2, :tokens, cols].reshape(CHUNK, HD)
                    v_cols = slice((KV_HEADS + h) * HD, (KV_HEADS + h + 1) * HD)
                    values = kv[2 * j : 2 * j + 2, :tokens, v_cols].reshape(CHUNK, HD)
                    prob_grad = contract_cols(values, grads)
                    score_grad = (part.astype(F32) * (prob_grad * factor - offset)).astype(BF)
                    dk = jnp.dot(score_grad, query, preferred_element_type=F32).astype(BF)
                    dv = jnp.dot(part, grads_scaled, preferred_element_type=F32).astype(BF)
                    for side_core in range(2):
                        cut = slice(side_core * tokens, (side_core + 1) * tokens)
                        dkv[side_core, j, :, cols] = dk[cut]
                        dkv[side_core, j, :, v_cols] = dv[cut]
                    dq = dq + contract_rows(keys, score_grad)
                for i in range(GROUP):
                    at = (h * GROUP + i) * HD
                    q_grad[:, at : at + HD] = turn_back(
                        dq[:, i * tokens : (i + 1) * tokens].T, cos_wide, sin_wide
                    ).astype(BF)

        pl.run_scoped(
            heads,
            pltpu.VMEM(expo_hbm.shape, BF),
            pltpu.VMEM(kv_hbm.shape, BF),
            pltpu.VMEM(query_hbm.shape, BF),
            pltpu.VMEM(mixed_hbm.shape, F32),
            pltpu.VMEM((3, count) + gu_x.shape[2:], BF),
        )
        swap_kv = copies.start(dkv.at[1 - core], kv_in, sibling)

        swap_o.wait_send()
        half_product(normed, q_grad, 1 - core, out_half)
        swap_q = copies.start(out_half, q_in, sibling)
        swap_kv.wait_recv()
        kv_in[...] = (dkv[core].astype(F32) + kv_in[...].astype(F32)).astype(BF)
        begin(kv_sends)
        z_dn.wait_recv()
        dn_z[...] = (dn_z[...].astype(F32) + dn_in[window_of(z_at), :].astype(F32)).astype(BF)
        begin(x_dn)
        o_z.wait_recv()
        add_over(o_in, o_over)
        begin(o_sends)
        swap_q.wait_recv()
        add_product(normed, q_grad, q_in)
        swap_kv.wait_send()
        swap_q.wait_send()

    pl.run_scoped(
        attention,
        pltpu.VMEM((tokens, width), BF),
        pltpu.VMEM((tokens, width), BF),
        pltpu.VMEM((tokens, width), BF),
        pltpu.VMEM((tokens, width), BF),
        pltpu.VMEM((width, side), BF),
        pltpu.VMEM((2, N_CTX // 2, tokens, kv_in.shape[2]), BF),
    )

    here, far = (c, f), (partner[0], f)
    x_one, x_two, x_three = along
    kv_width = KV_HEADS * HD
    at_rows, at_cols = at_own.shape

    def z_of(device):
        return lax.div(device[0], 8)

    def gu_place(device, part=None):
        size = count if part is None else count // 2
        start = count * z_of(device) + (0 if part is None else part * size)
        return all_gu.at[lax.rem(device[0], 2), x_of(device), pl.ds(start, size)]

    def dn_place(device, part=None):
        columns = pl.ds(pl.multiple_of(x_of(device) * strip, strip), strip)
        size = window // (1 if part is None else 2)
        span = pl.ds(0 if part is None else part * size, size)
        return all_dn.at[lax.rem(device[0], 2), z_of(device), span, columns]

    def at_span(device):
        return (
            pl.ds(pl.multiple_of(x_of(device) * at_rows, at_rows), at_rows),
            pl.ds(pl.multiple_of(z_of(device) * at_cols, at_cols), at_cols),
        )

    def at_place(device):
        return all_at.at[(lax.rem(device[0], 2),) + at_span(device)]

    def tail(gu_buf, dn_buf, far_buf, kv_buf, full_qkv, proj, kv_out, kv_keep, at_all, out_buf):
        rest, own = [], []
        load_qkv = local_copy(qkv_hbm, full_qkv, 0)
        load_nm = local_copy(normed_hbm, out_buf.at[N_FS - 1], 1)

        for copy in x_second:
            copy.wait_recv()
        sum_gu_x(z_at, gu_buf, 2)
        z_gu.wait_recv()

        def add_gu_z(j, carry):
            mine = gu_in[z_at * count + j, x_at].astype(F32)
            done_gu[j] = (mine + gu_z[j].astype(F32)).astype(BF)
            return carry

        lax.fori_loop(0, count, add_gu_z, 0)
        spot = lax.rem(f, 4)
        owners = [
            (8 * plane + lax.rem(c, 8), 4 * z_at + lax.rem(flip(f, i), 4)) for i in range(4)
        ]

        def gu_copy(i):
            return pltpu.make_async_remote_copy(
                src_ref=done_gu.at[lax.rem(flip(f, i), 4)],
                dst_ref=own_gu.at[spot],
                send_sem=own_send.at[i],
                recv_sem=own_recv.at[i],
                device_id=owners[i],
                device_id_type=MESH,
            )

        gu_own = pltpu.make_async_copy(done_gu.at[spot], own_gu.at[spot], local.at[4])

        @pl.when(plane == z_at)
        def _():
            gu_own.start()

        @pl.when(plane != z_at)
        def _():
            gu_copy(0).start()

        for i in range(1, 4):
            gu_copy(i).start()
        q_z.start()

        load_qkv.wait()
        in_norm_grad = contract_cols(q_grad[...], full_qkv[:, :width])

        for copy in kv_sends:
            copy.wait_recv()
        local_copy(kv_far, kv_buf, 3).wait()
        total = kv_in[pair_at].astype(F32)
        for i in range(N_CTX // 2 - 1):
            total = total + kv_buf[i].astype(F32)
        for h in range(KV_HEADS):
            at = width + h * HD
            proj[:, at : at + HD] = turn_back(
                total[:, h * HD : (h + 1) * HD], cos_wide, sin_wide
            ).astype(BF)
        proj[:, width + kv_width :] = total[:, kv_width:].astype(BF)
        proj[:, :width] = q_grad[...]

        def side_of(which):
            return pl.ds(pl.multiple_of(width + which * kv_width, kv_width), kv_width)

        load_nm.wait()
        normed = out_buf[N_FS - 1]
        kv_out[...] = contract_rows(normed, proj[:, side_of(1 - core)]).astype(BF)
        swap_part = copies.start(kv_out, kv_part, sibling)
        kv_keep[...] = contract_rows(normed, proj[:, side_of(core)]).astype(BF)

        swap_part.wait_recv()
        kv_part[...] = (kv_part[...].astype(F32) + kv_keep[...].astype(F32)).astype(BF)

        def rows_of(owner):
            return pl.ds(pl.multiple_of(owner * 192, 192), 192)

        part_z = copies.start(kv_part.at[plane_rows(1 - plane)], kv_over, over)
        q_z.wait_recv()
        add_over(q_in, q_over)
        begin(q_sends)

        @pl.when(plane == z_at)
        def _():
            gu_own.wait()

        @pl.when(plane != z_at)
        def _():
            gu_copy(0).wait()

        for i in range(1, 4):
            gu_copy(i).wait()
        gather_z = [copies.start(own_gu, gu_place(here), partner)]
        gu_xs = [copies.start(own_gu, gu_place(here), device) for device in (x_one, x_three)]
        rest.append(copies.start(own_gu, gu_place(here), sibling))
        own.append(local_copy(own_gu, gu_place(here), 6))

        forwards = []

        def around(place, one, three, z):
            sent = []
            for copy, device, part, other in ((one, x_one, 0, x_three), (three, x_three, 1, x_one)):
                at = (flip(device[0], 8), f) if z else device
                copy.wait_recv()
                sent.append(copies.start(place(at, part), place(at, part), other))
                rest.append(copies.start(place(at), place(at), sibling))
            forwards.extend(sent)
            return sent

        def opposite(place, sent, z):
            at = (flip(x_two[0], 8), f) if z else x_two
            for copy in sent:
                copy.wait_recv()
            rest.append(copies.start(place(at), place(at), sibling))

        part_z.wait_recv()
        add_over(kv_part, kv_over)
        part_sends = [
            copies.start(kv_part.at[rows_of(peer[1])], kv_parts.at[i], peer)
            for i, peer in enumerate(near)
        ]

        in_norm_grad = in_norm_grad + contract_cols(proj[:, width:], full_qkv[:, width:])
        inputs = input_ref[...].astype(F32)
        scale_one = lax.rsqrt(jnp.mean(inputs * inputs, axis=-1, keepdims=True) + EPSILON)
        norm = inputs * scale_one
        gain_one_grad = jnp.sum(in_norm_grad * norm, axis=0, keepdims=True)
        scaled = in_norm_grad * gains_ref[0:1, :]
        in_rows[...] = mid_ref[...] + scale_one * (
            scaled - norm * jnp.mean(scaled * norm, axis=-1, keepdims=True)
        )
        bias_grad = jnp.sum(proj[...].astype(F32), axis=0, keepdims=True)
        row = 0
        for vector in (gain_one_grad, gain_grad[...], bias_grad):
            for n in range(vector.shape[1] // 128):
                vec[row : row + 1, :] = vector[:, n * 128 : (n + 1) * 128]
                row += 1
        vec_sends = [copies.start(vec, vec_fs.at[i], peer) for i, peer in enumerate(peers)]


        gather_z[0].wait_recv()
        gu_xs2 = [copies.start(gu_place(far), gu_place(far), device) for device in (x_one, x_three)]
        rest.append(copies.start(gu_place(far), gu_place(far), sibling))
        load_mid = local_copy(middle_hbm, mid_ref, 10)
        gu_f = around(gu_place, *gu_xs, False)
        for copy in x_dn:
            copy.wait_recv()
        local_copy(dn_x, dn_buf, 5).wait()
        total = dn_z[:, pl.ds(pl.multiple_of(x_at * strip, strip), strip)].astype(F32)
        for i in range(3):
            total = total + dn_buf[i].astype(F32)
        done_dn[...] = total.astype(BF)
        own.append(local_copy(done_dn, dn_place(here), 7))
        gather_z.append(copies.start(done_dn, dn_place(here), partner))
        dn_xs = [copies.start(done_dn, dn_place(here), device) for device in (x_one, x_three)]
        rest.append(copies.start(done_dn, dn_place(here), sibling))

        owned = pl.ds(pl.multiple_of(f * 192, 192), 192)
        for n, (ref, sends, arrived) in enumerate(((o_in, o_sends, o_far), (q_in, q_sends, q_far))):
            for copy in sends:
                copy.wait_recv()
            local_copy(arrived, far_buf, 8 + n).wait()
            total = ref[owned, :].astype(F32)
            for i in range(3):
                total = total + far_buf[i].astype(F32)
            at_all[:, n * side : (n + 1) * side] = total.astype(BF)
        for copy in part_sends:
            copy.wait_recv()
        total = kv_part[owned, :].astype(F32)
        for i in range(3):
            total = total + kv_parts[i].astype(F32)
        at_all[:, 2 * side :] = total.astype(BF)
        at_sends = [
            copies.start(at_all.at[at_span(device)], at_far.at[i], device)
            for i, device in enumerate(ring)
        ]
        for copy in out_sends:
            copy.wait_recv()
        local_copy(out_ref.at[4], out_buf.at[1], 2).wait()
        local_copy(out_in.at[pl.ds(3, 3)], out_buf.at[pl.ds(2, 3)], 3).wait()
        total = out_buf[1].astype(F32)
        for i in range(3):
            total = total + out_buf[2 + i].astype(F32)
        out_buf[0] = total.astype(BF)

        gather_z[1].wait_recv()
        dn_xs2 = [copies.start(dn_place(far), dn_place(far), device) for device in (x_one, x_three)]
        rest.append(copies.start(dn_place(far), dn_place(far), sibling))
        gu_f2 = around(gu_place, *gu_xs2, True)
        for copy in vec_sends:
            copy.wait_recv()
        total = vec[...]
        for i in range(N_FS - 1):
            total = total + vec_fs[i]
        vec_mid[...] = total
        vec_near = [copies.start(vec_mid, vec_ctx.at[c], device) for device in ring]
        rest.append(copies.start(vec_mid, vec_ctx.at[c], sibling))
        vec_ctx[pl.ds(c, 1)] = total[None]
        for copy in at_sends:
            copy.wait_recv()
        total = at_all[at_span(here)].astype(F32)
        for i in range(N_CTX // 2 - 1):
            total = total + at_far[i].astype(F32)
        at_own[...] = total.astype(BF)
        at_near = [copies.start(at_own, at_place(here), device) for device in ring]
        rest.append(copies.start(at_own, at_place(here), sibling))
        out_z = copies.start(out_buf.at[0], out_in.at[N_FS - 2], turn)
        own.append(local_copy(at_own, at_place(here), 11))
        dn_f = around(dn_place, *dn_xs, False)
        for copy, device in zip(vec_near, ring):
            copy.wait_recv()
            place = vec_ctx.at[device[0]]
            rest.append(copies.start(place, place, sibling))
        dn_f2 = around(dn_place, *dn_xs2, True)
        opposite(gu_place, gu_f, False)
        opposite(dn_place, dn_f, False)
        out_z.wait_recv()
        local_copy(out_ref.at[0], out_buf.at[1], 1).wait()
        local_copy(out_in.at[pl.ds(0, 3)], out_buf.at[pl.ds(2, 3)], 3).wait()
        local_copy(out_in.at[N_FS - 2], out_buf.at[5], 2).wait()
        load_mid.wait()
        total = mid_ref[...]
        for i in range(1, 6):
            total = total + out_buf[i].astype(F32)
        out_rows[...] = total.astype(BF)
        opposite(gu_place, gu_f2, True)
        opposite(dn_place, dn_f2, True)
        for copy, device in zip(at_near, ring):
            copy.wait_recv()
            rest.append(copies.start(at_place(device), at_place(device), sibling))
        for copy in (
            [swap_part, part_z, out_z] + part_sends + gather_z + gu_xs + dn_xs + gu_xs2 + dn_xs2
            + forwards + at_sends + at_near + vec_sends + vec_near
        ):
            copy.wait_send()
        for copy in rest:
            copy.wait()
        total = vec_ctx[0]
        for i in range(1, N_CTX):
            total = total + vec_ctx[i]
        vec_sum[...] = total
        for copy in own:
            copy.wait()

    pl.run_scoped(
        tail,
        pltpu.VMEM((3, count) + gu_x.shape[2:], BF),
        pltpu.VMEM(dn_x.shape, BF),
        pltpu.VMEM(o_far.shape, BF),
        pltpu.VMEM(kv_far.shape, BF),
        pltpu.VMEM(qkv_hbm.shape, BF),
        pltpu.VMEM((tokens, qkv_hbm.shape[1]), BF),
        pltpu.VMEM(kv_part.shape, BF),
        pltpu.VMEM(kv_part.shape, BF),
        pltpu.VMEM((width // N_FS, width + kv_width), BF),
        pltpu.VMEM((N_FS, tokens, width), BF),
    )
    for copy in (
        up_y + [low_z] + low_y + up_z + x_first + x_second + x_dn + o_sends + q_sends + kv_sends + out_sends
        + [o_z, q_z, z_gu, z_dn]
    ):
        copy.wait_send()


def backward(cid, arrays, vmem_arrays):
    normed, cot_all, columns, down_weight, expo, kv_all, full_o = arrays[:7]
    tokens, width = normed.shape
    units = down_weight.shape[0]
    piece = columns.shape[3]
    half = units // 2
    strip = width // 4
    window = half // 2 + 8
    side = width // 2
    kv_width = KV_HEADS * HD
    rows = width // N_FS
    anywhere = pl.BlockSpec(memory_space=pl.ANY)
    vmem = pl.BlockSpec(memory_space=pltpu.VMEM)
    at_width = width + kv_width
    in_place = [
        ((2, 4, N_FS, piece, units), BF),
        ((2, 2, window, width), BF),
        ((2, rows, at_width), BF),
        ((N_FS, tokens, width), BF),
        ((N_FS - 1, tokens, width), BF),
        ((3, N_FS, piece, units), BF),
        ((3, window, strip), BF),
        ((3, rows, side), BF),
        ((3, rows, side), BF),
        ((N_CTX // 2 - 1, tokens, 2 * kv_width), BF),
    ]
    in_vmem = [((40, 128), F32), ((tokens, width), BF), ((tokens, width), F32)]
    results = pl.pallas_call(
        back_kernel,
        name="back",
        out_shape=[jax.ShapeDtypeStruct(*o) for o in in_place + in_vmem],
        in_specs=[anywhere] * len(arrays) + [vmem] * len(vmem_arrays),
        out_specs=[anywhere] * len(in_place) + [vmem] * len(in_vmem),
        scratch_shapes=[
            pltpu.VMEM((N_FS, tokens, width), BF),
            pltpu.VMEM((N_FS, tokens, width), BF),
            pltpu.VMEM((N_FS, 4, piece, units), BF),
            pltpu.VMEM((half, width), BF),
            pltpu.VMEM((N_FS // 2, piece, units), BF),
            pltpu.VMEM((window, width), BF),
            pltpu.VMEM((N_CTX // 2, tokens, 2 * kv_width), BF),
            pltpu.VMEM((width, side), BF),
            pltpu.VMEM((width, side), BF),
            pltpu.VMEM((width // 2, side), BF),
            pltpu.VMEM((width // 2, side), BF),
            pltpu.VMEM((width // 2, kv_width), BF),
            pltpu.VMEM((tokens, width), BF),
            pltpu.VMEM((tokens, width), F32),
            pltpu.VMEM((1, width), F32),
            pltpu.VMEM((N_FS // 2, piece, units), BF),
            pltpu.VMEM((window, strip), BF),
            pltpu.VMEM((N_FS // 2, piece, units), BF),
            pltpu.VMEM((width, kv_width), BF),
            pltpu.VMEM((3, rows, kv_width), BF),
            pltpu.VMEM((N_CTX // 2 - 1, rows // 4, at_width // 2), BF),
            pltpu.VMEM((rows // 4, at_width // 2), BF),
            pltpu.VMEM((40, 128), F32),
            pltpu.VMEM((N_FS - 1, 40, 128), F32),
            pltpu.VMEM((40, 128), F32),
            pltpu.VMEM((N_CTX, 40, 128), F32),
            pltpu.SemaphoreType.DMA((4,)),
            pltpu.SemaphoreType.DMA((4,)),
            pltpu.SemaphoreType.DMA((N_FS,)),
            pltpu.SemaphoreType.DMA((N_FS,)),
            pltpu.SemaphoreType.DMA((150,)),
            pltpu.SemaphoreType.DMA((150,)),
            pltpu.SemaphoreType.DMA((12,)),
        ],
        compiler_params=pltpu.CompilerParams(
            collective_id=cid, has_side_effects=True, vmem_limit_bytes=62 * 2**20
        ),
    )(*arrays, *vmem_arrays)
    return results[:3] + results[len(in_place) :]


def wide_kernel(gu_ref, gate_ref, up_ref):
    for which, out in enumerate((gate_ref, up_ref)):
        out[...] = jnp.concatenate(
            [gu_ref[which, 0, source].astype(F32) for source in range(N_FS)], axis=1
        )


def wide_results(all_gu):
    piece, units = all_gu.shape[3:]
    parts = all_gu.shape[1]
    shape = jax.ShapeDtypeStruct((parts * piece, N_FS * units), F32)
    return pl.pallas_call(
        wide_kernel,
        name="wide_results",
        grid=(parts,),
        in_specs=[pl.BlockSpec((2, 1, N_FS, piece, units), lambda p: (0, p, 0, 0, 0))],
        out_specs=[pl.BlockSpec((piece, N_FS * units), lambda p: (p, 0))] * 2,
        out_shape=[shape, shape],
        compiler_params=pltpu.CompilerParams(vmem_limit_bytes=60 * 2**20),
    )(all_gu)


def rest_kernel(dn_ref, at_ref, down_ref, o_ref, q_ref, k_ref, v_ref):
    z = lax.rem(pl.program_id(0), 2)
    rows = down_ref.shape[0]
    block = dn_ref[0, 0].astype(F32)
    down_ref[...] = jnp.where(z == 0, block[:rows], block[8 : 8 + rows])
    side = o_ref.shape[1] // 2
    for n in range(2):
        part = at_ref[n].astype(F32)
        o_ref[:, n * side : (n + 1) * side] = part[:, :side]
        q_ref[:, n * side : (n + 1) * side] = part[:, side : 2 * side]
        (k_ref, v_ref)[n][...] = part[:, 2 * side :]


def rest_results(all_dn, all_at):
    window, width = all_dn.shape[2:]
    rows = window - 8
    own, at_width = all_at.shape[1:]
    kv_width = KV_HEADS * HD
    return pl.pallas_call(
        rest_kernel,
        name="rest_results",
        grid=(4,),
        in_specs=[
            pl.BlockSpec((1, 1, window, width), lambda n: (n // 2, n % 2, 0, 0)),
            pl.BlockSpec((2, own // 4, at_width), lambda n: (0, n, 0)),
        ],
        out_specs=[
            pl.BlockSpec((rows, width), lambda n: (n, 0)),
            pl.BlockSpec((own // 4, width), lambda n: (n, 0)),
            pl.BlockSpec((own // 4, width), lambda n: (n, 0)),
            pl.BlockSpec((own // 4, kv_width), lambda n: (n, 0)),
            pl.BlockSpec((own // 4, kv_width), lambda n: (n, 0)),
        ],
        out_shape=[
            jax.ShapeDtypeStruct((4 * rows, width), F32),
            jax.ShapeDtypeStruct((own, width), F32),
            jax.ShapeDtypeStruct((own, width), F32),
            jax.ShapeDtypeStruct((own, kv_width), F32),
            jax.ShapeDtypeStruct((own, kv_width), F32),
        ],
        compiler_params=pltpu.CompilerParams(vmem_limit_bytes=60 * 2**20),
    )(all_dn, all_at)


def body(
    layer_input,
    segments,
    positions,
    attn_norm,
    q_weight,
    q_bias,
    k_weight,
    k_bias,
    v_weight,
    v_bias,
    o_weight,
    mlp_norm,
    gate_weight,
    up_weight,
    down_weight,
    out_cotangent,
):
    tokens, width = layer_input.shape[1:]
    rows = gate_weight.shape[0]
    units = gate_weight.shape[1] // N_FS
    q_width = HEADS * HD
    kv_width = KV_HEADS * HD
    half_block = tokens // 2
    ctx = lax.axis_index("ctx")
    segment = segments[0]
    small = jnp.concatenate([attn_norm, mlp_norm, q_bias, k_bias, v_bias]).astype(F32)[None]
    cosine, sine = rope_tables(positions[0], HD)
    within = jnp.arange(tokens, dtype=jnp.int32)
    row_place = jnp.where(
        within < half_block,
        ctx * half_block + within,
        (2 * N_CTX - 1 - ctx) * half_block + within - half_block,
    )
    row_info = jnp.stack([row_place.astype(F32), segment.astype(F32)])
    (
        full_qkv,
        full_o,
        kv_all,
        columns,
        cot_all,
        expo,
        gains,
        normed_in,
        query,
        mixed,
        inverse,
        attended,
        middle,
        normed_mid,
    ) = front(
        1,
        (q_weight, k_weight, v_weight, o_weight, gate_weight, up_weight),
        (small, layer_input[0], out_cotangent[0], row_info, cosine, sine),
    )
    full_qkv = full_qkv.reshape(width, q_width + 2 * kv_width)
    full_o = full_o.reshape(q_width, width)
    all_gu, all_dn, all_at, all_vec, output_rows, input_rows = backward(
        3,
        (
            normed_mid,
            cot_all,
            columns,
            down_weight,
            expo,
            kv_all,
            full_o,
            middle,
            query,
            mixed,
            attended,
            normed_in,
            full_qkv,
        ),
        (gains, inverse, cosine, sine, layer_input[0]),
    )
    gate_grad, up_grad = wide_results(all_gu)
    down_grad, o_grad, q_weight_grad, k_grad, v_grad = rest_results(all_dn, all_at)
    flat_vec = all_vec.reshape(-1)
    mine = lax.axis_index("fsdp")
    vectors = []
    start = 0
    for whole in (width, width, q_width, kv_width, kv_width):
        part = whole // N_FS
        vectors.append(lax.dynamic_slice_in_dim(flat_vec, start + mine * part, part, 0))
        start += whole
    return (
        output_rows[None],
        input_rows[None],
        vectors[0],
        q_weight_grad,
        vectors[2],
        k_grad,
        vectors[3],
        v_grad,
        vectors[4],
        o_grad,
        vectors[1],
        gate_grad,
        up_grad,
        down_grad,
    )


def solution(mesh):
    placed = (
        P("fsdp", "ctx", None),
        P("fsdp", "ctx"),
        P("fsdp", "ctx"),
        P("fsdp"),
        P("fsdp", None),
        P("fsdp"),
        P("fsdp", None),
        P("fsdp"),
        P("fsdp", None),
        P("fsdp"),
        P("fsdp", None),
        P("fsdp"),
        P("fsdp", None),
        P("fsdp", None),
        P("fsdp", None),
        P("fsdp", "ctx", None),
    )
    return jax.shard_map(
        body,
        mesh=mesh,
        in_specs=placed,
        out_specs=(
            P("fsdp", "ctx", None),
            P("fsdp", "ctx", None),
            P("fsdp"),
            P("fsdp", None),
            P("fsdp"),
            P("fsdp", None),
            P("fsdp"),
            P("fsdp", None),
            P("fsdp"),
            P("fsdp", None),
            P("fsdp"),
            P("fsdp", None),
            P("fsdp", None),
            P("fsdp", None),
        ),
        check_vma=False,
    )
```

```python
import functools

import jax
import jax.numpy as jnp
from jax import lax
from jax.experimental import pallas as pl
from jax.experimental.pallas import tpu as pltpu
from jax.sharding import PartitionSpec as P

HEADS = 12
KV_HEADS = 2
HD = 128
GROUP = HEADS // KV_HEADS
N_CTX = 16
N_FS = 8
EPSILON = 1e-06
THETA = 1000000.0
MESH = pl.DeviceIdType.MESH
BF = jnp.bfloat16
F32 = jnp.float32


def rope_tables(position, head_dim):
    freqs = THETA ** (-jnp.arange(0, head_dim, 2).astype(F32) / head_dim)
    angles = position.astype(F32)[:, None] * freqs[None, :]
    return (jnp.cos(angles), jnp.sin(angles))


def contract_rows(left, right):
    return lax.dot_general(
        left, right, (((0,), (0,)), ((), ())), preferred_element_type=F32
    )


def contract_cols(left, right):
    return lax.dot_general(
        left, right, (((1,), (1,)), ((), ())), preferred_element_type=F32
    )


def flip(value, mask):
    out = value
    bit = 1
    while bit <= mask:
        if mask & bit:
            out = out + bit * (1 - 2 * lax.rem(lax.div(value, bit), 2))
        bit *= 2
    return out


class Copies:
    def __init__(self, send, recv):
        self.send, self.recv, self.count = send, recv, 0

    def start(self, src, dst, device):
        copy = self.make(src, dst, device)
        copy.start()
        return copy

    def make(self, src, dst, device):
        copy = pltpu.make_async_remote_copy(
            src_ref=src,
            dst_ref=dst,
            send_sem=self.send.at[self.count],
            recv_sem=self.recv.at[self.count],
            device_id=device,
            device_id_type=MESH,
        )
        self.count += 1
        return copy


def greet(devices):
    barrier = pltpu.get_barrier_semaphore()
    for device in devices:
        pl.semaphore_signal(barrier, inc=1, device_id=device, device_id_type=MESH)
    pl.semaphore_wait(barrier, len(devices))


class SharedRows:
    def __init__(self, copies, ref, c, f, columns=None, direct=False):
        core = lax.rem(c, 2)
        self.copies, self.f = copies, f
        self.sibling = (flip(c, 1), f)
        self.over = (c + core * (flip(c, 8) - c), flip(f, 4))
        self.one, self.three = (c, flip(f, 1)), (c, flip(f, 3))
        rows = ref.shape[1] // 2

        def place(owner, part=None):
            if part is None:
                span = pl.ds(pl.multiple_of(core * rows, 16), rows)
            else:
                span = pl.ds(pl.multiple_of(core * rows + part * (rows // 2), 16), rows // 2)
            if columns is None:
                return ref.at[owner, span]
            return ref.at[owner, span, columns]

        self.place = place
        mine = place(f)
        self.from_one = copies.start(mine, mine, self.one)
        self.from_three = copies.start(mine, mine, self.three)
        self.z_copies = [copies.start(mine, mine, self.over)]
        self.sent = [self.from_one, self.from_three]
        self.far = [copies.start(mine, mine, (c, flip(f, 2)))] if direct else None
        self.rest = []

    def send(self, here, device):
        return self.copies.start(here, here, device)

    def pass_y(self):
        one, three = flip(self.f, 1), flip(self.f, 3)
        self.from_one.wait_recv()
        direct = self.far is not None
        if not direct:
            self.far = [self.send(self.place(one, 0), self.three)]
        self.z_copies.append(self.send(self.place(one), self.over))
        self.from_three.wait_recv()
        if not direct:
            self.far.append(self.send(self.place(three, 1), self.one))
        self.z_copies.append(self.send(self.place(three), self.over))
        self.rest.append(self.send(self.place(one), self.sibling))
        self.rest.append(self.send(self.place(three), self.sibling))
        for copy in self.far:
            copy.wait_recv()
        two = self.place(flip(self.f, 2))
        self.z_copies.append(self.send(two, self.over))
        self.rest.append(self.send(two, self.sibling))

    def pass_z(self):
        for copy, mask in zip(self.z_copies, (4, 5, 7, 6)):
            copy.wait_recv()
            self.rest.append(self.send(self.place(flip(self.f, mask)), self.sibling))

    def wait(self):
        for copy in self.rest:
            copy.wait_recv()

    def finish(self):
        for copy in self.sent + self.far + self.z_copies + self.rest:
            copy.wait_send()


CHUNK = 256


def turn_back(grad, cos_wide, sin_wide):
    half = grad.shape[1] // 2
    swapped = jnp.concatenate([grad[:, half:], grad[:, :half]], axis=1)
    return grad * cos_wide + swapped * sin_wide


def front_kernel(
    q_hbm,
    k_hbm,
    v_hbm,
    o_hbm,
    gate_hbm,
    up_hbm,
    small_ref,
    input_ref,
    out_cot_ref,
    row_ref,
    cos_ref,
    sin_ref,
    w_out,
    o_out,
    kv_out,
    g_out,
    t_out,
    e_out,
    gains_ref,
    normed_ref,
    query_ref,
    mixed_ref,
    inv_ref,
    attended_ref,
    middle_ref,
    normed_mid_ref,
    weights,
    full_o,
    small_all,
    strip,
    stage,
    cot_ref,
    kv_own,
    kv,
    s_ref,
    expo,
    send,
    recv,
    local,
):
    c, f = lax.axis_index("ctx"), lax.axis_index("fsdp")
    core = lax.rem(c, 2)
    sibling = (flip(c, 1), f)
    here = (c, f)
    peers = [(c, flip(f, i)) for i in range(1, N_FS)]
    ring = [(flip(c, 2 * i), f) for i in range(1, N_CTX // 2)]
    along = ring[:3]
    near, turn = peers[:3], peers[3]
    greet(peers + ring + [sibling, (flip(c, 8), flip(f, 4))])
    copies = Copies(send, recv)
    tokens, width = input_ref.shape
    rows = q_hbm.shape[0]
    kv_width = KV_HEADS * HD
    cut, units = stage.shape[1:]
    x_part = lax.rem(c, N_FS)

    def local_copy(src, dst, n):
        copy = pltpu.make_async_copy(src, dst, local.at[n])
        copy.start()
        return copy

    mine = weights.at[f]
    q_columns, kv_columns = pl.ds(0, width), pl.ds(width, 2 * kv_width)
    load_k = local_copy(k_hbm, mine.at[:, pl.ds(width, kv_width)], 1)
    load_v = local_copy(v_hbm, mine.at[:, pl.ds(width + kv_width, kv_width)], 2)
    block_rows = pl.ds(pl.multiple_of(lax.rem(x_part, 4) * cut, cut), cut)
    load_gate = local_copy(gate_hbm.at[block_rows], strip.at[0], 3)
    load_up = local_copy(up_hbm.at[block_rows], strip.at[1], 4)
    load_q = local_copy(q_hbm, mine.at[:, q_columns], 0)
    load_o = local_copy(o_hbm, full_o.at[f], 5)
    small_own = local_copy(small_ref, small_all.at[f], 7)
    small_sends = [copies.start(small_ref, small_all.at[f], peer) for peer in peers]
    load_k.wait()
    load_v.wait()
    share_kv = SharedRows(copies, weights, c, f, kv_columns, True)

    def columns(device, part=None):
        where = lax.rem(device[0], N_FS)
        if part is None:
            return g_out.at[lax.div(where, 4), :, lax.rem(where, 4)]
        half = N_FS // 2
        return g_out.at[lax.div(where, 4), pl.ds(part * half, half), lax.rem(where, 4)]

    def block(device, source):
        where = lax.rem(device[0], N_FS)
        return g_out.at[lax.div(where, 4), source, lax.rem(where, 4)]

    load_gate.wait()
    load_up.wait()
    which = lax.div(x_part, 4)
    for owner in range(N_FS):
        stage[owner] = strip[which, :, owner * units : (owner + 1) * units]
    block_own = local_copy(stage.at[f], block(here, f), 8)
    blocks = [copies.start(stage.at[peer[1]], block(here, f), peer) for peer in peers]
    load_q.wait()
    share_q = SharedRows(copies, weights, c, f, q_columns)
    inputs = input_ref[...].astype(F32)
    norm = inputs * lax.rsqrt(jnp.mean(inputs * inputs, axis=-1, keepdims=True) + EPSILON)
    small_own.wait()
    for copy in small_sends:
        copy.wait_recv()

    marks = [0, rows, 2 * rows, 3 * rows, 3 * rows + kv_width // N_FS, small_ref.shape[1]]
    gain_one, gain_two, bias_q, bias_k, bias_v = (
        jnp.concatenate([small_all[owner, :, lo:hi] for owner in range(N_FS)], axis=1)
        for lo, hi in zip(marks[:-1], marks[1:])
    )
    gains_ref[0:1, :] = gain_one
    gains_ref[1:2, :] = gain_two
    normed_ref[...] = (norm * gain_one).astype(BF)
    keep = jnp.where(row_ref[1:2, :] > 0.5, 1.0, 0.0)
    keep = jnp.broadcast_to(keep, (8, tokens)).T[:, 0:1]
    cot_ref[...] = (out_cot_ref[...].astype(F32) * keep).astype(BF)
    load_t = local_copy(cot_ref, t_out.at[0], 6)

    share_kv.pass_y()
    share_kv.pass_z()
    block_own.wait()
    for copy in blocks:
        copy.wait_recv()
    x_one, x_two, x_three = along
    from_one = [copies.start(columns(here, 0), columns(here, 0), x_one)]
    from_three = [copies.start(columns(here, 1), columns(here, 1), x_three)]
    share_kv.wait()
    cos_wide = jnp.concatenate([cos_ref[...], cos_ref[...]], axis=1)
    sin_wide = jnp.concatenate([-sin_ref[...], sin_ref[...]], axis=1)
    full = weights[:, :, width:].reshape(width, 2 * kv_width)
    projected = jnp.dot(normed_ref[...], full, preferred_element_type=F32)
    projected = projected + jnp.concatenate([bias_k, bias_v], axis=1)
    for h in range(KV_HEADS):
        cols = slice(h * HD, (h + 1) * HD)
        kv_own[:tokens, cols] = turn_back(projected[:, cols], cos_wide, sin_wide).astype(BF)
    kv_own[:tokens, kv_width:] = projected[:, kv_width:].astype(BF)
    marks = jnp.concatenate([row_ref[1:2, :]] * (2 * KV_HEADS), axis=1)
    kv_own[tokens:, :] = jnp.broadcast_to(marks, (16, 2 * kv_width)).astype(BF)
    keep_kv = local_copy(kv_own, kv.at[c], 9)
    keys = [copies.start(kv_own, kv.at[c], device) for device in ring]
    kv_rest = [copies.start(kv_own, kv.at[c], sibling)]

    from_one.append(copies.start(columns(here, 1), columns(here, 1), x_one))
    from_three.append(copies.start(columns(here, 0), columns(here, 0), x_three))
    g_rest = [copies.start(columns(here), columns(here), sibling)]

    share_q.pass_y()
    load_o.wait()
    share_o = SharedRows(copies, full_o, c, f)
    half = tokens // 2
    upper, lower = pl.ds(0, half), pl.ds(half, half)
    low_z = copies.start(cot_ref.at[lower], t_out.at[4, lower], turn)
    up_y = [
        copies.start(cot_ref.at[upper], t_out.at[i + 1, upper], device)
        for i, device in enumerate(near)
    ]
    up_z = [copies.start(cot_ref.at[upper], t_out.at[4, upper], turn)]
    low_y = [
        copies.start(cot_ref.at[lower], t_out.at[i + 1, lower], device)
        for i, device in enumerate(near)
    ]
    for key, device in zip(keys, ring):
        key.wait_recv()
        place = kv.at[device[0]]
        kv_rest.append(copies.start(place, place, sibling))
    share_q.pass_z()
    share_q.wait()

    full = weights[:, :, :width].reshape(width, width)
    projected = jnp.dot(normed_ref[...], full, preferred_element_type=F32) + bias_q
    for n in range(HEADS):
        at = (n % GROUP) * tokens
        query_ref[n // GROUP, at : at + tokens, :] = turn_back(
            projected[:, n * HD : (n + 1) * HD], cos_wide, sin_wide
        ).astype(BF)
    save_w = local_copy(weights, w_out, 0)

    from_one[0].wait_recv()
    far = [copies.start(columns(x_one, 0), columns(x_one, 0), x_three)]
    from_three[0].wait_recv()
    far.append(copies.start(columns(x_three, 1), columns(x_three, 1), x_one))
    share_o.pass_y()
    keep_kv.wait()
    for copy in kv_rest:
        copy.wait_recv()
    save_kv = local_copy(kv, kv_out, 1)

    length = N_CTX * tokens
    scale = HD ** (-0.5)
    row_place, row_seg = row_ref[0:1, :], row_ref[1:2, :]
    key_seg = kv[:, tokens : tokens + 16, :HD][:, 0, :].astype(F32).T
    within = lax.broadcasted_iota(jnp.int32, (tokens, tokens), 0)
    saves = []
    for h in range(KV_HEADS):
        query = query_ref[h]
        top = jnp.full((8, GROUP * tokens), -1e30, F32)
        for b in range(N_CTX):
            place = jnp.where(
                within < half, b * half + within, (2 * N_CTX - 1 - b) * half + within - half
            ).astype(F32)
            allowed = (place <= row_place) & (key_seg[:, b : b + 1] == row_seg) & (row_seg > 0.5)
            bias = jnp.where(allowed, 0.0, -1e30).astype(F32)
            scores = contract_cols(kv[b, :tokens, h * HD : (h + 1) * HD], query) * scale
            scores = scores + jnp.concatenate([bias] * GROUP, axis=1)
            s_ref[b * tokens : (b + 1) * tokens, :] = scores
            top = jnp.maximum(top, jnp.max(scores.reshape(tokens // 8, 8, -1), axis=0))
        highest = jnp.maximum(jnp.max(top, axis=0, keepdims=True), -1e29)
        total = jnp.zeros((8, GROUP * tokens), F32)
        mixed = jnp.zeros((HD, GROUP * tokens), F32)
        for j in range(length // CHUNK):
            part = jnp.exp(s_ref[j * CHUNK : (j + 1) * CHUNK, :] - highest)
            total = total + jnp.sum(part.reshape(CHUNK // 8, 8, -1), axis=0)
            low = part.astype(BF)
            expo[h, j * CHUNK : (j + 1) * CHUNK, :] = low
            at = (KV_HEADS + h) * HD
            values = kv[2 * j : 2 * j + 2, :tokens, at : at + HD].reshape(CHUNK, HD)
            mixed = mixed + contract_rows(values, low)
        total = jnp.sum(total, axis=0, keepdims=True)
        inverse = 1.0 / jnp.where(total > 0.5, total, 1.0)
        mixed = mixed * inverse
        mixed_ref[h] = mixed
        inv_ref[h] = jnp.broadcast_to(inverse, (8, GROUP * tokens))
        for i in range(GROUP):
            at = (h * GROUP + i) * HD
            attended_ref[:, at : at + HD] = mixed[:, i * tokens : (i + 1) * tokens].T.astype(BF)
        saves.append(local_copy(expo.at[h], e_out.at[h], 2 + h))
        if h == 0:
            low_z.wait_recv()
            for i, device in enumerate(near):
                low_y.append(copies.start(t_out.at[4, lower], t_out.at[5 + i, lower], device))
            for i, copy in enumerate(up_y):
                copy.wait_recv()
                up_z.append(copies.start(t_out.at[i + 1, upper], t_out.at[5 + i, upper], turn))
            share_o.pass_z()
            for copy, device in ((from_one[1], x_one), (from_three[1], x_three)):
                copy.wait_recv()
                g_rest.append(copies.start(columns(device), columns(device), sibling))

    for copy in far:
        copy.wait_recv()
    g_rest.append(copies.start(columns(x_two), columns(x_two), sibling))

    share_o.wait()
    product = jnp.dot(
        attended_ref[...], full_o[...].reshape(width, width), preferred_element_type=F32
    )
    middle = input_ref[...].astype(F32) + product
    middle_ref[...] = middle
    scale_two = lax.rsqrt(jnp.mean(middle * middle, axis=-1, keepdims=True) + EPSILON)
    normed_mid_ref[...] = (middle * scale_two * gains_ref[1:2, :]).astype(BF)
    save_o = local_copy(full_o, o_out, 4)
    for copy in low_y + up_z + g_rest:
        copy.wait_recv()
    for share in (share_kv, share_q, share_o):
        share.finish()
    for copy in (
        small_sends + blocks + from_one + from_three + far + g_rest + low_y + up_z + up_y
        + [low_z] + keys + kv_rest
    ):
        copy.wait_send()
    for copy in saves + [save_w, save_kv, save_o, load_t]:
        copy.wait()


def front(cid, arrays, vmem_arrays):
    tokens, width = vmem_arrays[1].shape
    rows, all_units = arrays[4].shape
    units = all_units // N_FS
    cut = rows // 4
    kv_width = KV_HEADS * HD
    wide = GROUP * tokens
    length = N_CTX * tokens
    anywhere = pl.BlockSpec(memory_space=pl.ANY)
    vmem = pl.BlockSpec(memory_space=pltpu.VMEM)
    weights = (N_FS, rows, width + 2 * kv_width)
    full_o = (N_FS, rows, width)
    kv = (N_CTX, tokens + 16, 2 * kv_width)
    expo = (KV_HEADS, length, wide)
    return pl.pallas_call(
        front_kernel,
        name="front",
        out_shape=[
            jax.ShapeDtypeStruct(weights, BF),
            jax.ShapeDtypeStruct(full_o, BF),
            jax.ShapeDtypeStruct(kv, BF),
            jax.ShapeDtypeStruct((2, N_FS, 4, cut, units), BF),
            jax.ShapeDtypeStruct((N_FS, tokens, width), BF),
            jax.ShapeDtypeStruct(expo, BF),
            jax.ShapeDtypeStruct((2, width), F32),
            jax.ShapeDtypeStruct((tokens, width), BF),
            jax.ShapeDtypeStruct((KV_HEADS, wide, HD), BF),
            jax.ShapeDtypeStruct((KV_HEADS, HD, wide), F32),
            jax.ShapeDtypeStruct((KV_HEADS, 8, wide), F32),
            jax.ShapeDtypeStruct((tokens, width), BF),
            jax.ShapeDtypeStruct((tokens, width), F32),
            jax.ShapeDtypeStruct((tokens, width), BF),
        ],
        in_specs=[anywhere] * len(arrays) + [vmem] * len(vmem_arrays),
        out_specs=[anywhere] * 6 + [vmem] * 8,
        scratch_shapes=[
            pltpu.VMEM(weights, BF),
            pltpu.VMEM(full_o, BF),
            pltpu.VMEM((N_FS,) + vmem_arrays[0].shape, F32),
            pltpu.VMEM((2, cut, all_units), BF),
            pltpu.VMEM((N_FS, cut, units), BF),
            pltpu.VMEM((tokens, width), BF),
            pltpu.VMEM(kv[1:], BF),
            pltpu.VMEM(kv, BF),
            pltpu.VMEM((length, wide), F32),
            pltpu.VMEM(expo, BF),
            pltpu.SemaphoreType.DMA((104,)),
            pltpu.SemaphoreType.DMA((104,)),
            pltpu.SemaphoreType.DMA((10,)),
        ],
        compiler_params=pltpu.CompilerParams(
            collective_id=cid, has_side_effects=True, vmem_limit_bytes=60 * 2**20
        ),
    )(*arrays, *vmem_arrays)


def back_kernel(
    nm_ref,
    cot_ref,
    gu_ref,
    down_ref,
    expo_hbm,
    kv_hbm,
    o_hbm,
    middle_hbm,
    query_hbm,
    mixed_hbm,
    attended_hbm,
    normed_hbm,
    qkv_hbm,
    gains_ref,
    inv_ref,
    cos_ref,
    sin_ref,
    input_ref,
    all_gu,
    all_dn,
    all_at,
    out_ref,
    out_in,
    gu_x,
    dn_x,
    o_far,
    q_far,
    kv_far,
    vec_sum,
    out_rows,
    in_rows,
    nm,
    part_in,
    gu_in,
    dn_in,
    gu_z,
    dn_z,
    kv_in,
    o_in,
    q_in,
    o_over,
    q_over,
    kv_over,
    q_grad,
    mid_ref,
    gain_grad,
    done_gu,
    done_dn,
    own_gu,
    kv_part,
    kv_parts,
    at_far,
    at_own,
    vec,
    vec_fs,
    vec_mid,
    vec_ctx,
    own_send,
    own_recv,
    part_send,
    part_recv,
    send,
    recv,
    local,
):
    c, f = lax.axis_index("ctx"), lax.axis_index("fsdp")
    core, pair_at = lax.rem(c, 2), lax.div(c, 2)
    x_at, z_at = lax.rem(pair_at, 4), lax.div(pair_at, 4)
    sibling = (flip(c, 1), f)
    partner = (flip(c, 8), f)
    ring = [(flip(c, 2 * i), f) for i in range(1, N_CTX // 2)]
    along = ring[:3]
    peers = [(c, flip(f, i)) for i in range(1, N_FS)]
    greet(ring + peers + [(flip(c, 8), flip(f, i)) for i in range(4, N_FS)] + [sibling])
    copies = Copies(send, recv)
    tokens, width = nm_ref.shape
    units = down_ref.shape[0]
    rows = 2 * tokens
    every = N_FS * tokens
    window, strip = done_dn.shape
    half = units // 2
    side = width // 2
    length = N_CTX * tokens
    scale = HD ** (-0.5)
    near, turn = peers[:3], peers[3]
    cos_wide = jnp.concatenate([cos_ref[...], cos_ref[...]], axis=1)
    sin_wide = jnp.concatenate([sin_ref[...], -sin_ref[...]], axis=1)

    def local_copy(src, dst, n):
        copy = pltpu.make_async_copy(src, dst, local.at[n])
        copy.start()
        return copy

    upper, lower = pl.ds(0, tokens // 2), pl.ds(tokens // 2, tokens // 2)
    up_y = [copies.start(nm_ref.at[upper], nm.at[i + 1, upper], near[i]) for i in range(3)]
    low_z = copies.start(nm_ref.at[lower], nm.at[4, lower], turn)
    low_y = [copies.start(nm_ref.at[lower], nm.at[i + 1, lower], near[i]) for i in range(3)]
    up_z = [copies.start(nm_ref.at[upper], nm.at[4, upper], turn)]

    def part_copy(part, i):
        return pltpu.make_async_remote_copy(
            src_ref=part.at[i],
            dst_ref=part_in.at[i],
            send_sem=part_send.at[i],
            recv_sem=part_recv.at[i],
            device_id=(c, flip(f, i)),
            device_id_type=MESH,
        )

    def x_of(device):
        return lax.rem(lax.div(device[0], 2), 4)

    def strip_of(ref, x):
        return ref.at[:, pl.ds(pl.multiple_of(x * strip, strip), strip)]

    def owner_rows(ref, owner):
        return ref.at[pl.ds(pl.multiple_of(owner * 192, 192), 192)]

    low_y += [
        copies.make(nm.at[4, lower], nm.at[4 + i, lower], near[i - 1]) for i in range(1, 4)
    ]
    up_z += [copies.make(nm.at[i, upper], nm.at[4 + i, upper], turn) for i in range(1, 4)]
    count = N_FS // 2

    def owners_of(z):
        return pl.ds(pl.multiple_of(z * count, count), count)

    def window_of(z):
        return pl.ds(pl.multiple_of(z * (half - window), 16), window)

    x_first, x_second = (
        [
            copies.make(gu_in.at[owners_of(z), x_of(device)], gu_x.at[i, owners_of(z)], device)
            for i, device in enumerate(along)
        ]
        for z in (1 - z_at, z_at)
    )
    z_gu = copies.make(gu_in.at[owners_of(1 - z_at), x_at], gu_z, partner)
    z_dn = copies.make(dn_in.at[window_of(1 - z_at)], dn_z, partner)
    x_dn = [
        copies.make(strip_of(dn_z, x_of(device)), dn_x.at[i], device)
        for i, device in enumerate(along)
    ]

    def sum_gu_x(z, gu_buf, n):
        local_copy(gu_x.at[:, owners_of(z)], gu_buf, n).wait()

        def step(j, carry):
            total = gu_in[z * count + j, x_at].astype(F32)
            for i in range(3):
                total = total + gu_buf[i, j].astype(F32)
            gu_in[z * count + j, x_at] = total.astype(BF)
            return carry

        lax.fori_loop(0, count, step, 0)

    plane = lax.div(f, 4)
    over = (c + core * (flip(c, 8) - c), flip(f, 4))
    block = 4 * 192

    def plane_rows(which):
        return pl.ds(pl.multiple_of(which * block, block), block)

    o_z = copies.make(o_in.at[plane_rows(1 - plane)], o_over, over)
    q_z = copies.make(q_in.at[plane_rows(1 - plane)], q_over, over)
    o_sends = [
        copies.make(owner_rows(o_in, peer[1]), o_far.at[i], peer) for i, peer in enumerate(near)
    ]
    q_sends = [
        copies.make(owner_rows(q_in, peer[1]), q_far.at[i], peer) for i, peer in enumerate(near)
    ]

    def add_over(ref, came):
        def step(m, carry):
            at = pl.multiple_of(m * 192, 192)
            rows = pl.ds(pl.multiple_of(plane * block + m * 192, 192), 192)
            ref[rows, :] = (ref[rows, :].astype(F32) + came[pl.ds(at, 192), :].astype(F32)).astype(BF)
            return carry

        lax.fori_loop(0, 4, step, 0)
    out_sends = [copies.make(out_ref.at[i + 1], out_in.at[i], near[i]) for i in range(3)]
    out_sends += [copies.make(out_ref.at[i + 5], out_in.at[i + 3], near[i]) for i in range(3)]
    kv_sends = [
        copies.make(kv_in.at[lax.div(device[0], 2)], kv_far.at[i], device)
        for i, device in enumerate(ring)
    ]

    def begin(group):
        for copy in group:
            copy.start()

    def feed_forward(cot, gu, down, act, low, part, outs):
        loads = [
            local_copy(nm_ref, nm.at[0], 0),
            local_copy(gu_ref, gu, 1),
            local_copy(cot_ref, cot, 2),
            local_copy(down_ref, down, 3),
        ]
        for load in loads:
            load.wait()

        def weight(which):
            return gu[which].reshape(width, units)

        saves = []

        def pair(s):
            at = s * rows
            span = slice(at, at + rows)
            x = nm[2 * s : 2 * s + 2].reshape(rows, width)
            gate = jnp.dot(x, weight(0), preferred_element_type=F32)
            up = jnp.dot(x, weight(1), preferred_element_type=F32)
            grad = low[1, span, :].astype(F32)
            sigma = jax.nn.sigmoid(gate)
            swish = gate * sigma
            act[span, :] = (swish * up).astype(BF)
            low[0, span, :] = (grad * up * sigma * (1.0 + gate * (1.0 - sigma))).astype(BF)
            low[1, span, :] = (grad * swish).astype(BF)
            summed = contract_cols(low[0, span, :], weight(0))
            summed = summed + contract_cols(low[1, span, :], weight(1))
            part[2 * s : 2 * s + 2] = summed.astype(BF).reshape(2, tokens, width)
            for i in (2 * s, 2 * s + 1):
                if i:
                    part_copy(part, i).start()
            if s > 1:
                saves[s - 2].wait()
            result = jnp.dot(act[span, :], down[...], preferred_element_type=F32)
            outs[s % 2] = result.astype(BF).reshape(2, tokens, width)
            saves.append(local_copy(outs.at[s % 2], out_ref.at[pl.ds(2 * s, 2)], 4 + s % 2))

        def arrived(i):
            up_y[i - 1].wait_recv()
            up_z[i].start()
            low_y[i - 1].wait_recv()

        def activation_grad(s, carry):
            at = pl.multiple_of(s * rows, rows)
            rows_of = cot[pl.ds(2 * s, 2)].reshape(rows, width)
            low[1, pl.ds(at, rows), :] = contract_cols(rows_of, down[...]).astype(BF)
            return carry

        lax.fori_loop(0, N_FS // 2, activation_grad, 0)
        arrived(1)
        low_z.wait_recv()
        begin(low_y[3:])
        pair(0)
        arrived(2)
        arrived(3)
        pair(1)
        up_z[0].wait_recv()
        up_z[1].wait_recv()
        low_y[3].wait_recv()
        pair(2)
        for i in (2, 3):
            up_z[i].wait_recv()
            low_y[2 + i].wait_recv()
        pair(3)

        def gate_up(which):
            def step(m, carry):
                at = pl.multiple_of(m * 384, 384)
                x = nm[:, :, pl.ds(at, 384)].reshape(every, 384)
                grad = contract_rows(x, low[which]).astype(BF)
                gu[which, pl.ds(2 * m, 2)] = grad.reshape((2,) + gu.shape[2:])
                return carry

            lax.fori_loop(0, width // 384, step, 0)

        gate_up(1 - core)
        swap_gu = copies.start(gu.at[1 - core], gu_in, sibling)
        gate_up(core)
        swap_gu.wait_recv()

        def add_gu(g, carry):
            gu_in[g] = (gu[core, g].astype(F32) + gu_in[g].astype(F32)).astype(BF)
            return carry

        lax.fori_loop(0, N_FS, add_gu, 0)
        begin(x_first)
        begin(x_second)
        turned = cot[...].reshape(every, width)

        def down_rows(m, carry):
            at = pl.multiple_of(m * 256, 256)
            down[pl.ds(at, 256), :] = contract_rows(act[:, pl.ds(at, 256)], turned).astype(BF)
            return carry

        whole = units // 256
        lax.fori_loop(0, whole, down_rows, 0)
        if units % 256:
            down[whole * 256 :, :] = contract_rows(act[:, whole * 256 :], turned).astype(BF)
        swap_dn = copies.start(
            down.at[pl.ds(pl.multiple_of((1 - core) * half, 16), half)], dn_in, sibling
        )
        swap_dn.wait_recv()

        def add_dn(m, carry):
            at = pl.multiple_of(m * 112, 16)
            own = down[pl.ds(pl.multiple_of(core * half + m * 112, 16), 112), :]
            dn_in[pl.ds(at, 112), :] = (
                own.astype(F32) + dn_in[pl.ds(at, 112), :].astype(F32)
            ).astype(BF)
            return carry

        lax.fori_loop(0, half // 112, add_dn, 0)
        z_dn.start()
        total = part[0].astype(F32)
        for i in range(1, N_FS):
            part_copy(part, i).wait_recv()
            total = total + part_in[i].astype(F32)
        mid_ref[...] = total
        for i in range(1, N_FS):
            part_copy(part, i).wait_send()
        for copy in [swap_gu, swap_dn]:
            copy.wait_send()
        for copy in saves[2:]:
            copy.wait()

    pl.run_scoped(
        feed_forward,
        pltpu.VMEM(cot_ref.shape, BF),
        pltpu.VMEM(gu_ref.shape, BF),
        pltpu.VMEM(down_ref.shape, BF),
        pltpu.VMEM((every, units), BF),
        pltpu.VMEM((2, every, units), BF),
        pltpu.VMEM((N_FS, tokens, width), BF),
        pltpu.VMEM((2, 2, tokens, width), BF),
    )
    begin(out_sends)

    def columns_of(which):
        return pl.ds(pl.multiple_of(which * side, side), side)

    def half_product(left, right, which, out):
        def step(m, carry):
            at = pl.multiple_of(m * 256, 256)
            out[pl.ds(at, 256), :] = contract_rows(
                left[:, pl.ds(at, 256)], right[:, columns_of(which)]
            ).astype(BF)
            return carry

        lax.fori_loop(0, width // 256, step, 0)

    def add_product(left, right, out):
        def step(m, carry):
            at = pl.multiple_of(m * 256, 256)
            product = contract_rows(left[:, pl.ds(at, 256)], right[:, columns_of(core)])
            out[pl.ds(at, 256), :] = (product + out[pl.ds(at, 256), :].astype(F32)).astype(BF)
            return carry

        lax.fori_loop(0, width // 256, step, 0)

    def attention(branch, back, attended, normed, out_half, dkv):
        load_at = local_copy(attended_hbm, attended, 0)
        load_nm = local_copy(normed_hbm, normed, 1)

        def second_norm(full_o, middle_ref):
            load_mid = local_copy(middle_hbm, middle_ref, 2)
            load_o = local_copy(o_hbm, full_o, 3)
            load_mid.wait()
            middle = middle_ref[...]
            scale_two = lax.rsqrt(jnp.mean(middle * middle, axis=-1, keepdims=True) + EPSILON)
            norm = middle * scale_two
            grad = mid_ref[...]
            gain_grad[...] = jnp.sum(grad * norm, axis=0, keepdims=True)
            scaled = grad * gains_ref[1:2, :]
            cot_copy = local_copy(cot_ref.at[0], back, 6)
            cot_copy.wait()
            mid = back[...].astype(F32) + scale_two * (
                scaled - norm * jnp.mean(scaled * norm, axis=-1, keepdims=True)
            )
            mid_ref[...] = mid
            branch[...] = mid.astype(BF)
            load_o.wait()
            back[...] = contract_cols(branch[...], full_o[...]).astype(BF)

        pl.run_scoped(second_norm, pltpu.VMEM(o_hbm.shape, BF), pltpu.VMEM((tokens, width), F32))
        load_at.wait()
        load_nm.wait()
        half_product(attended, branch, 1 - core, out_half)
        swap_o = copies.start(out_half, o_in, sibling)

        def heads(expo, kv, query_ref, mixed_ref, gu_buf):
            loads = [
                local_copy(kv_hbm, kv, 2),
                local_copy(query_hbm, query_ref, 3),
                local_copy(mixed_hbm, mixed_ref, 4),
                local_copy(expo_hbm, expo, 5),
            ]
            for load in loads:
                load.wait()
            for h in range(KV_HEADS):
                if h == 1:
                    swap_o.wait_recv()
                    add_product(attended, branch, o_in)
                    o_z.start()
                    for copy in x_first:
                        copy.wait_recv()
                    sum_gu_x(1 - z_at, gu_buf, 6)
                    z_gu.start()
                query = query_ref[h]
                head = back[:, h * GROUP * HD : (h + 1) * GROUP * HD]
                grads = jnp.concatenate(
                    [head[:, i * HD : (i + 1) * HD] for i in range(GROUP)], axis=0
                )
                inverse = inv_ref[h, 0:1, :]
                turned = grads.astype(F32).T
                weighted = jnp.sum(turned * mixed_ref[h], axis=0, keepdims=True)
                factor = inverse * scale
                offset = weighted * factor
                grads_scaled = (turned * inverse).T.astype(BF)
                dq = jnp.zeros((HD, GROUP * tokens), F32)
                for j in range(length // CHUNK):
                    part = expo[h, j * CHUNK : (j + 1) * CHUNK, :]
                    cols = slice(h * HD, (h + 1) * HD)
                    keys = kv[2 * j : 2 * j + 2, :tokens, cols].reshape(CHUNK, HD)
                    v_cols = slice((KV_HEADS + h) * HD, (KV_HEADS + h + 1) * HD)
                    values = kv[2 * j : 2 * j + 2, :tokens, v_cols].reshape(CHUNK, HD)
                    prob_grad = contract_cols(values, grads)
                    score_grad = (part.astype(F32) * (prob_grad * factor - offset)).astype(BF)
                    dk = jnp.dot(score_grad, query, preferred_element_type=F32).astype(BF)
                    dv = jnp.dot(part, grads_scaled, preferred_element_type=F32).astype(BF)
                    for side_core in range(2):
                        cut = slice(side_core * tokens, (side_core + 1) * tokens)
                        dkv[side_core, j, :, cols] = dk[cut]
                        dkv[side_core, j, :, v_cols] = dv[cut]
                    dq = dq + contract_rows(keys, score_grad)
                for i in range(GROUP):
                    at = (h * GROUP + i) * HD
                    q_grad[:, at : at + HD] = turn_back(
                        dq[:, i * tokens : (i + 1) * tokens].T, cos_wide, sin_wide
                    ).astype(BF)

        pl.run_scoped(
            heads,
            pltpu.VMEM(expo_hbm.shape, BF),
            pltpu.VMEM(kv_hbm.shape, BF),
            pltpu.VMEM(query_hbm.shape, BF),
            pltpu.VMEM(mixed_hbm.shape, F32),
            pltpu.VMEM((3, count) + gu_x.shape[2:], BF),
        )
        swap_kv = copies.start(dkv.at[1 - core], kv_in, sibling)

        swap_o.wait_send()
        half_product(normed, q_grad, 1 - core, out_half)
        swap_q = copies.start(out_half, q_in, sibling)
        swap_kv.wait_recv()
        kv_in[...] = (dkv[core].astype(F32) + kv_in[...].astype(F32)).astype(BF)
        begin(kv_sends)
        z_dn.wait_recv()
        dn_z[...] = (dn_z[...].astype(F32) + dn_in[window_of(z_at), :].astype(F32)).astype(BF)
        begin(x_dn)
        o_z.wait_recv()
        add_over(o_in, o_over)
        begin(o_sends)
        swap_q.wait_recv()
        add_product(normed, q_grad, q_in)
        swap_kv.wait_send()
        swap_q.wait_send()

    pl.run_scoped(
        attention,
        pltpu.VMEM((tokens, width), BF),
        pltpu.VMEM((tokens, width), BF),
        pltpu.VMEM((tokens, width), BF),
        pltpu.VMEM((tokens, width), BF),
        pltpu.VMEM((width, side), BF),
        pltpu.VMEM((2, N_CTX // 2, tokens, kv_in.shape[2]), BF),
    )

    here, far = (c, f), (partner[0], f)
    x_one, x_two, x_three = along
    kv_width = KV_HEADS * HD
    at_rows, at_cols = at_own.shape

    def z_of(device):
        return lax.div(device[0], 8)

    def gu_place(device, part=None):
        size = count if part is None else count // 2
        start = count * z_of(device) + (0 if part is None else part * size)
        return all_gu.at[lax.rem(device[0], 2), x_of(device), pl.ds(start, size)]

    def dn_place(device, part=None):
        columns = pl.ds(pl.multiple_of(x_of(device) * strip, strip), strip)
        size = window // (1 if part is None else 2)
        span = pl.ds(0 if part is None else part * size, size)
        return all_dn.at[lax.rem(device[0], 2), z_of(device), span, columns]

    def at_span(device):
        return (
            pl.ds(pl.multiple_of(x_of(device) * at_rows, at_rows), at_rows),
            pl.ds(pl.multiple_of(z_of(device) * at_cols, at_cols), at_cols),
        )

    def at_place(device):
        return all_at.at[(lax.rem(device[0], 2),) + at_span(device)]

    def tail(gu_buf, dn_buf, far_buf, kv_buf, full_qkv, proj, kv_out, kv_keep, at_all, out_buf):
        rest, own = [], []
        load_qkv = local_copy(qkv_hbm, full_qkv, 0)
        load_nm = local_copy(normed_hbm, out_buf.at[N_FS - 1], 1)

        for copy in x_second:
            copy.wait_recv()
        sum_gu_x(z_at, gu_buf, 2)
        z_gu.wait_recv()

        def add_gu_z(j, carry):
            mine = gu_in[z_at * count + j, x_at].astype(F32)
            done_gu[j] = (mine + gu_z[j].astype(F32)).astype(BF)
            return carry

        lax.fori_loop(0, count, add_gu_z, 0)
        spot = lax.rem(f, 4)
        owners = [
            (8 * plane + lax.rem(c, 8), 4 * z_at + lax.rem(flip(f, i), 4)) for i in range(4)
        ]

        def gu_copy(i):
            return pltpu.make_async_remote_copy(
                src_ref=done_gu.at[lax.rem(flip(f, i), 4)],
                dst_ref=own_gu.at[spot],
                send_sem=own_send.at[i],
                recv_sem=own_recv.at[i],
                device_id=owners[i],
                device_id_type=MESH,
            )

        gu_own = pltpu.make_async_copy(done_gu.at[spot], own_gu.at[spot], local.at[4])

        @pl.when(plane == z_at)
        def _():
            gu_own.start()

        @pl.when(plane != z_at)
        def _():
            gu_copy(0).start()

        for i in range(1, 4):
            gu_copy(i).start()
        q_z.start()

        load_qkv.wait()
        in_norm_grad = contract_cols(q_grad[...], full_qkv[:, :width])

        for copy in kv_sends:
            copy.wait_recv()
        local_copy(kv_far, kv_buf, 3).wait()
        total = kv_in[pair_at].astype(F32)
        for i in range(N_CTX // 2 - 1):
            total = total + kv_buf[i].astype(F32)
        for h in range(KV_HEADS):
            at = width + h * HD
            proj[:, at : at + HD] = turn_back(
                total[:, h * HD : (h + 1) * HD], cos_wide, sin_wide
            ).astype(BF)
        proj[:, width + kv_width :] = total[:, kv_width:].astype(BF)
        proj[:, :width] = q_grad[...]

        def side_of(which):
            return pl.ds(pl.multiple_of(width + which * kv_width, kv_width), kv_width)

        load_nm.wait()
        normed = out_buf[N_FS - 1]
        kv_out[...] = contract_rows(normed, proj[:, side_of(1 - core)]).astype(BF)
        swap_part = copies.start(kv_out, kv_part, sibling)
        kv_keep[...] = contract_rows(normed, proj[:, side_of(core)]).astype(BF)

        swap_part.wait_recv()
        kv_part[...] = (kv_part[...].astype(F32) + kv_keep[...].astype(F32)).astype(BF)

        def rows_of(owner):
            return pl.ds(pl.multiple_of(owner * 192, 192), 192)

        part_z = copies.start(kv_part.at[plane_rows(1 - plane)], kv_over, over)
        q_z.wait_recv()
        add_over(q_in, q_over)
        begin(q_sends)

        @pl.when(plane == z_at)
        def _():
            gu_own.wait()

        @pl.when(plane != z_at)
        def _():
            gu_copy(0).wait()

        for i in range(1, 4):
            gu_copy(i).wait()
        gather_z = [copies.start(own_gu, gu_place(here), partner)]
        gu_xs = [copies.start(own_gu, gu_place(here), device) for device in (x_one, x_three)]
        rest.append(copies.start(own_gu, gu_place(here), sibling))
        own.append(local_copy(own_gu, gu_place(here), 6))

        forwards = []

        def around(place, one, three, z):
            sent = []
            for copy, device, part, other in ((one, x_one, 0, x_three), (three, x_three, 1, x_one)):
                at = (flip(device[0], 8), f) if z else device
                copy.wait_recv()
                sent.append(copies.start(place(at, part), place(at, part), other))
                rest.append(copies.start(place(at), place(at), sibling))
            forwards.extend(sent)
            return sent

        def opposite(place, sent, z):
            at = (flip(x_two[0], 8), f) if z else x_two
            for copy in sent:
                copy.wait_recv()
            rest.append(copies.start(place(at), place(at), sibling))

        part_z.wait_recv()
        add_over(kv_part, kv_over)
        part_sends = [
            copies.start(kv_part.at[rows_of(peer[1])], kv_parts.at[i], peer)
            for i, peer in enumerate(near)
        ]

        in_norm_grad = in_norm_grad + contract_cols(proj[:, width:], full_qkv[:, width:])
        inputs = input_ref[...].astype(F32)
        scale_one = lax.rsqrt(jnp.mean(inputs * inputs, axis=-1, keepdims=True) + EPSILON)
        norm = inputs * scale_one
        gain_one_grad = jnp.sum(in_norm_grad * norm, axis=0, keepdims=True)
        scaled = in_norm_grad * gains_ref[0:1, :]
        in_rows[...] = mid_ref[...] + scale_one * (
            scaled - norm * jnp.mean(scaled * norm, axis=-1, keepdims=True)
        )
        bias_grad = jnp.sum(proj[...].astype(F32), axis=0, keepdims=True)
        row = 0
        for vector in (gain_one_grad, gain_grad[...], bias_grad):
            for n in range(vector.shape[1] // 128):
                vec[row : row + 1, :] = vector[:, n * 128 : (n + 1) * 128]
                row += 1
        vec_sends = [copies.start(vec, vec_fs.at[i], peer) for i, peer in enumerate(peers)]


        gather_z[0].wait_recv()
        gu_xs2 = [copies.start(gu_place(far), gu_place(far), device) for device in (x_one, x_three)]
        rest.append(copies.start(gu_place(far), gu_place(far), sibling))
        load_mid = local_copy(middle_hbm, mid_ref, 10)
        gu_f = around(gu_place, *gu_xs, False)
        for copy in x_dn:
            copy.wait_recv()
        local_copy(dn_x, dn_buf, 5).wait()
        total = dn_z[:, pl.ds(pl.multiple_of(x_at * strip, strip), strip)].astype(F32)
        for i in range(3):
            total = total + dn_buf[i].astype(F32)
        done_dn[...] = total.astype(BF)
        own.append(local_copy(done_dn, dn_place(here), 7))
        gather_z.append(copies.start(done_dn, dn_place(here), partner))
        dn_xs = [copies.start(done_dn, dn_place(here), device) for device in (x_one, x_three)]
        rest.append(copies.start(done_dn, dn_place(here), sibling))

        owned = pl.ds(pl.multiple_of(f * 192, 192), 192)
        for n, (ref, sends, arrived) in enumerate(((o_in, o_sends, o_far), (q_in, q_sends, q_far))):
            for copy in sends:
                copy.wait_recv()
            local_copy(arrived, far_buf, 8 + n).wait()
            total = ref[owned, :].astype(F32)
            for i in range(3):
                total = total + far_buf[i].astype(F32)
            at_all[:, n * side : (n + 1) * side] = total.astype(BF)
        for copy in part_sends:
            copy.wait_recv()
        total = kv_part[owned, :].astype(F32)
        for i in range(3):
            total = total + kv_parts[i].astype(F32)
        at_all[:, 2 * side :] = total.astype(BF)
        at_sends = [
            copies.start(at_all.at[at_span(device)], at_far.at[i], device)
            for i, device in enumerate(ring)
        ]
        for copy in out_sends:
            copy.wait_recv()
        local_copy(out_ref.at[4], out_buf.at[1], 2).wait()
        local_copy(out_in.at[pl.ds(3, 3)], out_buf.at[pl.ds(2, 3)], 3).wait()
        total = out_buf[1].astype(F32)
        for i in range(3):
            total = total + out_buf[2 + i].astype(F32)
        out_buf[0] = total.astype(BF)

        gather_z[1].wait_recv()
        dn_xs2 = [copies.start(dn_place(far), dn_place(far), device) for device in (x_one, x_three)]
        rest.append(copies.start(dn_place(far), dn_place(far), sibling))
        gu_f2 = around(gu_place, *gu_xs2, True)
        for copy in vec_sends:
            copy.wait_recv()
        total = vec[...]
        for i in range(N_FS - 1):
            total = total + vec_fs[i]
        vec_mid[...] = total
        vec_near = [copies.start(vec_mid, vec_ctx.at[c], device) for device in ring]
        rest.append(copies.start(vec_mid, vec_ctx.at[c], sibling))
        vec_ctx[pl.ds(c, 1)] = total[None]
        for copy in at_sends:
            copy.wait_recv()
        total = at_all[at_span(here)].astype(F32)
        for i in range(N_CTX // 2 - 1):
            total = total + at_far[i].astype(F32)
        at_own[...] = total.astype(BF)
        at_near = [copies.start(at_own, at_place(here), device) for device in ring]
        rest.append(copies.start(at_own, at_place(here), sibling))
        out_z = copies.start(out_buf.at[0], out_in.at[N_FS - 2], turn)
        own.append(local_copy(at_own, at_place(here), 11))
        dn_f = around(dn_place, *dn_xs, False)
        for copy, device in zip(vec_near, ring):
            copy.wait_recv()
            place = vec_ctx.at[device[0]]
            rest.append(copies.start(place, place, sibling))
        dn_f2 = around(dn_place, *dn_xs2, True)
        opposite(gu_place, gu_f, False)
        opposite(dn_place, dn_f, False)
        out_z.wait_recv()
        local_copy(out_ref.at[0], out_buf.at[1], 1).wait()
        local_copy(out_in.at[pl.ds(0, 3)], out_buf.at[pl.ds(2, 3)], 3).wait()
        local_copy(out_in.at[N_FS - 2], out_buf.at[5], 2).wait()
        load_mid.wait()
        total = mid_ref[...]
        for i in range(1, 6):
            total = total + out_buf[i].astype(F32)
        out_rows[...] = total.astype(BF)
        opposite(gu_place, gu_f2, True)
        opposite(dn_place, dn_f2, True)
        for copy, device in zip(at_near, ring):
            copy.wait_recv()
            rest.append(copies.start(at_place(device), at_place(device), sibling))
        for copy in (
            [swap_part, part_z, out_z] + part_sends + gather_z + gu_xs + dn_xs + gu_xs2 + dn_xs2
            + forwards + at_sends + at_near + vec_sends + vec_near
        ):
            copy.wait_send()
        for copy in rest:
            copy.wait()
        total = vec_ctx[0]
        for i in range(1, N_CTX):
            total = total + vec_ctx[i]
        vec_sum[...] = total
        for copy in own:
            copy.wait()

    pl.run_scoped(
        tail,
        pltpu.VMEM((3, count) + gu_x.shape[2:], BF),
        pltpu.VMEM(dn_x.shape, BF),
        pltpu.VMEM(o_far.shape, BF),
        pltpu.VMEM(kv_far.shape, BF),
        pltpu.VMEM(qkv_hbm.shape, BF),
        pltpu.VMEM((tokens, qkv_hbm.shape[1]), BF),
        pltpu.VMEM(kv_part.shape, BF),
        pltpu.VMEM(kv_part.shape, BF),
        pltpu.VMEM((width // N_FS, width + kv_width), BF),
        pltpu.VMEM((N_FS, tokens, width), BF),
    )
    for copy in (
        up_y + [low_z] + low_y + up_z + x_first + x_second + x_dn + o_sends + q_sends + kv_sends + out_sends
        + [o_z, q_z, z_gu, z_dn]
    ):
        copy.wait_send()


def backward(cid, arrays, vmem_arrays):
    normed, cot_all, columns, down_weight, expo, kv_all, full_o = arrays[:7]
    tokens, width = normed.shape
    units = down_weight.shape[0]
    piece = columns.shape[3]
    half = units // 2
    strip = width // 4
    window = half // 2 + 8
    side = width // 2
    kv_width = KV_HEADS * HD
    rows = width // N_FS
    anywhere = pl.BlockSpec(memory_space=pl.ANY)
    vmem = pl.BlockSpec(memory_space=pltpu.VMEM)
    at_width = width + kv_width
    in_place = [
        ((2, 4, N_FS, piece, units), BF),
        ((2, 2, window, width), BF),
        ((2, rows, at_width), BF),
        ((N_FS, tokens, width), BF),
        ((N_FS - 1, tokens, width), BF),
        ((3, N_FS, piece, units), BF),
        ((3, window, strip), BF),
        ((3, rows, side), BF),
        ((3, rows, side), BF),
        ((N_CTX // 2 - 1, tokens, 2 * kv_width), BF),
    ]
    in_vmem = [((40, 128), F32), ((tokens, width), BF), ((tokens, width), F32)]
    results = pl.pallas_call(
        back_kernel,
        name="back",
        out_shape=[jax.ShapeDtypeStruct(*o) for o in in_place + in_vmem],
        in_specs=[anywhere] * len(arrays) + [vmem] * len(vmem_arrays),
        out_specs=[anywhere] * len(in_place) + [vmem] * len(in_vmem),
        scratch_shapes=[
            pltpu.VMEM((N_FS, tokens, width), BF),
            pltpu.VMEM((N_FS, tokens, width), BF),
            pltpu.VMEM((N_FS, 4, piece, units), BF),
            pltpu.VMEM((half, width), BF),
            pltpu.VMEM((N_FS // 2, piece, units), BF),
            pltpu.VMEM((window, width), BF),
            pltpu.VMEM((N_CTX // 2, tokens, 2 * kv_width), BF),
            pltpu.VMEM((width, side), BF),
            pltpu.VMEM((width, side), BF),
            pltpu.VMEM((width // 2, side), BF),
            pltpu.VMEM((width // 2, side), BF),
            pltpu.VMEM((width // 2, kv_width), BF),
            pltpu.VMEM((tokens, width), BF),
            pltpu.VMEM((tokens, width), F32),
            pltpu.VMEM((1, width), F32),
            pltpu.VMEM((N_FS // 2, piece, units), BF),
            pltpu.VMEM((window, strip), BF),
            pltpu.VMEM((N_FS // 2, piece, units), BF),
            pltpu.VMEM((width, kv_width), BF),
            pltpu.VMEM((3, rows, kv_width), BF),
            pltpu.VMEM((N_CTX // 2 - 1, rows // 4, at_width // 2), BF),
            pltpu.VMEM((rows // 4, at_width // 2), BF),
            pltpu.VMEM((40, 128), F32),
            pltpu.VMEM((N_FS - 1, 40, 128), F32),
            pltpu.VMEM((40, 128), F32),
            pltpu.VMEM((N_CTX, 40, 128), F32),
            pltpu.SemaphoreType.DMA((4,)),
            pltpu.SemaphoreType.DMA((4,)),
            pltpu.SemaphoreType.DMA((N_FS,)),
            pltpu.SemaphoreType.DMA((N_FS,)),
            pltpu.SemaphoreType.DMA((150,)),
            pltpu.SemaphoreType.DMA((150,)),
            pltpu.SemaphoreType.DMA((12,)),
        ],
        compiler_params=pltpu.CompilerParams(
            collective_id=cid, has_side_effects=True, vmem_limit_bytes=62 * 2**20
        ),
    )(*arrays, *vmem_arrays)
    return results[:3] + results[len(in_place) :]


def wide_kernel(gu_ref, gate_ref, up_ref):
    for which, out in enumerate((gate_ref, up_ref)):
        out[...] = jnp.concatenate(
            [gu_ref[which, 0, source].astype(F32) for source in range(N_FS)], axis=1
        )


def wide_results(all_gu):
    piece, units = all_gu.shape[3:]
    parts = all_gu.shape[1]
    shape = jax.ShapeDtypeStruct((parts * piece, N_FS * units), F32)
    return pl.pallas_call(
        wide_kernel,
        name="wide_results",
        grid=(parts,),
        in_specs=[pl.BlockSpec((2, 1, N_FS, piece, units), lambda p: (0, p, 0, 0, 0))],
        out_specs=[pl.BlockSpec((piece, N_FS * units), lambda p: (p, 0))] * 2,
        out_shape=[shape, shape],
        compiler_params=pltpu.CompilerParams(vmem_limit_bytes=60 * 2**20),
    )(all_gu)


def rest_kernel(dn_ref, at_ref, down_ref, o_ref, q_ref, k_ref, v_ref):
    z = lax.rem(pl.program_id(0), 2)
    rows = down_ref.shape[0]
    block = dn_ref[0, 0].astype(F32)
    down_ref[...] = jnp.where(z == 0, block[:rows], block[8 : 8 + rows])
    side = o_ref.shape[1] // 2
    for n in range(2):
        part = at_ref[n].astype(F32)
        o_ref[:, n * side : (n + 1) * side] = part[:, :side]
        q_ref[:, n * side : (n + 1) * side] = part[:, side : 2 * side]
        (k_ref, v_ref)[n][...] = part[:, 2 * side :]


def rest_results(all_dn, all_at):
    window, width = all_dn.shape[2:]
    rows = window - 8
    own, at_width = all_at.shape[1:]
    kv_width = KV_HEADS * HD
    return pl.pallas_call(
        rest_kernel,
        name="rest_results",
        grid=(4,),
        in_specs=[
            pl.BlockSpec((1, 1, window, width), lambda n: (n // 2, n % 2, 0, 0)),
            pl.BlockSpec((2, own // 4, at_width), lambda n: (0, n, 0)),
        ],
        out_specs=[
            pl.BlockSpec((rows, width), lambda n: (n, 0)),
            pl.BlockSpec((own // 4, width), lambda n: (n, 0)),
            pl.BlockSpec((own // 4, width), lambda n: (n, 0)),
            pl.BlockSpec((own // 4, kv_width), lambda n: (n, 0)),
            pl.BlockSpec((own // 4, kv_width), lambda n: (n, 0)),
        ],
        out_shape=[
            jax.ShapeDtypeStruct((4 * rows, width), F32),
            jax.ShapeDtypeStruct((own, width), F32),
            jax.ShapeDtypeStruct((own, width), F32),
            jax.ShapeDtypeStruct((own, kv_width), F32),
            jax.ShapeDtypeStruct((own, kv_width), F32),
        ],
        compiler_params=pltpu.CompilerParams(vmem_limit_bytes=60 * 2**20),
    )(all_dn, all_at)


def body(
    layer_input,
    segments,
    positions,
    attn_norm,
    q_weight,
    q_bias,
    k_weight,
    k_bias,
    v_weight,
    v_bias,
    o_weight,
    mlp_norm,
    gate_weight,
    up_weight,
    down_weight,
    out_cotangent,
):
    tokens, width = layer_input.shape[1:]
    rows = gate_weight.shape[0]
    units = gate_weight.shape[1] // N_FS
    q_width = HEADS * HD
    kv_width = KV_HEADS * HD
    half_block = tokens // 2
    ctx = lax.axis_index("ctx")
    segment = segments[0]
    small = jnp.concatenate([attn_norm, mlp_norm, q_bias, k_bias, v_bias]).astype(F32)[None]
    cosine, sine = rope_tables(positions[0], HD)
    within = jnp.arange(tokens, dtype=jnp.int32)
    row_place = jnp.where(
        within < half_block,
        ctx * half_block + within,
        (2 * N_CTX - 1 - ctx) * half_block + within - half_block,
    )
    row_info = jnp.stack([row_place.astype(F32), segment.astype(F32)])
    (
        full_qkv,
        full_o,
        kv_all,
        columns,
        cot_all,
        expo,
        gains,
        normed_in,
        query,
        mixed,
        inverse,
        attended,
        middle,
        normed_mid,
    ) = front(
        1,
        (q_weight, k_weight, v_weight, o_weight, gate_weight, up_weight),
        (small, layer_input[0], out_cotangent[0], row_info, cosine, sine),
    )
    full_qkv = full_qkv.reshape(width, q_width + 2 * kv_width)
    full_o = full_o.reshape(q_width, width)
    all_gu, all_dn, all_at, all_vec, output_rows, input_rows = backward(
        3,
        (
            normed_mid,
            cot_all,
            columns,
            down_weight,
            expo,
            kv_all,
            full_o,
            middle,
            query,
            mixed,
            attended,
            normed_in,
            full_qkv,
        ),
        (gains, inverse, cosine, sine, layer_input[0]),
    )
    gate_grad, up_grad = wide_results(all_gu)
    down_grad, o_grad, q_weight_grad, k_grad, v_grad = rest_results(all_dn, all_at)
    flat_vec = all_vec.reshape(-1)
    mine = lax.axis_index("fsdp")
    vectors = []
    start = 0
    for whole in (width, width, q_width, kv_width, kv_width):
        part = whole // N_FS
        vectors.append(lax.dynamic_slice_in_dim(flat_vec, start + mine * part, part, 0))
        start += whole
    return (
        output_rows[None],
        input_rows[None],
        vectors[0],
        q_weight_grad,
        vectors[2],
        k_grad,
        vectors[3],
        v_grad,
        vectors[4],
        o_grad,
        vectors[1],
        gate_grad,
        up_grad,
        down_grad,
    )


def solution(mesh):
    placed = (
        P("fsdp", "ctx", None),
        P("fsdp", "ctx"),
        P("fsdp", "ctx"),
        P("fsdp"),
        P("fsdp", None),
        P("fsdp"),
        P("fsdp", None),
        P("fsdp"),
        P("fsdp", None),
        P("fsdp"),
        P("fsdp", None),
        P("fsdp"),
        P("fsdp", None),
        P("fsdp", None),
        P("fsdp", None),
        P("fsdp", "ctx", None),
    )
    return jax.shard_map(
        body,
        mesh=mesh,
        in_specs=placed,
        out_specs=(
            P("fsdp", "ctx", None),
            P("fsdp", "ctx", None),
            P("fsdp"),
            P("fsdp", None),
            P("fsdp"),
            P("fsdp", None),
            P("fsdp"),
            P("fsdp", None),
            P("fsdp"),
            P("fsdp", None),
            P("fsdp"),
            P("fsdp", None),
            P("fsdp", None),
            P("fsdp", None),
        ),
        check_vma=False,
    )
```
